32 devices in a mesh: grp: 2 (over y), gene: 4 (over z), row: 4 (over x, core).
Axes of the slice: x: 2, y: 2, z: 4, core: 2. Of those that a mesh axis runs over, the one named last changes fastest.
Arguments:
- x_slab: bfloat16 [24576, 2560], P(('grp', 'row'), 'gene'), parts along dimension 0, may hold values from -6 to 6
- cell_factor: bfloat16 [4096, 128], P(('grp', 'row')), parts along dimension 0, may hold values from -1.5 to 1.5
- row_index: int32 [24576], P(('grp', 'row')), parts along dimension 0, may hold values from 0 to 2047, as said below
- gene_scale: float32 [5120], P(('grp', 'gene')), parts along dimension 0, may hold values from 0.3 to 3
- gene_factor: float32 [5120, 128], P(('grp', 'gene', 'row')), parts along dimension 0, may hold values from -1.5 to 1.5
- first_moment: float32 [5120, 128], P(('grp', 'gene', 'row')), parts along dimension 0, may hold values from -1.2 to 1.2
- second_moment: float32 [5120, 128], P(('grp', 'gene', 'row')), parts along dimension 0, may hold values from 0.05 to 1
Outputs:
- grad_cells: float32 [24576, 128], P(('grp', 'row', 'gene')), parts along dimension 0
- new_factor: float32 [5120, 128], P(('grp', 'gene', 'row')), parts along dimension 0
- new_first: float32 [5120, 128], P(('grp', 'gene', 'row')), parts along dimension 0
- new_second: float32 [5120, 128], P(('grp', 'gene', 'row')), parts along dimension 0
The draws below stay inside these ranges and needn't reach their ends.
There are 2 independent parts, one for each index of `grp`. The reference program is written for one: setup_inputs(seed, part) draws one part's arguments, and reference() takes and returns one part's arrays. A program takes and returns all parts, laid end to end along the dimension named above; each array names one. Nothing has to cross between parts.
Inputs may be any that keep to these rules, and one draw needn't show every extreme that they name: `row_index`: rows r * 3072 to (r + 1) * 3072 - 1 name cells r * 512 to (r + 1) * 512 - 1; cells may repeat.
All inputs are finite; a program needn't handle non-finite values.
Results may differ from the reference program's by a relative error of at most 0.008.
Values may be sent and summed in bfloat16 or wider, within the bound.
No kernel may reach another device: no remote copies, remote signals or barrier semaphores. Data moves between devices by JAX's collectives and lax.ppermute only.
A program may use at most 64 MiB of HBM per device.

```python
import math
import jax
import jax.numpy as jnp
from jax import lax

R = 128
B_DEV = 3072
G_DEV = 640
CELLS_DEV = 512
B = 12288
G = 2560
CELLS = 2048


def draw_row_index(key, part):
    blocks = B // B_DEV
    key_a, key_b, key_c = jax.random.split(key, 3)
    local = jax.random.randint(key_a, (blocks, B_DEV), 0, CELLS_DEV)
    half = B_DEV // 2
    first_pos = jax.random.randint(key_b, (blocks,), 0, half)
    second_pos = half + jax.random.randint(key_c, (blocks,), 0, B_DEV - half)
    column = jnp.arange(B_DEV)[None, :]
    local = jnp.where(column == first_pos[:, None], 0, local)
    local = jnp.where(column == second_pos[:, None], CELLS_DEV - 1, local)
    offsets = jnp.arange(blocks) * CELLS_DEV
    return (local + offsets[:, None]).reshape(B).astype(jnp.int32)


def levels(own_key, shape, cuts, smallest, high):
    def one(axis_at, parts):
        heights = jax.random.uniform(jax.random.fold_in(jax.random.fold_in(own_key, 6), axis_at), (parts,), jnp.float32, smallest / len(cuts), high / len(cuts))
        return jnp.repeat(jnp.exp(heights), shape[axis_at] // parts).reshape((-1,) + (1,) * (len(shape) - axis_at - 1))

    level = one(*cuts[0])
    for cut in cuts[1:]:
        level = level * one(*cut)
    return level


def scatter_about(rng, extent, width, bound, cuts=(), kind=jnp.bfloat16):
    values = jax.random.normal(rng, extent, jnp.float32) * width
    if len(cuts) > 0:
        values = levels(rng, extent, cuts, -0.22, 0.18) * values
    return jnp.clip(values, min=-bound, max=bound).astype(kind)


def setup_inputs(seed: int = 0, part: int = 0) -> dict:
    streams_of = jax.random.split(jax.random.key(seed), 8)
    part_splits = jax.random.split(jax.random.fold_in(streams_of[7], part), 8)
    x_slab = scatter_about(part_splits[0], (B, G), 1.0, 6.0, ((0, 4), (1, 4)))
    cell_factor = scatter_about(part_splits[1], (CELLS, R), 0.25, 1.5, ((0, 4),))
    row_index = draw_row_index(jax.random.fold_in(jax.random.fold_in(streams_of[7], part), 71), part)
    gene_scale = jnp.clip(jnp.exp(math.log(3.0) - 2.3025851 * jax.random.uniform(part_splits[3], (G,), jnp.float32) ** levels(part_splits[3], (G,), ((0, 4),), -0.2, 0.2)), 0.3, 3.0)
    gene_factor = scatter_about(part_splits[4], (G, R), 0.25, 1.5, ((0, 16),), jnp.float32)
    first_moment = scatter_about(part_splits[5], (G, R), 0.2, 1.2, ((0, 16),), jnp.float32)
    second_moment = jnp.clip(jnp.exp(math.log(1.0) - 2.9957323 * jax.random.uniform(part_splits[6], (G, R), jnp.float32) ** levels(part_splits[6], (G, R), ((0, 16),), -0.2, 0.2)), 0.05, 1.0)
    return dict(x_slab=x_slab, cell_factor=cell_factor, row_index=row_index, gene_scale=gene_scale, gene_factor=gene_factor, first_moment=first_moment, second_moment=second_moment)


tukey_c = 4.685
beta_one = 0.9
beta_two = 0.999
learn_rate = 0.02
adam_eps = 1e-08

def influence(factors, x_part, factor_part, scale_part):
    pred = lax.dot_general(factors, factor_part, (((1,), (1,)), ((), ())), preferred_element_type=jnp.float32)
    resid = x_part.astype(jnp.float32) - pred
    scaled = resid / scale_part[None, :]
    ratio = scaled / tukey_c
    inside = 1.0 - ratio * ratio
    weight = jnp.where(jnp.abs(ratio) < 1.0, inside * inside, 0.0)
    return (scaled * weight / scale_part[None, :]).astype(jnp.bfloat16)

def reference(x_slab, cell_factor, row_index, gene_scale, gene_factor, first_moment, second_moment):
    factors = jnp.take(cell_factor, row_index.astype(jnp.int32), axis=0)
    factor_bf = gene_factor.astype(jnp.bfloat16)
    blocks = G // G_DEV
    x_blocks = x_slab.reshape(B, blocks, G_DEV).transpose(1, 0, 2)
    f_blocks = factor_bf.reshape(blocks, G_DEV, R)
    s_blocks = gene_scale.reshape(blocks, G_DEV)

    def one_block(total, items):
        x_part, f_part, s_part = items
        infl = influence(factors, x_part, f_part, s_part)
        total = total + jnp.dot(infl, f_part, preferred_element_type=jnp.float32)
        cols = lax.dot_general(infl, factors, (((0,), (0,)), ((), ())), preferred_element_type=jnp.float32)
        return (total, cols)
    grad_rows, cols = lax.scan(one_block, jnp.zeros((B, R), jnp.float32), (x_blocks, f_blocks, s_blocks))
    scale_k = 4.0 / math.sqrt(G)
    grad_cells = -scale_k * grad_rows
    grad_genes = -scale_k * cols.reshape(G, R)
    new_first = beta_one * first_moment + (1.0 - beta_one) * grad_genes
    new_second = beta_two * second_moment + (1.0 - beta_two) * grad_genes * grad_genes
    first_hat = new_first / (1.0 - beta_one ** 10)
    second_hat = new_second / (1.0 - beta_two ** 10)
    new_factor = gene_factor - learn_rate * first_hat / (jnp.sqrt(second_hat) + adam_eps)
    return (grad_cells, new_factor, new_first, new_second)
```

```python
import functools
import math

import jax
import jax.numpy as jnp
from jax import lax
from jax.experimental import pallas as pl
from jax.experimental.pallas import tpu as pltpu
from jax.sharding import PartitionSpec as P

tukey_c = 4.685
beta_one = 0.9
beta_two = 0.999
learn_rate = 0.02
adam_eps = 1e-08

DIRECT_MOST = 8
VMEM = pltpu.VMEM
IN_VMEM = pl.BlockSpec(memory_space=VMEM)
IN_ANY = pl.BlockSpec(memory_space=pl.ANY)


def tile_of(rows, most):
    best = [t for t in range(128, most + 1, 128) if rows % t == 0]
    return best[-1] if best else rows


def params():
    return pltpu.CompilerParams(vmem_limit_bytes=24 * 1024 * 1024)


def cost(flops, moved):
    return pl.CostEstimate(flops=int(flops), bytes_accessed=int(moved), transcendentals=0)


def pinned(*arrays):
    return [pltpu.with_memory_space_constraint(a, VMEM) for a in arrays]


def prepare_kernel(scale_k, x_ref, index_ref, cell_ref, scale_ref, x_out, f_out, ft_out, bend_out, shrink_out, sem):
    load = pltpu.make_async_copy(x_ref, x_out, sem)
    load.start()
    cells, rank = cell_ref.shape
    rows = index_ref.shape[1]
    genes = scale_ref.shape[1]
    inverse = 1.0 / scale_ref[...]
    bend_out[...] = (inverse * inverse) * (1.0 / (tukey_c * tukey_c))
    shrink_out[...] = jnp.transpose(jnp.broadcast_to(-scale_k * (inverse * inverse), (rank, genes)))
    table = jnp.transpose(cell_ref[...].astype(jnp.float32)).astype(jnp.bfloat16)
    base = lax.axis_index("row") * cells
    step = tile_of(rows, 512)
    for at in range(0, rows, step):
        local = index_ref[:, at : at + step] - base
        hot = lax.broadcasted_iota(jnp.int32, (cells, step), 0) == local
        hot = jnp.where(hot, 1.0, 0.0).astype(jnp.bfloat16)
        picked = jnp.dot(table, hot, preferred_element_type=jnp.float32)
        ft_out[:, at : at + step] = picked.astype(jnp.bfloat16)
        f_out[at : at + step, :] = jnp.transpose(picked).astype(jnp.bfloat16)
    load.wait()


def prepare(x_slab, row_index, cell_factor, gene_scale, scale_k):
    rows, genes = x_slab.shape
    cells, rank = cell_factor.shape
    return pl.pallas_call(
        functools.partial(prepare_kernel, scale_k),
        out_shape=(
            VMEM((rows, genes), jnp.bfloat16),
            VMEM((rows, rank), jnp.bfloat16),
            VMEM((rank, rows), jnp.bfloat16),
            VMEM((1, genes), jnp.float32),
            VMEM((genes, rank), jnp.float32),
        ),
        in_specs=[IN_ANY, IN_VMEM, IN_VMEM, IN_VMEM],
        out_specs=(IN_VMEM,) * 5,
        scratch_shapes=[pltpu.SemaphoreType.DMA],
        compiler_params=params(),
        cost_estimate=cost(2 * rows * cells * rank, 2 * rows * genes * 2),
        name="prepare",
    )(
        pltpu.with_memory_space_constraint(x_slab, pltpu.HBM),
        row_index.reshape(1, rows),
        cell_factor,
        gene_scale.reshape(1, genes),
    )


def pick(axis, table):
    me = lax.axis_index(axis)
    value = jnp.int32(table[0])
    for place, entry in enumerate(table[1:], 1):
        value = jnp.where(me == place, entry, value)
    return value


def partner(me, hop, size):
    return me ^ hop if size & (size - 1) == 0 else (me + hop) % size


def source(me, hop, size):
    return me ^ hop if size & (size - 1) == 0 else (me + size - hop) % size


def rows_kernel(table, block, first, last, n_row, *refs):
    refs = list(refs)
    take = lambda count: [refs.pop(0) for _ in range(count)]
    x_ref, f_ref, ft_ref, bend_ref, shrink_ref = take(5)
    shares = take(n_row) if first else None
    if not first:
        wide_in, scaled_in, total_in = take(3)
    (rows_out,) = take(1)
    if first and not last:
        wide_out, scaled_out = take(2)
    if last:
        parts_out = take(n_row)
    else:
        (total_out,) = take(1)
    if first:
        (piece,) = take(1)
    if last:
        (turned,) = take(1)

    if first:
        me = lax.axis_index("row")
        depth = shares[0].shape[0]
        for hop in range(n_row):
            start = pl.multiple_of(source(me, hop, n_row) * depth, depth)
            piece[pl.ds(start, depth), :] = shares[hop][...]
        whole = piece[...].astype(jnp.float32)
        wide = jnp.transpose(whole).astype(jnp.bfloat16)
        scaled = (whole * shrink_ref[...]).astype(jnp.bfloat16)
        if not last:
            wide_out[...] = wide
            scaled_out[...] = scaled
        total = None
    else:
        wide = wide_in[...]
        scaled = scaled_in[...]
        total = total_in[...]

    bend = bend_ref[...]
    origin = pick("gene", table) * block if len(table) > 1 else 0
    step = tile_of(block, 256)
    for at in range(0, block, step):
        start = origin + at
        if len(table) > 1:
            start = pl.multiple_of(start, math.gcd(block, step))
        factors = f_ref[pl.ds(start, step), :]
        pred = jnp.dot(factors, wide, preferred_element_type=jnp.float32)
        resid = x_ref[pl.ds(start, step), :].astype(jnp.float32) - pred
        inside = jnp.maximum(1.0 - resid * resid * bend, 0.0)
        infl = (resid * (inside * inside)).astype(jnp.bfloat16)
        rows_out[at : at + step, :] = jnp.dot(infl, scaled, preferred_element_type=jnp.float32).astype(rows_out.dtype)
        cols = jnp.dot(ft_ref[:, pl.ds(start, step)], infl, preferred_element_type=jnp.float32)
        total = cols if total is None else total + cols
    if not last:
        total_out[...] = total
        return
    turned[...] = jnp.transpose(total) * shrink_ref[...]
    me = lax.axis_index("row")
    depth = parts_out[0].shape[0]
    for hop in range(n_row):
        start = pl.multiple_of(partner(me, hop, n_row) * depth, depth)
        parts_out[hop][...] = turned[pl.ds(start, depth), :].astype(parts_out[hop].dtype)


def block_rows(table, block, first, last, n_row, kind, fixed, carried):
    genes, rank = fixed[4].shape
    out = [jax.ShapeDtypeStruct((block, rank), kind)]
    if first and not last:
        out += [VMEM((rank, genes), jnp.bfloat16), VMEM((genes, rank), jnp.bfloat16)]
    if last:
        depth = genes // n_row
        out += [jax.ShapeDtypeStruct((depth, rank), jnp.float32 if hop == 0 else jnp.bfloat16) for hop in range(n_row)]
    else:
        out += [VMEM((rank, genes), jnp.float32)]
    scratch = []
    if first:
        scratch.append(VMEM((genes, rank), jnp.bfloat16))
    if last:
        scratch.append(VMEM((genes, rank), jnp.float32))
    ins = pinned(*fixed) + (list(carried) if first else pinned(*carried))
    return pl.pallas_call(
        functools.partial(rows_kernel, table, block, first, last, n_row),
        out_shape=tuple(out),
        in_specs=[IN_VMEM] * len(ins),
        out_specs=(IN_VMEM,) * len(out),
        scratch_shapes=scratch,
        compiler_params=params(),
        cost_estimate=cost(6 * block * genes * rank * 2, block * genes * 4),
        name="block_rows",
    )(*ins)


def swap_row(value, hop, size):
    return lax.ppermute(value, "row", [(me, partner(me, hop, size)) for me in range(size)])


def add_bf(a, b):
    return (a.astype(jnp.float32) + b.astype(jnp.float32)).astype(jnp.bfloat16)


def cell_gradients(n_gene, rows, make):
    block = rows // n_gene
    me = lax.axis_index("gene")
    if n_gene == 1:
        return make((0,), rows, jnp.float32, True, True)
    if n_gene > DIRECT_MOST or block % 128:
        mine = make((0,), rows, jnp.float32, True, True)
        return lax.psum_scatter(mine, "gene", scatter_dimension=0, tiled=True)
    if n_gene == 4:
        is_end = (me == 0) | (me == 3)
        near = make((3, 0, 3, 0), block, jnp.bfloat16, True, False)
        got_a = lax.ppermute(near, "gene", [(0, 1), (1, 0), (2, 3), (3, 2)])
        middle = make((2, 2, 1, 1), block, jnp.bfloat16, False, False)
        got_b = lax.ppermute(middle, "gene", [(1, 2), (2, 1)])
        got_c = lax.ppermute(middle, "gene", [(0, 2), (3, 1)])
        far = make((1, 3, 0, 2), block, jnp.bfloat16, False, False)
        mine = make((0, 1, 2, 3), block, jnp.float32, False, True)
        passed = jnp.where(is_end, far, add_bf(far, got_a))
        got_d = lax.ppermute(passed, "gene", [(0, 1), (3, 2), (1, 3), (2, 0)])
        total = mine + got_b.astype(jnp.float32) + got_c.astype(jnp.float32)
        total = total + jnp.where(is_end, got_a, jnp.zeros_like(got_a)).astype(jnp.float32)
        return total + got_d.astype(jnp.float32)
    got = []
    for hop in [*range(1, n_gene), 0]:
        table = tuple((place + hop) % n_gene for place in range(n_gene))
        mine = make(table, block, jnp.bfloat16 if hop else jnp.float32, hop == 1, hop == 0)
        if hop:
            got.append(lax.ppermute(mine, "gene", [(place, (place + hop) % n_gene) for place in range(n_gene)]))
    for part in got:
        mine = mine + part.astype(jnp.float32)
    return mine


def local(x_slab, cell_factor, row_index, gene_scale, gene_factor, first_moment, second_moment):
    rows_dev, genes_dev = x_slab.shape
    n_gene = lax.axis_size("gene")
    n_row = lax.axis_size("row")
    scale_k = 4.0 / math.sqrt(genes_dev * n_gene)
    factor_bf = gene_factor.astype(jnp.bfloat16)
    shares = [factor_bf] + [swap_row(factor_bf, hop, n_row) for hop in range(1, n_row)]
    fixed = prepare(x_slab, row_index, cell_factor, gene_scale, scale_k)

    state = {"carried": shares, "parts": None}

    def make(table, block, kind, first, last):
        out = block_rows(table, block, first, last, n_row, kind, fixed, state["carried"])
        if last:
            state["parts"] = out[1:]
        elif first:
            state["carried"] = out[1:]
        else:
            state["carried"] = [*state["carried"][:2], out[1]]
        return out[0]

    grad_cells = cell_gradients(n_gene, rows_dev, make)
    parts = state["parts"]
    grad_genes = parts[0]
    for hop in range(1, n_row):
        grad_genes = grad_genes + swap_row(parts[hop], hop, n_row).astype(jnp.float32)
    new_first = beta_one * first_moment + (1.0 - beta_one) * grad_genes
    new_second = beta_two * second_moment + (1.0 - beta_two) * grad_genes * grad_genes
    first_hat = new_first / (1.0 - beta_one**10)
    second_hat = new_second / (1.0 - beta_two**10)
    new_factor = gene_factor - learn_rate * first_hat / (jnp.sqrt(second_hat) + adam_eps)
    return (grad_cells, new_factor, new_first, new_second)


def solution(mesh):
    in_specs = (
        P(("grp", "row"), "gene"),
        P(("grp", "row"), None),
        P(("grp", "row")),
        P(("grp", "gene")),
        P(("grp", "gene", "row"), None),
        P(("grp", "gene", "row"), None),
        P(("grp", "gene", "row"), None),
    )
    out_specs = (
        P(("grp", "row", "gene"), None),
        P(("grp", "gene", "row"), None),
        P(("grp", "gene", "row"), None),
        P(("grp", "gene", "row"), None),
    )
    return jax.shard_map(local, mesh=mesh, in_specs=in_specs, out_specs=out_specs, check_vma=False)
```

```python
import functools
import math

import jax
import jax.numpy as jnp
from jax import lax
from jax.experimental import pallas as pl
from jax.experimental.pallas import tpu as pltpu
from jax.sharding import PartitionSpec as P

tukey_c = 4.685
beta_one = 0.9
beta_two = 0.999
learn_rate = 0.02
adam_eps = 1e-08

VMEM = pltpu.VMEM
IN_VMEM = pl.BlockSpec(memory_space=VMEM)
IN_ANY = pl.BlockSpec(memory_space=pl.ANY)


def tile_of(rows, most):
    best = [t for t in range(128, most + 1, 128) if rows % t == 0]
    return best[-1] if best else rows


def params():
    return pltpu.CompilerParams(vmem_limit_bytes=24 * 1024 * 1024)


def cost(flops, moved):
    return pl.CostEstimate(flops=int(flops), bytes_accessed=int(moved), transcendentals=0)


def pinned(*arrays):
    return [pltpu.with_memory_space_constraint(a, VMEM) for a in arrays]


def prepare_kernel(scale_k, x_in, index_in, cell_in, scale_in, x_out, f_out, ft_out, bend_out, shrink_out, index, cell, scale, sems):
    loads = [
        pltpu.make_async_copy(src, dst, sems.at[at])
        for at, (src, dst) in enumerate(((scale_in, scale), (cell_in, cell), (index_in, index), (x_in, x_out)))
    ]
    for load in loads:
        load.start()
    cells, rank = cell.shape
    rows = index.shape[0]
    genes = scale.shape[0]
    loads[0].wait()
    inverse = 1.0 / scale[...].reshape(1, genes)
    bend_out[...] = (inverse * inverse) * (1.0 / (tukey_c * tukey_c))
    shrink_out[...] = jnp.transpose(jnp.broadcast_to(-scale_k * (inverse * inverse), (rank, genes)))
    loads[1].wait()
    table = jnp.transpose(cell[...].astype(jnp.float32)).astype(jnp.bfloat16)
    base = lax.axis_index("row") * cells
    loads[2].wait()
    step = tile_of(rows, 512)
    for at in range(0, rows, step):
        local = index[at : at + step].reshape(1, step) - base
        hot = lax.broadcasted_iota(jnp.int32, (cells, step), 0) == local
        hot = jnp.where(hot, 1.0, 0.0).astype(jnp.bfloat16)
        picked = jnp.dot(table, hot, preferred_element_type=jnp.float32)
        ft_out[:, at : at + step] = picked.astype(jnp.bfloat16)
        f_out[at : at + step, :] = jnp.transpose(picked).astype(jnp.bfloat16)
    loads[3].wait()


def prepare(x_slab, row_index, cell_factor, gene_scale, scale_k):
    rows, genes = x_slab.shape
    cells, rank = cell_factor.shape
    ins = (x_slab, row_index, cell_factor, gene_scale)
    return pl.pallas_call(
        functools.partial(prepare_kernel, scale_k),
        out_shape=(
            VMEM((rows, genes), jnp.bfloat16),
            VMEM((rows, rank), jnp.bfloat16),
            VMEM((rank, rows), jnp.bfloat16),
            VMEM((1, genes), jnp.float32),
            VMEM((genes, rank), jnp.float32),
        ),
        in_specs=[IN_ANY] * 4,
        out_specs=(IN_VMEM,) * 5,
        scratch_shapes=[
            VMEM((rows,), jnp.int32),
            VMEM((cells, rank), jnp.bfloat16),
            VMEM((genes,), jnp.float32),
            pltpu.SemaphoreType.DMA((4,)),
        ],
        compiler_params=params(),
        cost_estimate=cost(2 * rows * cells * rank, 2 * rows * genes * 2),
        name="prepare",
    )(*(pltpu.with_memory_space_constraint(a, pltpu.HBM) for a in ins))


def partner(me, hop, size):
    return me ^ hop if size & (size - 1) == 0 else (me + hop) % size


def source(me, hop, size):
    return me ^ hop if size & (size - 1) == 0 else (me + size - hop) % size


def rows_kernel(n_row, x_ref, f_ref, ft_ref, bend_ref, shrink_ref, *refs):
    shares, rows_out, parts_out = refs[:n_row], refs[n_row], refs[n_row + 1 : 2 * n_row + 1]
    piece, turned = refs[2 * n_row + 1 :]
    me = lax.axis_index("row")
    depth = shares[0].shape[0]
    for hop in range(n_row):
        start = pl.multiple_of(source(me, hop, n_row) * depth, depth)
        piece[pl.ds(start, depth), :] = shares[hop][...]
    whole = piece[...].astype(jnp.float32)
    wide = jnp.transpose(whole).astype(jnp.bfloat16)
    scaled = (whole * shrink_ref[...]).astype(jnp.bfloat16)
    bend = bend_ref[...]
    rows = x_ref.shape[0]
    step = tile_of(rows, 256)
    total = None
    for at in range(0, rows, step):
        here = slice(at, at + step)
        pred = jnp.dot(f_ref[here, :], wide, preferred_element_type=jnp.float32)
        resid = x_ref[here, :].astype(jnp.float32) - pred
        inside = jnp.maximum(1.0 - resid * resid * bend, 0.0)
        infl = (resid * (inside * inside)).astype(jnp.bfloat16)
        rows_out[here, :] = jnp.dot(infl, scaled, preferred_element_type=jnp.float32).astype(rows_out.dtype)
        cols = jnp.dot(ft_ref[:, here], infl, preferred_element_type=jnp.float32)
        total = cols if total is None else total + cols
    turned[...] = jnp.transpose(total) * shrink_ref[...]
    for hop in range(n_row):
        start = pl.multiple_of(partner(me, hop, n_row) * depth, depth)
        parts_out[hop][...] = turned[pl.ds(start, depth), :].astype(parts_out[hop].dtype)


def all_rows(n_row, fixed, shares):
    rows, genes = fixed[0].shape
    depth, rank = shares[0].shape
    out = [jax.ShapeDtypeStruct((rows, rank), jnp.bfloat16)]
    out += [jax.ShapeDtypeStruct((depth, rank), jnp.bfloat16 if hop else jnp.float32) for hop in range(n_row)]
    ins = pinned(*fixed) + list(shares)
    return pl.pallas_call(
        functools.partial(rows_kernel, n_row),
        out_shape=tuple(out),
        in_specs=[IN_VMEM] * len(ins),
        out_specs=(IN_VMEM,) * len(out),
        scratch_shapes=[VMEM((genes, rank), jnp.bfloat16), VMEM((genes, rank), jnp.float32)],
        compiler_params=params(),
        cost_estimate=cost(12 * rows * genes * rank, rows * genes * 4),
        name="all_rows",
    )(*ins)


def swap_row(value, hop, size):
    return lax.ppermute(value, "row", [(me, partner(me, hop, size)) for me in range(size)])


def local(x_slab, cell_factor, row_index, gene_scale, gene_factor, first_moment, second_moment):
    rows_dev, genes_dev = x_slab.shape
    n_gene = lax.axis_size("gene")
    n_row = lax.axis_size("row")
    scale_k = 4.0 / math.sqrt(genes_dev * n_gene)
    factor_bf = gene_factor.astype(jnp.bfloat16)
    shares = [factor_bf] + [swap_row(factor_bf, hop, n_row) for hop in range(1, n_row)]
    fixed = prepare(x_slab, row_index, cell_factor, gene_scale, scale_k)
    rows, *parts = all_rows(n_row, fixed, shares)

    grad_genes = parts[0]
    for hop in range(1, n_row):
        grad_genes = grad_genes + swap_row(parts[hop], hop, n_row).astype(jnp.float32)
    new_first = beta_one * first_moment + (1.0 - beta_one) * grad_genes
    new_second = beta_two * second_moment + (1.0 - beta_two) * grad_genes * grad_genes
    first_hat = new_first / (1.0 - beta_one**10)
    second_hat = new_second / (1.0 - beta_two**10)
    new_factor = gene_factor - learn_rate * first_hat / (jnp.sqrt(second_hat) + adam_eps)

    rank = rows.shape[1]
    rows = rows.reshape(n_gene, rows_dev // n_gene, rank)
    got = lax.all_to_all(rows, "gene", split_axis=0, concat_axis=0)
    grad_cells = got[0].astype(jnp.float32)
    for place in range(1, n_gene):
        grad_cells = grad_cells + got[place].astype(jnp.float32)
    return (grad_cells, new_factor, new_first, new_second)


def solution(mesh):
    in_specs = (
        P(("grp", "row"), "gene"),
        P(("grp", "row"), None),
        P(("grp", "row")),
        P(("grp", "gene")),
        P(("grp", "gene", "row"), None),
        P(("grp", "gene", "row"), None),
        P(("grp", "gene", "row"), None),
    )
    out_specs = (
        P(("grp", "row", "gene"), None),
        P(("grp", "gene", "row"), None),
        P(("grp", "gene", "row"), None),
        P(("grp", "gene", "row"), None),
    )
    return jax.shard_map(local, mesh=mesh, in_specs=in_specs, out_specs=out_specs, check_vma=False)
```

```python
import functools
import math

import jax
import jax.numpy as jnp
from jax import lax
from jax.experimental import pallas as pl
from jax.experimental.pallas import tpu as pltpu
from jax.sharding import PartitionSpec as P

tukey_c = 4.685
beta_one = 0.9
beta_two = 0.999
learn_rate = 0.02
adam_eps = 1e-08

PLAN_MOST = 8
VMEM = pltpu.VMEM
IN_VMEM = pl.BlockSpec(memory_space=VMEM)
IN_ANY = pl.BlockSpec(memory_space=pl.ANY)


def tile_of(rows, most):
    best = [t for t in range(128, most + 1, 128) if rows % t == 0]
    return best[-1] if best else rows


def params():
    return pltpu.CompilerParams(vmem_limit_bytes=24 * 1024 * 1024)


def cost(flops, moved):
    return pl.CostEstimate(flops=int(flops), bytes_accessed=int(moved), transcendentals=0)


def pinned(*arrays):
    return [pltpu.with_memory_space_constraint(a, VMEM) for a in arrays]


def prepare_kernel(scale_k, x_in, index_in, cell_in, scale_in, x_out, f_out, ft_out, bend_out, shrink_out, index, cell, scale, sems):
    loads = [
        pltpu.make_async_copy(src, dst, sems.at[at])
        for at, (src, dst) in enumerate(((scale_in, scale), (cell_in, cell), (index_in, index), (x_in, x_out)))
    ]
    for load in loads:
        load.start()
    cells, rank = cell.shape
    rows = index.shape[0]
    genes = scale.shape[0]
    loads[0].wait()
    inverse = 1.0 / scale[...].reshape(1, genes)
    bend_out[...] = (inverse * inverse) * (1.0 / (tukey_c * tukey_c))
    shrink_out[...] = jnp.transpose(jnp.broadcast_to(-scale_k * (inverse * inverse), (rank, genes)))
    loads[1].wait()
    table = jnp.transpose(cell[...].astype(jnp.float32)).astype(jnp.bfloat16)
    base = lax.axis_index("row") * cells
    loads[2].wait()
    step = tile_of(rows, 512)
    for at in range(0, rows, step):
        local = index[at : at + step].reshape(1, step) - base
        hot = lax.broadcasted_iota(jnp.int32, (cells, step), 0) == local
        hot = jnp.where(hot, 1.0, 0.0).astype(jnp.bfloat16)
        picked = jnp.dot(table, hot, preferred_element_type=jnp.float32)
        ft_out[:, at : at + step] = picked.astype(jnp.bfloat16)
        f_out[at : at + step, :] = jnp.transpose(picked).astype(jnp.bfloat16)
    loads[3].wait()


def prepare(x_slab, row_index, cell_factor, gene_scale, scale_k):
    rows, genes = x_slab.shape
    cells, rank = cell_factor.shape
    ins = (x_slab, row_index, cell_factor, gene_scale)
    return pl.pallas_call(
        functools.partial(prepare_kernel, scale_k),
        out_shape=(
            VMEM((rows, genes), jnp.bfloat16),
            VMEM((rows, rank), jnp.bfloat16),
            VMEM((rank, rows), jnp.bfloat16),
            VMEM((1, genes), jnp.float32),
            VMEM((genes, rank), jnp.float32),
        ),
        in_specs=[IN_ANY] * 4,
        out_specs=(IN_VMEM,) * 5,
        scratch_shapes=[
            VMEM((rows,), jnp.int32),
            VMEM((cells, rank), jnp.bfloat16),
            VMEM((genes,), jnp.float32),
            pltpu.SemaphoreType.DMA((4,)),
        ],
        compiler_params=params(),
        cost_estimate=cost(2 * rows * cells * rank, 2 * rows * genes * 2),
        name="prepare",
    )(*(pltpu.with_memory_space_constraint(a, pltpu.HBM) for a in ins))


def pick(axis, table):
    me = lax.axis_index(axis)
    value = jnp.int32(table[0])
    for place, entry in enumerate(table[1:], 1):
        value = jnp.where(me == place, jnp.int32(entry), value)
    return value


def partner(me, hop, size):
    return me ^ hop if size & (size - 1) == 0 else (me + hop) % size


def source(me, hop, size):
    return me ^ hop if size & (size - 1) == 0 else (me + size - hop) % size


def rows_kernel(tables, block, first, last, n_row, *refs):
    refs = list(refs)
    take = lambda count: [refs.pop(0) for _ in range(count)]
    x_ref, f_ref, ft_ref, bend_ref, shrink_ref = take(5)
    shares = take(n_row) if first else None
    carried_in = None if first else take(3)
    rows_out = take(len(tables))
    carried_out = None if last else take(3)
    parts_out = take(n_row) if last else None
    me = lax.axis_index("row")

    if first:
        (piece,) = take(1)
        depth = shares[0].shape[0]
        for hop in range(n_row):
            start = pl.multiple_of(source(me, hop, n_row) * depth, depth)
            piece[pl.ds(start, depth), :] = shares[hop][...]
        whole = piece[...].astype(jnp.float32)
        wide = jnp.transpose(whole).astype(jnp.bfloat16)
        scaled = (whole * shrink_ref[...]).astype(jnp.bfloat16)
        total = None
    else:
        wide, scaled, total = (ref[...] for ref in carried_in)

    bend = bend_ref[...]
    step = tile_of(block, 256)
    for table, out in zip(tables, rows_out):
        origin = pick("gene", table) * block if len(table) > 1 else 0
        for at in range(0, block, step):
            start = origin + at
            if len(table) > 1:
                start = pl.multiple_of(start, math.gcd(block, step))
            here = pl.ds(start, step)
            pred = jnp.dot(f_ref[here, :], wide, preferred_element_type=jnp.float32)
            resid = x_ref[here, :].astype(jnp.float32) - pred
            inside = jnp.maximum(1.0 - resid * resid * bend, 0.0)
            infl = (resid * (inside * inside)).astype(jnp.bfloat16)
            out[at : at + step, :] = jnp.dot(infl, scaled, preferred_element_type=jnp.float32).astype(out.dtype)
            cols = jnp.dot(ft_ref[:, here], infl, preferred_element_type=jnp.float32)
            total = cols if total is None else total + cols
    if not last:
        for ref, value in zip(carried_out, (wide, scaled, total)):
            ref[...] = value
        return
    (turned,) = take(1)
    turned[...] = jnp.transpose(total) * shrink_ref[...]
    depth = parts_out[0].shape[0]
    for hop in range(n_row):
        start = pl.multiple_of(partner(me, hop, n_row) * depth, depth)
        parts_out[hop][...] = turned[pl.ds(start, depth), :].astype(parts_out[hop].dtype)


def block_rows(tables, kinds, block, first, last, n_row, fixed, carried):
    genes, rank = fixed[4].shape
    out = [jax.ShapeDtypeStruct((block, rank), kind) for kind in kinds]
    if last:
        out += [jax.ShapeDtypeStruct((genes // n_row, rank), jnp.bfloat16 if hop else jnp.float32) for hop in range(n_row)]
    else:
        out += [VMEM((rank, genes), jnp.bfloat16), VMEM((genes, rank), jnp.bfloat16), VMEM((rank, genes), jnp.float32)]
    scratch = [VMEM((genes, rank), jnp.bfloat16)] if first else []
    if last:
        scratch.append(VMEM((genes, rank), jnp.float32))
    ins = pinned(*fixed) + (list(carried) if first else pinned(*carried))
    work = len(tables) * block * genes
    out = pl.pallas_call(
        functools.partial(rows_kernel, tables, block, first, last, n_row),
        out_shape=tuple(out),
        in_specs=[IN_VMEM] * len(ins),
        out_specs=(IN_VMEM,) * len(out),
        scratch_shapes=scratch,
        compiler_params=params(),
        cost_estimate=cost(12 * work * rank, work * 4),
        name="block_rows",
    )(*ins)
    return out[: len(tables)], out[len(tables) :]


def swap_row(value, hop, size):
    return lax.ppermute(value, "row", [(me, partner(me, hop, size)) for me in range(size)])


def plan_of(size):
    if size == 4:
        return [((1, 2, 3, 0), (3, 2, 1, 0)), ((2, 0, 3, 1), (2, 0, 3, 1)), ((1, 3, 0, 2), (1, 3, 0, 2))]
    hops = [tuple((place + hop) % size for place in range(size)) for hop in range(1, size)]
    return [(hop, hop) for hop in hops]


def received(step):
    targets, blocks = step
    return [blocks[targets.index(place)] for place in range(len(targets))]


def chosen(value, flags):
    if all(flags):
        return value
    return jnp.where(pick("gene", flags) == 1, value, jnp.zeros_like(value))


def exchange(steps, blocks, mine):
    size = len(steps[0][0])
    got = []
    for at, (step, block) in enumerate(zip(steps, blocks)):
        for earlier, value in zip(steps[:at], got):
            flags = [int(came == sent and came != me) for me, (came, sent) in enumerate(zip(received(earlier), step[1]))]
            if any(flags):
                block = (block.astype(jnp.float32) + chosen(value, flags).astype(jnp.float32)).astype(jnp.bfloat16)
        got.append(lax.ppermute(block, "gene", list(enumerate(step[0]))))
    for step, value in zip(steps, got):
        flags = [int(came == me) for me, came in enumerate(received(step))]
        mine = mine + chosen(value, flags).astype(jnp.float32)
    return mine


def local(x_slab, cell_factor, row_index, gene_scale, gene_factor, first_moment, second_moment):
    rows_dev, genes_dev = x_slab.shape
    n_gene = lax.axis_size("gene")
    n_row = lax.axis_size("row")
    block = rows_dev // n_gene
    scale_k = 4.0 / math.sqrt(genes_dev * n_gene)
    factor_bf = gene_factor.astype(jnp.bfloat16)
    shares = [factor_bf] + [swap_row(factor_bf, hop, n_row) for hop in range(1, n_row)]
    fixed = prepare(x_slab, row_index, cell_factor, gene_scale, scale_k)

    if 1 < n_gene <= PLAN_MOST and block % 128 == 0:
        steps = plan_of(n_gene)
        tables = [step[1] for step in steps] + [tuple(range(n_gene))]
        kinds = [jnp.bfloat16] * len(steps) + [jnp.float32]
        near, carried = block_rows(tables[:1], kinds[:1], block, True, False, n_row, fixed, shares)
        others, parts = block_rows(tables[1:], kinds[1:], block, False, True, n_row, fixed, carried)
        grad_cells = exchange(steps, [*near, *others[:-1]], others[-1])
    else:
        (rows,), parts = block_rows([(0,)], [jnp.float32], rows_dev, True, True, n_row, fixed, shares)
        grad_cells = lax.psum_scatter(rows, "gene", scatter_dimension=0, tiled=True)

    grad_genes = parts[0]
    for hop in range(1, n_row):
        grad_genes = grad_genes + swap_row(parts[hop], hop, n_row).astype(jnp.float32)
    new_first = beta_one * first_moment + (1.0 - beta_one) * grad_genes
    new_second = beta_two * second_moment + (1.0 - beta_two) * grad_genes * grad_genes
    first_hat = new_first / (1.0 - beta_one**10)
    second_hat = new_second / (1.0 - beta_two**10)
    new_factor = gene_factor - learn_rate * first_hat / (jnp.sqrt(second_hat) + adam_eps)
    return (grad_cells, new_factor, new_first, new_second)


def solution(mesh):
    in_specs = (
        P(("grp", "row"), "gene"),
        P(("grp", "row"), None),
        P(("grp", "row")),
        P(("grp", "gene")),
        P(("grp", "gene", "row"), None),
        P(("grp", "gene", "row"), None),
        P(("grp", "gene", "row"), None),
    )
    out_specs = (
        P(("grp", "row", "gene"), None),
        P(("grp", "gene", "row"), None),
        P(("grp", "gene", "row"), None),
        P(("grp", "gene", "row"), None),
    )
    return jax.shard_map(local, mesh=mesh, in_specs=in_specs, out_specs=out_specs, check_vma=False)
```

```python
import functools
import itertools
import math

import jax
import jax.numpy as jnp
from jax import lax
from jax.experimental import pallas as pl
from jax.experimental.pallas import tpu as pltpu
from jax.sharding import PartitionSpec as P

tukey_c = 4.685
beta_one = 0.9
beta_two = 0.999
learn_rate = 0.02
adam_eps = 1e-08

RING_MOST = 8
VMEM = pltpu.VMEM
IN_VMEM = pl.BlockSpec(memory_space=VMEM)
IN_ANY = pl.BlockSpec(memory_space=pl.ANY)


def tile_of(rows, most):
    best = [t for t in range(128, most + 1, 128) if rows % t == 0]
    return best[-1] if best else rows


def params():
    return pltpu.CompilerParams(vmem_limit_bytes=24 * 1024 * 1024)


def cost(flops, moved):
    return pl.CostEstimate(flops=int(flops), bytes_accessed=int(moved), transcendentals=0)


def pinned(*arrays):
    return [pltpu.with_memory_space_constraint(a, VMEM) for a in arrays]


def prepare_kernel(scale_k, x_in, index_in, cell_in, scale_in, x_out, f_out, ft_out, bend_out, shrink_out, index, cell, scale, sems):
    loads = [
        pltpu.make_async_copy(src, dst, sems.at[at])
        for at, (src, dst) in enumerate(((scale_in, scale), (cell_in, cell), (index_in, index), (x_in, x_out)))
    ]
    for load in loads:
        load.start()
    cells, rank = cell.shape
    rows = index.shape[0]
    genes = scale.shape[0]
    loads[0].wait()
    inverse = 1.0 / scale[...].reshape(1, genes)
    bend_out[...] = (inverse * inverse) * (1.0 / (tukey_c * tukey_c))
    shrink_out[...] = jnp.transpose(jnp.broadcast_to(-scale_k * (inverse * inverse), (rank, genes)))
    loads[1].wait()
    table = jnp.transpose(cell[...].astype(jnp.float32)).astype(jnp.bfloat16)
    base = lax.axis_index("row") * cells
    loads[2].wait()
    step = tile_of(rows, 512)
    for at in range(0, rows, step):
        local = index[at : at + step].reshape(1, step) - base
        hot = lax.broadcasted_iota(jnp.int32, (cells, step), 0) == local
        hot = jnp.where(hot, 1.0, 0.0).astype(jnp.bfloat16)
        picked = jnp.dot(table, hot, preferred_element_type=jnp.float32)
        ft_out[:, at : at + step] = picked.astype(jnp.bfloat16)
        f_out[at : at + step, :] = jnp.transpose(picked).astype(jnp.bfloat16)
    loads[3].wait()


def prepare(x_slab, row_index, cell_factor, gene_scale, scale_k):
    rows, genes = x_slab.shape
    cells, rank = cell_factor.shape
    ins = (x_slab, row_index, cell_factor, gene_scale)
    return pl.pallas_call(
        functools.partial(prepare_kernel, scale_k),
        out_shape=(
            VMEM((rows, genes), jnp.bfloat16),
            VMEM((rows, rank), jnp.bfloat16),
            VMEM((rank, rows), jnp.bfloat16),
            VMEM((1, genes), jnp.float32),
            VMEM((genes, rank), jnp.float32),
        ),
        in_specs=[IN_ANY] * 4,
        out_specs=(IN_VMEM,) * 5,
        scratch_shapes=[
            VMEM((rows,), jnp.int32),
            VMEM((cells, rank), jnp.bfloat16),
            VMEM((genes,), jnp.float32),
            pltpu.SemaphoreType.DMA((4,)),
        ],
        compiler_params=params(),
        cost_estimate=cost(2 * rows * cells * rank, 2 * rows * genes * 2),
        name="prepare",
    )(*(pltpu.with_memory_space_constraint(a, pltpu.HBM) for a in ins))


def pick(axis, table):
    me = lax.axis_index(axis)
    value = jnp.int32(table[0])
    for place, entry in enumerate(table[1:], 1):
        value = jnp.where(me == place, jnp.int32(entry), value)
    return value


def partner(me, hop, size):
    return me ^ hop if size & (size - 1) == 0 else (me + hop) % size


def source(me, hop, size):
    return me ^ hop if size & (size - 1) == 0 else (me + size - hop) % size


def rows_kernel(tables, block, first, last, n_row, *refs):
    refs = list(refs)
    take = lambda count: [refs.pop(0) for _ in range(count)]
    x_ref, f_ref, ft_ref, bend_ref, shrink_ref = take(5)
    shares = take(n_row) if first else None
    carried_in = None if first else take(3)
    rows_out = take(len(tables))
    carried_out = None if last else take(3 if first else 1)
    parts_out = take(n_row) if last else None
    me = lax.axis_index("row")

    if first:
        (piece,) = take(1)
        depth = shares[0].shape[0]
        for hop in range(n_row):
            start = pl.multiple_of(source(me, hop, n_row) * depth, depth)
            piece[pl.ds(start, depth), :] = shares[hop][...]
        whole = piece[...].astype(jnp.float32)
        wide = jnp.transpose(whole).astype(jnp.bfloat16)
        scaled = (whole * shrink_ref[...]).astype(jnp.bfloat16)
        total = None
    else:
        total, wide, scaled = (ref[...] for ref in carried_in)

    bend = bend_ref[...]
    step = tile_of(block, 256)
    for table, out in zip(tables, rows_out):
        origin = pick("gene", table) * block if len(table) > 1 else 0
        for at in range(0, block, step):
            start = origin + at
            if len(table) > 1:
                start = pl.multiple_of(start, math.gcd(block, step))
            here = pl.ds(start, step)
            pred = jnp.dot(f_ref[here, :], wide, preferred_element_type=jnp.float32)
            resid = x_ref[here, :].astype(jnp.float32) - pred
            inside = jnp.maximum(1.0 - resid * resid * bend, 0.0)
            infl = (resid * (inside * inside)).astype(jnp.bfloat16)
            out[at : at + step, :] = jnp.dot(infl, scaled, preferred_element_type=jnp.float32).astype(out.dtype)
            cols = jnp.dot(ft_ref[:, here], infl, preferred_element_type=jnp.float32)
            total = cols if total is None else total + cols
    if first and not last:
        carried_out[1][...] = wide
        carried_out[2][...] = scaled
    if not last:
        carried_out[0][...] = total
        return
    (turned,) = take(1)
    turned[...] = jnp.transpose(total) * shrink_ref[...]
    depth = parts_out[0].shape[0]
    for hop in range(n_row):
        start = pl.multiple_of(partner(me, hop, n_row) * depth, depth)
        parts_out[hop][...] = turned[pl.ds(start, depth), :].astype(parts_out[hop].dtype)


def block_rows(tables, kinds, block, first, last, n_row, fixed, carried):
    genes, rank = fixed[4].shape
    out = [jax.ShapeDtypeStruct((block, rank), kind) for kind in kinds]
    if last:
        out += [jax.ShapeDtypeStruct((genes // n_row, rank), jnp.bfloat16 if hop else jnp.float32) for hop in range(n_row)]
    else:
        out += [VMEM((rank, genes), jnp.float32)]
    if first and not last:
        out += [VMEM((rank, genes), jnp.bfloat16), VMEM((genes, rank), jnp.bfloat16)]
    scratch = [VMEM((genes, rank), jnp.bfloat16)] if first else []
    if last:
        scratch.append(VMEM((genes, rank), jnp.float32))
    ins = pinned(*fixed) + (list(carried) if first else pinned(*carried))
    work = len(tables) * block * genes
    out = pl.pallas_call(
        functools.partial(rows_kernel, tables, block, first, last, n_row),
        out_shape=tuple(out),
        in_specs=[IN_VMEM] * len(ins),
        out_specs=(IN_VMEM,) * len(out),
        scratch_shapes=scratch,
        compiler_params=params(),
        cost_estimate=cost(12 * work * rank, work * 4),
        name="block_rows",
    )(*ins)
    done, rest = list(out[: len(tables)]), list(out[len(tables) :])
    return done, rest if first or last else rest + list(carried[1:])


def swap_row(value, hop, size):
    return lax.ppermute(value, "row", [(me, partner(me, hop, size)) for me in range(size)])


def ring_of(size):
    return [*range(0, size, 2), *reversed(range(1, size, 2))]


def steps_of(size):
    ahead = [(1, distance) for distance in range(size // 2, 0, -1)]
    back = [(-1, distance) for distance in range((size - 1) // 2, 0, -1)]
    return [step for pair in itertools.zip_longest(ahead, back) for step in pair if step]


def around(size, hops):
    ring = ring_of(size)
    return tuple(ring[(ring.index(place) + hops) % size] for place in range(size))


def plus(wide, narrow):
    return wide.astype(jnp.float32) + narrow.astype(jnp.float32)


def reduce_scatter(size, steps, blocks, mine):
    came = {}
    for (way, _), block in zip(steps, blocks):
        if way in came:
            block = plus(block, came[way]).astype(jnp.bfloat16)
        came[way] = lax.ppermute(block, "gene", list(enumerate(around(size, way))))
    for value in came.values():
        mine = plus(mine, value)
    return mine


def local(x_slab, cell_factor, row_index, gene_scale, gene_factor, first_moment, second_moment):
    rows_dev, genes_dev = x_slab.shape
    n_gene = lax.axis_size("gene")
    n_row = lax.axis_size("row")
    block = rows_dev // n_gene
    scale_k = 4.0 / math.sqrt(genes_dev * n_gene)
    factor_bf = gene_factor.astype(jnp.bfloat16)
    shares = [factor_bf] + [swap_row(factor_bf, hop, n_row) for hop in range(1, n_row)]
    fixed = prepare(x_slab, row_index, cell_factor, gene_scale, scale_k)

    if 1 < n_gene <= RING_MOST and block % 128 == 0:
        steps = steps_of(n_gene)
        tables = [around(n_gene, way * distance) for way, distance in steps] + [tuple(range(n_gene))]
        kinds = [jnp.bfloat16] * len(steps) + [jnp.float32]
        cuts = [0, 1, 2, len(tables)] if len(steps) > 2 else [0, 1, len(tables)]
        carried, blocks = shares, []
        for low, high in zip(cuts, cuts[1:]):
            last = high == len(tables)
            done, carried = block_rows(tables[low:high], kinds[low:high], block, low == 0, last, n_row, fixed, carried)
            blocks += done
        parts = carried
        grad_cells = reduce_scatter(n_gene, steps, blocks[:-1], blocks[-1])
    else:
        (rows,), parts = block_rows([(0,)], [jnp.float32], rows_dev, True, True, n_row, fixed, shares)
        grad_cells = lax.psum_scatter(rows, "gene", scatter_dimension=0, tiled=True)

    grad_genes = parts[0]
    for hop in range(1, n_row):
        grad_genes = grad_genes + swap_row(parts[hop], hop, n_row).astype(jnp.float32)
    new_first = beta_one * first_moment + (1.0 - beta_one) * grad_genes
    new_second = beta_two * second_moment + (1.0 - beta_two) * grad_genes * grad_genes
    first_hat = new_first / (1.0 - beta_one**10)
    second_hat = new_second / (1.0 - beta_two**10)
    new_factor = gene_factor - learn_rate * first_hat / (jnp.sqrt(second_hat) + adam_eps)
    return (grad_cells, new_factor, new_first, new_second)


def solution(mesh):
    in_specs = (
        P(("grp", "row"), "gene"),
        P(("grp", "row"), None),
        P(("grp", "row")),
        P(("grp", "gene")),
        P(("grp", "gene", "row"), None),
        P(("grp", "gene", "row"), None),
        P(("grp", "gene", "row"), None),
    )
    out_specs = (
        P(("grp", "row", "gene"), None),
        P(("grp", "gene", "row"), None),
        P(("grp", "gene", "row"), None),
        P(("grp", "gene", "row"), None),
    )
    return jax.shard_map(local, mesh=mesh, in_specs=in_specs, out_specs=out_specs, check_vma=False)
```

```python
import functools
import itertools
import math

import jax
import jax.numpy as jnp
from jax import lax
from jax.experimental import pallas as pl
from jax.experimental.pallas import tpu as pltpu
from jax.sharding import PartitionSpec as P

tukey_c = 4.685
beta_one = 0.9
beta_two = 0.999
learn_rate = 0.02
adam_eps = 1e-08

RING_MOST = 8
VMEM = pltpu.VMEM
IN_VMEM = pl.BlockSpec(memory_space=VMEM)
IN_ANY = pl.BlockSpec(memory_space=pl.ANY)


def tile_of(rows, most):
    best = [t for t in range(128, most + 1, 128) if rows % t == 0]
    return best[-1] if best else rows


def params():
    return pltpu.CompilerParams(vmem_limit_bytes=24 * 1024 * 1024)


def cost(flops, moved):
    return pl.CostEstimate(flops=int(flops), bytes_accessed=int(moved), transcendentals=0)


def pinned(*arrays):
    return [pltpu.with_memory_space_constraint(a, VMEM) for a in arrays]


def prepare_kernel(scale_k, x_in, index_in, cell_in, scale_in, x_out, f_out, ft_out, bend_out, shrink_out, index, cell, scale, sems):
    loads = [
        pltpu.make_async_copy(src, dst, sems.at[at])
        for at, (src, dst) in enumerate(((scale_in, scale), (cell_in, cell), (index_in, index), (x_in, x_out)))
    ]
    for load in loads:
        load.start()
    cells, rank = cell.shape
    rows = index.shape[0]
    genes = scale.shape[0]
    loads[0].wait()
    inverse = 1.0 / scale[...].reshape(1, genes)
    bend_out[...] = (inverse * inverse) * (1.0 / (tukey_c * tukey_c))
    shrink_out[...] = jnp.transpose(jnp.broadcast_to(-scale_k * (inverse * inverse), (rank, genes)))
    loads[1].wait()
    table = jnp.transpose(cell[...].astype(jnp.float32)).astype(jnp.bfloat16)
    base = lax.axis_index("row") * cells
    loads[2].wait()
    step = tile_of(rows, 512)
    for at in range(0, rows, step):
        local = index[at : at + step].reshape(1, step) - base
        hot = lax.broadcasted_iota(jnp.int32, (cells, step), 0) == local
        hot = jnp.where(hot, 1.0, 0.0).astype(jnp.bfloat16)
        picked = jnp.dot(table, hot, preferred_element_type=jnp.float32)
        ft_out[:, at : at + step] = picked.astype(jnp.bfloat16)
        f_out[at : at + step, :] = jnp.transpose(picked).astype(jnp.bfloat16)
    loads[3].wait()


def prepare(x_slab, row_index, cell_factor, gene_scale, scale_k):
    rows, genes = x_slab.shape
    cells, rank = cell_factor.shape
    ins = (x_slab, row_index, cell_factor, gene_scale)
    return pl.pallas_call(
        functools.partial(prepare_kernel, scale_k),
        out_shape=(
            VMEM((rows, genes), jnp.bfloat16),
            VMEM((rows, rank), jnp.bfloat16),
            VMEM((rank, rows), jnp.bfloat16),
            VMEM((1, genes), jnp.float32),
            VMEM((genes, rank), jnp.float32),
        ),
        in_specs=[IN_ANY] * 4,
        out_specs=(IN_VMEM,) * 5,
        scratch_shapes=[
            VMEM((rows,), jnp.int32),
            VMEM((cells, rank), jnp.bfloat16),
            VMEM((genes,), jnp.float32),
            pltpu.SemaphoreType.DMA((4,)),
        ],
        compiler_params=params(),
        cost_estimate=cost(2 * rows * cells * rank, 2 * rows * genes * 2),
        name="prepare",
    )(*(pltpu.with_memory_space_constraint(a, pltpu.HBM) for a in ins))


def pick(axis, table):
    me = lax.axis_index(axis)
    value = jnp.int32(table[0])
    for place, entry in enumerate(table[1:], 1):
        value = jnp.where(me == place, jnp.int32(entry), value)
    return value


def partner(me, hop, size):
    return me ^ hop if size & (size - 1) == 0 else (me + hop) % size


def source(me, hop, size):
    return me ^ hop if size & (size - 1) == 0 else (me + size - hop) % size


def rows_kernel(tables, block, first, last, n_row, *refs):
    refs = list(refs)
    take = lambda count: [refs.pop(0) for _ in range(count)]
    x_ref, f_ref, ft_ref, bend_ref, shrink_ref = take(5)
    shares = take(n_row) if first else None
    carried_in = None if first else take(3)
    rows_out = take(len(tables))
    carried_out = None if last else take(3 if first else 1)
    parts_out = take(n_row) if last else None
    me = lax.axis_index("row")

    if first:
        (piece,) = take(1)
        depth = shares[0].shape[0]
        for hop in range(n_row):
            start = pl.multiple_of(source(me, hop, n_row) * depth, depth)
            piece[pl.ds(start, depth), :] = shares[hop][...]
        whole = piece[...].astype(jnp.float32)
        wide = jnp.transpose(whole).astype(jnp.bfloat16)
        scaled = (whole * shrink_ref[...]).astype(jnp.bfloat16)
        total = None
    else:
        total, wide, scaled = (ref[...] for ref in carried_in)

    bend = bend_ref[...]
    step = tile_of(block, 256)
    for table, out in zip(tables, rows_out):
        origin = pick("gene", table) * block if len(table) > 1 else 0
        for at in range(0, block, step):
            start = origin + at
            if len(table) > 1:
                start = pl.multiple_of(start, math.gcd(block, step))
            here = pl.ds(start, step)
            pred = jnp.dot(f_ref[here, :], wide, preferred_element_type=jnp.float32)
            resid = x_ref[here, :].astype(jnp.float32) - pred
            inside = jnp.maximum(1.0 - resid * resid * bend, 0.0)
            infl = (resid * (inside * inside)).astype(jnp.bfloat16)
            out[at : at + step, :] = jnp.dot(infl, scaled, preferred_element_type=jnp.float32).astype(out.dtype)
            cols = jnp.dot(ft_ref[:, here], infl, preferred_element_type=jnp.float32)
            total = cols if total is None else total + cols
    if first and not last:
        carried_out[1][...] = wide
        carried_out[2][...] = scaled
    if not last:
        carried_out[0][...] = total
        return
    (turned,) = take(1)
    turned[...] = jnp.transpose(total) * shrink_ref[...]
    depth = parts_out[0].shape[0]
    for hop in range(n_row):
        start = pl.multiple_of(partner(me, hop, n_row) * depth, depth)
        parts_out[hop][...] = turned[pl.ds(start, depth), :].astype(parts_out[hop].dtype)


def block_rows(tables, kinds, block, first, last, n_row, fixed, carried):
    genes, rank = fixed[4].shape
    out = [jax.ShapeDtypeStruct((block, rank), kind) for kind in kinds]
    if last:
        out += [jax.ShapeDtypeStruct((genes // n_row, rank), jnp.bfloat16 if hop else jnp.float32) for hop in range(n_row)]
    else:
        out += [VMEM((rank, genes), jnp.float32)]
    if first and not last:
        out += [VMEM((rank, genes), jnp.bfloat16), VMEM((genes, rank), jnp.bfloat16)]
    scratch = [VMEM((genes, rank), jnp.bfloat16)] if first else []
    if last:
        scratch.append(VMEM((genes, rank), jnp.float32))
    ins = pinned(*fixed) + (list(carried) if first else pinned(*carried))
    work = len(tables) * block * genes
    out = pl.pallas_call(
        functools.partial(rows_kernel, tables, block, first, last, n_row),
        out_shape=tuple(out),
        in_specs=[IN_VMEM] * len(ins),
        out_specs=(IN_VMEM,) * len(out),
        scratch_shapes=scratch,
        compiler_params=params(),
        cost_estimate=cost(6 * work * rank, work * 2),
        name="block_rows",
    )(*ins)
    done, rest = list(out[: len(tables)]), list(out[len(tables) :])
    return done, rest if first or last else rest + list(carried[1:])


def swap_row(value, hop, size):
    return lax.ppermute(value, "row", [(me, partner(me, hop, size)) for me in range(size)])


def ring_of(size):
    return [*range(0, size, 2), *reversed(range(1, size, 2))]


def steps_of(size):
    ahead = [(1, distance) for distance in range(size // 2, 0, -1)]
    back = [(-1, distance) for distance in range((size - 1) // 2, 0, -1)]
    return [step for pair in itertools.zip_longest(ahead, back) for step in pair if step]


def around(size, hops):
    ring = ring_of(size)
    return tuple(ring[(ring.index(place) + hops) % size] for place in range(size))


def plus(wide, narrow):
    return wide.astype(jnp.float32) + narrow.astype(jnp.float32)


def reduce_scatter(size, steps, blocks, mine, parts):
    came = {}
    for at, ((way, _), block) in enumerate(zip(steps, blocks), 1):
        if way in came:
            block = plus(block, came[way]).astype(jnp.bfloat16)
        if at == len(steps):
            block, *parts = lax.optimization_barrier((block, *parts))
        came[way] = lax.ppermute(block, "gene", list(enumerate(around(size, way))))
    for value in came.values():
        mine = plus(mine, value)
    return mine, list(came.values()), parts


def local(x_slab, cell_factor, row_index, gene_scale, gene_factor, first_moment, second_moment):
    rows_dev, genes_dev = x_slab.shape
    n_gene = lax.axis_size("gene")
    n_row = lax.axis_size("row")
    block = rows_dev // n_gene
    scale_k = 4.0 / math.sqrt(genes_dev * n_gene)
    factor_bf = gene_factor.astype(jnp.bfloat16)
    shares = [factor_bf] + [swap_row(factor_bf, hop, n_row) for hop in range(1, n_row)]
    fixed = prepare(x_slab, row_index, cell_factor, gene_scale, scale_k)

    if 1 < n_gene <= RING_MOST and block % 128 == 0:
        steps = steps_of(n_gene)
        tables = [around(n_gene, way * distance) for way, distance in steps] + [tuple(range(n_gene))]
        kinds = [jnp.bfloat16] * len(steps) + [jnp.float32]
        cuts = [0, 1, 2, len(tables)] if len(steps) > 2 else [0, 1, len(tables)]
        carried, blocks = shares, []
        for low, high in zip(cuts, cuts[1:]):
            last = high == len(tables)
            done, carried = block_rows(tables[low:high], kinds[low:high], block, low == 0, last, n_row, fixed, carried)
            blocks += done
        grad_cells, ends, parts = reduce_scatter(n_gene, steps, blocks[:-1], blocks[-1], carried)
    else:
        (rows,), parts = block_rows([(0,)], [jnp.float32], rows_dev, True, True, n_row, fixed, shares)
        grad_cells, ends = lax.psum_scatter(rows, "gene", scatter_dimension=0, tiled=True), []

    grad_genes = parts[0]
    others = [swap_row(parts[hop], hop, n_row) for hop in range(1, n_row)]
    if others and len(ends) > 1:
        others[0], _ = lax.optimization_barrier((others[0], ends[1]))
    for value in others:
        grad_genes = grad_genes + value.astype(jnp.float32)
    new_first = beta_one * first_moment + (1.0 - beta_one) * grad_genes
    new_second = beta_two * second_moment + (1.0 - beta_two) * grad_genes * grad_genes
    first_hat = new_first / (1.0 - beta_one**10)
    second_hat = new_second / (1.0 - beta_two**10)
    new_factor = gene_factor - learn_rate * first_hat / (jnp.sqrt(second_hat) + adam_eps)
    return (grad_cells, new_factor, new_first, new_second)


def solution(mesh):
    in_specs = (
        P(("grp", "row"), "gene"),
        P(("grp", "row"), None),
        P(("grp", "row")),
        P(("grp", "gene")),
        P(("grp", "gene", "row"), None),
        P(("grp", "gene", "row"), None),
        P(("grp", "gene", "row"), None),
    )
    out_specs = (
        P(("grp", "row", "gene"), None),
        P(("grp", "gene", "row"), None),
        P(("grp", "gene", "row"), None),
        P(("grp", "gene", "row"), None),
    )
    return jax.shard_map(local, mesh=mesh, in_specs=in_specs, out_specs=out_specs, check_vma=False)
```

```python
import functools
import itertools
import math

import jax
import jax.numpy as jnp
from jax import lax
from jax.experimental import pallas as pl
from jax.experimental.pallas import tpu as pltpu
from jax.sharding import PartitionSpec as P

tukey_c = 4.685
beta_one = 0.9
beta_two = 0.999
learn_rate = 0.02
adam_eps = 1e-08

RING_MOST = 8
VMEM = pltpu.VMEM
IN_VMEM = pl.BlockSpec(memory_space=VMEM)
IN_ANY = pl.BlockSpec(memory_space=pl.ANY)


def tile_of(rows, most):
    best = [t for t in range(128, most + 1, 128) if rows % t == 0]
    return best[-1] if best else rows


def params():
    return pltpu.CompilerParams(vmem_limit_bytes=24 * 1024 * 1024)


def cost(flops, moved):
    return pl.CostEstimate(flops=int(flops), bytes_accessed=int(moved), transcendentals=0)


def pinned(*arrays):
    return [pltpu.with_memory_space_constraint(a, VMEM) for a in arrays]


def prepare_kernel(scale_k, x_in, index_in, cell_in, scale_in, x_out, f_out, ft_out, bend_out, shrink_out, index, cell, scale, sems):
    loads = [
        pltpu.make_async_copy(src, dst, sems.at[at])
        for at, (src, dst) in enumerate(((scale_in, scale), (cell_in, cell), (index_in, index), (x_in, x_out)))
    ]
    for load in loads:
        load.start()
    cells, rank = cell.shape
    rows = index.shape[0]
    genes = scale.shape[0]
    loads[0].wait()
    inverse = 1.0 / scale[...].reshape(1, genes)
    bend_out[...] = (inverse * inverse) * (1.0 / (tukey_c * tukey_c))
    shrink_out[...] = jnp.transpose(jnp.broadcast_to(-scale_k * (inverse * inverse), (rank, genes)))
    loads[1].wait()
    table = jnp.transpose(cell[...].astype(jnp.float32)).astype(jnp.bfloat16)
    base = lax.axis_index("row") * cells
    loads[2].wait()
    step = tile_of(rows, 512)
    for at in range(0, rows, step):
        local = index[at : at + step].reshape(1, step) - base
        hot = lax.broadcasted_iota(jnp.int32, (cells, step), 0) == local
        hot = jnp.where(hot, 1.0, 0.0).astype(jnp.bfloat16)
        picked = jnp.dot(table, hot, preferred_element_type=jnp.float32)
        ft_out[:, at : at + step] = picked.astype(jnp.bfloat16)
        f_out[at : at + step, :] = jnp.transpose(picked).astype(jnp.bfloat16)
    loads[3].wait()


def prepare(x_slab, row_index, cell_factor, gene_scale, scale_k):
    rows, genes = x_slab.shape
    cells, rank = cell_factor.shape
    ins = (x_slab, row_index, cell_factor, gene_scale)
    return pl.pallas_call(
        functools.partial(prepare_kernel, scale_k),
        out_shape=(
            VMEM((rows, genes), jnp.bfloat16),
            VMEM((rows, rank), jnp.bfloat16),
            VMEM((rank, rows), jnp.bfloat16),
            VMEM((1, genes), jnp.float32),
            VMEM((genes, rank), jnp.float32),
        ),
        in_specs=[IN_ANY] * 4,
        out_specs=(IN_VMEM,) * 5,
        scratch_shapes=[
            VMEM((rows,), jnp.int32),
            VMEM((cells, rank), jnp.bfloat16),
            VMEM((genes,), jnp.float32),
            pltpu.SemaphoreType.DMA((4,)),
        ],
        compiler_params=params(),
        cost_estimate=cost(2 * rows * cells * rank, 2 * rows * genes * 2),
        name="prepare",
    )(*(pltpu.with_memory_space_constraint(a, pltpu.HBM) for a in ins))


def pick(axis, table):
    me = lax.axis_index(axis)
    value = jnp.int32(table[0])
    for place, entry in enumerate(table[1:], 1):
        value = jnp.where(me == place, jnp.int32(entry), value)
    return value


def partner(me, hop, size):
    return me ^ hop if size & (size - 1) == 0 else (me + hop) % size


def source(me, hop, size):
    return me ^ hop if size & (size - 1) == 0 else (me + size - hop) % size


def rows_kernel(tables, block, first, last, n_row, *refs):
    refs = list(refs)
    take = lambda count: [refs.pop(0) for _ in range(count)]
    x_ref, f_ref, ft_ref, bend_ref, shrink_ref = take(5)
    shares = take(n_row) if first else None
    carried_in = None if first else take(3)
    rows_out = take(len(tables))
    carried_out = None if last else take(3 if first else 1)
    parts_out = take(n_row) if last else None
    me = lax.axis_index("row")

    if first:
        (piece,) = take(1)
        depth = shares[0].shape[0]
        for hop in range(n_row):
            start = pl.multiple_of(source(me, hop, n_row) * depth, depth)
            piece[pl.ds(start, depth), :] = shares[hop][...]
        whole = piece[...].astype(jnp.float32)
        wide = jnp.transpose(whole).astype(jnp.bfloat16)
        scaled = (whole * shrink_ref[...]).astype(jnp.bfloat16)
        total = None
    else:
        total, wide, scaled = (ref[...] for ref in carried_in)

    bend = bend_ref[...]
    step = tile_of(block, 256)
    for table, out in zip(tables, rows_out):
        origin = pick("gene", table) * block if len(table) > 1 else 0
        for at in range(0, block, step):
            start = origin + at
            if len(table) > 1:
                start = pl.multiple_of(start, math.gcd(block, step))
            here = pl.ds(start, step)
            pred = jnp.dot(f_ref[here, :], wide, preferred_element_type=jnp.float32)
            resid = x_ref[here, :].astype(jnp.float32) - pred
            inside = jnp.maximum(1.0 - resid * resid * bend, 0.0)
            infl = (resid * (inside * inside)).astype(jnp.bfloat16)
            out[at : at + step, :] = jnp.dot(infl, scaled, preferred_element_type=jnp.float32).astype(out.dtype)
            cols = jnp.dot(ft_ref[:, here], infl, preferred_element_type=jnp.float32)
            total = cols if total is None else total + cols
    if first and not last:
        carried_out[1][...] = wide
        carried_out[2][...] = scaled
    if not last:
        carried_out[0][...] = total
        return
    (turned,) = take(1)
    turned[...] = jnp.transpose(total) * shrink_ref[...]
    depth = parts_out[0].shape[0]
    for hop in range(n_row):
        start = pl.multiple_of(partner(me, hop, n_row) * depth, depth)
        parts_out[hop][...] = turned[pl.ds(start, depth), :].astype(parts_out[hop].dtype)


def block_rows(tables, kinds, block, first, last, n_row, fixed, carried):
    genes, rank = fixed[4].shape
    out = [jax.ShapeDtypeStruct((block, rank), kind) for kind in kinds]
    if last:
        out += [jax.ShapeDtypeStruct((genes // n_row, rank), jnp.bfloat16 if hop else jnp.float32) for hop in range(n_row)]
    else:
        out += [VMEM((rank, genes), jnp.float32)]
    if first and not last:
        out += [VMEM((rank, genes), jnp.bfloat16), VMEM((genes, rank), jnp.bfloat16)]
    scratch = [VMEM((genes, rank), jnp.bfloat16)] if first else []
    if last:
        scratch.append(VMEM((genes, rank), jnp.float32))
    ins = pinned(*fixed) + (list(carried) if first else pinned(*carried))
    work = len(tables) * block * genes
    out = pl.pallas_call(
        functools.partial(rows_kernel, tables, block, first, last, n_row),
        out_shape=tuple(out),
        in_specs=[IN_VMEM] * len(ins),
        out_specs=(IN_VMEM,) * len(out),
        scratch_shapes=scratch,
        compiler_params=params(),
        cost_estimate=cost(6 * work * rank, work * 2),
        name="block_rows",
    )(*ins)
    done, rest = list(out[: len(tables)]), list(out[len(tables) :])
    return done, rest if first or last else rest + list(carried[1:])


def swap_row(value, hop, size):
    return lax.ppermute(value, "row", [(me, partner(me, hop, size)) for me in range(size)])


def ring_of(size):
    return [*range(0, size, 2), *reversed(range(1, size, 2))]


def steps_of(size):
    ahead = [(1, distance) for distance in range(size // 2, 0, -1)]
    back = [(-1, distance) for distance in range((size - 1) // 2, 0, -1)]
    return [step for pair in itertools.zip_longest(ahead, back) for step in pair if step]


def around(size, hops):
    ring = ring_of(size)
    return tuple(ring[(ring.index(place) + hops) % size] for place in range(size))


def plus(wide, narrow):
    return wide.astype(jnp.float32) + narrow.astype(jnp.float32)


def finish_kernel(n_ends, n_parts, *refs):
    ins, outs = refs[: n_ends + n_parts + 3], refs[n_ends + n_parts + 3 :]
    ends, parts = ins[:n_ends], ins[n_ends : n_ends + n_parts]
    factor, first, second = ins[n_ends + n_parts :]
    grad = parts[0][...]
    for part in parts[1:]:
        grad = plus(grad, part[...])
    new_first = beta_one * first[...] + (1.0 - beta_one) * grad
    new_second = beta_two * second[...] + (1.0 - beta_two) * grad * grad
    first_hat = new_first / (1.0 - beta_one**10)
    second_hat = new_second / (1.0 - beta_two**10)
    outs[0][...] = factor[...] - learn_rate * first_hat / (jnp.sqrt(second_hat) + adam_eps)
    outs[1][...] = new_first
    outs[2][...] = new_second
    if ends:
        rows = ends[0][...]
        for end in ends[1:]:
            rows = plus(rows, end[...])
        outs[3][...] = rows


def finish(ends, parts, factor, first, second):
    ins = [*ends, *parts, factor, first, second]
    shapes = [factor, factor, factor] + list(ends[:1])
    return pl.pallas_call(
        functools.partial(finish_kernel, len(ends), len(parts)),
        out_shape=tuple(jax.ShapeDtypeStruct(like.shape, jnp.float32) for like in shapes),
        in_specs=[IN_VMEM] * len(ins),
        out_specs=(IN_VMEM,) * len(shapes),
        compiler_params=params(),
        cost_estimate=cost(20 * factor.size, sum(4 * a.size for a in ins)),
        name="finish",
    )(*ins)


def local(x_slab, cell_factor, row_index, gene_scale, gene_factor, first_moment, second_moment):
    rows_dev, genes_dev = x_slab.shape
    n_gene = lax.axis_size("gene")
    n_row = lax.axis_size("row")
    block = rows_dev // n_gene
    scale_k = 4.0 / math.sqrt(genes_dev * n_gene)
    factor_bf = gene_factor.astype(jnp.bfloat16)
    shares = [factor_bf] + [swap_row(factor_bf, hop, n_row) for hop in range(1, n_row)]
    fixed = prepare(x_slab, row_index, cell_factor, gene_scale, scale_k)
    adam = (gene_factor, first_moment, second_moment)

    if n_gene == 1 or n_gene > RING_MOST or block % 128:
        (rows,), parts = block_rows([(0,)], [jnp.float32], rows_dev, True, True, n_row, fixed, shares)
        grad_cells = lax.psum_scatter(rows, "gene", scatter_dimension=0, tiled=True)
        others = [swap_row(parts[hop], hop, n_row) for hop in range(1, n_row)]
        return (grad_cells, *finish([], [parts[0], *others], *adam))

    steps = steps_of(n_gene)
    tables = [around(n_gene, way * distance) for way, distance in steps] + [tuple(range(n_gene))]
    kinds = [jnp.bfloat16] * len(steps) + [jnp.float32]
    cuts = [0, 1, 2, len(tables)] if len(steps) > 2 else [0, 1, len(tables)]
    carried, blocks = shares, []
    for low, high in zip(cuts, cuts[1:]):
        last = high == len(tables)
        done, carried = block_rows(tables[low:high], kinds[low:high], block, low == 0, last, n_row, fixed, carried)
        blocks += done
    parts = carried

    came = {}
    for (way, _), own in zip(steps, blocks):
        if way in came:
            own = plus(own, came[way]).astype(jnp.bfloat16)
        came[way] = lax.ppermute(own, "gene", list(enumerate(around(n_gene, way))))
    others = [swap_row(parts[hop], hop, n_row) for hop in range(1, n_row)]
    *adam_out, grad_cells = finish([blocks[-1], *came.values()], [parts[0], *others], *adam)
    return (grad_cells, *adam_out)


def solution(mesh):
    in_specs = (
        P(("grp", "row"), "gene"),
        P(("grp", "row"), None),
        P(("grp", "row")),
        P(("grp", "gene")),
        P(("grp", "gene", "row"), None),
        P(("grp", "gene", "row"), None),
        P(("grp", "gene", "row"), None),
    )
    out_specs = (
        P(("grp", "row", "gene"), None),
        P(("grp", "gene", "row"), None),
        P(("grp", "gene", "row"), None),
        P(("grp", "gene", "row"), None),
    )
    return jax.shard_map(local, mesh=mesh, in_specs=in_specs, out_specs=out_specs, check_vma=False)
```

```python
import functools
import itertools
import math

import jax
import jax.numpy as jnp
from jax import lax
from jax.experimental import pallas as pl
from jax.experimental.pallas import tpu as pltpu
from jax.sharding import PartitionSpec as P

tukey_c = 4.685
beta_one = 0.9
beta_two = 0.999
learn_rate = 0.02
adam_eps = 1e-08

RING_MOST = 8
VMEM = pltpu.VMEM
IN_VMEM = pl.BlockSpec(memory_space=VMEM)
IN_ANY = pl.BlockSpec(memory_space=pl.ANY)


def tile_of(rows, most):
    best = [t for t in range(128, most + 1, 128) if rows % t == 0]
    return best[-1] if best else rows


def params():
    return pltpu.CompilerParams(vmem_limit_bytes=24 * 1024 * 1024)


def cost(flops, moved):
    return pl.CostEstimate(flops=int(flops), bytes_accessed=int(moved), transcendentals=0)


def pinned(*arrays):
    return [pltpu.with_memory_space_constraint(a, VMEM) for a in arrays]


def prepare_kernel(scale_k, x_in, index_in, cell_in, scale_in, x_out, f_out, ft_out, bend_out, shrink_out, index, cell, scale, sems):
    loads = [
        pltpu.make_async_copy(src, dst, sems.at[at])
        for at, (src, dst) in enumerate(((scale_in, scale), (cell_in, cell), (index_in, index), (x_in, x_out)))
    ]
    for load in loads:
        load.start()
    cells, rank = cell.shape
    rows = index.shape[0]
    genes = scale.shape[0]
    loads[0].wait()
    inverse = 1.0 / scale[...].reshape(1, genes)
    bend_out[...] = (inverse * inverse) * (1.0 / (tukey_c * tukey_c))
    shrink_out[...] = jnp.transpose(jnp.broadcast_to(-scale_k * (inverse * inverse), (rank, genes)))
    loads[1].wait()
    table = jnp.transpose(cell[...].astype(jnp.float32)).astype(jnp.bfloat16)
    base = lax.axis_index("row") * cells
    loads[2].wait()
    step = tile_of(rows, 512)
    for at in range(0, rows, step):
        local = index[at : at + step].reshape(1, step) - base
        hot = lax.broadcasted_iota(jnp.int32, (cells, step), 0) == local
        hot = jnp.where(hot, 1.0, 0.0).astype(jnp.bfloat16)
        picked = jnp.dot(table, hot, preferred_element_type=jnp.float32)
        ft_out[:, at : at + step] = picked.astype(jnp.bfloat16)
        f_out[at : at + step, :] = jnp.transpose(picked).astype(jnp.bfloat16)
    loads[3].wait()


def prepare(x_slab, row_index, cell_factor, gene_scale, scale_k):
    rows, genes = x_slab.shape
    cells, rank = cell_factor.shape
    ins = (x_slab, row_index, cell_factor, gene_scale)
    return pl.pallas_call(
        functools.partial(prepare_kernel, scale_k),
        out_shape=(
            VMEM((rows, genes), jnp.bfloat16),
            VMEM((rows, rank), jnp.bfloat16),
            VMEM((rank, rows), jnp.bfloat16),
            VMEM((1, genes), jnp.float32),
            VMEM((genes, rank), jnp.float32),
        ),
        in_specs=[IN_ANY] * 4,
        out_specs=(IN_VMEM,) * 5,
        scratch_shapes=[
            VMEM((rows,), jnp.int32),
            VMEM((cells, rank), jnp.bfloat16),
            VMEM((genes,), jnp.float32),
            pltpu.SemaphoreType.DMA((4,)),
        ],
        compiler_params=params(),
        cost_estimate=cost(2 * rows * cells * rank, 2 * rows * genes * 2),
        name="prepare",
    )(*(pltpu.with_memory_space_constraint(a, pltpu.HBM) for a in ins))


def pick(axis, table):
    me = lax.axis_index(axis)
    value = jnp.int32(table[0])
    for place, entry in enumerate(table[1:], 1):
        value = jnp.where(me == place, jnp.int32(entry), value)
    return value


def partner(me, hop, size):
    return me ^ hop if size & (size - 1) == 0 else (me + hop) % size


def source(me, hop, size):
    return me ^ hop if size & (size - 1) == 0 else (me + size - hop) % size


def rows_kernel(tables, block, first, last, n_row, *refs):
    refs = list(refs)
    take = lambda count: [refs.pop(0) for _ in range(count)]
    x_ref, f_ref, ft_ref, bend_ref, shrink_ref = take(5)
    shares = take(n_row) if first else None
    carried_in = None if first else take(3)
    rows_out = take(len(tables))
    carried_out = None if last else take(3 if first else 1)
    parts_out = take(n_row) if last else None
    me = lax.axis_index("row")

    if first:
        (piece,) = take(1)
        depth = shares[0].shape[0]
        for hop in range(n_row):
            start = pl.multiple_of(source(me, hop, n_row) * depth, depth)
            piece[pl.ds(start, depth), :] = shares[hop][...]
        whole = piece[...].astype(jnp.float32)
        wide = jnp.transpose(whole).astype(jnp.bfloat16)
        scaled = (whole * shrink_ref[...]).astype(jnp.bfloat16)
        total = None
    else:
        total, wide, scaled = (ref[...] for ref in carried_in)

    bend = bend_ref[...]
    step = tile_of(block, 256)
    for table, out in zip(tables, rows_out):
        origin = pick("gene", table) * block if len(table) > 1 else 0
        for at in range(0, block, step):
            start = origin + at
            if len(table) > 1:
                start = pl.multiple_of(start, math.gcd(block, step))
            here = pl.ds(start, step)
            pred = jnp.dot(f_ref[here, :], wide, preferred_element_type=jnp.float32)
            resid = x_ref[here, :].astype(jnp.float32) - pred
            inside = jnp.maximum(1.0 - resid * resid * bend, 0.0)
            infl = (resid * (inside * inside)).astype(jnp.bfloat16)
            out[at : at + step, :] = jnp.dot(infl, scaled, preferred_element_type=jnp.float32).astype(out.dtype)
            cols = jnp.dot(ft_ref[:, here], infl, preferred_element_type=jnp.float32)
            total = cols if total is None else total + cols
    if first and not last:
        carried_out[1][...] = wide
        carried_out[2][...] = scaled
    if not last:
        carried_out[0][...] = total
        return
    (turned,) = take(1)
    turned[...] = jnp.transpose(total) * shrink_ref[...]
    depth = parts_out[0].shape[0]
    for hop in range(n_row):
        start = pl.multiple_of(partner(me, hop, n_row) * depth, depth)
        parts_out[hop][...] = turned[pl.ds(start, depth), :].astype(parts_out[hop].dtype)


def block_rows(tables, kinds, block, first, last, n_row, fixed, carried):
    genes, rank = fixed[4].shape
    out = [jax.ShapeDtypeStruct((block, rank), kind) for kind in kinds]
    if last:
        out += [jax.ShapeDtypeStruct((genes // n_row, rank), jnp.bfloat16 if hop else jnp.float32) for hop in range(n_row)]
    else:
        out += [VMEM((rank, genes), jnp.float32)]
    if first and not last:
        out += [VMEM((rank, genes), jnp.bfloat16), VMEM((genes, rank), jnp.bfloat16)]
    scratch = [VMEM((genes, rank), jnp.bfloat16)] if first else []
    if last:
        scratch.append(VMEM((genes, rank), jnp.float32))
    ins = pinned(*fixed) + (list(carried) if first else pinned(*carried))
    work = len(tables) * block * genes
    out = pl.pallas_call(
        functools.partial(rows_kernel, tables, block, first, last, n_row),
        out_shape=tuple(out),
        in_specs=[IN_VMEM] * len(ins),
        out_specs=(IN_VMEM,) * len(out),
        scratch_shapes=scratch,
        compiler_params=params(),
        cost_estimate=cost(6 * work * rank, work * 2),
        name="block_rows",
    )(*ins)
    done, rest = list(out[: len(tables)]), list(out[len(tables) :])
    return done, rest if first or last else rest + list(carried[1:])


def swap_row(value, hop, size):
    return lax.ppermute(value, "row", [(me, partner(me, hop, size)) for me in range(size)])


def steps_of(size):
    ahead = [(1, distance) for distance in range(size // 2, 0, -1)]
    back = [(-1, distance) for distance in range((size - 1) // 2, 0, -1)]
    return [step for pair in itertools.zip_longest(ahead, back) for step in pair if step]


def around(size, hops):
    return tuple((place + hops) % size for place in range(size))


def plus(wide, narrow):
    return wide.astype(jnp.float32) + narrow.astype(jnp.float32)


def finish_kernel(n_ends, n_parts, *refs):
    ins, outs = refs[: n_ends + n_parts + 3], refs[n_ends + n_parts + 3 :]
    ends, parts = ins[:n_ends], ins[n_ends : n_ends + n_parts]
    factor, first, second = ins[n_ends + n_parts :]
    grad = parts[0][...]
    for part in parts[1:]:
        grad = plus(grad, part[...])
    new_first = beta_one * first[...] + (1.0 - beta_one) * grad
    new_second = beta_two * second[...] + (1.0 - beta_two) * grad * grad
    first_hat = new_first / (1.0 - beta_one**10)
    second_hat = new_second / (1.0 - beta_two**10)
    outs[0][...] = factor[...] - learn_rate * first_hat / (jnp.sqrt(second_hat) + adam_eps)
    outs[1][...] = new_first
    outs[2][...] = new_second
    if ends:
        rows = ends[0][...]
        for end in ends[1:]:
            rows = plus(rows, end[...])
        outs[3][...] = rows


def finish(ends, parts, factor, first, second):
    ins = [*ends, *parts, factor, first, second]
    shapes = [factor, factor, factor] + list(ends[:1])
    return pl.pallas_call(
        functools.partial(finish_kernel, len(ends), len(parts)),
        out_shape=tuple(jax.ShapeDtypeStruct(like.shape, jnp.float32) for like in shapes),
        in_specs=[IN_VMEM] * len(ins),
        out_specs=(IN_VMEM,) * len(shapes),
        compiler_params=params(),
        cost_estimate=cost(20 * factor.size, sum(4 * a.size for a in ins)),
        name="finish",
    )(*ins)


def local(x_slab, cell_factor, row_index, gene_scale, gene_factor, first_moment, second_moment):
    rows_dev, genes_dev = x_slab.shape
    n_gene = lax.axis_size("gene")
    n_row = lax.axis_size("row")
    block = rows_dev // n_gene
    scale_k = 4.0 / math.sqrt(genes_dev * n_gene)
    factor_bf = gene_factor.astype(jnp.bfloat16)
    shares = [factor_bf] + [swap_row(factor_bf, hop, n_row) for hop in range(1, n_row)]
    fixed = prepare(x_slab, row_index, cell_factor, gene_scale, scale_k)
    adam = (gene_factor, first_moment, second_moment)

    if n_gene == 1 or n_gene > RING_MOST or block % 128:
        (rows,), parts = block_rows([(0,)], [jnp.float32], rows_dev, True, True, n_row, fixed, shares)
        grad_cells = lax.psum_scatter(rows, "gene", scatter_dimension=0, tiled=True)
        others = [swap_row(parts[hop], hop, n_row) for hop in range(1, n_row)]
        return (grad_cells, *finish([], [parts[0], *others], *adam))

    steps = steps_of(n_gene)
    tables = [around(n_gene, way * distance) for way, distance in steps] + [tuple(range(n_gene))]
    kinds = [jnp.bfloat16] * len(steps) + [jnp.float32]
    cuts = [0, 1, 2, len(tables)] if len(steps) > 2 else [0, 1, len(tables)]
    carried, blocks = shares, []
    for low, high in zip(cuts, cuts[1:]):
        last = high == len(tables)
        done, carried = block_rows(tables[low:high], kinds[low:high], block, low == 0, last, n_row, fixed, carried)
        blocks += done
    parts = carried

    came = {}
    for (way, _), own in zip(steps, blocks):
        if way in came:
            own = plus(own, came[way]).astype(jnp.bfloat16)
        came[way] = lax.ppermute(own, "gene", list(enumerate(around(n_gene, way))))
    others = [swap_row(parts[hop], hop, n_row) for hop in range(1, n_row)]
    *adam_out, grad_cells = finish([blocks[-1], *came.values()], [parts[0], *others], *adam)
    return (grad_cells, *adam_out)


def solution(mesh):
    in_specs = (
        P(("grp", "row"), "gene"),
        P(("grp", "row"), None),
        P(("grp", "row")),
        P(("grp", "gene")),
        P(("grp", "gene", "row"), None),
        P(("grp", "gene", "row"), None),
        P(("grp", "gene", "row"), None),
    )
    out_specs = (
        P(("grp", "row", "gene"), None),
        P(("grp", "gene", "row"), None),
        P(("grp", "gene", "row"), None),
        P(("grp", "gene", "row"), None),
    )
    return jax.shard_map(local, mesh=mesh, in_specs=in_specs, out_specs=out_specs, check_vma=False)
```

```python
import functools
import itertools
import math

import jax
import jax.numpy as jnp
from jax import lax
from jax.experimental import pallas as pl
from jax.experimental.pallas import tpu as pltpu
from jax.sharding import PartitionSpec as P

tukey_c = 4.685
beta_one = 0.9
beta_two = 0.999
learn_rate = 0.02
adam_eps = 1e-08

RING_MOST = 8
VMEM = pltpu.VMEM
IN_VMEM = pl.BlockSpec(memory_space=VMEM)
IN_ANY = pl.BlockSpec(memory_space=pl.ANY)


def tile_of(rows, most):
    best = [t for t in range(128, most + 1, 128) if rows % t == 0]
    return best[-1] if best else rows


def params():
    return pltpu.CompilerParams(vmem_limit_bytes=24 * 1024 * 1024)


def cost(flops, moved):
    return pl.CostEstimate(flops=int(flops), bytes_accessed=int(moved), transcendentals=0)


def pinned(*arrays):
    return [pltpu.with_memory_space_constraint(a, VMEM) for a in arrays]


def prepare_kernel(scale_k, x_in, index_in, cell_in, scale_in, x_out, f_out, ft_out, bend_out, shrink_out, index, cell, scale, sems):
    loads = [
        pltpu.make_async_copy(src, dst, sems.at[at])
        for at, (src, dst) in enumerate(((scale_in, scale), (cell_in, cell), (index_in, index), (x_in, x_out)))
    ]
    for load in loads:
        load.start()
    cells, rank = cell.shape
    rows = index.shape[0]
    genes = scale.shape[0]
    loads[0].wait()
    inverse = 1.0 / scale[...].reshape(1, genes)
    bend_out[...] = (inverse * inverse) * (1.0 / (tukey_c * tukey_c))
    shrink_out[...] = jnp.transpose(jnp.broadcast_to(-scale_k * (inverse * inverse), (rank, genes)))
    loads[1].wait()
    table = jnp.transpose(cell[...].astype(jnp.float32)).astype(jnp.bfloat16)
    base = lax.axis_index("row") * cells
    loads[2].wait()
    step = tile_of(rows, 512)
    for at in range(0, rows, step):
        local = index[at : at + step].reshape(1, step) - base
        hot = lax.broadcasted_iota(jnp.int32, (cells, step), 0) == local
        hot = jnp.where(hot, 1.0, 0.0).astype(jnp.bfloat16)
        picked = jnp.dot(table, hot, preferred_element_type=jnp.float32)
        ft_out[:, at : at + step] = picked.astype(jnp.bfloat16)
        f_out[at : at + step, :] = jnp.transpose(picked).astype(jnp.bfloat16)
    loads[3].wait()


def prepare(x_slab, row_index, cell_factor, gene_scale, scale_k):
    rows, genes = x_slab.shape
    cells, rank = cell_factor.shape
    ins = (x_slab, row_index, cell_factor, gene_scale)
    return pl.pallas_call(
        functools.partial(prepare_kernel, scale_k),
        out_shape=(
            VMEM((rows, genes), jnp.bfloat16),
            VMEM((rows, rank), jnp.bfloat16),
            VMEM((rank, rows), jnp.bfloat16),
            VMEM((1, genes), jnp.float32),
            VMEM((genes, rank), jnp.float32),
        ),
        in_specs=[IN_ANY] * 4,
        out_specs=(IN_VMEM,) * 5,
        scratch_shapes=[
            VMEM((rows,), jnp.int32),
            VMEM((cells, rank), jnp.bfloat16),
            VMEM((genes,), jnp.float32),
            pltpu.SemaphoreType.DMA((4,)),
        ],
        compiler_params=params(),
        cost_estimate=cost(2 * rows * cells * rank, 2 * rows * genes * 2),
        name="prepare",
    )(*(pltpu.with_memory_space_constraint(a, pltpu.HBM) for a in ins))


def pick(axis, table):
    me = lax.axis_index(axis)
    value = jnp.int32(table[0])
    for place, entry in enumerate(table[1:], 1):
        value = jnp.where(me == place, jnp.int32(entry), value)
    return value


def partner(me, hop, size):
    return me ^ hop if size & (size - 1) == 0 else (me + hop) % size


def source(me, hop, size):
    return me ^ hop if size & (size - 1) == 0 else (me + size - hop) % size


def rows_kernel(tables, block, first, last, n_row, *refs):
    refs = list(refs)
    take = lambda count: [refs.pop(0) for _ in range(count)]
    x_ref, f_ref, ft_ref, bend_ref, shrink_ref = take(5)
    shares = take(n_row) if first else None
    carried_in = None if first else take(3)
    rows_out = take(len(tables))
    carried_out = None if last else take(3 if first else 1)
    parts_out = take(n_row) if last else None
    me = lax.axis_index("row")

    if first:
        (piece,) = take(1)
        depth = shares[0].shape[0]
        for hop in range(n_row):
            start = pl.multiple_of(source(me, hop, n_row) * depth, depth)
            piece[pl.ds(start, depth), :] = shares[hop][...]
        whole = piece[...].astype(jnp.float32)
        wide = jnp.transpose(whole).astype(jnp.bfloat16)
        scaled = (whole * shrink_ref[...]).astype(jnp.bfloat16)
        total = None
    else:
        total, wide, scaled = (ref[...] for ref in carried_in)

    bend = bend_ref[...]
    step = tile_of(block, 256)
    tiles = []
    for table, out in zip(tables, rows_out):
        origin = pick("gene", table) * block if len(table) > 1 else 0
        for at in range(0, block, step):
            start = origin + at
            if len(table) > 1:
                start = pl.multiple_of(start, math.gcd(block, step))
            tiles.append((out, at, pl.ds(start, step)))

    def predict(here):
        return jnp.dot(f_ref[here, :], wide, preferred_element_type=jnp.float32)

    def influence(here, pred):
        resid = x_ref[here, :].astype(jnp.float32) - pred
        inside = jnp.maximum(1.0 - resid * resid * bend, 0.0)
        return (resid * (inside * inside)).astype(jnp.bfloat16)

    def gradients(tile, infl, total):
        out, at, here = tile
        cols = jnp.dot(ft_ref[:, here], infl, preferred_element_type=jnp.float32)
        out[at : at + step, :] = jnp.dot(infl, scaled, preferred_element_type=jnp.float32).astype(out.dtype)
        return cols if total is None else total + cols

    pred = predict(tiles[0][2])
    infl = None
    for at, tile in enumerate(tiles):
        later = predict(tiles[at + 1][2]) if at + 1 < len(tiles) else None
        now = influence(tile[2], pred)
        if at:
            total = gradients(tiles[at - 1], infl, total)
        infl, pred = now, later
    total = gradients(tiles[-1], infl, total)

    if first and not last:
        carried_out[1][...] = wide
        carried_out[2][...] = scaled
    if not last:
        carried_out[0][...] = total
        return
    (turned,) = take(1)
    turned[...] = jnp.transpose(total) * shrink_ref[...]
    depth = parts_out[0].shape[0]
    for hop in range(n_row):
        start = pl.multiple_of(partner(me, hop, n_row) * depth, depth)
        parts_out[hop][...] = turned[pl.ds(start, depth), :].astype(parts_out[hop].dtype)


def block_rows(tables, kinds, block, first, last, n_row, fixed, carried):
    genes, rank = fixed[4].shape
    out = [jax.ShapeDtypeStruct((block, rank), kind) for kind in kinds]
    if last:
        out += [jax.ShapeDtypeStruct((genes // n_row, rank), jnp.bfloat16 if hop else jnp.float32) for hop in range(n_row)]
    else:
        out += [VMEM((rank, genes), jnp.float32)]
    if first and not last:
        out += [VMEM((rank, genes), jnp.bfloat16), VMEM((genes, rank), jnp.bfloat16)]
    scratch = [VMEM((genes, rank), jnp.bfloat16)] if first else []
    if last:
        scratch.append(VMEM((genes, rank), jnp.float32))
    ins = pinned(*fixed) + (list(carried) if first else pinned(*carried))
    work = len(tables) * block * genes
    out = pl.pallas_call(
        functools.partial(rows_kernel, tables, block, first, last, n_row),
        out_shape=tuple(out),
        in_specs=[IN_VMEM] * len(ins),
        out_specs=(IN_VMEM,) * len(out),
        scratch_shapes=scratch,
        compiler_params=params(),
        cost_estimate=cost(6 * work * rank, work * 2),
        name="block_rows",
    )(*ins)
    done, rest = list(out[: len(tables)]), list(out[len(tables) :])
    return done, rest if first or last else rest + list(carried[1:])


def swap_row(value, hop, size):
    return lax.ppermute(value, "row", [(me, partner(me, hop, size)) for me in range(size)])


def ring_of(size):
    return [*range(0, size, 2), *reversed(range(1, size, 2))]


def steps_of(size):
    ahead = [(1, distance) for distance in range(size // 2, 0, -1)]
    back = [(-1, distance) for distance in range((size - 1) // 2, 0, -1)]
    return [step for pair in itertools.zip_longest(ahead, back) for step in pair if step]


def around(size, hops):
    ring = ring_of(size)
    return tuple(ring[(ring.index(place) + hops) % size] for place in range(size))


def plus(wide, narrow):
    return wide.astype(jnp.float32) + narrow.astype(jnp.float32)


def finish_kernel(n_ends, n_parts, *refs):
    ins, outs = refs[: n_ends + n_parts + 3], refs[n_ends + n_parts + 3 :]
    ends, parts = ins[:n_ends], ins[n_ends : n_ends + n_parts]
    factor, first, second = ins[n_ends + n_parts :]
    grad = parts[0][...]
    for part in parts[1:]:
        grad = plus(grad, part[...])
    new_first = beta_one * first[...] + (1.0 - beta_one) * grad
    new_second = beta_two * second[...] + (1.0 - beta_two) * grad * grad
    first_hat = new_first / (1.0 - beta_one**10)
    second_hat = new_second / (1.0 - beta_two**10)
    outs[0][...] = factor[...] - learn_rate * first_hat / (jnp.sqrt(second_hat) + adam_eps)
    outs[1][...] = new_first
    outs[2][...] = new_second
    if ends:
        rows = ends[0][...]
        for end in ends[1:]:
            rows = plus(rows, end[...])
        outs[3][...] = rows


def finish(ends, parts, factor, first, second):
    ins = [*ends, *parts, factor, first, second]
    shapes = [factor, factor, factor] + list(ends[:1])
    return pl.pallas_call(
        functools.partial(finish_kernel, len(ends), len(parts)),
        out_shape=tuple(jax.ShapeDtypeStruct(like.shape, jnp.float32) for like in shapes),
        in_specs=[IN_VMEM] * len(ins),
        out_specs=(IN_VMEM,) * len(shapes),
        compiler_params=params(),
        cost_estimate=cost(20 * factor.size, sum(4 * a.size for a in ins)),
        name="finish",
    )(*ins)


def local(x_slab, cell_factor, row_index, gene_scale, gene_factor, first_moment, second_moment):
    rows_dev, genes_dev = x_slab.shape
    n_gene = lax.axis_size("gene")
    n_row = lax.axis_size("row")
    block = rows_dev // n_gene
    scale_k = 4.0 / math.sqrt(genes_dev * n_gene)
    factor_bf = gene_factor.astype(jnp.bfloat16)
    shares = [factor_bf] + [swap_row(factor_bf, hop, n_row) for hop in range(1, n_row)]
    fixed = prepare(x_slab, row_index, cell_factor, gene_scale, scale_k)
    adam = (gene_factor, first_moment, second_moment)

    if n_gene == 1 or n_gene > RING_MOST or block % 128:
        (rows,), parts = block_rows([(0,)], [jnp.float32], rows_dev, True, True, n_row, fixed, shares)
        grad_cells = lax.psum_scatter(rows, "gene", scatter_dimension=0, tiled=True)
        others = [swap_row(parts[hop], hop, n_row) for hop in range(1, n_row)]
        return (grad_cells, *finish([], [parts[0], *others], *adam))

    steps = steps_of(n_gene)
    tables = [around(n_gene, way * distance) for way, distance in steps] + [tuple(range(n_gene))]
    kinds = [jnp.bfloat16] * len(steps) + [jnp.float32]
    cuts = [0, 1, 2, len(tables)] if len(steps) > 2 else [0, 1, len(tables)]
    carried, blocks = shares, []
    for low, high in zip(cuts, cuts[1:]):
        last = high == len(tables)
        done, carried = block_rows(tables[low:high], kinds[low:high], block, low == 0, last, n_row, fixed, carried)
        blocks += done
    parts = carried

    came = {}
    for (way, _), own in zip(steps, blocks):
        if way in came:
            own = plus(own, came[way]).astype(jnp.bfloat16)
        came[way] = lax.ppermute(own, "gene", list(enumerate(around(n_gene, way))))
    others = [swap_row(parts[hop], hop, n_row) for hop in range(1, n_row)]
    *adam_out, grad_cells = finish([blocks[-1], *came.values()], [parts[0], *others], *adam)
    return (grad_cells, *adam_out)


def solution(mesh):
    in_specs = (
        P(("grp", "row"), "gene"),
        P(("grp", "row"), None),
        P(("grp", "row")),
        P(("grp", "gene")),
        P(("grp", "gene", "row"), None),
        P(("grp", "gene", "row"), None),
        P(("grp", "gene", "row"), None),
    )
    out_specs = (
        P(("grp", "row", "gene"), None),
        P(("grp", "gene", "row"), None),
        P(("grp", "gene", "row"), None),
        P(("grp", "gene", "row"), None),
    )
    return jax.shard_map(local, mesh=mesh, in_specs=in_specs, out_specs=out_specs, check_vma=False)
```

```python
import functools
import itertools
import math

import jax
import jax.numpy as jnp
from jax import lax
from jax.experimental import pallas as pl
from jax.experimental.pallas import tpu as pltpu
from jax.sharding import PartitionSpec as P

tukey_c = 4.685
beta_one = 0.9
beta_two = 0.999
learn_rate = 0.02
adam_eps = 1e-08

RING_MOST = 8
VMEM = pltpu.VMEM
IN_VMEM = pl.BlockSpec(memory_space=VMEM)
IN_ANY = pl.BlockSpec(memory_space=pl.ANY)


def tile_of(rows, most):
    best = [t for t in range(128, most + 1, 128) if rows % t == 0]
    return best[-1] if best else rows


def params():
    return pltpu.CompilerParams(vmem_limit_bytes=24 * 1024 * 1024)


def cost(flops, moved):
    return pl.CostEstimate(flops=int(flops), bytes_accessed=int(moved), transcendentals=0)


def pinned(*arrays):
    return [pltpu.with_memory_space_constraint(a, VMEM) for a in arrays]


def prepare_kernel(scale_k, x_in, index_in, cell_in, scale_in, x_out, f_out, ft_out, bend_out, shrink_out, index, cell, scale, sems):
    loads = [
        pltpu.make_async_copy(src, dst, sems.at[at])
        for at, (src, dst) in enumerate(((scale_in, scale), (cell_in, cell), (index_in, index), (x_in, x_out)))
    ]
    for load in loads:
        load.start()
    cells, rank = cell.shape
    rows = index.shape[0]
    genes = scale.shape[0]
    loads[0].wait()
    inverse = 1.0 / scale[...].reshape(1, genes)
    bend_out[...] = (inverse * inverse) * (1.0 / (tukey_c * tukey_c))
    shrink_out[...] = jnp.transpose(jnp.broadcast_to(-scale_k * (inverse * inverse), (rank, genes)))
    loads[1].wait()
    table = jnp.transpose(cell[...].astype(jnp.float32)).astype(jnp.bfloat16)
    base = lax.axis_index("row") * cells
    loads[2].wait()
    step = tile_of(rows, 512)
    for at in range(0, rows, step):
        local = index[at : at + step].reshape(1, step) - base
        hot = lax.broadcasted_iota(jnp.int32, (cells, step), 0) == local
        hot = jnp.where(hot, 1.0, 0.0).astype(jnp.bfloat16)
        picked = jnp.dot(table, hot, preferred_element_type=jnp.float32)
        ft_out[:, at : at + step] = picked.astype(jnp.bfloat16)
        f_out[at : at + step, :] = jnp.transpose(picked).astype(jnp.bfloat16)
    loads[3].wait()


def prepare(x_slab, row_index, cell_factor, gene_scale, scale_k):
    rows, genes = x_slab.shape
    cells, rank = cell_factor.shape
    ins = (x_slab, row_index, cell_factor, gene_scale)
    return pl.pallas_call(
        functools.partial(prepare_kernel, scale_k),
        out_shape=(
            VMEM((rows, genes), jnp.bfloat16),
            VMEM((rows, rank), jnp.bfloat16),
            VMEM((rank, rows), jnp.bfloat16),
            VMEM((1, genes), jnp.float32),
            VMEM((genes, rank), jnp.float32),
        ),
        in_specs=[IN_ANY] * 4,
        out_specs=(IN_VMEM,) * 5,
        scratch_shapes=[
            VMEM((rows,), jnp.int32),
            VMEM((cells, rank), jnp.bfloat16),
            VMEM((genes,), jnp.float32),
            pltpu.SemaphoreType.DMA((4,)),
        ],
        compiler_params=params(),
        cost_estimate=cost(2 * rows * cells * rank, 2 * rows * genes * 2),
        name="prepare",
    )(*(pltpu.with_memory_space_constraint(a, pltpu.HBM) for a in ins))


def pick(axis, table):
    me = lax.axis_index(axis)
    value = jnp.int32(table[0])
    for place, entry in enumerate(table[1:], 1):
        value = jnp.where(me == place, jnp.int32(entry), value)
    return value


def partner(me, hop, size):
    return me ^ hop if size & (size - 1) == 0 else (me + hop) % size


def source(me, hop, size):
    return me ^ hop if size & (size - 1) == 0 else (me + size - hop) % size


def rows_kernel(pieces, block, first, last, n_row, *refs):
    refs = list(refs)
    take = lambda count: [refs.pop(0) for _ in range(count)]
    x_ref, f_ref, ft_ref, bend_ref, shrink_ref = take(5)
    shares = take(n_row) if first else None
    carried_in = None if first else take(3)
    rows_out = take(len(pieces))
    carried_out = None if last else take(3 if first else 1)
    parts_out = take(n_row) if last else None
    me = lax.axis_index("row")

    if first:
        (piece,) = take(1)
        depth = shares[0].shape[0]
        for hop in range(n_row):
            start = pl.multiple_of(source(me, hop, n_row) * depth, depth)
            piece[pl.ds(start, depth), :] = shares[hop][...]
        whole = piece[...].astype(jnp.float32)
        wide = jnp.transpose(whole).astype(jnp.bfloat16)
        scaled = (whole * shrink_ref[...]).astype(jnp.bfloat16)
        total = None
    else:
        total, wide, scaled = (ref[...] for ref in carried_in)

    bend = bend_ref[...]
    tiles = []
    for (table, low, high), out in zip(pieces, rows_out):
        step = tile_of(high - low, 256)
        origin = pick("gene", table) * block if len(table) > 1 else 0
        for at in range(low, high, step):
            start = origin + at
            if len(table) > 1:
                start = pl.multiple_of(start, math.gcd(block, low, step))
            tiles.append((out, at - low, pl.ds(start, step)))

    def predict(here):
        return jnp.dot(f_ref[here, :], wide, preferred_element_type=jnp.float32)

    def influence(here, pred):
        resid = x_ref[here, :].astype(jnp.float32) - pred
        inside = jnp.maximum(1.0 - resid * resid * bend, 0.0)
        return (resid * (inside * inside)).astype(jnp.bfloat16)

    def gradients(tile, infl, total):
        out, at, here = tile
        cols = jnp.dot(ft_ref[:, here], infl, preferred_element_type=jnp.float32)
        rows = jnp.dot(infl, scaled, preferred_element_type=jnp.float32)
        out[at : at + rows.shape[0], :] = rows.astype(out.dtype)
        return cols if total is None else total + cols

    pred = predict(tiles[0][2])
    infl = None
    for at, tile in enumerate(tiles):
        later = predict(tiles[at + 1][2]) if at + 1 < len(tiles) else None
        now = influence(tile[2], pred)
        if at:
            total = gradients(tiles[at - 1], infl, total)
        infl, pred = now, later
    total = gradients(tiles[-1], infl, total)

    if first and not last:
        carried_out[1][...] = wide
        carried_out[2][...] = scaled
    if not last:
        carried_out[0][...] = total
        return
    (turned,) = take(1)
    turned[...] = jnp.transpose(total) * shrink_ref[...]
    depth = parts_out[0].shape[0]
    for hop in range(n_row):
        start = pl.multiple_of(partner(me, hop, n_row) * depth, depth)
        parts_out[hop][...] = turned[pl.ds(start, depth), :].astype(parts_out[hop].dtype)


def block_rows(pieces, kinds, block, first, last, n_row, fixed, carried):
    genes, rank = fixed[4].shape
    out = [jax.ShapeDtypeStruct((high - low, rank), kind) for (_, low, high), kind in zip(pieces, kinds)]
    if last:
        out += [jax.ShapeDtypeStruct((genes // n_row, rank), jnp.bfloat16 if hop else jnp.float32) for hop in range(n_row)]
    else:
        out += [VMEM((rank, genes), jnp.float32)]
    if first and not last:
        out += [VMEM((rank, genes), jnp.bfloat16), VMEM((genes, rank), jnp.bfloat16)]
    scratch = [VMEM((genes, rank), jnp.bfloat16)] if first else []
    if last:
        scratch.append(VMEM((genes, rank), jnp.float32))
    ins = pinned(*fixed) + (list(carried) if first else pinned(*carried))
    work = sum(high - low for _, low, high in pieces) * genes
    out = pl.pallas_call(
        functools.partial(rows_kernel, pieces, block, first, last, n_row),
        out_shape=tuple(out),
        in_specs=[IN_VMEM] * len(ins),
        out_specs=(IN_VMEM,) * len(out),
        scratch_shapes=scratch,
        compiler_params=params(),
        cost_estimate=cost(6 * work * rank, work * 2),
        name="block_rows",
    )(*ins)
    done, rest = list(out[: len(pieces)]), list(out[len(pieces) :])
    return done, rest if first or last else rest + list(carried[1:])


def swap_row(value, hop, size):
    return lax.ppermute(value, "row", [(me, partner(me, hop, size)) for me in range(size)])


def ring_of(size):
    return [*range(0, size, 2), *reversed(range(1, size, 2))]


def steps_of(size):
    ahead = [(1, distance) for distance in range(size // 2, 0, -1)]
    back = [(-1, distance) for distance in range((size - 1) // 2, 0, -1)]
    return [step for pair in itertools.zip_longest(ahead, back) for step in pair if step]


def around(size, hops):
    ring = ring_of(size)
    return tuple(ring[(ring.index(place) + hops) % size] for place in range(size))


def plus(wide, narrow):
    return wide.astype(jnp.float32) + narrow.astype(jnp.float32)


def finish_kernel(n_ends, n_parts, *refs):
    ins, outs = refs[: n_ends + n_parts + 3], refs[n_ends + n_parts + 3 :]
    ends, parts = ins[:n_ends], ins[n_ends : n_ends + n_parts]
    factor, first, second = ins[n_ends + n_parts :]
    grad = parts[0][...]
    for part in parts[1:]:
        grad = plus(grad, part[...])
    new_first = beta_one * first[...] + (1.0 - beta_one) * grad
    new_second = beta_two * second[...] + (1.0 - beta_two) * grad * grad
    first_hat = new_first / (1.0 - beta_one**10)
    second_hat = new_second / (1.0 - beta_two**10)
    outs[0][...] = factor[...] - learn_rate * first_hat / (jnp.sqrt(second_hat) + adam_eps)
    outs[1][...] = new_first
    outs[2][...] = new_second
    if ends:
        rows = ends[0][...]
        for end in ends[1:]:
            rows = plus(rows, end[...])
        outs[3][...] = rows


def finish(ends, parts, factor, first, second):
    ins = [*ends, *parts, factor, first, second]
    shapes = [factor, factor, factor] + list(ends[:1])
    return pl.pallas_call(
        functools.partial(finish_kernel, len(ends), len(parts)),
        out_shape=tuple(jax.ShapeDtypeStruct(like.shape, jnp.float32) for like in shapes),
        in_specs=[IN_VMEM] * len(ins),
        out_specs=(IN_VMEM,) * len(shapes),
        compiler_params=params(),
        cost_estimate=cost(20 * factor.size, sum(4 * a.size for a in ins)),
        name="finish",
    )(*ins)


def local(x_slab, cell_factor, row_index, gene_scale, gene_factor, first_moment, second_moment):
    rows_dev, genes_dev = x_slab.shape
    n_gene = lax.axis_size("gene")
    n_row = lax.axis_size("row")
    block = rows_dev // n_gene
    scale_k = 4.0 / math.sqrt(genes_dev * n_gene)
    factor_bf = gene_factor.astype(jnp.bfloat16)
    shares = [factor_bf] + [swap_row(factor_bf, hop, n_row) for hop in range(1, n_row)]
    fixed = prepare(x_slab, row_index, cell_factor, gene_scale, scale_k)
    adam = (gene_factor, first_moment, second_moment)

    if n_gene == 1 or n_gene > RING_MOST or block % 128:
        (rows,), parts = block_rows([((0,), 0, rows_dev)], [jnp.float32], rows_dev, True, True, n_row, fixed, shares)
        grad_cells = lax.psum_scatter(rows, "gene", scatter_dimension=0, tiled=True)
        others = [swap_row(parts[hop], hop, n_row) for hop in range(1, n_row)]
        return (grad_cells, *finish([], [parts[0], *others], *adam))

    steps = steps_of(n_gene)
    cut = tile_of(block, 256)
    sent = [[(0, cut), (cut, block)] if at == 0 and cut < block else [(0, block)] for at in range(len(steps))]
    pieces = [(around(n_gene, way * far), low, high) for (way, far), part in zip(steps, sent) for low, high in part]
    pieces.append((tuple(range(n_gene)), 0, block))
    alone = len(pieces) - 2
    targets = {way: list(enumerate(around(n_gene, way))) for way in (1, -1)}
    carried, blocks, early = shares, [], None
    for low in range(alone + 1):
        last = low == alone
        group = pieces[low:] if last else pieces[low : low + 1]
        kinds = [jnp.bfloat16] * len(group)
        if last:
            kinds[-1] = jnp.float32
        if last and early is not None:
            total, _ = lax.optimization_barrier((carried[0], early))
            carried = [total, *carried[1:]]
        done, carried = block_rows(group, kinds, block, low == 0, last, n_row, fixed, carried)
        blocks += done
        if low == 0 and len(sent[0]) > 1:
            early = lax.ppermute(done[0], "gene", targets[1])
    parts = carried

    came, at = {}, 0
    for (way, _), part in zip(steps, sent):
        values = blocks[at : at + len(part)]
        at += len(part)
        if way in came:
            values = [plus(jnp.concatenate(values), jnp.concatenate(came[way])).astype(jnp.bfloat16)]
        came[way] = [lax.ppermute(value, "gene", targets[way]) for value in values]
        if len(part) > 1:
            came[way][0] = early
    ends = [jnp.concatenate(value) for value in came.values()]
    others = [swap_row(parts[hop], hop, n_row) for hop in range(1, n_row)]
    *adam_out, grad_cells = finish([blocks[-1], *ends], [parts[0], *others], *adam)
    return (grad_cells, *adam_out)


def solution(mesh):
    in_specs = (
        P(("grp", "row"), "gene"),
        P(("grp", "row"), None),
        P(("grp", "row")),
        P(("grp", "gene")),
        P(("grp", "gene", "row"), None),
        P(("grp", "gene", "row"), None),
        P(("grp", "gene", "row"), None),
    )
    out_specs = (
        P(("grp", "row", "gene"), None),
        P(("grp", "gene", "row"), None),
        P(("grp", "gene", "row"), None),
        P(("grp", "gene", "row"), None),
    )
    return jax.shard_map(local, mesh=mesh, in_specs=in_specs, out_specs=out_specs, check_vma=False)
```

```python
import functools
import itertools
import math

import jax
import jax.numpy as jnp
from jax import lax
from jax.experimental import pallas as pl
from jax.experimental.pallas import tpu as pltpu
from jax.sharding import PartitionSpec as P

tukey_c = 4.685
beta_one = 0.9
beta_two = 0.999
learn_rate = 0.02
adam_eps = 1e-08

RING_MOST = 8
VMEM = pltpu.VMEM
IN_VMEM = pl.BlockSpec(memory_space=VMEM)
IN_ANY = pl.BlockSpec(memory_space=pl.ANY)


def tile_of(rows, most):
    best = [t for t in range(128, most + 1, 128) if rows % t == 0]
    return best[-1] if best else rows


def params():
    return pltpu.CompilerParams(vmem_limit_bytes=24 * 1024 * 1024)


def cost(flops, moved):
    return pl.CostEstimate(flops=int(flops), bytes_accessed=int(moved), transcendentals=0)


def pinned(*arrays):
    return [pltpu.with_memory_space_constraint(a, VMEM) for a in arrays]


def prepare_kernel(scale_k, x_in, index_in, cell_in, scale_in, x_out, f_out, ft_out, bend_out, shrink_out, index, cell, scale, sems):
    loads = [
        pltpu.make_async_copy(src, dst, sems.at[at])
        for at, (src, dst) in enumerate(((scale_in, scale), (cell_in, cell), (index_in, index), (x_in, x_out)))
    ]
    for load in loads:
        load.start()
    cells, rank = cell.shape
    rows = index.shape[0]
    genes = scale.shape[0]
    loads[0].wait()
    inverse = 1.0 / scale[...].reshape(1, genes)
    bend_out[...] = (inverse * inverse) * (1.0 / (tukey_c * tukey_c))
    shrink_out[...] = jnp.transpose(jnp.broadcast_to(-scale_k * (inverse * inverse), (rank, genes)))
    loads[1].wait()
    table = jnp.transpose(cell[...].astype(jnp.float32)).astype(jnp.bfloat16)
    base = lax.axis_index("row") * cells
    loads[2].wait()
    step = tile_of(rows, 512)
    for at in range(0, rows, step):
        local = index[at : at + step].reshape(1, step) - base
        hot = lax.broadcasted_iota(jnp.int32, (cells, step), 0) == local
        hot = jnp.where(hot, 1.0, 0.0).astype(jnp.bfloat16)
        picked = jnp.dot(table, hot, preferred_element_type=jnp.float32)
        ft_out[:, at : at + step] = picked.astype(jnp.bfloat16)
        f_out[at : at + step, :] = jnp.transpose(picked).astype(jnp.bfloat16)
    loads[3].wait()


def prepare(x_slab, row_index, cell_factor, gene_scale, scale_k):
    rows, genes = x_slab.shape
    cells, rank = cell_factor.shape
    ins = (x_slab, row_index, cell_factor, gene_scale)
    return pl.pallas_call(
        functools.partial(prepare_kernel, scale_k),
        out_shape=(
            VMEM((rows, genes), jnp.bfloat16),
            VMEM((rows, rank), jnp.bfloat16),
            VMEM((rank, rows), jnp.bfloat16),
            VMEM((1, genes), jnp.float32),
            VMEM((genes, rank), jnp.float32),
        ),
        in_specs=[IN_ANY] * 4,
        out_specs=(IN_VMEM,) * 5,
        scratch_shapes=[
            VMEM((rows,), jnp.int32),
            VMEM((cells, rank), jnp.bfloat16),
            VMEM((genes,), jnp.float32),
            pltpu.SemaphoreType.DMA((4,)),
        ],
        compiler_params=params(),
        cost_estimate=cost(2 * rows * cells * rank, 2 * rows * genes * 2),
        name="prepare",
    )(*(pltpu.with_memory_space_constraint(a, pltpu.HBM) for a in ins))


def pick(axis, table):
    me = lax.axis_index(axis)
    value = jnp.int32(table[0])
    for place, entry in enumerate(table[1:], 1):
        value = jnp.where(me == place, jnp.int32(entry), value)
    return value


def partner(me, hop, size):
    return me ^ hop if size & (size - 1) == 0 else (me + hop) % size


def source(me, hop, size):
    return me ^ hop if size & (size - 1) == 0 else (me + size - hop) % size


def rows_kernel(tables, block, first, last, n_row, *refs):
    refs = list(refs)
    take = lambda count: [refs.pop(0) for _ in range(count)]
    x_ref, f_ref, ft_ref, bend_ref, shrink_ref = take(5)
    shares = take(n_row) if first else None
    carried_in = None if first else take(3)
    rows_out = take(len(tables))
    carried_out = None if last else take(3 if first else 1)
    parts_out = take(n_row) if last else None
    me = lax.axis_index("row")

    if first:
        (piece,) = take(1)
        depth = shares[0].shape[0]
        for hop in range(n_row):
            start = pl.multiple_of(source(me, hop, n_row) * depth, depth)
            piece[pl.ds(start, depth), :] = shares[hop][...]
        whole = piece[...].astype(jnp.float32)
        wide = jnp.transpose(whole).astype(jnp.bfloat16)
        scaled = (whole * shrink_ref[...]).astype(jnp.bfloat16)
        total = None
    else:
        total, wide, scaled = (ref[...] for ref in carried_in)

    bend = bend_ref[...]
    step = tile_of(block, 256)
    tiles = []
    for table, out in zip(tables, rows_out):
        origin = pick("gene", table) * block if len(table) > 1 else 0
        for at in range(0, block, step):
            start = origin + at
            if len(table) > 1:
                start = pl.multiple_of(start, math.gcd(block, step))
            tiles.append((out, at, pl.ds(start, step)))

    def predict(here):
        return jnp.dot(f_ref[here, :], wide, preferred_element_type=jnp.float32)

    def influence(here, pred):
        resid = x_ref[here, :].astype(jnp.float32) - pred
        inside = jnp.maximum(1.0 - resid * resid * bend, 0.0)
        return (resid * (inside * inside)).astype(jnp.bfloat16)

    def gradients(tile, infl, total):
        out, at, here = tile
        cols = jnp.dot(ft_ref[:, here], infl, preferred_element_type=jnp.float32)
        out[at : at + step, :] = jnp.dot(infl, scaled, preferred_element_type=jnp.float32).astype(out.dtype)
        return cols if total is None else total + cols

    pred = predict(tiles[0][2])
    infl = None
    for at, tile in enumerate(tiles):
        later = predict(tiles[at + 1][2]) if at + 1 < len(tiles) else None
        now = influence(tile[2], pred)
        if at:
            total = gradients(tiles[at - 1], infl, total)
        infl, pred = now, later
    total = gradients(tiles[-1], infl, total)

    if first and not last:
        carried_out[1][...] = wide
        carried_out[2][...] = scaled
    if not last:
        carried_out[0][...] = total
        return
    (turned,) = take(1)
    turned[...] = jnp.transpose(total) * shrink_ref[...]
    depth = parts_out[0].shape[0]
    for hop in range(n_row):
        start = pl.multiple_of(partner(me, hop, n_row) * depth, depth)
        parts_out[hop][...] = turned[pl.ds(start, depth), :].astype(parts_out[hop].dtype)


def block_rows(tables, kinds, block, first, last, n_row, fixed, carried):
    genes, rank = fixed[4].shape
    out = [jax.ShapeDtypeStruct((block, rank), kind) for kind in kinds]
    if last:
        out += [jax.ShapeDtypeStruct((genes // n_row, rank), jnp.bfloat16 if hop else jnp.float32) for hop in range(n_row)]
    else:
        out += [VMEM((rank, genes), jnp.float32)]
    if first and not last:
        out += [VMEM((rank, genes), jnp.bfloat16), VMEM((genes, rank), jnp.bfloat16)]
    scratch = [VMEM((genes, rank), jnp.bfloat16)] if first else []
    if last:
        scratch.append(VMEM((genes, rank), jnp.float32))
    ins = pinned(*fixed) + (list(carried) if first else pinned(*carried))
    work = len(tables) * block * genes
    out = pl.pallas_call(
        functools.partial(rows_kernel, tables, block, first, last, n_row),
        out_shape=tuple(out),
        in_specs=[IN_VMEM] * len(ins),
        out_specs=(IN_VMEM,) * len(out),
        scratch_shapes=scratch,
        compiler_params=params(),
        cost_estimate=cost(6 * work * rank, work * 2),
        name="block_rows",
    )(*ins)
    done, rest = list(out[: len(tables)]), list(out[len(tables) :])
    return done, rest if first or last else rest + list(carried[1:])


def swap_row(value, hop, size):
    return lax.ppermute(value, "row", [(me, partner(me, hop, size)) for me in range(size)])


def ring_of(size):
    return [0, *range(1, size, 2), *reversed(range(2, size, 2))]


def steps_of(size):
    ahead = [(1, distance) for distance in range(size // 2, 0, -1)]
    back = [(-1, distance) for distance in range((size - 1) // 2, 0, -1)]
    return [step for pair in itertools.zip_longest(ahead, back) for step in pair if step]


def around(size, hops):
    ring = ring_of(size)
    return tuple(ring[(ring.index(place) + hops) % size] for place in range(size))


def plus(wide, narrow):
    return wide.astype(jnp.float32) + narrow.astype(jnp.float32)


def finish_kernel(n_ends, n_parts, *refs):
    ins, outs = refs[: n_ends + n_parts + 3], refs[n_ends + n_parts + 3 :]
    ends, parts = ins[:n_ends], ins[n_ends : n_ends + n_parts]
    factor, first, second = ins[n_ends + n_parts :]
    grad = parts[0][...]
    for part in parts[1:]:
        grad = plus(grad, part[...])
    new_first = beta_one * first[...] + (1.0 - beta_one) * grad
    new_second = beta_two * second[...] + (1.0 - beta_two) * grad * grad
    first_hat = new_first / (1.0 - beta_one**10)
    second_hat = new_second / (1.0 - beta_two**10)
    outs[0][...] = factor[...] - learn_rate * first_hat / (jnp.sqrt(second_hat) + adam_eps)
    outs[1][...] = new_first
    outs[2][...] = new_second
    if ends:
        rows = ends[0][...]
        for end in ends[1:]:
            rows = plus(rows, end[...])
        outs[3][...] = rows


def finish(ends, parts, factor, first, second):
    ins = [*ends, *parts, factor, first, second]
    shapes = [factor, factor, factor] + list(ends[:1])
    return pl.pallas_call(
        functools.partial(finish_kernel, len(ends), len(parts)),
        out_shape=tuple(jax.ShapeDtypeStruct(like.shape, jnp.float32) for like in shapes),
        in_specs=[IN_VMEM] * len(ins),
        out_specs=(IN_VMEM,) * len(shapes),
        compiler_params=params(),
        cost_estimate=cost(20 * factor.size, sum(4 * a.size for a in ins)),
        name="finish",
    )(*ins)


def local(x_slab, cell_factor, row_index, gene_scale, gene_factor, first_moment, second_moment):
    rows_dev, genes_dev = x_slab.shape
    n_gene = lax.axis_size("gene")
    n_row = lax.axis_size("row")
    block = rows_dev // n_gene
    scale_k = 4.0 / math.sqrt(genes_dev * n_gene)
    factor_bf = gene_factor.astype(jnp.bfloat16)
    shares = [factor_bf] + [swap_row(factor_bf, hop, n_row) for hop in range(1, n_row)]
    fixed = prepare(x_slab, row_index, cell_factor, gene_scale, scale_k)
    adam = (gene_factor, first_moment, second_moment)

    if n_gene == 1 or n_gene > RING_MOST or block % 128:
        (rows,), parts = block_rows([(0,)], [jnp.float32], rows_dev, True, True, n_row, fixed, shares)
        grad_cells = lax.psum_scatter(rows, "gene", scatter_dimension=0, tiled=True)
        others = [swap_row(parts[hop], hop, n_row) for hop in range(1, n_row)]
        return (grad_cells, *finish([], [parts[0], *others], *adam))

    steps = steps_of(n_gene)
    tables = [around(n_gene, way * distance) for way, distance in steps] + [tuple(range(n_gene))]
    kinds = [jnp.bfloat16] * len(steps) + [jnp.float32]
    cuts = [0, 1, 2, len(tables)] if len(steps) > 2 else [0, 1, len(tables)]
    carried, blocks = shares, []
    for low, high in zip(cuts, cuts[1:]):
        last = high == len(tables)
        done, carried = block_rows(tables[low:high], kinds[low:high], block, low == 0, last, n_row, fixed, carried)
        blocks += done
    parts = carried

    came = {}
    for (way, _), own in zip(steps, blocks):
        if way in came:
            own = plus(own, came[way]).astype(jnp.bfloat16)
        came[way] = lax.ppermute(own, "gene", list(enumerate(around(n_gene, way))))
    others = [swap_row(parts[hop], hop, n_row) for hop in range(1, n_row)]
    *adam_out, grad_cells = finish([blocks[-1], *came.values()], [parts[0], *others], *adam)
    return (grad_cells, *adam_out)


def solution(mesh):
    in_specs = (
        P(("grp", "row"), "gene"),
        P(("grp", "row"), None),
        P(("grp", "row")),
        P(("grp", "gene")),
        P(("grp", "gene", "row"), None),
        P(("grp", "gene", "row"), None),
        P(("grp", "gene", "row"), None),
    )
    out_specs = (
        P(("grp", "row", "gene"), None),
        P(("grp", "gene", "row"), None),
        P(("grp", "gene", "row"), None),
        P(("grp", "gene", "row"), None),
    )
    return jax.shard_map(local, mesh=mesh, in_specs=in_specs, out_specs=out_specs, check_vma=False)
```

```python
import functools
import itertools
import math

import jax
import jax.numpy as jnp
from jax import lax
from jax.experimental import pallas as pl
from jax.experimental.pallas import tpu as pltpu
from jax.sharding import PartitionSpec as P

tukey_c = 4.685
beta_one = 0.9
beta_two = 0.999
learn_rate = 0.02
adam_eps = 1e-08

RING_MOST = 8
VMEM = pltpu.VMEM
IN_VMEM = pl.BlockSpec(memory_space=VMEM)
IN_ANY = pl.BlockSpec(memory_space=pl.ANY)


def tile_of(rows, most):
    best = [t for t in range(128, most + 1, 128) if rows % t == 0]
    return best[-1] if best else rows


def params():
    return pltpu.CompilerParams(vmem_limit_bytes=24 * 1024 * 1024)


def cost(flops, moved):
    return pl.CostEstimate(flops=int(flops), bytes_accessed=int(moved), transcendentals=0)


def pinned(*arrays):
    return [pltpu.with_memory_space_constraint(a, VMEM) for a in arrays]


def prepare_kernel(scale_k, x_in, index_in, cell_in, scale_in, x_out, f_out, ft_out, bend_out, shrink_out, index, cell, scale, sems):
    loads = [
        pltpu.make_async_copy(src, dst, sems.at[at])
        for at, (src, dst) in enumerate(((scale_in, scale), (cell_in, cell), (index_in, index), (x_in, x_out)))
    ]
    for load in loads:
        load.start()
    cells, rank = cell.shape
    rows = index.shape[0]
    genes = scale.shape[0]
    loads[0].wait()
    inverse = 1.0 / scale[...].reshape(1, genes)
    bend_out[...] = (inverse * inverse) * (1.0 / (tukey_c * tukey_c))
    shrink_out[...] = jnp.transpose(jnp.broadcast_to(-scale_k * (inverse * inverse), (rank, genes)))
    loads[1].wait()
    table = jnp.transpose(cell[...].astype(jnp.float32)).astype(jnp.bfloat16)
    base = lax.axis_index("row") * cells
    loads[2].wait()
    step = tile_of(rows, 512)
    for at in range(0, rows, step):
        local = index[at : at + step].reshape(1, step) - base
        hot = lax.broadcasted_iota(jnp.int32, (cells, step), 0) == local
        hot = jnp.where(hot, 1.0, 0.0).astype(jnp.bfloat16)
        picked = jnp.dot(table, hot, preferred_element_type=jnp.float32)
        ft_out[:, at : at + step] = picked.astype(jnp.bfloat16)
        f_out[at : at + step, :] = jnp.transpose(picked).astype(jnp.bfloat16)
    loads[3].wait()


def prepare(x_slab, row_index, cell_factor, gene_scale, scale_k):
    rows, genes = x_slab.shape
    cells, rank = cell_factor.shape
    ins = (x_slab, row_index, cell_factor, gene_scale)
    return pl.pallas_call(
        functools.partial(prepare_kernel, scale_k),
        out_shape=(
            VMEM((rows, genes), jnp.bfloat16),
            VMEM((rows, rank), jnp.bfloat16),
            VMEM((rank, rows), jnp.bfloat16),
            VMEM((1, genes), jnp.float32),
            VMEM((genes, rank), jnp.float32),
        ),
        in_specs=[IN_ANY] * 4,
        out_specs=(IN_VMEM,) * 5,
        scratch_shapes=[
            VMEM((rows,), jnp.int32),
            VMEM((cells, rank), jnp.bfloat16),
            VMEM((genes,), jnp.float32),
            pltpu.SemaphoreType.DMA((4,)),
        ],
        compiler_params=params(),
        cost_estimate=cost(2 * rows * cells * rank, 2 * rows * genes * 2),
        name="prepare",
    )(*(pltpu.with_memory_space_constraint(a, pltpu.HBM) for a in ins))


def pick(axis, table):
    me = lax.axis_index(axis)
    value = jnp.int32(table[0])
    for place, entry in enumerate(table[1:], 1):
        value = jnp.where(me == place, jnp.int32(entry), value)
    return value


def partner(me, hop, size):
    return me ^ hop if size & (size - 1) == 0 else (me + hop) % size


def source(me, hop, size):
    return me ^ hop if size & (size - 1) == 0 else (me + size - hop) % size


def rows_kernel(tables, block, first, last, n_row, *refs):
    refs = list(refs)
    take = lambda count: [refs.pop(0) for _ in range(count)]
    x_ref, f_ref, ft_ref, bend_ref, shrink_ref = take(5)
    shares = take(n_row) if first else None
    carried_in = None if first else take(3)
    rows_out = take(len(tables))
    carried_out = None if last else take(3 if first else 1)
    parts_out = take(n_row) if last else None
    me = lax.axis_index("row")

    if first:
        (piece,) = take(1)
        depth = shares[0].shape[0]
        for hop in range(n_row):
            start = pl.multiple_of(source(me, hop, n_row) * depth, depth)
            piece[pl.ds(start, depth), :] = shares[hop][...]
        whole = piece[...].astype(jnp.float32)
        wide = jnp.transpose(whole).astype(jnp.bfloat16)
        scaled = (whole * shrink_ref[...]).astype(jnp.bfloat16)
        total = None
    else:
        total, wide, scaled = (ref[...] for ref in carried_in)

    bend = bend_ref[...]
    step = tile_of(block, 256)
    tiles = []
    for table, out in zip(tables, rows_out):
        origin = pick("gene", table) * block if len(table) > 1 else 0
        for at in range(0, block, step):
            start = origin + at
            if len(table) > 1:
                start = pl.multiple_of(start, math.gcd(block, step))
            tiles.append((out, at, pl.ds(start, step)))

    def predict(here):
        return jnp.dot(f_ref[here, :], wide, preferred_element_type=jnp.float32)

    def influence(here, pred):
        resid = x_ref[here, :].astype(jnp.float32) - pred
        inside = jnp.maximum(1.0 - resid * resid * bend, 0.0)
        return (resid * (inside * inside)).astype(jnp.bfloat16)

    def gradients(tile, infl, total):
        out, at, here = tile
        cols = jnp.dot(ft_ref[:, here], infl, preferred_element_type=jnp.float32)
        out[at : at + step, :] = jnp.dot(infl, scaled, preferred_element_type=jnp.float32).astype(out.dtype)
        return cols if total is None else total + cols

    pred = predict(tiles[0][2])
    infl = None
    for at, tile in enumerate(tiles):
        later = predict(tiles[at + 1][2]) if at + 1 < len(tiles) else None
        now = influence(tile[2], pred)
        if at:
            total = gradients(tiles[at - 1], infl, total)
        infl, pred = now, later
    total = gradients(tiles[-1], infl, total)

    if first and not last:
        carried_out[1][...] = wide
        carried_out[2][...] = scaled
    if not last:
        carried_out[0][...] = total
        return
    (turned,) = take(1)
    turned[...] = jnp.transpose(total) * shrink_ref[...]
    depth = parts_out[0].shape[0]
    for hop in range(n_row):
        start = pl.multiple_of(partner(me, hop, n_row) * depth, depth)
        parts_out[hop][...] = turned[pl.ds(start, depth), :].astype(parts_out[hop].dtype)


def block_rows(tables, kinds, block, first, last, n_row, fixed, carried):
    genes, rank = fixed[4].shape
    out = [jax.ShapeDtypeStruct((block, rank), kind) for kind in kinds]
    if last:
        out += [jax.ShapeDtypeStruct((genes // n_row, rank), jnp.bfloat16 if hop else jnp.float32) for hop in range(n_row)]
    else:
        out += [VMEM((rank, genes), jnp.float32)]
    if first and not last:
        out += [VMEM((rank, genes), jnp.bfloat16), VMEM((genes, rank), jnp.bfloat16)]
    scratch = [VMEM((genes, rank), jnp.bfloat16)] if first else []
    if last:
        scratch.append(VMEM((genes, rank), jnp.float32))
    ins = pinned(*fixed) + (list(carried) if first else pinned(*carried))
    work = len(tables) * block * genes
    out = pl.pallas_call(
        functools.partial(rows_kernel, tables, block, first, last, n_row),
        out_shape=tuple(out),
        in_specs=[IN_VMEM] * len(ins),
        out_specs=(IN_VMEM,) * len(out),
        scratch_shapes=scratch,
        compiler_params=params(),
        cost_estimate=cost(6 * work * rank, work * 2),
        name="block_rows",
    )(*ins)
    done, rest = list(out[: len(tables)]), list(out[len(tables) :])
    return done, rest if first or last else rest + list(carried[1:])


def swap_row(value, hop, size):
    return lax.ppermute(value, "row", [(me, partner(me, hop, size)) for me in range(size)])


def steps_of(size):
    ahead = [(1, distance) for distance in range(size // 2, 0, -1)]
    back = [(-1, distance) for distance in range((size - 1) // 2, 0, -1)]
    return [step for pair in itertools.zip_longest(ahead, back) for step in pair if step]


def around(size, hops):
    return tuple((place + hops) % size for place in range(size))


def plus(wide, narrow):
    return wide.astype(jnp.float32) + narrow.astype(jnp.float32)


def finish_kernel(n_ends, n_parts, *refs):
    ins, outs = refs[: n_ends + n_parts + 3], refs[n_ends + n_parts + 3 :]
    ends, parts = ins[:n_ends], ins[n_ends : n_ends + n_parts]
    factor, first, second = ins[n_ends + n_parts :]
    grad = parts[0][...]
    for part in parts[1:]:
        grad = plus(grad, part[...])
    new_first = beta_one * first[...] + (1.0 - beta_one) * grad
    new_second = beta_two * second[...] + (1.0 - beta_two) * grad * grad
    first_hat = new_first / (1.0 - beta_one**10)
    second_hat = new_second / (1.0 - beta_two**10)
    outs[0][...] = factor[...] - learn_rate * first_hat / (jnp.sqrt(second_hat) + adam_eps)
    outs[1][...] = new_first
    outs[2][...] = new_second
    if ends:
        rows = ends[0][...]
        for end in ends[1:]:
            rows = plus(rows, end[...])
        outs[3][...] = rows


def finish(ends, parts, factor, first, second):
    ins = [*ends, *parts, factor, first, second]
    shapes = [factor, factor, factor] + list(ends[:1])
    return pl.pallas_call(
        functools.partial(finish_kernel, len(ends), len(parts)),
        out_shape=tuple(jax.ShapeDtypeStruct(like.shape, jnp.float32) for like in shapes),
        in_specs=[IN_VMEM] * len(ins),
        out_specs=(IN_VMEM,) * len(shapes),
        compiler_params=params(),
        cost_estimate=cost(20 * factor.size, sum(4 * a.size for a in ins)),
        name="finish",
    )(*ins)


def local(x_slab, cell_factor, row_index, gene_scale, gene_factor, first_moment, second_moment):
    rows_dev, genes_dev = x_slab.shape
    n_gene = lax.axis_size("gene")
    n_row = lax.axis_size("row")
    block = rows_dev // n_gene
    scale_k = 4.0 / math.sqrt(genes_dev * n_gene)
    factor_bf = gene_factor.astype(jnp.bfloat16)
    shares = [factor_bf] + [swap_row(factor_bf, hop, n_row) for hop in range(1, n_row)]
    fixed = prepare(x_slab, row_index, cell_factor, gene_scale, scale_k)
    adam = (gene_factor, first_moment, second_moment)

    if n_gene == 1 or n_gene > RING_MOST or block % 128:
        (rows,), parts = block_rows([(0,)], [jnp.float32], rows_dev, True, True, n_row, fixed, shares)
        grad_cells = lax.psum_scatter(rows, "gene", scatter_dimension=0, tiled=True)
        others = [swap_row(parts[hop], hop, n_row) for hop in range(1, n_row)]
        return (grad_cells, *finish([], [parts[0], *others], *adam))

    steps = steps_of(n_gene)
    tables = [around(n_gene, way * distance) for way, distance in steps] + [tuple(range(n_gene))]
    kinds = [jnp.bfloat16] * len(steps) + [jnp.float32]
    cuts = [0, 1, len(tables)]
    carried, blocks = shares, []
    for low, high in zip(cuts, cuts[1:]):
        last = high == len(tables)
        done, carried = block_rows(tables[low:high], kinds[low:high], block, low == 0, last, n_row, fixed, carried)
        blocks += done
    parts = carried

    came = {}
    for (way, _), own in zip(steps, blocks):
        if way in came:
            own = plus(own, came[way]).astype(jnp.bfloat16)
        came[way] = lax.ppermute(own, "gene", list(enumerate(around(n_gene, way))))
    others = [swap_row(parts[hop], hop, n_row) for hop in range(1, n_row)]
    *adam_out, grad_cells = finish([blocks[-1], *came.values()], [parts[0], *others], *adam)
    return (grad_cells, *adam_out)


def solution(mesh):
    in_specs = (
        P(("grp", "row"), "gene"),
        P(("grp", "row"), None),
        P(("grp", "row")),
        P(("grp", "gene")),
        P(("grp", "gene", "row"), None),
        P(("grp", "gene", "row"), None),
        P(("grp", "gene", "row"), None),
    )
    out_specs = (
        P(("grp", "row", "gene"), None),
        P(("grp", "gene", "row"), None),
        P(("grp", "gene", "row"), None),
        P(("grp", "gene", "row"), None),
    )
    return jax.shard_map(local, mesh=mesh, in_specs=in_specs, out_specs=out_specs, check_vma=False)
```

```python
import functools
import itertools
import math

import jax
import jax.numpy as jnp
from jax import lax
from jax.experimental import pallas as pl
from jax.experimental.pallas import tpu as pltpu
from jax.sharding import PartitionSpec as P

tukey_c = 4.685
beta_one = 0.9
beta_two = 0.999
learn_rate = 0.02
adam_eps = 1e-08

RING_MOST = 8
VMEM = pltpu.VMEM
IN_VMEM = pl.BlockSpec(memory_space=VMEM)
IN_ANY = pl.BlockSpec(memory_space=pl.ANY)


def tile_of(rows, most):
    best = [t for t in range(128, most + 1, 128) if rows % t == 0]
    return best[-1] if best else rows


def params():
    return pltpu.CompilerParams(vmem_limit_bytes=24 * 1024 * 1024)


def cost(flops, moved):
    return pl.CostEstimate(flops=int(flops), bytes_accessed=int(moved), transcendentals=0)


def pinned(*arrays):
    return [pltpu.with_memory_space_constraint(a, VMEM) for a in arrays]


def prepare_kernel(scale_k, x_in, index_in, cell_in, scale_in, x_out, f_out, ft_out, bend_out, shrink_out, index, cell, scale, sems):
    loads = [
        pltpu.make_async_copy(src, dst, sems.at[at])
        for at, (src, dst) in enumerate(((scale_in, scale), (cell_in, cell), (index_in, index), (x_in, x_out)))
    ]
    for load in loads:
        load.start()
    cells, rank = cell.shape
    rows = index.shape[0]
    genes = scale.shape[0]
    loads[0].wait()
    inverse = 1.0 / scale[...].reshape(1, genes)
    bend_out[...] = (inverse * inverse) * (1.0 / (tukey_c * tukey_c))
    shrink_out[...] = jnp.transpose(jnp.broadcast_to(-scale_k * (inverse * inverse), (rank, genes)))
    loads[1].wait()
    table = jnp.transpose(cell[...].astype(jnp.float32)).astype(jnp.bfloat16)
    base = lax.axis_index("row") * cells
    loads[2].wait()
    step = tile_of(rows, 512)
    for at in range(0, rows, step):
        local = index[at : at + step].reshape(1, step) - base
        hot = lax.broadcasted_iota(jnp.int32, (cells, step), 0) == local
        hot = jnp.where(hot, 1.0, 0.0).astype(jnp.bfloat16)
        picked = jnp.dot(table, hot, preferred_element_type=jnp.float32)
        ft_out[:, at : at + step] = picked.astype(jnp.bfloat16)
        f_out[at : at + step, :] = jnp.transpose(picked).astype(jnp.bfloat16)
    loads[3].wait()


def prepare(x_slab, row_index, cell_factor, gene_scale, scale_k):
    rows, genes = x_slab.shape
    cells, rank = cell_factor.shape
    ins = (x_slab, row_index, cell_factor, gene_scale)
    return pl.pallas_call(
        functools.partial(prepare_kernel, scale_k),
        out_shape=(
            VMEM((rows, genes), jnp.bfloat16),
            VMEM((rows, rank), jnp.bfloat16),
            VMEM((rank, rows), jnp.bfloat16),
            VMEM((1, genes), jnp.float32),
            VMEM((genes, rank), jnp.float32),
        ),
        in_specs=[IN_ANY] * 4,
        out_specs=(IN_VMEM,) * 5,
        scratch_shapes=[
            VMEM((rows,), jnp.int32),
            VMEM((cells, rank), jnp.bfloat16),
            VMEM((genes,), jnp.float32),
            pltpu.SemaphoreType.DMA((4,)),
        ],
        compiler_params=params(),
        cost_estimate=cost(2 * rows * cells * rank, 2 * rows * genes * 2),
        name="prepare",
    )(*(pltpu.with_memory_space_constraint(a, pltpu.HBM) for a in ins))


def pick(axis, table):
    me = lax.axis_index(axis)
    value = jnp.int32(table[0])
    for place, entry in enumerate(table[1:], 1):
        value = jnp.where(me == place, jnp.int32(entry), value)
    return value


def partner(me, hop, size):
    return me ^ hop if size & (size - 1) == 0 else (me + hop) % size


def source(me, hop, size):
    return me ^ hop if size & (size - 1) == 0 else (me + size - hop) % size


def rows_kernel(tables, block, first, last, n_row, *refs):
    refs = list(refs)
    take = lambda count: [refs.pop(0) for _ in range(count)]
    x_ref, f_ref, ft_ref, bend_ref, shrink_ref = take(5)
    shares = take(n_row) if first else None
    carried_in = None if first else take(3)
    rows_out = take(len(tables))
    carried_out = None if last else take(3 if first else 1)
    parts_out = take(n_row) if last else None
    me = lax.axis_index("row")

    if first:
        (piece,) = take(1)
        depth = shares[0].shape[0]
        for hop in range(n_row):
            start = pl.multiple_of(source(me, hop, n_row) * depth, depth)
            piece[pl.ds(start, depth), :] = shares[hop][...]
        whole = piece[...].astype(jnp.float32)
        wide = jnp.transpose(whole).astype(jnp.bfloat16)
        scaled = (whole * shrink_ref[...]).astype(jnp.bfloat16)
        total = None
    else:
        total, wide, scaled = (ref[...] for ref in carried_in)

    bend = bend_ref[...]
    step = tile_of(block, 256)
    tiles = []
    for table, out in zip(tables, rows_out):
        origin = pick("gene", table) * block if len(table) > 1 else 0
        for at in range(0, block, step):
            start = origin + at
            if len(table) > 1:
                start = pl.multiple_of(start, math.gcd(block, step))
            tiles.append((out, at, pl.ds(start, step)))

    def predict(here):
        return jnp.dot(f_ref[here, :], wide, preferred_element_type=jnp.float32)

    def influence(here, pred):
        resid = x_ref[here, :].astype(jnp.float32) - pred
        inside = jnp.maximum(1.0 - resid * resid * bend, 0.0)
        return (resid * (inside * inside)).astype(jnp.bfloat16)

    def gradients(tile, infl, total):
        out, at, here = tile
        cols = jnp.dot(ft_ref[:, here], infl, preferred_element_type=jnp.float32)
        out[at : at + step, :] = jnp.dot(infl, scaled, preferred_element_type=jnp.float32).astype(out.dtype)
        return cols if total is None else total + cols

    pred = predict(tiles[0][2])
    infl = None
    for at, tile in enumerate(tiles):
        later = predict(tiles[at + 1][2]) if at + 1 < len(tiles) else None
        now = influence(tile[2], pred)
        if at:
            total = gradients(tiles[at - 1], infl, total)
        infl, pred = now, later
    total = gradients(tiles[-1], infl, total)

    if first and not last:
        carried_out[1][...] = wide
        carried_out[2][...] = scaled
    if not last:
        carried_out[0][...] = total
        return
    (turned,) = take(1)
    turned[...] = jnp.transpose(total) * shrink_ref[...]
    depth = parts_out[0].shape[0]
    for hop in range(n_row):
        start = pl.multiple_of(partner(me, hop, n_row) * depth, depth)
        parts_out[hop][...] = turned[pl.ds(start, depth), :].astype(parts_out[hop].dtype)


def block_rows(tables, kinds, block, first, last, n_row, fixed, carried):
    genes, rank = fixed[4].shape
    out = [jax.ShapeDtypeStruct((block, rank), kind) for kind in kinds]
    if last:
        out += [jax.ShapeDtypeStruct((genes // n_row, rank), jnp.bfloat16 if hop else jnp.float32) for hop in range(n_row)]
    else:
        out += [VMEM((rank, genes), jnp.float32)]
    if first and not last:
        out += [VMEM((rank, genes), jnp.bfloat16), VMEM((genes, rank), jnp.bfloat16)]
    scratch = [VMEM((genes, rank), jnp.bfloat16)] if first else []
    if last:
        scratch.append(VMEM((genes, rank), jnp.float32))
    ins = pinned(*fixed) + (list(carried) if first else pinned(*carried))
    work = len(tables) * block * genes
    out = pl.pallas_call(
        functools.partial(rows_kernel, tables, block, first, last, n_row),
        out_shape=tuple(out),
        in_specs=[IN_VMEM] * len(ins),
        out_specs=(IN_VMEM,) * len(out),
        scratch_shapes=scratch,
        compiler_params=params(),
        cost_estimate=cost(6 * work * rank, work * 2),
        name="block_rows",
    )(*ins)
    done, rest = list(out[: len(tables)]), list(out[len(tables) :])
    return done, rest if first or last else rest + list(carried[1:])


def swap_row(value, hop, size):
    return lax.ppermute(value, "row", [(me, partner(me, hop, size)) for me in range(size)])


def ring_of(size):
    return [*range(0, size, 2), *reversed(range(1, size, 2))]


def steps_of(size):
    ahead = [(1, distance) for distance in range(size // 2, 0, -1)]
    back = [(-1, distance) for distance in range((size - 1) // 2, 0, -1)]
    return [step for pair in itertools.zip_longest(ahead, back) for step in pair if step]


def around(size, hops):
    ring = ring_of(size)
    return tuple(ring[(ring.index(place) + hops) % size] for place in range(size))


def plus(wide, narrow):
    return wide.astype(jnp.float32) + narrow.astype(jnp.float32)


def finish_kernel(n_ends, n_parts, *refs):
    ins, outs = refs[: n_ends + n_parts + 3], refs[n_ends + n_parts + 3 :]
    ends, parts = ins[:n_ends], ins[n_ends : n_ends + n_parts]
    factor, first, second = ins[n_ends + n_parts :]
    grad = parts[0][...]
    for part in parts[1:]:
        grad = plus(grad, part[...])
    new_first = beta_one * first[...] + (1.0 - beta_one) * grad
    new_second = beta_two * second[...] + (1.0 - beta_two) * grad * grad
    first_hat = new_first / (1.0 - beta_one**10)
    second_hat = new_second / (1.0 - beta_two**10)
    outs[0][...] = factor[...] - learn_rate * first_hat / (jnp.sqrt(second_hat) + adam_eps)
    outs[1][...] = new_first
    outs[2][...] = new_second
    if ends:
        rows = ends[0][...]
        for end in ends[1:]:
            rows = plus(rows, end[...])
        outs[3][...] = rows


def finish(ends, parts, factor, first, second):
    ins = [*ends, *parts, factor, first, second]
    shapes = [factor, factor, factor] + list(ends[:1])
    return pl.pallas_call(
        functools.partial(finish_kernel, len(ends), len(parts)),
        out_shape=tuple(jax.ShapeDtypeStruct(like.shape, jnp.float32) for like in shapes),
        in_specs=[IN_VMEM] * len(ins),
        out_specs=(IN_VMEM,) * len(shapes),
        compiler_params=params(),
        cost_estimate=cost(20 * factor.size, sum(4 * a.size for a in ins)),
        name="finish",
    )(*ins)


def local(x_slab, cell_factor, row_index, gene_scale, gene_factor, first_moment, second_moment):
    rows_dev, genes_dev = x_slab.shape
    n_gene = lax.axis_size("gene")
    n_row = lax.axis_size("row")
    block = rows_dev // n_gene
    scale_k = 4.0 / math.sqrt(genes_dev * n_gene)
    factor_bf = gene_factor.astype(jnp.bfloat16)
    shares = [factor_bf] + [swap_row(factor_bf, hop, n_row) for hop in range(1, n_row)]
    fixed = prepare(x_slab, row_index, cell_factor, gene_scale, scale_k)
    adam = (gene_factor, first_moment, second_moment)

    if n_gene == 1 or n_gene > RING_MOST or block % 128:
        (rows,), parts = block_rows([(0,)], [jnp.float32], rows_dev, True, True, n_row, fixed, shares)
        grad_cells = lax.psum_scatter(rows, "gene", scatter_dimension=0, tiled=True)
        others = [swap_row(parts[hop], hop, n_row) for hop in range(1, n_row)]
        return (grad_cells, *finish([], [parts[0], *others], *adam))

    steps = steps_of(n_gene)
    tables = [around(n_gene, way * distance) for way, distance in steps] + [tuple(range(n_gene))]
    kinds = [jnp.bfloat16] * len(steps) + [jnp.float32]
    cuts = [0, 1, len(tables)]
    carried, blocks = shares, []
    for low, high in zip(cuts, cuts[1:]):
        last = high == len(tables)
        done, carried = block_rows(tables[low:high], kinds[low:high], block, low == 0, last, n_row, fixed, carried)
        blocks += done
    parts = carried

    came = {}
    for (way, _), own in zip(steps, blocks):
        if way in came:
            own = plus(own, came[way]).astype(jnp.bfloat16)
        came[way] = lax.ppermute(own, "gene", list(enumerate(around(n_gene, way))))
    others = [swap_row(parts[hop], hop, n_row) for hop in range(1, n_row)]
    *adam_out, grad_cells = finish([blocks[-1], *came.values()], [parts[0], *others], *adam)
    return (grad_cells, *adam_out)


def solution(mesh):
    in_specs = (
        P(("grp", "row"), "gene"),
        P(("grp", "row"), None),
        P(("grp", "row")),
        P(("grp", "gene")),
        P(("grp", "gene", "row"), None),
        P(("grp", "gene", "row"), None),
        P(("grp", "gene", "row"), None),
    )
    out_specs = (
        P(("grp", "row", "gene"), None),
        P(("grp", "gene", "row"), None),
        P(("grp", "gene", "row"), None),
        P(("grp", "gene", "row"), None),
    )
    return jax.shard_map(local, mesh=mesh, in_specs=in_specs, out_specs=out_specs, check_vma=False)
```

```python
import functools
import itertools
import math

import jax
import jax.numpy as jnp
from jax import lax
from jax.experimental import pallas as pl
from jax.experimental.pallas import tpu as pltpu
from jax.sharding import PartitionSpec as P

tukey_c = 4.685
beta_one = 0.9
beta_two = 0.999
learn_rate = 0.02
adam_eps = 1e-08

RING_MOST = 8
VMEM = pltpu.VMEM
IN_VMEM = pl.BlockSpec(memory_space=VMEM)
IN_ANY = pl.BlockSpec(memory_space=pl.ANY)


def tile_of(rows, most):
    best = [t for t in range(128, most + 1, 128) if rows % t == 0]
    return best[-1] if best else rows


def params():
    return pltpu.CompilerParams(vmem_limit_bytes=24 * 1024 * 1024)


def cost(flops, moved):
    return pl.CostEstimate(flops=int(flops), bytes_accessed=int(moved), transcendentals=0)


def pinned(*arrays):
    return [pltpu.with_memory_space_constraint(a, VMEM) for a in arrays]


def prepare_kernel(scale_k, x_in, index_in, cell_in, scale_in, x_out, f_out, ft_out, bend_out, shrink_out, index, cell, scale, sems):
    loads = [
        pltpu.make_async_copy(src, dst, sems.at[at])
        for at, (src, dst) in enumerate(((scale_in, scale), (cell_in, cell), (index_in, index), (x_in, x_out)))
    ]
    for load in loads:
        load.start()
    cells, rank = cell.shape
    rows = index.shape[0]
    genes = scale.shape[0]
    loads[0].wait()
    inverse = 1.0 / scale[...].reshape(1, genes)
    bend_out[...] = (inverse * inverse) * (1.0 / (tukey_c * tukey_c))
    shrink_out[...] = jnp.transpose(jnp.broadcast_to(-scale_k * (inverse * inverse), (rank, genes)))
    loads[1].wait()
    table = jnp.transpose(cell[...].astype(jnp.float32)).astype(jnp.bfloat16)
    base = lax.axis_index("row") * cells
    loads[2].wait()
    step = tile_of(rows, 512)
    for at in range(0, rows, step):
        local = index[at : at + step].reshape(1, step) - base
        hot = lax.broadcasted_iota(jnp.int32, (cells, step), 0) == local
        hot = jnp.where(hot, 1.0, 0.0).astype(jnp.bfloat16)
        picked = jnp.dot(table, hot, preferred_element_type=jnp.float32)
        ft_out[:, at : at + step] = picked.astype(jnp.bfloat16)
        f_out[at : at + step, :] = jnp.transpose(picked).astype(jnp.bfloat16)
    loads[3].wait()


def prepare(x_slab, row_index, cell_factor, gene_scale, scale_k):
    rows, genes = x_slab.shape
    cells, rank = cell_factor.shape
    ins = (x_slab, row_index, cell_factor, gene_scale)
    return pl.pallas_call(
        functools.partial(prepare_kernel, scale_k),
        out_shape=(
            VMEM((rows, genes), jnp.bfloat16),
            VMEM((rows, rank), jnp.bfloat16),
            VMEM((rank, rows), jnp.bfloat16),
            VMEM((1, genes), jnp.float32),
            VMEM((genes, rank), jnp.float32),
        ),
        in_specs=[IN_ANY] * 4,
        out_specs=(IN_VMEM,) * 5,
        scratch_shapes=[
            VMEM((rows,), jnp.int32),
            VMEM((cells, rank), jnp.bfloat16),
            VMEM((genes,), jnp.float32),
            pltpu.SemaphoreType.DMA((4,)),
        ],
        compiler_params=params(),
        cost_estimate=cost(2 * rows * cells * rank, 2 * rows * genes * 2),
        name="prepare",
    )(*(pltpu.with_memory_space_constraint(a, pltpu.HBM) for a in ins))


def pick(axis, table):
    me = lax.axis_index(axis)
    value = jnp.int32(table[0])
    for place, entry in enumerate(table[1:], 1):
        value = jnp.where(me == place, jnp.int32(entry), value)
    return value


def partner(me, hop, size):
    return me ^ hop if size & (size - 1) == 0 else (me + hop) % size


def source(me, hop, size):
    return me ^ hop if size & (size - 1) == 0 else (me + size - hop) % size


def rows_kernel(tables, block, first, last, n_row, *refs):
    refs = list(refs)
    take = lambda count: [refs.pop(0) for _ in range(count)]
    x_ref, f_ref, ft_ref, bend_ref, shrink_ref = take(5)
    shares = take(n_row) if first else None
    carried_in = None if first else take(3)
    rows_out = take(len(tables))
    carried_out = None if last else take(3 if first else 1)
    parts_out = take(n_row) if last else None
    me = lax.axis_index("row")

    if first:
        (piece,) = take(1)
        depth = shares[0].shape[0]
        for hop in range(n_row):
            start = pl.multiple_of(source(me, hop, n_row) * depth, depth)
            piece[pl.ds(start, depth), :] = shares[hop][...]
        whole = piece[...].astype(jnp.float32)
        wide = jnp.transpose(whole).astype(jnp.bfloat16)
        scaled = (whole * shrink_ref[...]).astype(jnp.bfloat16)
        total = None
    else:
        total, wide, scaled = (ref[...] for ref in carried_in)

    bend = bend_ref[...]
    step = tile_of(block, 256)
    tiles = []
    for table, out in zip(tables, rows_out):
        origin = pick("gene", table) * block if len(table) > 1 else 0
        for at in range(0, block, step):
            start = origin + at
            if len(table) > 1:
                start = pl.multiple_of(start, math.gcd(block, step))
            tiles.append((out, at, pl.ds(start, step)))

    def predict(here):
        return jnp.dot(f_ref[here, :], wide, preferred_element_type=jnp.float32)

    def gradients(tile, infl, total):
        out, at, here = tile
        cols = jnp.dot(ft_ref[:, here], infl, preferred_element_type=jnp.float32)
        out[at : at + step, :] = jnp.dot(infl, scaled, preferred_element_type=jnp.float32).astype(out.dtype)
        return cols if total is None else total + cols

    pred = predict(tiles[0][2])
    infl = None
    for at, tile in enumerate(tiles):
        later = predict(tiles[at + 1][2]) if at + 1 < len(tiles) else None
        now = influence(x_ref[tile[2], :], pred, bend)
        if at:
            total = gradients(tiles[at - 1], infl, total)
        infl, pred = now, later
    total = gradients(tiles[-1], infl, total)

    if first and not last:
        carried_out[1][...] = wide
        carried_out[2][...] = scaled
    if not last:
        carried_out[0][...] = total
        return
    (turned,) = take(1)
    turned[...] = jnp.transpose(total) * shrink_ref[...]
    depth = parts_out[0].shape[0]
    for hop in range(n_row):
        start = pl.multiple_of(partner(me, hop, n_row) * depth, depth)
        parts_out[hop][...] = turned[pl.ds(start, depth), :].astype(parts_out[hop].dtype)


def block_rows(tables, kinds, block, first, last, n_row, fixed, carried):
    genes, rank = fixed[4].shape
    out = [jax.ShapeDtypeStruct((block, rank), kind) for kind in kinds]
    if last:
        out += [jax.ShapeDtypeStruct((genes // n_row, rank), jnp.bfloat16 if hop else jnp.float32) for hop in range(n_row)]
    else:
        out += [VMEM((rank, genes), jnp.float32)]
    if first and not last:
        out += [VMEM((rank, genes), jnp.bfloat16), VMEM((genes, rank), jnp.bfloat16)]
    scratch = [VMEM((genes, rank), jnp.bfloat16)] if first else []
    if last:
        scratch.append(VMEM((genes, rank), jnp.float32))
    ins = pinned(*fixed) + (list(carried) if first else pinned(*carried))
    work = len(tables) * block * genes
    out = pl.pallas_call(
        functools.partial(rows_kernel, tables, block, first, last, n_row),
        out_shape=tuple(out),
        in_specs=[IN_VMEM] * len(ins),
        out_specs=(IN_VMEM,) * len(out),
        scratch_shapes=scratch,
        compiler_params=params(),
        cost_estimate=cost(6 * work * rank, work * 2),
        name="block_rows",
    )(*ins)
    done, rest = list(out[: len(tables)]), list(out[len(tables) :])
    return done, rest if first or last else rest + list(carried[1:])


def lane_parts(genes, depth, n_row):
    if n_row != 4:
        return None
    pairs = [(2 * depth * (place // 2), 2 * depth * (place // 2 + 1)) for place in range(n_row)]
    low = [-(-begin // 128) * 128 for begin, _ in pairs]
    width = min(end // 128 * 128 - begin for begin, (_, end) in zip(low, pairs))
    if width <= 0 or any(begin not in (0, genes - width) for begin in low):
        return None
    return low, width, [width if begin == 0 else 0 for begin in low]


def lanes(table, width):
    return pl.ds(pl.multiple_of(pick("row", table), 128), width)


def influence(x, pred, bend):
    resid = x.astype(jnp.float32) - pred
    inside = jnp.maximum(1.0 - resid * resid * bend, 0.0)
    return (resid * (inside * inside)).astype(jnp.bfloat16)


def part_of_block(table, block, here, x_ref, f_ref, ft_ref, bend_ref, wide, scaled):
    step = tile_of(block, 256)
    origin = pick("gene", table) * block
    tiles = [pl.ds(pl.multiple_of(origin + at, math.gcd(block, step)), step) for at in range(0, block, step)]
    bend = bend_ref[:, here]
    preds = [jnp.dot(f_ref[tile, :], wide, preferred_element_type=jnp.float32) for tile in tiles]
    infls = [influence(x_ref[tile, here], pred, bend) for tile, pred in zip(tiles, preds)]
    rows, total = [], None
    for tile, infl in zip(tiles, infls):
        cols = jnp.dot(ft_ref[:, tile], infl, preferred_element_type=jnp.float32)
        rows.append(jnp.dot(infl, scaled, preferred_element_type=jnp.float32))
        total = cols if total is None else total + cols
    return rows, total


def early_kernel(table, block, parts, x_ref, f_ref, ft_ref, bend_ref, shrink_ref, own, other, *refs):
    rows_out, total_out, wide_out, scaled_out, pair = refs
    low, width, _ = parts
    depth = own.shape[0]
    odd = lax.axis_index("row") % 2
    pair[pl.ds(pl.multiple_of(odd * depth, depth), depth), :] = own[...]
    pair[pl.ds(pl.multiple_of((1 - odd) * depth, depth), depth), :] = other[...]
    inset = [begin - 2 * depth * (place // 2) for place, begin in enumerate(low)]
    whole = pair[pl.ds(pl.multiple_of(pick("row", inset), math.gcd(*inset, 128)), width), :].astype(jnp.float32)
    here = lanes(low, width)
    wide = jnp.transpose(whole).astype(jnp.bfloat16)
    scaled = (whole * shrink_ref[here, :]).astype(jnp.bfloat16)
    wide_out[...] = wide
    scaled_out[...] = scaled
    rows, total = part_of_block(table, block, here, x_ref, f_ref, ft_ref, bend_ref, wide, scaled)
    for at, value in enumerate(rows):
        rows_out[at * value.shape[0] : (at + 1) * value.shape[0], :] = value
    total_out[...] = total


def rest_kernel(table, block, parts, n_row, x_ref, f_ref, ft_ref, bend_ref, shrink_ref, *refs):
    shares, (rows_in, total_in, wide_in, scaled_in) = refs[:n_row], refs[n_row : n_row + 4]
    rows_out, total_out, wide_out, scaled_out, piece = refs[n_row + 4 :]
    low, width, rest = parts
    me = lax.axis_index("row")
    depth = shares[0].shape[0]
    for hop in range(n_row):
        start = pl.multiple_of(source(me, hop, n_row) * depth, depth)
        piece[pl.ds(start, depth), :] = shares[hop][...]
    here = lanes(rest, n_row * depth - width)
    whole = piece[here, :].astype(jnp.float32)
    wide = jnp.transpose(whole).astype(jnp.bfloat16)
    scaled = (whole * shrink_ref[here, :]).astype(jnp.bfloat16)
    rows, total = part_of_block(table, block, here, x_ref, f_ref, ft_ref, bend_ref, wide, scaled)
    for at, value in enumerate(rows):
        span = slice(at * value.shape[0], (at + 1) * value.shape[0])
        rows_out[span, :] = (rows_in[span, :] + value).astype(rows_out.dtype)
    done = lanes(low, width)
    total_out[:, here] = total
    total_out[:, done] = total_in[...]
    wide_out[:, here] = wide
    wide_out[:, done] = wide_in[...]
    scaled_out[here, :] = scaled
    scaled_out[done, :] = scaled_in[...]


def first_block(table, block, parts, n_row, fixed, shares):
    genes, rank = fixed[4].shape
    depth = genes // n_row
    width = parts[1]
    ins = pinned(*fixed)
    early = pl.pallas_call(
        functools.partial(early_kernel, table, block, parts),
        out_shape=(
            VMEM((block, rank), jnp.float32),
            VMEM((rank, width), jnp.float32),
            VMEM((rank, width), jnp.bfloat16),
            VMEM((width, rank), jnp.bfloat16),
        ),
        in_specs=[IN_VMEM] * 7,
        out_specs=(IN_VMEM,) * 4,
        scratch_shapes=[VMEM((2 * depth, rank), jnp.bfloat16)],
        compiler_params=params(),
        cost_estimate=cost(12 * block * width * rank, block * width * 4),
        name="early_part",
    )(*ins, *shares[:2])
    done, *carried = pl.pallas_call(
        functools.partial(rest_kernel, table, block, parts, n_row),
        out_shape=(
            jax.ShapeDtypeStruct((block, rank), jnp.bfloat16),
            VMEM((rank, genes), jnp.float32),
            VMEM((rank, genes), jnp.bfloat16),
            VMEM((genes, rank), jnp.bfloat16),
        ),
        in_specs=[IN_VMEM] * (9 + n_row),
        out_specs=(IN_VMEM,) * 4,
        scratch_shapes=[VMEM((genes, rank), jnp.bfloat16)],
        compiler_params=params(),
        cost_estimate=cost(12 * block * (genes - width) * rank, block * (genes - width) * 4),
        name="rest_part",
    )(*ins, *shares, *pinned(*early))
    return [done], carried


def swap_row(value, hop, size):
    return lax.ppermute(value, "row", [(me, partner(me, hop, size)) for me in range(size)])


def ring_of(size):
    return [*range(0, size, 2), *reversed(range(1, size, 2))]


def steps_of(size):
    ahead = [(1, distance) for distance in range(size // 2, 0, -1)]
    back = [(-1, distance) for distance in range((size - 1) // 2, 0, -1)]
    return [step for pair in itertools.zip_longest(ahead, back) for step in pair if step]


def around(size, hops):
    ring = ring_of(size)
    return tuple(ring[(ring.index(place) + hops) % size] for place in range(size))


def plus(wide, narrow):
    return wide.astype(jnp.float32) + narrow.astype(jnp.float32)


def finish_kernel(n_ends, n_parts, *refs):
    n_ins = n_ends + n_parts + 3
    ins, outs = refs[:n_ins], refs[n_ins : n_ins + 3 + bool(n_ends)]
    *held, sems = refs[n_ins + len(outs) :]
    ends, parts = ins[:n_ends], ins[n_ends : n_ends + n_parts]
    factor, first, second = ins[n_ends + n_parts :]
    copies = []

    def send(at, span, value):
        held[at][span, :] = value
        copies.append(pltpu.make_async_copy(held[at].at[span, :], outs[at].at[span, :], sems.at[len(copies)]))
        copies[-1].start()

    if ends:
        step = tile_of(ends[0].shape[0], 256)
        for low in range(0, ends[0].shape[0], step):
            span = pl.ds(low, step)
            rows = ends[0][span, :]
            for end in ends[1:]:
                rows = plus(rows, end[span, :])
            send(3, span, rows)
    grad = parts[0][...]
    for part in parts[1:]:
        grad = plus(grad, part[...])
    span = pl.ds(0, grad.shape[0])
    new_first = beta_one * first[...] + (1.0 - beta_one) * grad
    new_second = beta_two * second[...] + (1.0 - beta_two) * grad * grad
    send(1, span, new_first)
    send(2, span, new_second)
    first_hat = new_first / (1.0 - beta_one**10)
    second_hat = new_second / (1.0 - beta_two**10)
    send(0, span, factor[...] - learn_rate * first_hat / (jnp.sqrt(second_hat) + adam_eps))
    for copy in copies:
        copy.wait()


def finish(ends, parts, factor, first, second):
    ins = [*ends, *parts, factor, first, second]
    shapes = [factor, factor, factor] + list(ends[:1])
    n_copies = 3 + (ends[0].shape[0] // tile_of(ends[0].shape[0], 256) if ends else 0)
    return pl.pallas_call(
        functools.partial(finish_kernel, len(ends), len(parts)),
        out_shape=tuple(jax.ShapeDtypeStruct(like.shape, jnp.float32) for like in shapes),
        in_specs=[IN_VMEM] * len(ins),
        out_specs=(IN_ANY,) * len(shapes),
        scratch_shapes=[VMEM(like.shape, jnp.float32) for like in shapes] + [pltpu.SemaphoreType.DMA((n_copies,))],
        compiler_params=params(),
        cost_estimate=cost(20 * factor.size, sum(4 * a.size for a in ins)),
        name="finish",
    )(*ins)


def local(x_slab, cell_factor, row_index, gene_scale, gene_factor, first_moment, second_moment):
    rows_dev, genes_dev = x_slab.shape
    n_gene = lax.axis_size("gene")
    n_row = lax.axis_size("row")
    block = rows_dev // n_gene
    scale_k = 4.0 / math.sqrt(genes_dev * n_gene)
    factor_bf = gene_factor.astype(jnp.bfloat16)
    shares = [factor_bf] + [swap_row(factor_bf, hop, n_row) for hop in range(1, n_row)]
    fixed = prepare(x_slab, row_index, cell_factor, gene_scale, scale_k)
    adam = (gene_factor, first_moment, second_moment)

    if n_gene == 1 or n_gene > RING_MOST or block % 128:
        (rows,), parts = block_rows([(0,)], [jnp.float32], rows_dev, True, True, n_row, fixed, shares)
        grad_cells = lax.psum_scatter(rows, "gene", scatter_dimension=0, tiled=True)
        others = [swap_row(parts[hop], hop, n_row) for hop in range(1, n_row)]
        return (grad_cells, *finish([], [parts[0], *others], *adam))

    steps = steps_of(n_gene)
    tables = [around(n_gene, way * distance) for way, distance in steps] + [tuple(range(n_gene))]
    kinds = [jnp.bfloat16] * len(steps) + [jnp.float32]
    cuts = [0, 1, 2, len(tables)] if len(steps) > 2 else [0, 1, len(tables)]
    parted = lane_parts(genes_dev, genes_dev // n_row, n_row)
    carried, blocks = shares, []
    for low, high in zip(cuts, cuts[1:]):
        last = high == len(tables)
        if low == 0 and parted:
            done, carried = first_block(tables[0], block, parted, n_row, fixed, shares)
            blocks += done
            continue
        done, carried = block_rows(tables[low:high], kinds[low:high], block, low == 0, last, n_row, fixed, carried)
        blocks += done
    parts = carried

    came = {}
    for (way, _), own in zip(steps, blocks):
        if way in came:
            own = plus(own, came[way]).astype(jnp.bfloat16)
        came[way] = lax.ppermute(own, "gene", list(enumerate(around(n_gene, way))))
    others = [swap_row(parts[hop], hop, n_row) for hop in range(1, n_row)]
    *adam_out, grad_cells = finish([blocks[-1], *came.values()], [parts[0], *others], *adam)
    return (grad_cells, *adam_out)


def solution(mesh):
    in_specs = (
        P(("grp", "row"), "gene"),
        P(("grp", "row"), None),
        P(("grp", "row")),
        P(("grp", "gene")),
        P(("grp", "gene", "row"), None),
        P(("grp", "gene", "row"), None),
        P(("grp", "gene", "row"), None),
    )
    out_specs = (
        P(("grp", "row", "gene"), None),
        P(("grp", "gene", "row"), None),
        P(("grp", "gene", "row"), None),
        P(("grp", "gene", "row"), None),
    )
    return jax.shard_map(local, mesh=mesh, in_specs=in_specs, out_specs=out_specs, check_vma=False)
```

```python
import functools
import itertools
import math

import jax
import jax.numpy as jnp
from jax import lax
from jax.experimental import pallas as pl
from jax.experimental.pallas import tpu as pltpu
from jax.sharding import PartitionSpec as P

tukey_c = 4.685
beta_one = 0.9
beta_two = 0.999
learn_rate = 0.02
adam_eps = 1e-08

RING_MOST = 8
VMEM = pltpu.VMEM
IN_VMEM = pl.BlockSpec(memory_space=VMEM)
IN_ANY = pl.BlockSpec(memory_space=pl.ANY)


def tile_of(rows, most):
    best = [t for t in range(128, most + 1, 128) if rows % t == 0]
    return best[-1] if best else rows


def params():
    return pltpu.CompilerParams(vmem_limit_bytes=24 * 1024 * 1024)


def cost(flops, moved):
    return pl.CostEstimate(flops=int(flops), bytes_accessed=int(moved), transcendentals=0)


def pinned(*arrays):
    return [pltpu.with_memory_space_constraint(a, VMEM) for a in arrays]


def prepare_kernel(scale_k, x_in, index_in, cell_in, scale_in, x_out, f_out, ft_out, bend_out, shrink_out, index, cell, scale, sems):
    loads = [
        pltpu.make_async_copy(src, dst, sems.at[at])
        for at, (src, dst) in enumerate(((scale_in, scale), (cell_in, cell), (index_in, index), (x_in, x_out)))
    ]
    for load in loads:
        load.start()
    cells, rank = cell.shape
    rows = index.shape[0]
    genes = scale.shape[0]
    loads[0].wait()
    inverse = 1.0 / scale[...].reshape(1, genes)
    bend_out[...] = (inverse * inverse) * (1.0 / (tukey_c * tukey_c))
    shrink_out[...] = jnp.transpose(jnp.broadcast_to(-scale_k * (inverse * inverse), (rank, genes)))
    loads[1].wait()
    table = jnp.transpose(cell[...].astype(jnp.float32)).astype(jnp.bfloat16)
    base = lax.axis_index("row") * cells
    loads[2].wait()
    step = tile_of(rows, 512)
    for at in range(0, rows, step):
        local = index[at : at + step].reshape(1, step) - base
        hot = lax.broadcasted_iota(jnp.int32, (cells, step), 0) == local
        hot = jnp.where(hot, 1.0, 0.0).astype(jnp.bfloat16)
        picked = jnp.dot(table, hot, preferred_element_type=jnp.float32)
        ft_out[:, at : at + step] = picked.astype(jnp.bfloat16)
        f_out[at : at + step, :] = jnp.transpose(picked).astype(jnp.bfloat16)
    loads[3].wait()


def prepare(x_slab, row_index, cell_factor, gene_scale, scale_k):
    rows, genes = x_slab.shape
    cells, rank = cell_factor.shape
    ins = (x_slab, row_index, cell_factor, gene_scale)
    return pl.pallas_call(
        functools.partial(prepare_kernel, scale_k),
        out_shape=(
            VMEM((rows, genes), jnp.bfloat16),
            VMEM((rows, rank), jnp.bfloat16),
            VMEM((rank, rows), jnp.bfloat16),
            VMEM((1, genes), jnp.float32),
            VMEM((genes, rank), jnp.float32),
        ),
        in_specs=[IN_ANY] * 4,
        out_specs=(IN_VMEM,) * 5,
        scratch_shapes=[
            VMEM((rows,), jnp.int32),
            VMEM((cells, rank), jnp.bfloat16),
            VMEM((genes,), jnp.float32),
            pltpu.SemaphoreType.DMA((4,)),
        ],
        compiler_params=params(),
        cost_estimate=cost(8 * rows * cells * rank, 8 * rows * genes * 2),
        name="prepare",
    )(*(pltpu.with_memory_space_constraint(a, pltpu.HBM) for a in ins))


def pick(axis, table):
    me = lax.axis_index(axis)
    value = jnp.int32(table[0])
    for place, entry in enumerate(table[1:], 1):
        value = jnp.where(me == place, jnp.int32(entry), value)
    return value


def partner(me, hop, size):
    return me ^ hop if size & (size - 1) == 0 else (me + hop) % size


def source(me, hop, size):
    return me ^ hop if size & (size - 1) == 0 else (me + size - hop) % size


def rows_kernel(tables, block, first, last, n_row, *refs):
    refs = list(refs)
    take = lambda count: [refs.pop(0) for _ in range(count)]
    x_ref, f_ref, ft_ref, bend_ref, shrink_ref = take(5)
    shares = take(n_row) if first else None
    carried_in = None if first else take(3)
    rows_out = take(len(tables))
    carried_out = None if last else take(3 if first else 1)
    parts_out = take(n_row) if last else None
    me = lax.axis_index("row")

    if first:
        (piece,) = take(1)
        depth = shares[0].shape[0]
        for hop in range(n_row):
            start = pl.multiple_of(source(me, hop, n_row) * depth, depth)
            piece[pl.ds(start, depth), :] = shares[hop][...]
        whole = piece[...].astype(jnp.float32)
        wide = jnp.transpose(whole).astype(jnp.bfloat16)
        scaled = (whole * shrink_ref[...]).astype(jnp.bfloat16)
        total = None
    else:
        total, wide, scaled = (ref[...] for ref in carried_in)

    bend = bend_ref[...]
    step = tile_of(block, 256)
    tiles = []
    for table, out in zip(tables, rows_out):
        origin = pick("gene", table) * block if len(table) > 1 else 0
        for at in range(0, block, step):
            start = origin + at
            if len(table) > 1:
                start = pl.multiple_of(start, math.gcd(block, step))
            tiles.append((out, at, pl.ds(start, step)))

    def predict(here):
        return jnp.dot(f_ref[here, :], wide, preferred_element_type=jnp.float32)

    def gradients(tile, infl, total):
        out, at, here = tile
        cols = jnp.dot(ft_ref[:, here], infl, preferred_element_type=jnp.float32)
        out[at : at + step, :] = jnp.dot(infl, scaled, preferred_element_type=jnp.float32).astype(out.dtype)
        return cols if total is None else total + cols

    pred = predict(tiles[0][2])
    infl = None
    for at, tile in enumerate(tiles):
        later = predict(tiles[at + 1][2]) if at + 1 < len(tiles) else None
        now = influence(x_ref[tile[2], :], pred, bend)
        if at:
            total = gradients(tiles[at - 1], infl, total)
        infl, pred = now, later
    total = gradients(tiles[-1], infl, total)

    if first and not last:
        carried_out[1][...] = wide
        carried_out[2][...] = scaled
    if not last:
        carried_out[0][...] = total
        return
    (turned,) = take(1)
    turned[...] = jnp.transpose(total) * shrink_ref[...]
    depth = parts_out[0].shape[0]
    for hop in range(n_row):
        start = pl.multiple_of(partner(me, hop, n_row) * depth, depth)
        parts_out[hop][...] = turned[pl.ds(start, depth), :].astype(parts_out[hop].dtype)


def block_rows(tables, kinds, block, first, last, n_row, fixed, carried):
    genes, rank = fixed[4].shape
    out = [jax.ShapeDtypeStruct((block, rank), kind) for kind in kinds]
    if last:
        out += [jax.ShapeDtypeStruct((genes // n_row, rank), jnp.bfloat16 if hop else jnp.float32) for hop in range(n_row)]
    else:
        out += [VMEM((rank, genes), jnp.float32)]
    if first and not last:
        out += [VMEM((rank, genes), jnp.bfloat16), VMEM((genes, rank), jnp.bfloat16)]
    scratch = [VMEM((genes, rank), jnp.bfloat16)] if first else []
    if last:
        scratch.append(VMEM((genes, rank), jnp.float32))
    ins = pinned(*fixed) + (list(carried) if first else pinned(*carried))
    work = len(tables) * block * genes
    out = pl.pallas_call(
        functools.partial(rows_kernel, tables, block, first, last, n_row),
        out_shape=tuple(out),
        in_specs=[IN_VMEM] * len(ins),
        out_specs=(IN_VMEM,) * len(out),
        scratch_shapes=scratch,
        compiler_params=params(),
        cost_estimate=cost(6 * work * rank, work * 2),
        name="block_rows",
    )(*ins)
    done, rest = list(out[: len(tables)]), list(out[len(tables) :])
    return done, rest if first or last else rest + list(carried[1:])


def lane_parts(genes, depth, n_row):
    if n_row != 4:
        return None
    pairs = [(2 * depth * (place // 2), 2 * depth * (place // 2 + 1)) for place in range(n_row)]
    low = [-(-begin // 128) * 128 for begin, _ in pairs]
    width = min(end // 128 * 128 - begin for begin, (_, end) in zip(low, pairs))
    if width <= 0 or any(begin not in (0, genes - width) for begin in low):
        return None
    return low, width, [width if begin == 0 else 0 for begin in low]


def lanes(table, width):
    return pl.ds(pl.multiple_of(pick("row", table), 128), width)


def influence(x, pred, bend):
    resid = x.astype(jnp.float32) - pred
    inside = jnp.maximum(1.0 - resid * resid * bend, 0.0)
    return (resid * (inside * inside)).astype(jnp.bfloat16)


def part_of_block(table, block, here, x_ref, f_ref, ft_ref, bend_ref, wide, scaled):
    step = tile_of(block, 256)
    origin = pick("gene", table) * block
    tiles = [pl.ds(pl.multiple_of(origin + at, math.gcd(block, step)), step) for at in range(0, block, step)]
    bend = bend_ref[:, here]
    preds = [jnp.dot(f_ref[tile, :], wide, preferred_element_type=jnp.float32) for tile in tiles]
    infls = [influence(x_ref[tile, here], pred, bend) for tile, pred in zip(tiles, preds)]
    rows, total = [], None
    for tile, infl in zip(tiles, infls):
        cols = jnp.dot(ft_ref[:, tile], infl, preferred_element_type=jnp.float32)
        rows.append(jnp.dot(infl, scaled, preferred_element_type=jnp.float32))
        total = cols if total is None else total + cols
    return rows, total


def early_kernel(table, block, parts, x_ref, f_ref, ft_ref, bend_ref, shrink_ref, own, other, *refs):
    rows_out, total_out, wide_out, scaled_out, pair = refs
    low, width, _ = parts
    depth = own.shape[0]
    odd = lax.axis_index("row") % 2
    pair[pl.ds(pl.multiple_of(odd * depth, depth), depth), :] = own[...]
    pair[pl.ds(pl.multiple_of((1 - odd) * depth, depth), depth), :] = other[...]
    inset = [begin - 2 * depth * (place // 2) for place, begin in enumerate(low)]
    whole = pair[pl.ds(pl.multiple_of(pick("row", inset), math.gcd(*inset, 128)), width), :].astype(jnp.float32)
    here = lanes(low, width)
    wide = jnp.transpose(whole).astype(jnp.bfloat16)
    scaled = (whole * shrink_ref[here, :]).astype(jnp.bfloat16)
    wide_out[...] = wide
    scaled_out[...] = scaled
    rows, total = part_of_block(table, block, here, x_ref, f_ref, ft_ref, bend_ref, wide, scaled)
    for at, value in enumerate(rows):
        rows_out[at * value.shape[0] : (at + 1) * value.shape[0], :] = value
    total_out[...] = total


def rest_kernel(table, block, parts, n_row, x_ref, f_ref, ft_ref, bend_ref, shrink_ref, *refs):
    shares, (rows_in, total_in, wide_in, scaled_in) = refs[:n_row], refs[n_row : n_row + 4]
    rows_out, total_out, wide_out, scaled_out, piece = refs[n_row + 4 :]
    low, width, rest = parts
    me = lax.axis_index("row")
    depth = shares[0].shape[0]
    for hop in range(n_row):
        start = pl.multiple_of(source(me, hop, n_row) * depth, depth)
        piece[pl.ds(start, depth), :] = shares[hop][...]
    here = lanes(rest, n_row * depth - width)
    whole = piece[here, :].astype(jnp.float32)
    wide = jnp.transpose(whole).astype(jnp.bfloat16)
    scaled = (whole * shrink_ref[here, :]).astype(jnp.bfloat16)
    rows, total = part_of_block(table, block, here, x_ref, f_ref, ft_ref, bend_ref, wide, scaled)
    for at, value in enumerate(rows):
        span = slice(at * value.shape[0], (at + 1) * value.shape[0])
        rows_out[span, :] = (rows_in[span, :] + value).astype(rows_out.dtype)
    done = lanes(low, width)
    total_out[:, here] = total
    total_out[:, done] = total_in[...]
    wide_out[:, here] = wide
    wide_out[:, done] = wide_in[...]
    scaled_out[here, :] = scaled
    scaled_out[done, :] = scaled_in[...]


def first_block(table, block, parts, n_row, fixed, shares):
    genes, rank = fixed[4].shape
    depth = genes // n_row
    width = parts[1]
    ins = pinned(*fixed)
    early = pl.pallas_call(
        functools.partial(early_kernel, table, block, parts),
        out_shape=(
            VMEM((block, rank), jnp.float32),
            VMEM((rank, width), jnp.float32),
            VMEM((rank, width), jnp.bfloat16),
            VMEM((width, rank), jnp.bfloat16),
        ),
        in_specs=[IN_VMEM] * 7,
        out_specs=(IN_VMEM,) * 4,
        scratch_shapes=[VMEM((2 * depth, rank), jnp.bfloat16)],
        compiler_params=params(),
        cost_estimate=cost(12 * block * width * rank, block * width * 4),
        name="early_part",
    )(*ins, *shares[:2])
    done, *carried = pl.pallas_call(
        functools.partial(rest_kernel, table, block, parts, n_row),
        out_shape=(
            jax.ShapeDtypeStruct((block, rank), jnp.bfloat16),
            VMEM((rank, genes), jnp.float32),
            VMEM((rank, genes), jnp.bfloat16),
            VMEM((genes, rank), jnp.bfloat16),
        ),
        in_specs=[IN_VMEM] * (9 + n_row),
        out_specs=(IN_VMEM,) * 4,
        scratch_shapes=[VMEM((genes, rank), jnp.bfloat16)],
        compiler_params=params(),
        cost_estimate=cost(12 * block * (genes - width) * rank, block * (genes - width) * 4),
        name="rest_part",
    )(*ins, *shares, *pinned(*early))
    return [done], carried


def swap_row(value, hop, size):
    return lax.ppermute(value, "row", [(me, partner(me, hop, size)) for me in range(size)])


def ring_of(size):
    return [*range(0, size, 2), *reversed(range(1, size, 2))]


def steps_of(size):
    ahead = [(1, distance) for distance in range(size // 2, 0, -1)]
    back = [(-1, distance) for distance in range((size - 1) // 2, 0, -1)]
    return [step for pair in itertools.zip_longest(ahead, back) for step in pair if step]


def around(size, hops):
    ring = ring_of(size)
    return tuple(ring[(ring.index(place) + hops) % size] for place in range(size))


def plus(wide, narrow):
    return wide.astype(jnp.float32) + narrow.astype(jnp.float32)


def finish_kernel(n_ends, n_parts, *refs):
    n_ins = n_ends + n_parts + 3
    ins, outs = refs[:n_ins], refs[n_ins : n_ins + 3 + bool(n_ends)]
    *held, sems = refs[n_ins + len(outs) :]
    ends, parts = ins[:n_ends], ins[n_ends : n_ends + n_parts]
    factor, first, second = ins[n_ends + n_parts :]
    copies = []

    def send(at, span, value):
        held[at][span, :] = value
        copies.append(pltpu.make_async_copy(held[at].at[span, :], outs[at].at[span, :], sems.at[len(copies)]))
        copies[-1].start()

    if ends:
        step = tile_of(ends[0].shape[0], 256)
        for low in range(0, ends[0].shape[0], step):
            span = pl.ds(low, step)
            rows = ends[0][span, :]
            for end in ends[1:]:
                rows = plus(rows, end[span, :])
            send(3, span, rows)
    grad = parts[0][...]
    for part in parts[1:]:
        grad = plus(grad, part[...])
    span = pl.ds(0, grad.shape[0])
    new_first = beta_one * first[...] + (1.0 - beta_one) * grad
    new_second = beta_two * second[...] + (1.0 - beta_two) * grad * grad
    send(1, span, new_first)
    send(2, span, new_second)
    first_hat = new_first / (1.0 - beta_one**10)
    second_hat = new_second / (1.0 - beta_two**10)
    send(0, span, factor[...] - learn_rate * first_hat / (jnp.sqrt(second_hat) + adam_eps))
    for copy in copies:
        copy.wait()


def finish(ends, parts, factor, first, second):
    ins = [*ends, *parts, factor, first, second]
    shapes = [factor, factor, factor] + list(ends[:1])
    n_copies = 3 + (ends[0].shape[0] // tile_of(ends[0].shape[0], 256) if ends else 0)
    return pl.pallas_call(
        functools.partial(finish_kernel, len(ends), len(parts)),
        out_shape=tuple(jax.ShapeDtypeStruct(like.shape, jnp.float32) for like in shapes),
        in_specs=[IN_VMEM] * len(ins),
        out_specs=(IN_ANY,) * len(shapes),
        scratch_shapes=[VMEM(like.shape, jnp.float32) for like in shapes] + [pltpu.SemaphoreType.DMA((n_copies,))],
        compiler_params=params(),
        cost_estimate=cost(20 * factor.size, sum(4 * a.size for a in ins)),
        name="finish",
    )(*ins)


def local(x_slab, cell_factor, row_index, gene_scale, gene_factor, first_moment, second_moment):
    rows_dev, genes_dev = x_slab.shape
    n_gene = lax.axis_size("gene")
    n_row = lax.axis_size("row")
    block = rows_dev // n_gene
    scale_k = 4.0 / math.sqrt(genes_dev * n_gene)
    factor_bf = gene_factor.astype(jnp.bfloat16)
    shares = [factor_bf] + [swap_row(factor_bf, hop, n_row) for hop in range(1, n_row)]
    fixed = prepare(x_slab, row_index, cell_factor, gene_scale, scale_k)
    adam = (gene_factor, first_moment, second_moment)

    if n_gene == 1 or n_gene > RING_MOST or block % 128:
        (rows,), parts = block_rows([(0,)], [jnp.float32], rows_dev, True, True, n_row, fixed, shares)
        grad_cells = lax.psum_scatter(rows, "gene", scatter_dimension=0, tiled=True)
        others = [swap_row(parts[hop], hop, n_row) for hop in range(1, n_row)]
        return (grad_cells, *finish([], [parts[0], *others], *adam))

    steps = steps_of(n_gene)
    tables = [around(n_gene, way * distance) for way, distance in steps] + [tuple(range(n_gene))]
    kinds = [jnp.bfloat16] * len(steps) + [jnp.float32]
    cuts = [0, 1, 2, len(tables)] if len(steps) > 2 else [0, 1, len(tables)]
    parted = lane_parts(genes_dev, genes_dev // n_row, n_row)
    carried, blocks = shares, []
    for low, high in zip(cuts, cuts[1:]):
        last = high == len(tables)
        if low == 0 and parted:
            done, carried = first_block(tables[0], block, parted, n_row, fixed, shares)
            blocks += done
            continue
        done, carried = block_rows(tables[low:high], kinds[low:high], block, low == 0, last, n_row, fixed, carried)
        blocks += done
    parts = carried

    came = {}
    for (way, _), own in zip(steps, blocks):
        if way in came:
            own = plus(own, came[way]).astype(jnp.bfloat16)
        came[way] = lax.ppermute(own, "gene", list(enumerate(around(n_gene, way))))
    others = [swap_row(parts[hop], hop, n_row) for hop in range(1, n_row)]
    *adam_out, grad_cells = finish([blocks[-1], *came.values()], [parts[0], *others], *adam)
    return (grad_cells, *adam_out)


def solution(mesh):
    in_specs = (
        P(("grp", "row"), "gene"),
        P(("grp", "row"), None),
        P(("grp", "row")),
        P(("grp", "gene")),
        P(("grp", "gene", "row"), None),
        P(("grp", "gene", "row"), None),
        P(("grp", "gene", "row"), None),
    )
    out_specs = (
        P(("grp", "row", "gene"), None),
        P(("grp", "gene", "row"), None),
        P(("grp", "gene", "row"), None),
        P(("grp", "gene", "row"), None),
    )
    return jax.shard_map(local, mesh=mesh, in_specs=in_specs, out_specs=out_specs, check_vma=False)
```

```python
import functools
import itertools
import math

import jax
import jax.numpy as jnp
from jax import lax
from jax.experimental import pallas as pl
from jax.experimental.pallas import tpu as pltpu
from jax.sharding import PartitionSpec as P

tukey_c = 4.685
beta_one = 0.9
beta_two = 0.999
learn_rate = 0.02
adam_eps = 1e-08

RING_MOST = 8
LINES = ("grp", "gene")
VMEM = pltpu.VMEM
IN_VMEM = pl.BlockSpec(memory_space=VMEM)
IN_ANY = pl.BlockSpec(memory_space=pl.ANY)


def tile_of(rows, most):
    best = [t for t in range(128, most + 1, 128) if rows % t == 0]
    return best[-1] if best else rows


def params():
    return pltpu.CompilerParams(vmem_limit_bytes=24 * 1024 * 1024)


def cost(flops, moved):
    return pl.CostEstimate(flops=int(flops), bytes_accessed=int(moved), transcendentals=0)


def pinned(*arrays):
    return [pltpu.with_memory_space_constraint(a, VMEM) for a in arrays]


def prepare_kernel(scale_k, x_in, index_in, cell_in, scale_in, x_out, f_out, ft_out, bend_out, shrink_out, index, cell, scale, sems):
    loads = [
        pltpu.make_async_copy(src, dst, sems.at[at])
        for at, (src, dst) in enumerate(((scale_in, scale), (cell_in, cell), (index_in, index), (x_in, x_out)))
    ]
    for load in loads:
        load.start()
    cells, rank = cell.shape
    rows = index.shape[0]
    genes = scale.shape[0]
    loads[0].wait()
    inverse = 1.0 / scale[...].reshape(1, genes)
    bend_out[...] = (inverse * inverse) * (1.0 / (tukey_c * tukey_c))
    shrink_out[...] = jnp.transpose(jnp.broadcast_to(-scale_k * (inverse * inverse), (rank, genes)))
    loads[1].wait()
    table = jnp.transpose(cell[...].astype(jnp.float32)).astype(jnp.bfloat16)
    base = lax.axis_index("row") * cells
    loads[2].wait()
    step = tile_of(rows, 512)
    for at in range(0, rows, step):
        local = index[at : at + step].reshape(1, step) - base
        hot = lax.broadcasted_iota(jnp.int32, (cells, step), 0) == local
        hot = jnp.where(hot, 1.0, 0.0).astype(jnp.bfloat16)
        picked = jnp.dot(table, hot, preferred_element_type=jnp.float32)
        ft_out[:, at : at + step] = picked.astype(jnp.bfloat16)
        f_out[at : at + step, :] = jnp.transpose(picked).astype(jnp.bfloat16)
    loads[3].wait()


def prepare(x_slab, row_index, cell_factor, gene_scale, scale_k):
    rows, genes = x_slab.shape
    cells, rank = cell_factor.shape
    ins = (x_slab, row_index, cell_factor, gene_scale)
    return pl.pallas_call(
        functools.partial(prepare_kernel, scale_k),
        out_shape=(
            VMEM((rows, genes), jnp.bfloat16),
            VMEM((rows, rank), jnp.bfloat16),
            VMEM((rank, rows), jnp.bfloat16),
            VMEM((1, genes), jnp.float32),
            VMEM((genes, rank), jnp.float32),
        ),
        in_specs=[IN_ANY] * 4,
        out_specs=(IN_VMEM,) * 5,
        scratch_shapes=[
            VMEM((rows,), jnp.int32),
            VMEM((cells, rank), jnp.bfloat16),
            VMEM((genes,), jnp.float32),
            pltpu.SemaphoreType.DMA((4,)),
        ],
        compiler_params=params(),
        cost_estimate=cost(8 * rows * cells * rank, 8 * rows * genes * 2),
        name="prepare",
    )(*(pltpu.with_memory_space_constraint(a, pltpu.HBM) for a in ins))


def pick(axes, table):
    me = lax.axis_index(axes)
    value = jnp.int32(table[0])
    for place, entry in enumerate(table[1:], 1):
        value = jnp.where(me == place, jnp.int32(entry), value)
    return value


def partner(me, hop, size):
    return me ^ hop if size & (size - 1) == 0 else (me + hop) % size


def source(me, hop, size):
    return me ^ hop if size & (size - 1) == 0 else (me + size - hop) % size


def rows_kernel(tables, block, first, last, n_row, *refs):
    refs = list(refs)
    take = lambda count: [refs.pop(0) for _ in range(count)]
    x_ref, f_ref, ft_ref, bend_ref, shrink_ref = take(5)
    shares = take(n_row) if first else None
    carried_in = None if first else take(3)
    rows_out = take(len(tables))
    carried_out = None if last else take(3 if first else 1)
    parts_out = take(n_row) if last else None
    me = lax.axis_index("row")

    if first:
        (piece,) = take(1)
        depth = shares[0].shape[0]
        for hop in range(n_row):
            start = pl.multiple_of(source(me, hop, n_row) * depth, depth)
            piece[pl.ds(start, depth), :] = shares[hop][...]
        whole = piece[...].astype(jnp.float32)
        wide = jnp.transpose(whole).astype(jnp.bfloat16)
        scaled = (whole * shrink_ref[...]).astype(jnp.bfloat16)
        total = None
    else:
        total, wide, scaled = (ref[...] for ref in carried_in)

    bend = bend_ref[...]
    step = tile_of(block, 256)
    tiles = []
    for table, out in zip(tables, rows_out):
        origin = pick(LINES, table) * block if len(table) > 1 else 0
        for at in range(0, block, step):
            start = origin + at
            if len(table) > 1:
                start = pl.multiple_of(start, math.gcd(block, step))
            tiles.append((out, at, pl.ds(start, step)))

    def predict(here):
        return jnp.dot(f_ref[here, :], wide, preferred_element_type=jnp.float32)

    def gradients(tile, infl, total):
        out, at, here = tile
        cols = jnp.dot(ft_ref[:, here], infl, preferred_element_type=jnp.float32)
        out[at : at + step, :] = jnp.dot(infl, scaled, preferred_element_type=jnp.float32).astype(out.dtype)
        return cols if total is None else total + cols

    pred = predict(tiles[0][2])
    infl = None
    for at, tile in enumerate(tiles):
        later = predict(tiles[at + 1][2]) if at + 1 < len(tiles) else None
        now = influence(x_ref[tile[2], :], pred, bend)
        if at:
            total = gradients(tiles[at - 1], infl, total)
        infl, pred = now, later
    total = gradients(tiles[-1], infl, total)

    if first and not last:
        carried_out[1][...] = wide
        carried_out[2][...] = scaled
    if not last:
        carried_out[0][...] = total
        return
    (turned,) = take(1)
    turned[...] = jnp.transpose(total) * shrink_ref[...]
    depth = parts_out[0].shape[0]
    for hop in range(n_row):
        start = pl.multiple_of(partner(me, hop, n_row) * depth, depth)
        parts_out[hop][...] = turned[pl.ds(start, depth), :].astype(parts_out[hop].dtype)


def block_rows(tables, kinds, block, first, last, n_row, fixed, carried):
    genes, rank = fixed[4].shape
    out = [jax.ShapeDtypeStruct((block, rank), kind) for kind in kinds]
    if last:
        out += [jax.ShapeDtypeStruct((genes // n_row, rank), jnp.bfloat16 if hop else jnp.float32) for hop in range(n_row)]
    else:
        out += [VMEM((rank, genes), jnp.float32)]
    if first and not last:
        out += [VMEM((rank, genes), jnp.bfloat16), VMEM((genes, rank), jnp.bfloat16)]
    scratch = [VMEM((genes, rank), jnp.bfloat16)] if first else []
    if last:
        scratch.append(VMEM((genes, rank), jnp.float32))
    ins = pinned(*fixed) + (list(carried) if first else pinned(*carried))
    work = len(tables) * block * genes
    out = pl.pallas_call(
        functools.partial(rows_kernel, tables, block, first, last, n_row),
        out_shape=tuple(out),
        in_specs=[IN_VMEM] * len(ins),
        out_specs=(IN_VMEM,) * len(out),
        scratch_shapes=scratch,
        compiler_params=params(),
        cost_estimate=cost(6 * work * rank, work * 2),
        name="block_rows",
    )(*ins)
    done, rest = list(out[: len(tables)]), list(out[len(tables) :])
    return done, rest if first or last else rest + list(carried[1:])


def lane_parts(genes, depth, n_row):
    if n_row != 4:
        return None
    pairs = [(2 * depth * (place // 2), 2 * depth * (place // 2 + 1)) for place in range(n_row)]
    low = [-(-begin // 128) * 128 for begin, _ in pairs]
    width = min(end // 128 * 128 - begin for begin, (_, end) in zip(low, pairs))
    if width <= 0 or any(begin not in (0, genes - width) for begin in low):
        return None
    return low, width, [width if begin == 0 else 0 for begin in low]


def lanes(table, width):
    return pl.ds(pl.multiple_of(pick("row", table), 128), width)


def influence(x, pred, bend):
    resid = x.astype(jnp.float32) - pred
    inside = jnp.maximum(1.0 - resid * resid * bend, 0.0)
    return (resid * (inside * inside)).astype(jnp.bfloat16)


def part_of_block(table, block, here, x_ref, f_ref, ft_ref, bend_ref, wide, scaled):
    step = tile_of(block, 256)
    origin = pick(LINES, table) * block
    tiles = [pl.ds(pl.multiple_of(origin + at, math.gcd(block, step)), step) for at in range(0, block, step)]
    bend = bend_ref[:, here]
    preds = [jnp.dot(f_ref[tile, :], wide, preferred_element_type=jnp.float32) for tile in tiles]
    infls = [influence(x_ref[tile, here], pred, bend) for tile, pred in zip(tiles, preds)]
    rows, total = [], None
    for tile, infl in zip(tiles, infls):
        cols = jnp.dot(ft_ref[:, tile], infl, preferred_element_type=jnp.float32)
        rows.append(jnp.dot(infl, scaled, preferred_element_type=jnp.float32))
        total = cols if total is None else total + cols
    return rows, total


def early_kernel(table, block, parts, x_ref, f_ref, ft_ref, bend_ref, shrink_ref, own, other, *refs):
    rows_out, total_out, wide_out, scaled_out, pair = refs
    low, width, _ = parts
    depth = own.shape[0]
    odd = lax.axis_index("row") % 2
    pair[pl.ds(pl.multiple_of(odd * depth, depth), depth), :] = own[...]
    pair[pl.ds(pl.multiple_of((1 - odd) * depth, depth), depth), :] = other[...]
    inset = [begin - 2 * depth * (place // 2) for place, begin in enumerate(low)]
    whole = pair[pl.ds(pl.multiple_of(pick("row", inset), math.gcd(*inset, 128)), width), :].astype(jnp.float32)
    here = lanes(low, width)
    wide = jnp.transpose(whole).astype(jnp.bfloat16)
    scaled = (whole * shrink_ref[here, :]).astype(jnp.bfloat16)
    wide_out[...] = wide
    scaled_out[...] = scaled
    rows, total = part_of_block(table, block, here, x_ref, f_ref, ft_ref, bend_ref, wide, scaled)
    for at, value in enumerate(rows):
        rows_out[at * value.shape[0] : (at + 1) * value.shape[0], :] = value
    total_out[...] = total


def rest_kernel(table, block, parts, n_row, x_ref, f_ref, ft_ref, bend_ref, shrink_ref, *refs):
    shares, (rows_in, total_in, wide_in, scaled_in) = refs[:n_row], refs[n_row : n_row + 4]
    rows_out, total_out, wide_out, scaled_out, piece = refs[n_row + 4 :]
    low, width, rest = parts
    me = lax.axis_index("row")
    depth = shares[0].shape[0]
    for hop in range(n_row):
        start = pl.multiple_of(source(me, hop, n_row) * depth, depth)
        piece[pl.ds(start, depth), :] = shares[hop][...]
    here = lanes(rest, n_row * depth - width)
    whole = piece[here, :].astype(jnp.float32)
    wide = jnp.transpose(whole).astype(jnp.bfloat16)
    scaled = (whole * shrink_ref[here, :]).astype(jnp.bfloat16)
    rows, total = part_of_block(table, block, here, x_ref, f_ref, ft_ref, bend_ref, wide, scaled)
    for at, value in enumerate(rows):
        span = slice(at * value.shape[0], (at + 1) * value.shape[0])
        rows_out[span, :] = (rows_in[span, :] + value).astype(rows_out.dtype)
    done = lanes(low, width)
    total_out[:, here] = total
    total_out[:, done] = total_in[...]
    wide_out[:, here] = wide
    wide_out[:, done] = wide_in[...]
    scaled_out[here, :] = scaled
    scaled_out[done, :] = scaled_in[...]


def first_block(table, block, parts, n_row, fixed, shares):
    genes, rank = fixed[4].shape
    depth = genes // n_row
    width = parts[1]
    ins = pinned(*fixed)
    early = pl.pallas_call(
        functools.partial(early_kernel, table, block, parts),
        out_shape=(
            VMEM((block, rank), jnp.float32),
            VMEM((rank, width), jnp.float32),
            VMEM((rank, width), jnp.bfloat16),
            VMEM((width, rank), jnp.bfloat16),
        ),
        in_specs=[IN_VMEM] * 7,
        out_specs=(IN_VMEM,) * 4,
        scratch_shapes=[VMEM((2 * depth, rank), jnp.bfloat16)],
        compiler_params=params(),
        cost_estimate=cost(12 * block * width * rank, block * width * 4),
        name="early_part",
    )(*ins, *shares[:2])
    done, *carried = pl.pallas_call(
        functools.partial(rest_kernel, table, block, parts, n_row),
        out_shape=(
            jax.ShapeDtypeStruct((block, rank), jnp.bfloat16),
            VMEM((rank, genes), jnp.float32),
            VMEM((rank, genes), jnp.bfloat16),
            VMEM((genes, rank), jnp.bfloat16),
        ),
        in_specs=[IN_VMEM] * (9 + n_row),
        out_specs=(IN_VMEM,) * 4,
        scratch_shapes=[VMEM((genes, rank), jnp.bfloat16)],
        compiler_params=params(),
        cost_estimate=cost(12 * block * (genes - width) * rank, block * (genes - width) * 4),
        name="rest_part",
    )(*ins, *shares, *pinned(*early))
    return [done], carried


def swap_row(value, hop, size):
    return lax.ppermute(value, "row", [(me, partner(me, hop, size)) for me in range(size)])


def ring_of(size):
    return [*range(0, size, 2), *reversed(range(1, size, 2))]


def steps_of(size):
    ahead = [(1, distance) for distance in range(size // 2, 0, -1)]
    back = [(-1, distance) for distance in range((size - 1) // 2, 0, -1)]
    return [step for pair in itertools.zip_longest(ahead, back) for step in pair if step]


def around(groups, size, hops):
    ring = ring_of(size)
    ways = [-hops if group % 2 == 0 else hops for group in range(groups)]
    return tuple(ring[(ring.index(place) + way) % size] for way in ways for place in range(size))


def plus(wide, narrow):
    return wide.astype(jnp.float32) + narrow.astype(jnp.float32)


def finish_kernel(n_ends, n_parts, *refs):
    n_ins = n_ends + n_parts + 3
    ins, outs = refs[:n_ins], refs[n_ins : n_ins + 3 + bool(n_ends)]
    *held, sems = refs[n_ins + len(outs) :]
    ends, parts = ins[:n_ends], ins[n_ends : n_ends + n_parts]
    factor, first, second = ins[n_ends + n_parts :]
    copies = []

    def send(at, span, value):
        held[at][span, :] = value
        copies.append(pltpu.make_async_copy(held[at].at[span, :], outs[at].at[span, :], sems.at[len(copies)]))
        copies[-1].start()

    if ends:
        step = tile_of(ends[0].shape[0], 256)
        for low in range(0, ends[0].shape[0], step):
            span = pl.ds(low, step)
            rows = ends[0][span, :]
            for end in ends[1:]:
                rows = plus(rows, end[span, :])
            send(3, span, rows)
    grad = parts[0][...]
    for part in parts[1:]:
        grad = plus(grad, part[...])
    span = pl.ds(0, grad.shape[0])
    new_first = beta_one * first[...] + (1.0 - beta_one) * grad
    new_second = beta_two * second[...] + (1.0 - beta_two) * grad * grad
    send(1, span, new_first)
    send(2, span, new_second)
    first_hat = new_first / (1.0 - beta_one**10)
    second_hat = new_second / (1.0 - beta_two**10)
    send(0, span, factor[...] - learn_rate * first_hat / (jnp.sqrt(second_hat) + adam_eps))
    for copy in copies:
        copy.wait()


def finish(ends, parts, factor, first, second):
    ins = [*ends, *parts, factor, first, second]
    shapes = [factor, factor, factor] + list(ends[:1])
    n_copies = 3 + (ends[0].shape[0] // tile_of(ends[0].shape[0], 256) if ends else 0)
    return pl.pallas_call(
        functools.partial(finish_kernel, len(ends), len(parts)),
        out_shape=tuple(jax.ShapeDtypeStruct(like.shape, jnp.float32) for like in shapes),
        in_specs=[IN_VMEM] * len(ins),
        out_specs=(IN_ANY,) * len(shapes),
        scratch_shapes=[VMEM(like.shape, jnp.float32) for like in shapes] + [pltpu.SemaphoreType.DMA((n_copies,))],
        compiler_params=params(),
        cost_estimate=cost(20 * factor.size, sum(4 * a.size for a in ins)),
        name="finish",
    )(*ins)


def local(x_slab, cell_factor, row_index, gene_scale, gene_factor, first_moment, second_moment):
    rows_dev, genes_dev = x_slab.shape
    n_gene = lax.axis_size("gene")
    n_row = lax.axis_size("row")
    block = rows_dev // n_gene
    scale_k = 4.0 / math.sqrt(genes_dev * n_gene)
    factor_bf = gene_factor.astype(jnp.bfloat16)
    shares = [factor_bf] + [swap_row(factor_bf, hop, n_row) for hop in range(1, n_row)]
    fixed = prepare(x_slab, row_index, cell_factor, gene_scale, scale_k)
    adam = (gene_factor, first_moment, second_moment)

    if n_gene == 1 or n_gene > RING_MOST or block % 128:
        (rows,), parts = block_rows([(0,)], [jnp.float32], rows_dev, True, True, n_row, fixed, shares)
        grad_cells = lax.psum_scatter(rows, "gene", scatter_dimension=0, tiled=True)
        others = [swap_row(parts[hop], hop, n_row) for hop in range(1, n_row)]
        return (grad_cells, *finish([], [parts[0], *others], *adam))

    steps = steps_of(n_gene)
    groups = lax.axis_size("grp")
    tables = [around(groups, n_gene, way * distance) for way, distance in steps] + [around(groups, n_gene, 0)]
    kinds = [jnp.bfloat16] * len(steps) + [jnp.float32]
    cuts = [0, 1, 2, len(tables)] if len(steps) > 2 else [0, 1, len(tables)]
    parted = lane_parts(genes_dev, genes_dev // n_row, n_row)
    carried, blocks = shares, []
    for low, high in zip(cuts, cuts[1:]):
        last = high == len(tables)
        if low == 0 and parted:
            done, carried = first_block(tables[0], block, parted, n_row, fixed, shares)
            blocks += done
            continue
        done, carried = block_rows(tables[low:high], kinds[low:high], block, low == 0, last, n_row, fixed, carried)
        blocks += done
    parts = carried

    came = {}
    for (way, _), own in zip(steps, blocks):
        if way in came:
            own = plus(own, came[way]).astype(jnp.bfloat16)
        came[way] = lax.ppermute(own, LINES, [(at, at // n_gene * n_gene + to) for at, to in enumerate(around(groups, n_gene, way))])
    others = [swap_row(parts[hop], hop, n_row) for hop in range(1, n_row)]
    *adam_out, grad_cells = finish([blocks[-1], *came.values()], [parts[0], *others], *adam)
    return (grad_cells, *adam_out)


def solution(mesh):
    in_specs = (
        P(("grp", "row"), "gene"),
        P(("grp", "row"), None),
        P(("grp", "row")),
        P(("grp", "gene")),
        P(("grp", "gene", "row"), None),
        P(("grp", "gene", "row"), None),
        P(("grp", "gene", "row"), None),
    )
    out_specs = (
        P(("grp", "row", "gene"), None),
        P(("grp", "gene", "row"), None),
        P(("grp", "gene", "row"), None),
        P(("grp", "gene", "row"), None),
    )
    return jax.shard_map(local, mesh=mesh, in_specs=in_specs, out_specs=out_specs, check_vma=False)
```

```python
import functools
import itertools
import math

import jax
import jax.numpy as jnp
from jax import lax
from jax.experimental import pallas as pl
from jax.experimental.pallas import tpu as pltpu
from jax.sharding import PartitionSpec as P

tukey_c = 4.685
beta_one = 0.9
beta_two = 0.999
learn_rate = 0.02
adam_eps = 1e-08

RING_MOST = 8
VMEM = pltpu.VMEM
IN_VMEM = pl.BlockSpec(memory_space=VMEM)
IN_ANY = pl.BlockSpec(memory_space=pl.ANY)


def tile_of(rows, most):
    best = [t for t in range(128, most + 1, 128) if rows % t == 0]
    return best[-1] if best else rows


def params():
    return pltpu.CompilerParams(vmem_limit_bytes=24 * 1024 * 1024)


def cost(flops, moved):
    return pl.CostEstimate(flops=int(flops), bytes_accessed=int(moved), transcendentals=0)


def pinned(*arrays):
    return [pltpu.with_memory_space_constraint(a, VMEM) for a in arrays]


def prepare_kernel(scale_k, x_in, index_in, cell_in, scale_in, x_out, f_out, ft_out, bend_out, shrink_out, index, cell, scale, sems):
    loads = [
        pltpu.make_async_copy(src, dst, sems.at[at])
        for at, (src, dst) in enumerate(((scale_in, scale), (cell_in, cell), (index_in, index), (x_in, x_out)))
    ]
    for load in loads:
        load.start()
    cells, rank = cell.shape
    rows = index.shape[0]
    genes = scale.shape[0]
    loads[0].wait()
    inverse = 1.0 / scale[...].reshape(1, genes)
    bend_out[...] = (inverse * inverse) * (1.0 / (tukey_c * tukey_c))
    shrink_out[...] = jnp.transpose(jnp.broadcast_to(-scale_k * (inverse * inverse), (rank, genes)))
    loads[1].wait()
    table = jnp.transpose(cell[...].astype(jnp.float32)).astype(jnp.bfloat16)
    base = lax.axis_index("row") * cells
    loads[2].wait()
    step = tile_of(rows, 512)
    for at in range(0, rows, step):
        local = index[at : at + step].reshape(1, step) - base
        hot = lax.broadcasted_iota(jnp.int32, (cells, step), 0) == local
        hot = jnp.where(hot, 1.0, 0.0).astype(jnp.bfloat16)
        picked = jnp.dot(table, hot, preferred_element_type=jnp.float32)
        ft_out[:, at : at + step] = picked.astype(jnp.bfloat16)
        f_out[at : at + step, :] = jnp.transpose(picked).astype(jnp.bfloat16)
    loads[3].wait()


def prepare(x_slab, row_index, cell_factor, gene_scale, scale_k):
    rows, genes = x_slab.shape
    cells, rank = cell_factor.shape
    ins = (x_slab, row_index, cell_factor, gene_scale)
    return pl.pallas_call(
        functools.partial(prepare_kernel, scale_k),
        out_shape=(
            VMEM((rows, genes), jnp.bfloat16),
            VMEM((rows, rank), jnp.bfloat16),
            VMEM((rank, rows), jnp.bfloat16),
            VMEM((1, genes), jnp.float32),
            VMEM((genes, rank), jnp.float32),
        ),
        in_specs=[IN_ANY] * 4,
        out_specs=(IN_VMEM,) * 5,
        scratch_shapes=[
            VMEM((rows,), jnp.int32),
            VMEM((cells, rank), jnp.bfloat16),
            VMEM((genes,), jnp.float32),
            pltpu.SemaphoreType.DMA((4,)),
        ],
        compiler_params=params(),
        cost_estimate=cost(8 * rows * cells * rank, 8 * rows * genes * 2),
        name="prepare",
    )(*(pltpu.with_memory_space_constraint(a, pltpu.HBM) for a in ins))


def pick(axis, table):
    me = lax.axis_index(axis)
    value = jnp.int32(table[0])
    for place, entry in enumerate(table[1:], 1):
        value = jnp.where(me == place, jnp.int32(entry), value)
    return value


def partner(me, hop, size):
    return me ^ hop if size & (size - 1) == 0 else (me + hop) % size


def source(me, hop, size):
    return me ^ hop if size & (size - 1) == 0 else (me + size - hop) % size


def rows_kernel(tables, block, first, last, n_row, *refs):
    refs = list(refs)
    take = lambda count: [refs.pop(0) for _ in range(count)]
    x_ref, f_ref, ft_ref, bend_ref, shrink_ref = take(5)
    shares = take(n_row) if first else None
    carried_in = None if first else take(3)
    rows_out = take(len(tables))
    carried_out = None if last else take(3 if first else 1)
    parts_out = take(n_row) if last else None
    me = lax.axis_index("row")

    if first:
        (piece,) = take(1)
        depth = shares[0].shape[0]
        for hop in range(n_row):
            start = pl.multiple_of(source(me, hop, n_row) * depth, depth)
            piece[pl.ds(start, depth), :] = shares[hop][...]
        whole = piece[...].astype(jnp.float32)
        wide = jnp.transpose(whole).astype(jnp.bfloat16)
        scaled = (whole * shrink_ref[...]).astype(jnp.bfloat16)
        total = None
    else:
        total, wide, scaled = (ref[...] for ref in carried_in)

    bend = bend_ref[...]
    step = tile_of(block, 256)
    tiles = []
    for table, out in zip(tables, rows_out):
        origin = pick("gene", table) * block if len(table) > 1 else 0
        for at in range(0, block, step):
            start = origin + at
            if len(table) > 1:
                start = pl.multiple_of(start, math.gcd(block, step))
            tiles.append((out, at, pl.ds(start, step)))

    def predict(here):
        return jnp.dot(f_ref[here, :], wide, preferred_element_type=jnp.float32)

    def gradients(tile, infl, total):
        out, at, here = tile
        cols = jnp.dot(ft_ref[:, here], infl, preferred_element_type=jnp.float32)
        out[at : at + step, :] = jnp.dot(infl, scaled, preferred_element_type=jnp.float32).astype(out.dtype)
        return cols if total is None else total + cols

    pred = predict(tiles[0][2])
    infl = None
    for at, tile in enumerate(tiles):
        later = predict(tiles[at + 1][2]) if at + 1 < len(tiles) else None
        now = influence(x_ref[tile[2], :], pred, bend)
        if at:
            total = gradients(tiles[at - 1], infl, total)
        infl, pred = now, later
    total = gradients(tiles[-1], infl, total)

    if first and not last:
        carried_out[1][...] = wide
        carried_out[2][...] = scaled
    if not last:
        carried_out[0][...] = total
        return
    (turned,) = take(1)
    turned[...] = jnp.transpose(total) * shrink_ref[...]
    depth = parts_out[0].shape[0]
    for hop in range(n_row):
        start = pl.multiple_of(partner(me, hop, n_row) * depth, depth)
        parts_out[hop][...] = turned[pl.ds(start, depth), :].astype(parts_out[hop].dtype)


def block_rows(tables, kinds, block, first, last, n_row, fixed, carried):
    genes, rank = fixed[4].shape
    out = [jax.ShapeDtypeStruct((block, rank), kind) for kind in kinds]
    if last:
        out += [jax.ShapeDtypeStruct((genes // n_row, rank), jnp.bfloat16 if hop else jnp.float32) for hop in range(n_row)]
    else:
        out += [VMEM((rank, genes), jnp.float32)]
    if first and not last:
        out += [VMEM((rank, genes), jnp.bfloat16), VMEM((genes, rank), jnp.bfloat16)]
    scratch = [VMEM((genes, rank), jnp.bfloat16)] if first else []
    if last:
        scratch.append(VMEM((genes, rank), jnp.float32))
    ins = pinned(*fixed) + (list(carried) if first else pinned(*carried))
    work = len(tables) * block * genes
    out = pl.pallas_call(
        functools.partial(rows_kernel, tables, block, first, last, n_row),
        out_shape=tuple(out),
        in_specs=[IN_VMEM] * len(ins),
        out_specs=(IN_VMEM,) * len(out),
        scratch_shapes=scratch,
        compiler_params=params(),
        cost_estimate=cost(6 * work * rank, work * 2),
        name="block_rows",
    )(*ins)
    done, rest = list(out[: len(tables)]), list(out[len(tables) :])
    return done, rest if first or last else rest + list(carried[1:])


def lane_parts(genes, depth, n_row):
    if n_row != 4:
        return None
    pairs = [(2 * depth * (place // 2), 2 * depth * (place // 2 + 1)) for place in range(n_row)]
    low = [-(-begin // 128) * 128 for begin, _ in pairs]
    width = min(end // 128 * 128 - begin for begin, (_, end) in zip(low, pairs))
    if width <= 0 or any(begin not in (0, genes - width) for begin in low):
        return None
    return low, width, [width if begin == 0 else 0 for begin in low]


def lanes(table, width):
    return pl.ds(pl.multiple_of(pick("row", table), 128), width)


def influence(x, pred, bend):
    resid = x.astype(jnp.float32) - pred
    inside = jnp.maximum(1.0 - resid * resid * bend, 0.0)
    return (resid * (inside * inside)).astype(jnp.bfloat16)


def part_of_block(table, block, here, x_ref, f_ref, ft_ref, bend_ref, wide, scaled):
    step = tile_of(block, 256)
    origin = pick("gene", table) * block
    tiles = [pl.ds(pl.multiple_of(origin + at, math.gcd(block, step)), step) for at in range(0, block, step)]
    bend = bend_ref[:, here]
    preds = [jnp.dot(f_ref[tile, :], wide, preferred_element_type=jnp.float32) for tile in tiles]
    infls = [influence(x_ref[tile, here], pred, bend) for tile, pred in zip(tiles, preds)]
    rows, total = [], None
    for tile, infl in zip(tiles, infls):
        cols = jnp.dot(ft_ref[:, tile], infl, preferred_element_type=jnp.float32)
        rows.append(jnp.dot(infl, scaled, preferred_element_type=jnp.float32))
        total = cols if total is None else total + cols
    return rows, total


def early_kernel(table, block, parts, x_ref, f_ref, ft_ref, bend_ref, shrink_ref, own, other, *refs):
    rows_out, total_out, wide_out, scaled_out, pair = refs
    low, width, _ = parts
    depth = own.shape[0]
    odd = lax.axis_index("row") % 2
    pair[pl.ds(pl.multiple_of(odd * depth, depth), depth), :] = own[...]
    pair[pl.ds(pl.multiple_of((1 - odd) * depth, depth), depth), :] = other[...]
    inset = [begin - 2 * depth * (place // 2) for place, begin in enumerate(low)]
    whole = pair[pl.ds(pl.multiple_of(pick("row", inset), math.gcd(*inset, 128)), width), :].astype(jnp.float32)
    here = lanes(low, width)
    wide = jnp.transpose(whole).astype(jnp.bfloat16)
    scaled = (whole * shrink_ref[here, :]).astype(jnp.bfloat16)
    wide_out[...] = wide
    scaled_out[...] = scaled
    rows, total = part_of_block(table, block, here, x_ref, f_ref, ft_ref, bend_ref, wide, scaled)
    for at, value in enumerate(rows):
        rows_out[at * value.shape[0] : (at + 1) * value.shape[0], :] = value
    total_out[...] = total


def rest_kernel(table, block, parts, n_row, x_ref, f_ref, ft_ref, bend_ref, shrink_ref, *refs):
    shares, (rows_in, total_in, wide_in, scaled_in) = refs[:n_row], refs[n_row : n_row + 4]
    rows_out, total_out, wide_out, scaled_out, piece = refs[n_row + 4 :]
    low, width, rest = parts
    me = lax.axis_index("row")
    depth = shares[0].shape[0]
    for hop in range(n_row):
        start = pl.multiple_of(source(me, hop, n_row) * depth, depth)
        piece[pl.ds(start, depth), :] = shares[hop][...]
    here = lanes(rest, n_row * depth - width)
    whole = piece[here, :].astype(jnp.float32)
    wide = jnp.transpose(whole).astype(jnp.bfloat16)
    scaled = (whole * shrink_ref[here, :]).astype(jnp.bfloat16)
    rows, total = part_of_block(table, block, here, x_ref, f_ref, ft_ref, bend_ref, wide, scaled)
    for at, value in enumerate(rows):
        span = slice(at * value.shape[0], (at + 1) * value.shape[0])
        rows_out[span, :] = (rows_in[span, :] + value).astype(rows_out.dtype)
    done = lanes(low, width)
    total_out[:, here] = total
    total_out[:, done] = total_in[...]
    wide_out[:, here] = wide
    wide_out[:, done] = wide_in[...]
    scaled_out[here, :] = scaled
    scaled_out[done, :] = scaled_in[...]


def first_block(table, block, parts, n_row, fixed, shares):
    genes, rank = fixed[4].shape
    depth = genes // n_row
    width = parts[1]
    ins = pinned(*fixed)
    early = pl.pallas_call(
        functools.partial(early_kernel, table, block, parts),
        out_shape=(
            VMEM((block, rank), jnp.float32),
            VMEM((rank, width), jnp.float32),
            VMEM((rank, width), jnp.bfloat16),
            VMEM((width, rank), jnp.bfloat16),
        ),
        in_specs=[IN_VMEM] * 7,
        out_specs=(IN_VMEM,) * 4,
        scratch_shapes=[VMEM((2 * depth, rank), jnp.bfloat16)],
        compiler_params=params(),
        cost_estimate=cost(12 * block * width * rank, block * width * 4),
        name="early_part",
    )(*ins, *shares[:2])
    done, *carried = pl.pallas_call(
        functools.partial(rest_kernel, table, block, parts, n_row),
        out_shape=(
            jax.ShapeDtypeStruct((block, rank), jnp.bfloat16),
            VMEM((rank, genes), jnp.float32),
            VMEM((rank, genes), jnp.bfloat16),
            VMEM((genes, rank), jnp.bfloat16),
        ),
        in_specs=[IN_VMEM] * (9 + n_row),
        out_specs=(IN_VMEM,) * 4,
        scratch_shapes=[VMEM((genes, rank), jnp.bfloat16)],
        compiler_params=params(),
        cost_estimate=cost(12 * block * (genes - width) * rank, block * (genes - width) * 4),
        name="rest_part",
    )(*ins, *shares, *pinned(*early))
    return [done], carried


def swap_row(value, hop, size):
    return lax.ppermute(value, "row", [(me, partner(me, hop, size)) for me in range(size)])


def ring_of(size):
    return [0, *range(1, size, 2), *reversed(range(2, size, 2))]


def steps_of(size):
    ahead = [(1, distance) for distance in range(size // 2, 0, -1)]
    back = [(-1, distance) for distance in range((size - 1) // 2, 0, -1)]
    return [step for pair in itertools.zip_longest(ahead, back) for step in pair if step]


def around(size, hops):
    ring = ring_of(size)
    return tuple(ring[(ring.index(place) + hops) % size] for place in range(size))


def plus(wide, narrow):
    return wide.astype(jnp.float32) + narrow.astype(jnp.float32)


def finish_kernel(n_ends, n_parts, *refs):
    n_ins = n_ends + n_parts + 3
    ins, outs = refs[:n_ins], refs[n_ins : n_ins + 3 + bool(n_ends)]
    *held, sems = refs[n_ins + len(outs) :]
    ends, parts = ins[:n_ends], ins[n_ends : n_ends + n_parts]
    factor, first, second = ins[n_ends + n_parts :]
    copies = []

    def send(at, span, value):
        held[at][span, :] = value
        copies.append(pltpu.make_async_copy(held[at].at[span, :], outs[at].at[span, :], sems.at[len(copies)]))
        copies[-1].start()

    if ends:
        step = tile_of(ends[0].shape[0], 256)
        for low in range(0, ends[0].shape[0], step):
            span = pl.ds(low, step)
            rows = ends[0][span, :]
            for end in ends[1:]:
                rows = plus(rows, end[span, :])
            send(3, span, rows)
    grad = parts[0][...]
    for part in parts[1:]:
        grad = plus(grad, part[...])
    span = pl.ds(0, grad.shape[0])
    new_first = beta_one * first[...] + (1.0 - beta_one) * grad
    new_second = beta_two * second[...] + (1.0 - beta_two) * grad * grad
    send(1, span, new_first)
    send(2, span, new_second)
    first_hat = new_first / (1.0 - beta_one**10)
    second_hat = new_second / (1.0 - beta_two**10)
    send(0, span, factor[...] - learn_rate * first_hat / (jnp.sqrt(second_hat) + adam_eps))
    for copy in copies:
        copy.wait()


def finish(ends, parts, factor, first, second):
    ins = [*ends, *parts, factor, first, second]
    shapes = [factor, factor, factor] + list(ends[:1])
    n_copies = 3 + (ends[0].shape[0] // tile_of(ends[0].shape[0], 256) if ends else 0)
    return pl.pallas_call(
        functools.partial(finish_kernel, len(ends), len(parts)),
        out_shape=tuple(jax.ShapeDtypeStruct(like.shape, jnp.float32) for like in shapes),
        in_specs=[IN_VMEM] * len(ins),
        out_specs=(IN_ANY,) * len(shapes),
        scratch_shapes=[VMEM(like.shape, jnp.float32) for like in shapes] + [pltpu.SemaphoreType.DMA((n_copies,))],
        compiler_params=params(),
        cost_estimate=cost(20 * factor.size, sum(4 * a.size for a in ins)),
        name="finish",
    )(*ins)


def local(x_slab, cell_factor, row_index, gene_scale, gene_factor, first_moment, second_moment):
    rows_dev, genes_dev = x_slab.shape
    n_gene = lax.axis_size("gene")
    n_row = lax.axis_size("row")
    block = rows_dev // n_gene
    scale_k = 4.0 / math.sqrt(genes_dev * n_gene)
    factor_bf = gene_factor.astype(jnp.bfloat16)
    shares = [factor_bf] + [swap_row(factor_bf, hop, n_row) for hop in range(1, n_row)]
    fixed = prepare(x_slab, row_index, cell_factor, gene_scale, scale_k)
    adam = (gene_factor, first_moment, second_moment)

    if n_gene == 1 or n_gene > RING_MOST or block % 128:
        (rows,), parts = block_rows([(0,)], [jnp.float32], rows_dev, True, True, n_row, fixed, shares)
        grad_cells = lax.psum_scatter(rows, "gene", scatter_dimension=0, tiled=True)
        others = [swap_row(parts[hop], hop, n_row) for hop in range(1, n_row)]
        return (grad_cells, *finish([], [parts[0], *others], *adam))

    steps = steps_of(n_gene)
    tables = [around(n_gene, way * distance) for way, distance in steps] + [tuple(range(n_gene))]
    kinds = [jnp.bfloat16] * len(steps) + [jnp.float32]
    cuts = [0, 1, len(tables)]
    parted = lane_parts(genes_dev, genes_dev // n_row, n_row)
    carried, blocks = shares, []
    for low, high in zip(cuts, cuts[1:]):
        last = high == len(tables)
        if low == 0 and parted:
            done, carried = first_block(tables[0], block, parted, n_row, fixed, shares)
            blocks += done
            continue
        done, carried = block_rows(tables[low:high], kinds[low:high], block, low == 0, last, n_row, fixed, carried)
        blocks += done
    parts = carried

    came = {}
    for (way, _), own in zip(steps, blocks):
        if way in came:
            own = plus(own, came[way]).astype(jnp.bfloat16)
        came[way] = lax.ppermute(own, "gene", list(enumerate(around(n_gene, way))))
    others = [swap_row(parts[hop], hop, n_row) for hop in range(1, n_row)]
    *adam_out, grad_cells = finish([blocks[-1], *came.values()], [parts[0], *others], *adam)
    return (grad_cells, *adam_out)


def solution(mesh):
    in_specs = (
        P(("grp", "row"), "gene"),
        P(("grp", "row"), None),
        P(("grp", "row")),
        P(("grp", "gene")),
        P(("grp", "gene", "row"), None),
        P(("grp", "gene", "row"), None),
        P(("grp", "gene", "row"), None),
    )
    out_specs = (
        P(("grp", "row", "gene"), None),
        P(("grp", "gene", "row"), None),
        P(("grp", "gene", "row"), None),
        P(("grp", "gene", "row"), None),
    )
    return jax.shard_map(local, mesh=mesh, in_specs=in_specs, out_specs=out_specs, check_vma=False)
```

```python
import functools
import itertools
import math

import jax
import jax.numpy as jnp
from jax import lax
from jax.experimental import pallas as pl
from jax.experimental.pallas import tpu as pltpu
from jax.sharding import PartitionSpec as P

tukey_c = 4.685
beta_one = 0.9
beta_two = 0.999
learn_rate = 0.02
adam_eps = 1e-08

RING_MOST = 8
VMEM = pltpu.VMEM
IN_VMEM = pl.BlockSpec(memory_space=VMEM)
IN_ANY = pl.BlockSpec(memory_space=pl.ANY)


def tile_of(rows, most):
    best = [t for t in range(128, most + 1, 128) if rows % t == 0]
    return best[-1] if best else rows


def params():
    return pltpu.CompilerParams(vmem_limit_bytes=24 * 1024 * 1024)


def cost(flops, moved):
    return pl.CostEstimate(flops=int(flops), bytes_accessed=int(moved), transcendentals=0)


def pinned(*arrays):
    return [pltpu.with_memory_space_constraint(a, VMEM) for a in arrays]


def pick(axis, table):
    me = lax.axis_index(axis)
    value = jnp.int32(table[0])
    for place, entry in enumerate(table[1:], 1):
        value = jnp.where(me == place, jnp.int32(entry), value)
    return value


def partner(me, hop, size):
    return me ^ hop if size & (size - 1) == 0 else (me + hop) % size


def source(me, hop, size):
    return me ^ hop if size & (size - 1) == 0 else (me + size - hop) % size


def first_row(table, block):
    return pl.multiple_of(pick("gene", table) * block, block) if len(table) > 1 else 0


def gather(cells, local):
    hot = lax.broadcasted_iota(jnp.int32, (cells.shape[1], local.shape[1]), 0) == local
    hot = jnp.where(hot, 1.0, 0.0).astype(jnp.bfloat16)
    return jnp.dot(cells, hot, preferred_element_type=jnp.float32)


def predict(factors, wide):
    return jnp.dot(factors, wide, preferred_element_type=jnp.float32)


def influence(x, pred, bend):
    resid = x.astype(jnp.float32) - pred
    inside = jnp.maximum(1.0 - resid * resid * bend, 0.0)
    return (resid * (inside * inside)).astype(jnp.bfloat16)


def add_to(total, cols):
    return cols if total is None else total + cols


def prepare_kernel(scale_k, table, block, x_in, index_in, cell_in, scale_in, *refs):
    x_out, f_out, ft_out, bend_out, shrink_out, index_out, cells_out, index, cell, scale, sems = refs
    here = pl.ds(first_row(table, block), block)
    pairs = ((scale_in, scale), (cell_in, cell), (index_in, index), (x_in.at[here, :], x_out))
    loads = [pltpu.make_async_copy(src, dst, sems.at[at]) for at, (src, dst) in enumerate(pairs)]
    for load in loads:
        load.start()
    cells, rank = cell.shape
    rows = index.shape[0]
    genes = scale.shape[0]
    loads[0].wait()
    inverse = 1.0 / scale[...].reshape(1, genes)
    bend_out[...] = (inverse * inverse) * (1.0 / (tukey_c * tukey_c))
    shrink_out[...] = jnp.transpose(jnp.broadcast_to(-scale_k * (inverse * inverse), (rank, genes)))
    loads[1].wait()
    turned = jnp.transpose(cell[...].astype(jnp.float32)).astype(jnp.bfloat16)
    cells_out[...] = turned
    loads[2].wait()
    step = tile_of(rows, 512)
    for at in range(0, rows, step):
        index_out[:, at : at + step] = index[at : at + step].reshape(1, step) - lax.axis_index("row") * cells
    step = tile_of(block, 256)
    for at in range(0, block, step):
        start = first_row(table, block) + at
        if len(table) > 1:
            start = pl.multiple_of(start, math.gcd(block, step))
        picked = gather(turned, index_out[:, pl.ds(start, step)])
        ft_out[:, at : at + step] = picked.astype(jnp.bfloat16)
        f_out[at : at + step, :] = jnp.transpose(picked).astype(jnp.bfloat16)
    loads[3].wait()


def prepare(table, block, x_slab, row_index, cell_factor, gene_scale, scale_k):
    rows, genes = x_slab.shape
    cells, rank = cell_factor.shape
    ins = (x_slab, row_index, cell_factor, gene_scale)
    return pl.pallas_call(
        functools.partial(prepare_kernel, scale_k, table, block),
        out_shape=(
            VMEM((block, genes), jnp.bfloat16),
            VMEM((block, rank), jnp.bfloat16),
            VMEM((rank, block), jnp.bfloat16),
            VMEM((1, genes), jnp.float32),
            VMEM((genes, rank), jnp.float32),
            VMEM((1, rows), jnp.int32),
            VMEM((rank, cells), jnp.bfloat16),
        ),
        in_specs=[IN_ANY] * 4,
        out_specs=(IN_VMEM,) * 7,
        scratch_shapes=[
            VMEM((rows,), jnp.int32),
            VMEM((cells, rank), jnp.bfloat16),
            VMEM((genes,), jnp.float32),
            pltpu.SemaphoreType.DMA((4,)),
        ],
        compiler_params=params(),
        cost_estimate=cost(8 * block * cells * rank, 16 * block * genes),
        name="prepare",
    )(*(pltpu.with_memory_space_constraint(a, pltpu.HBM) for a in ins))


def lane_parts(genes, depth, n_row):
    if n_row != 4:
        return None
    pairs = [(2 * depth * (place // 2), 2 * depth * (place // 2 + 1)) for place in range(n_row)]
    low = [-(-begin // 128) * 128 for begin, _ in pairs]
    width = min(end // 128 * 128 - begin for begin, (_, end) in zip(low, pairs))
    if width <= 0 or any(begin not in (0, genes - width) for begin in low):
        return None
    return low, width, [width if begin == 0 else 0 for begin in low]


def lanes(table, width):
    return pl.ds(pl.multiple_of(pick("row", table), 128), width)


def over_lanes(here, x_ref, f_ref, ft_ref, bend_ref, wide, scaled):
    block = x_ref.shape[0]
    step = tile_of(block, 256)
    tiles = [pl.ds(at, step) for at in range(0, block, step)]
    bend = bend_ref[:, here]
    preds = [predict(f_ref[tile, :], wide) for tile in tiles]
    infls = [influence(x_ref[tile, here], pred, bend) for tile, pred in zip(tiles, preds)]
    rows, total = [], None
    for tile, infl in zip(tiles, infls):
        rows.append((tile, jnp.dot(infl, scaled, preferred_element_type=jnp.float32)))
        total = add_to(total, jnp.dot(ft_ref[:, tile], infl, preferred_element_type=jnp.float32))
    return rows, total


def early_kernel(parts, x_ref, f_ref, ft_ref, bend_ref, shrink_ref, own, other, *refs):
    rows_out, total_out, wide_out, scaled_out, pair = refs
    low, width, _ = parts
    depth = own.shape[0]
    odd = lax.axis_index("row") % 2
    pair[pl.ds(pl.multiple_of(odd * depth, depth), depth), :] = own[...]
    pair[pl.ds(pl.multiple_of((1 - odd) * depth, depth), depth), :] = other[...]
    inset = [begin - 2 * depth * (place // 2) for place, begin in enumerate(low)]
    whole = pair[pl.ds(pl.multiple_of(pick("row", inset), math.gcd(*inset, 128)), width), :].astype(jnp.float32)
    here = lanes(low, width)
    wide = jnp.transpose(whole).astype(jnp.bfloat16)
    scaled = (whole * shrink_ref[here, :]).astype(jnp.bfloat16)
    wide_out[...] = wide
    scaled_out[...] = scaled
    rows, total = over_lanes(here, x_ref, f_ref, ft_ref, bend_ref, wide, scaled)
    for tile, value in rows:
        rows_out[tile, :] = value
    total_out[...] = total


def rest_kernel(parts, n_row, x_ref, f_ref, ft_ref, bend_ref, shrink_ref, *refs):
    shares, refs = refs[:n_row], refs[n_row:]
    if parts:
        (rows_in, total_in, wide_in, scaled_in), refs = refs[:4], refs[4:]
    rows_out, total_out, wide_out, scaled_out, piece = refs
    me = lax.axis_index("row")
    depth = shares[0].shape[0]
    for hop in range(n_row):
        start = pl.multiple_of(source(me, hop, n_row) * depth, depth)
        piece[pl.ds(start, depth), :] = shares[hop][...]
    here = lanes(parts[2], n_row * depth - parts[1]) if parts else pl.ds(0, n_row * depth)
    whole = piece[here, :].astype(jnp.float32)
    wide = jnp.transpose(whole).astype(jnp.bfloat16)
    scaled = (whole * shrink_ref[here, :]).astype(jnp.bfloat16)
    rows, total = over_lanes(here, x_ref, f_ref, ft_ref, bend_ref, wide, scaled)
    for tile, value in rows:
        rows_out[tile, :] = (rows_in[tile, :] + value if parts else value).astype(rows_out.dtype)
    total_out[:, here] = total
    wide_out[:, here] = wide
    scaled_out[here, :] = scaled
    if parts:
        done = lanes(parts[0], parts[1])
        total_out[:, done] = total_in[...]
        wide_out[:, done] = wide_in[...]
        scaled_out[done, :] = scaled_in[...]


def first_block(kind, parts, n_row, fixed, shares):
    block, genes = fixed[0].shape
    rank = fixed[1].shape[1]
    width = parts[1] if parts else 0
    ins = pinned(*fixed)
    early = []
    if parts:
        early = pl.pallas_call(
            functools.partial(early_kernel, parts),
            out_shape=(
                VMEM((block, rank), jnp.float32),
                VMEM((rank, width), jnp.float32),
                VMEM((rank, width), jnp.bfloat16),
                VMEM((width, rank), jnp.bfloat16),
            ),
            in_specs=[IN_VMEM] * 7,
            out_specs=(IN_VMEM,) * 4,
            scratch_shapes=[VMEM((2 * (genes // n_row), rank), jnp.bfloat16)],
            compiler_params=params(),
            cost_estimate=cost(12 * block * width * rank, block * width * 4),
            name="early_part",
        )(*ins, *shares[:2])
    done, *carried = pl.pallas_call(
        functools.partial(rest_kernel, parts, n_row),
        out_shape=(
            jax.ShapeDtypeStruct((block, rank), kind),
            VMEM((rank, genes), jnp.float32),
            VMEM((rank, genes), jnp.bfloat16),
            VMEM((genes, rank), jnp.bfloat16),
        ),
        in_specs=[IN_VMEM] * (5 + n_row + len(early)),
        out_specs=(IN_VMEM,) * 4,
        scratch_shapes=[VMEM((genes, rank), jnp.bfloat16)],
        compiler_params=params(),
        cost_estimate=cost(12 * block * (genes - width) * rank, block * (genes - width) * 4),
        name="rest_part",
    )(*ins, *shares, *pinned(*early))
    return done, carried


def more_kernel(tables, block, last, n_row, x_in, index_ref, cells_ref, bend_ref, shrink_ref, *refs):
    (total_in, wide_in, scaled_in), refs = refs[:3], refs[3:]
    rows_out, refs = refs[: len(tables)], refs[len(tables) :]
    grads_out, refs = (refs[:n_row], refs[n_row:]) if last else (refs[:1], refs[1:])
    loads = []
    if tables:
        *refs, held, sems = refs
        for at, table in enumerate(tables):
            span = x_in.at[pl.ds(first_row(table, block), block), :]
            loads.append(pltpu.make_async_copy(span, held.at[at], sems.at[at]))
            loads[-1].start()
    wide, scaled, cells, bend = wide_in[...], scaled_in[...], cells_ref[...], bend_ref[...]
    total = total_in[...]
    step = tile_of(block, 256)
    tiles = [(at, low) for at in range(len(tables)) for low in range(0, block, step)]

    def factors(tile):
        at, low = tile
        start = first_row(tables[at], block) + low
        if len(tables[at]) > 1:
            start = pl.multiple_of(start, math.gcd(block, step))
        picked = gather(cells, index_ref[:, pl.ds(start, step)])
        return picked.astype(jnp.bfloat16), jnp.transpose(picked).astype(jnp.bfloat16)

    ahead, behind = None, None
    for number, (at, low) in enumerate(tiles):
        if ahead is None:
            turned, flat = factors(tiles[0])
            ahead = turned, predict(flat, wide)
        (turned, pred), ahead = ahead, None
        if number + 1 < len(tiles):
            later, flat = factors(tiles[number + 1])
            ahead = later, predict(flat, wide)
        if low == 0:
            loads[at].wait()
        now = influence(held[at, low : low + step, :], pred, bend)
        for tile in [behind] if behind else []:
            total = more_gradients(rows_out, tile, scaled, total)
        behind = at, low, turned, now
    if behind:
        total = more_gradients(rows_out, behind, scaled, total)
    if not last:
        grads_out[0][...] = total
        return
    (flipped,) = refs
    flipped[...] = jnp.transpose(total) * shrink_ref[...]
    me = lax.axis_index("row")
    depth = grads_out[0].shape[0]
    for hop in range(n_row):
        start = pl.multiple_of(partner(me, hop, n_row) * depth, depth)
        grads_out[hop][...] = flipped[pl.ds(start, depth), :].astype(grads_out[hop].dtype)


def more_gradients(rows_out, tile, scaled, total):
    at, low, turned, infl = tile
    rows = jnp.dot(infl, scaled, preferred_element_type=jnp.float32)
    rows_out[at][low : low + rows.shape[0], :] = rows.astype(rows_out[at].dtype)
    return total + jnp.dot(turned, infl, preferred_element_type=jnp.float32)


def more_blocks(tables, kinds, block, last, n_row, x_slab, shared, carried):
    genes, rank = shared[3].shape
    out = [jax.ShapeDtypeStruct((block, rank), kind) for kind in kinds]
    if last:
        out += [jax.ShapeDtypeStruct((genes // n_row, rank), jnp.bfloat16 if hop else jnp.float32) for hop in range(n_row)]
    else:
        out += [VMEM((rank, genes), jnp.float32)]
    scratch = [VMEM((genes, rank), jnp.float32)] if last else []
    if tables:
        scratch += [VMEM((len(tables), block, genes), jnp.bfloat16), pltpu.SemaphoreType.DMA((len(tables),))]
    ins = [pltpu.with_memory_space_constraint(x_slab, pltpu.HBM), *pinned(*shared, *carried)]
    work = len(tables) * block * genes
    out = pl.pallas_call(
        functools.partial(more_kernel, tables, block, last, n_row),
        out_shape=tuple(out),
        in_specs=[IN_ANY] + [IN_VMEM] * (len(ins) - 1),
        out_specs=(IN_VMEM,) * len(out),
        scratch_shapes=scratch,
        compiler_params=params(),
        cost_estimate=cost(12 * work * rank, work * 4),
        name="more_blocks",
    )(*ins)
    done, rest = list(out[: len(tables)]), list(out[len(tables) :])
    return done, rest if last else rest + list(carried[1:])


def swap_row(value, hop, size):
    return lax.ppermute(value, "row", [(me, partner(me, hop, size)) for me in range(size)])


def gather_row(own, size, before):
    shares = [own]
    for hop in range(1, size):
        fast = hop & -hop
        if size & (size - 1) or hop == fast:
            shares.append(swap_row(own, hop, size))
        else:
            held, _ = lax.optimization_barrier((shares[hop ^ fast], before))
            shares.append(swap_row(held, fast, size))
    return shares


def ring_of(size):
    return [*range(0, size, 2), *reversed(range(1, size, 2))]


def steps_of(size):
    ahead = [(1, distance) for distance in range(size // 2, 0, -1)]
    back = [(-1, distance) for distance in range((size - 1) // 2, 0, -1)]
    return [step for pair in itertools.zip_longest(ahead, back) for step in pair if step]


def around(size, hops):
    ring = ring_of(size)
    return tuple(ring[(ring.index(place) + hops) % size] for place in range(size))


def plus(wide, narrow):
    return wide.astype(jnp.float32) + narrow.astype(jnp.float32)


def finish_kernel(n_ends, n_parts, *refs):
    n_ins = n_ends + n_parts + 3
    ins, outs = refs[:n_ins], refs[n_ins : n_ins + 3 + bool(n_ends)]
    *held, sems = refs[n_ins + len(outs) :]
    ends, parts = ins[:n_ends], ins[n_ends : n_ends + n_parts]
    factor, first, second = ins[n_ends + n_parts :]
    copies = []

    def send(at, span, value):
        held[at][span, :] = value
        copies.append(pltpu.make_async_copy(held[at].at[span, :], outs[at].at[span, :], sems.at[len(copies)]))
        copies[-1].start()

    if ends:
        step = tile_of(ends[0].shape[0], 256)
        for low in range(0, ends[0].shape[0], step):
            span = pl.ds(low, step)
            rows = ends[0][span, :]
            for end in ends[1:]:
                rows = plus(rows, end[span, :])
            send(3, span, rows)
    grad = parts[0][...]
    for part in parts[1:]:
        grad = plus(grad, part[...])
    span = pl.ds(0, grad.shape[0])
    new_first = beta_one * first[...] + (1.0 - beta_one) * grad
    new_second = beta_two * second[...] + (1.0 - beta_two) * grad * grad
    send(1, span, new_first)
    send(2, span, new_second)
    first_hat = new_first / (1.0 - beta_one**10)
    second_hat = new_second / (1.0 - beta_two**10)
    send(0, span, factor[...] - learn_rate * first_hat / (jnp.sqrt(second_hat) + adam_eps))
    for copy in copies:
        copy.wait()


def finish(ends, parts, factor, first, second):
    ins = [*ends, *parts, factor, first, second]
    shapes = [factor, factor, factor] + list(ends[:1])
    n_copies = 3 + (ends[0].shape[0] // tile_of(ends[0].shape[0], 256) if ends else 0)
    return pl.pallas_call(
        functools.partial(finish_kernel, len(ends), len(parts)),
        out_shape=tuple(jax.ShapeDtypeStruct(like.shape, jnp.float32) for like in shapes),
        in_specs=[IN_VMEM] * len(ins),
        out_specs=(IN_ANY,) * len(shapes),
        scratch_shapes=[VMEM(like.shape, jnp.float32) for like in shapes] + [pltpu.SemaphoreType.DMA((n_copies,))],
        compiler_params=params(),
        cost_estimate=cost(20 * factor.size, sum(4 * a.size for a in ins)),
        name="finish",
    )(*ins)


def local(x_slab, cell_factor, row_index, gene_scale, gene_factor, first_moment, second_moment):
    rows_dev, genes_dev = x_slab.shape
    n_gene = lax.axis_size("gene")
    n_row = lax.axis_size("row")
    block = rows_dev // n_gene
    scale_k = 4.0 / math.sqrt(genes_dev * n_gene)
    factor_bf = gene_factor.astype(jnp.bfloat16)
    adam = (gene_factor, first_moment, second_moment)
    ringed = 1 < n_gene <= RING_MOST and block % 128 == 0
    steps = steps_of(n_gene) if ringed else []
    tables = [around(n_gene, way * far) for way, far in steps] + [tuple(range(n_gene))] if ringed else [(0,)]
    if not ringed:
        block = rows_dev
    *fixed, index, cells = prepare(tables[0], block, x_slab, row_index, cell_factor, gene_scale, scale_k)
    shared = (index, cells, fixed[3], fixed[4])
    shares = gather_row(factor_bf, n_row, fixed[3])
    parted = lane_parts(genes_dev, genes_dev // n_row, n_row) if ringed else None
    done, carried = first_block(jnp.bfloat16 if ringed else jnp.float32, parted, n_row, fixed, shares)

    if not ringed:
        _, parts = more_blocks([], [], block, True, n_row, x_slab, shared, carried)
        grad_cells = lax.psum_scatter(done, "gene", scatter_dimension=0, tiled=True)
        others = [swap_row(parts[hop], hop, n_row) for hop in range(1, n_row)]
        return (grad_cells, *finish([], [parts[0], *others], *adam))

    blocks = [done]
    cuts = [1, 2, len(tables)] if len(steps) > 2 else [1, len(tables)]
    for low, high in zip(cuts, cuts[1:]):
        last = high == len(tables)
        kinds = [jnp.bfloat16 if at < len(steps) else jnp.float32 for at in range(low, high)]
        done, carried = more_blocks(tables[low:high], kinds, block, last, n_row, x_slab, shared, carried)
        blocks += done
    parts = carried

    came = {}
    for (way, _), own in zip(steps, blocks):
        if way in came:
            own = plus(own, came[way]).astype(jnp.bfloat16)
        came[way] = lax.ppermute(own, "gene", list(enumerate(around(n_gene, way))))
    others = [swap_row(parts[hop], hop, n_row) for hop in range(1, n_row)]
    *adam_out, grad_cells = finish([blocks[-1], *came.values()], [parts[0], *others], *adam)
    return (grad_cells, *adam_out)


def solution(mesh):
    in_specs = (
        P(("grp", "row"), "gene"),
        P(("grp", "row"), None),
        P(("grp", "row")),
        P(("grp", "gene")),
        P(("grp", "gene", "row"), None),
        P(("grp", "gene", "row"), None),
        P(("grp", "gene", "row"), None),
    )
    out_specs = (
        P(("grp", "row", "gene"), None),
        P(("grp", "gene", "row"), None),
        P(("grp", "gene", "row"), None),
        P(("grp", "gene", "row"), None),
    )
    return jax.shard_map(local, mesh=mesh, in_specs=in_specs, out_specs=out_specs, check_vma=False)
```

```python
import functools
import itertools
import math

import jax
import jax.numpy as jnp
from jax import lax
from jax.experimental import pallas as pl
from jax.experimental.pallas import tpu as pltpu
from jax.sharding import PartitionSpec as P

tukey_c = 4.685
beta_one = 0.9
beta_two = 0.999
learn_rate = 0.02
adam_eps = 1e-08

RING_MOST = 8
VMEM = pltpu.VMEM
IN_VMEM = pl.BlockSpec(memory_space=VMEM)
IN_ANY = pl.BlockSpec(memory_space=pl.ANY)


def tile_of(rows, most):
    best = [t for t in range(128, most + 1, 128) if rows % t == 0]
    return best[-1] if best else rows


def params():
    return pltpu.CompilerParams(vmem_limit_bytes=24 * 1024 * 1024)


def cost(flops, moved):
    return pl.CostEstimate(flops=int(flops), bytes_accessed=int(moved), transcendentals=0)


def pinned(*arrays):
    return [pltpu.with_memory_space_constraint(a, VMEM) for a in arrays]


def prepare_kernel(scale_k, x_in, index_in, cell_in, scale_in, x_out, f_out, ft_out, bend_out, shrink_out, index, cell, scale, sems):
    loads = [
        pltpu.make_async_copy(src, dst, sems.at[at])
        for at, (src, dst) in enumerate(((scale_in, scale), (cell_in, cell), (index_in, index), (x_in, x_out)))
    ]
    for load in loads:
        load.start()
    cells, rank = cell.shape
    rows = index.shape[0]
    genes = scale.shape[0]
    loads[0].wait()
    inverse = 1.0 / scale[...].reshape(1, genes)
    bend_out[...] = (inverse * inverse) * (1.0 / (tukey_c * tukey_c))
    shrink_out[...] = jnp.transpose(jnp.broadcast_to(-scale_k * (inverse * inverse), (rank, genes)))
    loads[1].wait()
    table = jnp.transpose(cell[...].astype(jnp.float32)).astype(jnp.bfloat16)
    base = lax.axis_index("row") * cells
    loads[2].wait()
    step = tile_of(rows, 512)
    for at in range(0, rows, step):
        local = index[at : at + step].reshape(1, step) - base
        hot = lax.broadcasted_iota(jnp.int32, (cells, step), 0) == local
        hot = jnp.where(hot, 1.0, 0.0).astype(jnp.bfloat16)
        picked = jnp.dot(table, hot, preferred_element_type=jnp.float32)
        ft_out[:, at : at + step] = picked.astype(jnp.bfloat16)
        f_out[at : at + step, :] = jnp.transpose(picked).astype(jnp.bfloat16)
    loads[3].wait()


def prepare(x_slab, row_index, cell_factor, gene_scale, scale_k):
    rows, genes = x_slab.shape
    cells, rank = cell_factor.shape
    ins = (x_slab, row_index, cell_factor, gene_scale)
    return pl.pallas_call(
        functools.partial(prepare_kernel, scale_k),
        out_shape=(
            VMEM((rows, genes), jnp.bfloat16),
            VMEM((rows, rank), jnp.bfloat16),
            VMEM((rank, rows), jnp.bfloat16),
            VMEM((1, genes), jnp.float32),
            VMEM((genes, rank), jnp.float32),
        ),
        in_specs=[IN_ANY] * 4,
        out_specs=(IN_VMEM,) * 5,
        scratch_shapes=[
            VMEM((rows,), jnp.int32),
            VMEM((cells, rank), jnp.bfloat16),
            VMEM((genes,), jnp.float32),
            pltpu.SemaphoreType.DMA((4,)),
        ],
        compiler_params=params(),
        cost_estimate=cost(8 * rows * cells * rank, 8 * rows * genes * 2),
        name="prepare",
    )(*(pltpu.with_memory_space_constraint(a, pltpu.HBM) for a in ins))


def pick(axis, table):
    me = lax.axis_index(axis)
    value = jnp.int32(table[0])
    for place, entry in enumerate(table[1:], 1):
        value = jnp.where(me == place, jnp.int32(entry), value)
    return value


def partner(me, hop, size):
    return me ^ hop if size & (size - 1) == 0 else (me + hop) % size


def source(me, hop, size):
    return me ^ hop if size & (size - 1) == 0 else (me + size - hop) % size


def rows_kernel(tables, block, first, last, n_row, *refs):
    refs = list(refs)
    take = lambda count: [refs.pop(0) for _ in range(count)]
    x_ref, f_ref, ft_ref, bend_ref, shrink_ref = take(5)
    shares = take(n_row) if first else None
    carried_in = None if first else take(3)
    rows_out = take(len(tables))
    carried_out = None if last else take(3 if first else 1)
    parts_out = take(n_row) if last else None
    me = lax.axis_index("row")

    if first:
        (piece,) = take(1)
        depth = shares[0].shape[0]
        for hop in range(n_row):
            start = pl.multiple_of(source(me, hop, n_row) * depth, depth)
            piece[pl.ds(start, depth), :] = shares[hop][...]
        whole = piece[...].astype(jnp.float32)
        wide = jnp.transpose(whole).astype(jnp.bfloat16)
        scaled = (whole * shrink_ref[...]).astype(jnp.bfloat16)
        total = None
    else:
        total, wide, scaled = (ref[...] for ref in carried_in)

    bend = bend_ref[...]
    step = tile_of(block, 512)
    tiles = []
    for table, out in zip(tables, rows_out):
        origin = pick("gene", table) * block if len(table) > 1 else 0
        for at in range(0, block, step):
            start = origin + at
            if len(table) > 1:
                start = pl.multiple_of(start, math.gcd(block, step))
            tiles.append((out, at, pl.ds(start, step)))

    def predict(here):
        return jnp.dot(f_ref[here, :], wide, preferred_element_type=jnp.float32)

    def gradients(tile, infl, total):
        out, at, here = tile
        cols = jnp.dot(ft_ref[:, here], infl, preferred_element_type=jnp.float32)
        out[at : at + step, :] = jnp.dot(infl, scaled, preferred_element_type=jnp.float32).astype(out.dtype)
        return cols if total is None else total + cols

    pred = predict(tiles[0][2])
    infl = None
    for at, tile in enumerate(tiles):
        later = predict(tiles[at + 1][2]) if at + 1 < len(tiles) else None
        now = influence(x_ref[tile[2], :], pred, bend)
        if at:
            total = gradients(tiles[at - 1], infl, total)
        infl, pred = now, later
    total = gradients(tiles[-1], infl, total)

    if first and not last:
        carried_out[1][...] = wide
        carried_out[2][...] = scaled
    if not last:
        carried_out[0][...] = total
        return
    (turned,) = take(1)
    turned[...] = jnp.transpose(total) * shrink_ref[...]
    depth = parts_out[0].shape[0]
    for hop in range(n_row):
        start = pl.multiple_of(partner(me, hop, n_row) * depth, depth)
        parts_out[hop][...] = turned[pl.ds(start, depth), :].astype(parts_out[hop].dtype)


def block_rows(tables, kinds, block, first, last, n_row, fixed, carried):
    genes, rank = fixed[4].shape
    out = [jax.ShapeDtypeStruct((block, rank), kind) for kind in kinds]
    if last:
        out += [jax.ShapeDtypeStruct((genes // n_row, rank), jnp.bfloat16 if hop else jnp.float32) for hop in range(n_row)]
    else:
        out += [VMEM((rank, genes), jnp.float32)]
    if first and not last:
        out += [VMEM((rank, genes), jnp.bfloat16), VMEM((genes, rank), jnp.bfloat16)]
    scratch = [VMEM((genes, rank), jnp.bfloat16)] if first else []
    if last:
        scratch.append(VMEM((genes, rank), jnp.float32))
    ins = pinned(*fixed) + (list(carried) if first else pinned(*carried))
    work = len(tables) * block * genes
    out = pl.pallas_call(
        functools.partial(rows_kernel, tables, block, first, last, n_row),
        out_shape=tuple(out),
        in_specs=[IN_VMEM] * len(ins),
        out_specs=(IN_VMEM,) * len(out),
        scratch_shapes=scratch,
        compiler_params=params(),
        cost_estimate=cost(6 * work * rank, work * 2),
        name="block_rows",
    )(*ins)
    done, rest = list(out[: len(tables)]), list(out[len(tables) :])
    return done, rest if first or last else rest + list(carried[1:])


def lane_parts(genes, depth, n_row):
    if n_row != 4:
        return None
    pairs = [(2 * depth * (place // 2), 2 * depth * (place // 2 + 1)) for place in range(n_row)]
    low = [-(-begin // 128) * 128 for begin, _ in pairs]
    width = min(end // 128 * 128 - begin for begin, (_, end) in zip(low, pairs))
    if width <= 0 or any(begin not in (0, genes - width) for begin in low):
        return None
    return low, width, [width if begin == 0 else 0 for begin in low]


def lanes(table, width):
    return pl.ds(pl.multiple_of(pick("row", table), 128), width)


def influence(x, pred, bend):
    resid = x.astype(jnp.float32) - pred
    inside = jnp.maximum(1.0 - resid * resid * bend, 0.0)
    return (resid * (inside * inside)).astype(jnp.bfloat16)


def part_of_block(table, block, here, x_ref, f_ref, ft_ref, bend_ref, wide, scaled):
    step = tile_of(block, 1024)
    origin = pick("gene", table) * block
    tiles = [pl.ds(pl.multiple_of(origin + at, math.gcd(block, step)), step) for at in range(0, block, step)]
    bend = bend_ref[:, here]
    preds = [jnp.dot(f_ref[tile, :], wide, preferred_element_type=jnp.float32) for tile in tiles]
    infls = [influence(x_ref[tile, here], pred, bend) for tile, pred in zip(tiles, preds)]
    rows, total = [], None
    for tile, infl in zip(tiles, infls):
        cols = jnp.dot(ft_ref[:, tile], infl, preferred_element_type=jnp.float32)
        rows.append(jnp.dot(infl, scaled, preferred_element_type=jnp.float32))
        total = cols if total is None else total + cols
    return rows, total


def early_kernel(table, block, parts, x_ref, f_ref, ft_ref, bend_ref, shrink_ref, own, other, *refs):
    rows_out, total_out, wide_out, scaled_out, pair = refs
    low, width, _ = parts
    depth = own.shape[0]
    odd = lax.axis_index("row") % 2
    pair[pl.ds(pl.multiple_of(odd * depth, depth), depth), :] = own[...]
    pair[pl.ds(pl.multiple_of((1 - odd) * depth, depth), depth), :] = other[...]
    inset = [begin - 2 * depth * (place // 2) for place, begin in enumerate(low)]
    whole = pair[pl.ds(pl.multiple_of(pick("row", inset), math.gcd(*inset, 128)), width), :].astype(jnp.float32)
    here = lanes(low, width)
    wide = jnp.transpose(whole).astype(jnp.bfloat16)
    scaled = (whole * shrink_ref[here, :]).astype(jnp.bfloat16)
    wide_out[...] = wide
    scaled_out[...] = scaled
    rows, total = part_of_block(table, block, here, x_ref, f_ref, ft_ref, bend_ref, wide, scaled)
    for at, value in enumerate(rows):
        rows_out[at * value.shape[0] : (at + 1) * value.shape[0], :] = value
    total_out[...] = total


def rest_kernel(table, block, parts, n_row, x_ref, f_ref, ft_ref, bend_ref, shrink_ref, *refs):
    shares, (rows_in, total_in, wide_in, scaled_in) = refs[:n_row], refs[n_row : n_row + 4]
    rows_out, total_out, wide_out, scaled_out, piece = refs[n_row + 4 :]
    low, width, rest = parts
    me = lax.axis_index("row")
    depth = shares[0].shape[0]
    for hop in range(n_row):
        start = pl.multiple_of(source(me, hop, n_row) * depth, depth)
        piece[pl.ds(start, depth), :] = shares[hop][...]
    here = lanes(rest, n_row * depth - width)
    whole = piece[here, :].astype(jnp.float32)
    wide = jnp.transpose(whole).astype(jnp.bfloat16)
    scaled = (whole * shrink_ref[here, :]).astype(jnp.bfloat16)
    rows, total = part_of_block(table, block, here, x_ref, f_ref, ft_ref, bend_ref, wide, scaled)
    for at, value in enumerate(rows):
        span = slice(at * value.shape[0], (at + 1) * value.shape[0])
        rows_out[span, :] = (rows_in[span, :] + value).astype(rows_out.dtype)
    done = lanes(low, width)
    total_out[:, here] = total
    total_out[:, done] = total_in[...]
    wide_out[:, here] = wide
    wide_out[:, done] = wide_in[...]
    scaled_out[here, :] = scaled
    scaled_out[done, :] = scaled_in[...]


def first_block(table, block, parts, n_row, fixed, shares):
    genes, rank = fixed[4].shape
    depth = genes // n_row
    width = parts[1]
    ins = pinned(*fixed)
    early = pl.pallas_call(
        functools.partial(early_kernel, table, block, parts),
        out_shape=(
            VMEM((block, rank), jnp.float32),
            VMEM((rank, width), jnp.float32),
            VMEM((rank, width), jnp.bfloat16),
            VMEM((width, rank), jnp.bfloat16),
        ),
        in_specs=[IN_VMEM] * 7,
        out_specs=(IN_VMEM,) * 4,
        scratch_shapes=[VMEM((2 * depth, rank), jnp.bfloat16)],
        compiler_params=params(),
        cost_estimate=cost(12 * block * width * rank, block * width * 4),
        name="early_part",
    )(*ins, *shares[:2])
    done, *carried = pl.pallas_call(
        functools.partial(rest_kernel, table, block, parts, n_row),
        out_shape=(
            jax.ShapeDtypeStruct((block, rank), jnp.bfloat16),
            VMEM((rank, genes), jnp.float32),
            VMEM((rank, genes), jnp.bfloat16),
            VMEM((genes, rank), jnp.bfloat16),
        ),
        in_specs=[IN_VMEM] * (9 + n_row),
        out_specs=(IN_VMEM,) * 4,
        scratch_shapes=[VMEM((genes, rank), jnp.bfloat16)],
        compiler_params=params(),
        cost_estimate=cost(12 * block * (genes - width) * rank, block * (genes - width) * 4),
        name="rest_part",
    )(*ins, *shares, *pinned(*early))
    return [done], carried


def swap_row(value, hop, size):
    return lax.ppermute(value, "row", [(me, partner(me, hop, size)) for me in range(size)])


def ring_of(size):
    return [*range(0, size, 2), *reversed(range(1, size, 2))]


def steps_of(size):
    ahead = [(1, distance) for distance in range(size // 2, 0, -1)]
    back = [(-1, distance) for distance in range((size - 1) // 2, 0, -1)]
    return [step for pair in itertools.zip_longest(ahead, back) for step in pair if step]


def around(size, hops):
    ring = ring_of(size)
    return tuple(ring[(ring.index(place) + hops) % size] for place in range(size))


def plus(wide, narrow):
    return wide.astype(jnp.float32) + narrow.astype(jnp.float32)


def finish_kernel(n_ends, n_parts, *refs):
    n_ins = n_ends + n_parts + 3
    ins, outs = refs[:n_ins], refs[n_ins : n_ins + 3 + bool(n_ends)]
    *held, sems = refs[n_ins + len(outs) :]
    ends, parts = ins[:n_ends], ins[n_ends : n_ends + n_parts]
    factor, first, second = ins[n_ends + n_parts :]
    copies = []

    def send(at, span, value):
        held[at][span, :] = value
        copies.append(pltpu.make_async_copy(held[at].at[span, :], outs[at].at[span, :], sems.at[len(copies)]))
        copies[-1].start()

    if ends:
        step = tile_of(ends[0].shape[0], 256)
        for low in range(0, ends[0].shape[0], step):
            span = pl.ds(low, step)
            rows = ends[0][span, :]
            for end in ends[1:]:
                rows = plus(rows, end[span, :])
            send(3, span, rows)
    grad = parts[0][...]
    for part in parts[1:]:
        grad = plus(grad, part[...])
    span = pl.ds(0, grad.shape[0])
    new_first = beta_one * first[...] + (1.0 - beta_one) * grad
    new_second = beta_two * second[...] + (1.0 - beta_two) * grad * grad
    send(1, span, new_first)
    send(2, span, new_second)
    first_hat = new_first / (1.0 - beta_one**10)
    second_hat = new_second / (1.0 - beta_two**10)
    send(0, span, factor[...] - learn_rate * first_hat / (jnp.sqrt(second_hat) + adam_eps))
    for copy in copies:
        copy.wait()


def finish(ends, parts, factor, first, second):
    ins = [*ends, *parts, factor, first, second]
    shapes = [factor, factor, factor] + list(ends[:1])
    n_copies = 3 + (ends[0].shape[0] // tile_of(ends[0].shape[0], 256) if ends else 0)
    return pl.pallas_call(
        functools.partial(finish_kernel, len(ends), len(parts)),
        out_shape=tuple(jax.ShapeDtypeStruct(like.shape, jnp.float32) for like in shapes),
        in_specs=[IN_VMEM] * len(ins),
        out_specs=(IN_ANY,) * len(shapes),
        scratch_shapes=[VMEM(like.shape, jnp.float32) for like in shapes] + [pltpu.SemaphoreType.DMA((n_copies,))],
        compiler_params=params(),
        cost_estimate=cost(20 * factor.size, sum(4 * a.size for a in ins)),
        name="finish",
    )(*ins)


def local(x_slab, cell_factor, row_index, gene_scale, gene_factor, first_moment, second_moment):
    rows_dev, genes_dev = x_slab.shape
    n_gene = lax.axis_size("gene")
    n_row = lax.axis_size("row")
    block = rows_dev // n_gene
    scale_k = 4.0 / math.sqrt(genes_dev * n_gene)
    factor_bf = gene_factor.astype(jnp.bfloat16)
    shares = [factor_bf] + [swap_row(factor_bf, hop, n_row) for hop in range(1, n_row)]
    fixed = prepare(x_slab, row_index, cell_factor, gene_scale, scale_k)
    adam = (gene_factor, first_moment, second_moment)

    if n_gene == 1 or n_gene > RING_MOST or block % 128:
        (rows,), parts = block_rows([(0,)], [jnp.float32], rows_dev, True, True, n_row, fixed, shares)
        grad_cells = lax.psum_scatter(rows, "gene", scatter_dimension=0, tiled=True)
        others = [swap_row(parts[hop], hop, n_row) for hop in range(1, n_row)]
        return (grad_cells, *finish([], [parts[0], *others], *adam))

    steps = steps_of(n_gene)
    tables = [around(n_gene, way * distance) for way, distance in steps] + [tuple(range(n_gene))]
    kinds = [jnp.bfloat16] * len(steps) + [jnp.float32]
    cuts = [0, 1, 2, len(tables)] if len(steps) > 2 else [0, 1, len(tables)]
    parted = lane_parts(genes_dev, genes_dev // n_row, n_row)
    carried, blocks = shares, []
    for low, high in zip(cuts, cuts[1:]):
        last = high == len(tables)
        if low == 0 and parted:
            done, carried = first_block(tables[0], block, parted, n_row, fixed, shares)
            blocks += done
            continue
        done, carried = block_rows(tables[low:high], kinds[low:high], block, low == 0, last, n_row, fixed, carried)
        blocks += done
    parts = carried

    came = {}
    for (way, _), own in zip(steps, blocks):
        if way in came:
            own = plus(own, came[way]).astype(jnp.bfloat16)
        came[way] = lax.ppermute(own, "gene", list(enumerate(around(n_gene, way))))
    others = [swap_row(parts[hop], hop, n_row) for hop in range(1, n_row)]
    *adam_out, grad_cells = finish([blocks[-1], *came.values()], [parts[0], *others], *adam)
    return (grad_cells, *adam_out)


def solution(mesh):
    in_specs = (
        P(("grp", "row"), "gene"),
        P(("grp", "row"), None),
        P(("grp", "row")),
        P(("grp", "gene")),
        P(("grp", "gene", "row"), None),
        P(("grp", "gene", "row"), None),
        P(("grp", "gene", "row"), None),
    )
    out_specs = (
        P(("grp", "row", "gene"), None),
        P(("grp", "gene", "row"), None),
        P(("grp", "gene", "row"), None),
        P(("grp", "gene", "row"), None),
    )
    return jax.shard_map(local, mesh=mesh, in_specs=in_specs, out_specs=out_specs, check_vma=False)
```

```python
import functools
import itertools
import math

import jax
import jax.numpy as jnp
from jax import lax
from jax.experimental import pallas as pl
from jax.experimental.pallas import tpu as pltpu
from jax.sharding import PartitionSpec as P

tukey_c = 4.685
beta_one = 0.9
beta_two = 0.999
learn_rate = 0.02
adam_eps = 1e-08

RING_MOST = 8
VMEM = pltpu.VMEM
IN_VMEM = pl.BlockSpec(memory_space=VMEM)
IN_ANY = pl.BlockSpec(memory_space=pl.ANY)


def tile_of(rows, most):
    best = [t for t in range(128, most + 1, 128) if rows % t == 0]
    return best[-1] if best else rows


def params():
    return pltpu.CompilerParams(vmem_limit_bytes=24 * 1024 * 1024)


def cost(flops, moved):
    return pl.CostEstimate(flops=int(flops), bytes_accessed=int(moved), transcendentals=0)


def pinned(*arrays):
    return [pltpu.with_memory_space_constraint(a, VMEM) for a in arrays]


def prepare_kernel(scale_k, x_in, index_in, cell_in, scale_in, x_out, f_out, ft_out, bend_out, shrink_out, index, cell, scale, sems):
    loads = [
        pltpu.make_async_copy(src, dst, sems.at[at])
        for at, (src, dst) in enumerate(((scale_in, scale), (cell_in, cell), (index_in, index), (x_in, x_out)))
    ]
    for load in loads:
        load.start()
    cells, rank = cell.shape
    rows = index.shape[0]
    genes = scale.shape[0]
    loads[0].wait()
    inverse = 1.0 / scale[...].reshape(1, genes)
    bend_out[...] = (inverse * inverse) * (1.0 / (tukey_c * tukey_c))
    shrink_out[...] = jnp.transpose(jnp.broadcast_to(-scale_k * (inverse * inverse), (rank, genes)))
    loads[1].wait()
    table = jnp.transpose(cell[...].astype(jnp.float32)).astype(jnp.bfloat16)
    base = lax.axis_index("row") * cells
    loads[2].wait()
    step = tile_of(rows, 512)
    for at in range(0, rows, step):
        local = index[at : at + step].reshape(1, step) - base
        hot = lax.broadcasted_iota(jnp.int32, (cells, step), 0) == local
        hot = jnp.where(hot, 1.0, 0.0).astype(jnp.bfloat16)
        picked = jnp.dot(table, hot, preferred_element_type=jnp.float32)
        ft_out[:, at : at + step] = picked.astype(jnp.bfloat16)
        f_out[at : at + step, :] = jnp.transpose(picked).astype(jnp.bfloat16)
    loads[3].wait()


def prepare(x_slab, row_index, cell_factor, gene_scale, scale_k):
    rows, genes = x_slab.shape
    cells, rank = cell_factor.shape
    ins = (x_slab, row_index, cell_factor, gene_scale)
    return pl.pallas_call(
        functools.partial(prepare_kernel, scale_k),
        out_shape=(
            VMEM((rows, genes), jnp.bfloat16),
            VMEM((rows, rank), jnp.bfloat16),
            VMEM((rank, rows), jnp.bfloat16),
            VMEM((1, genes), jnp.float32),
            VMEM((genes, rank), jnp.float32),
        ),
        in_specs=[IN_ANY] * 4,
        out_specs=(IN_VMEM,) * 5,
        scratch_shapes=[
            VMEM((rows,), jnp.int32),
            VMEM((cells, rank), jnp.bfloat16),
            VMEM((genes,), jnp.float32),
            pltpu.SemaphoreType.DMA((4,)),
        ],
        compiler_params=params(),
        cost_estimate=cost(8 * rows * cells * rank, 8 * rows * genes * 2),
        name="prepare",
    )(*(pltpu.with_memory_space_constraint(a, pltpu.HBM) for a in ins))


def pick(axis, table):
    me = lax.axis_index(axis)
    value = jnp.int32(table[0])
    for place, entry in enumerate(table[1:], 1):
        value = jnp.where(me == place, jnp.int32(entry), value)
    return value


def partner(me, hop, size):
    return me ^ hop if size & (size - 1) == 0 else (me + hop) % size


def source(me, hop, size):
    return me ^ hop if size & (size - 1) == 0 else (me + size - hop) % size


class Cut:
    def __init__(self, refs):
        self.refs = refs
        self.dtype = refs[0].dtype

    def store(self, low, value):
        depth = self.refs[0].shape[0]
        for at, ref in enumerate(self.refs):
            begin, end = max(low, at * depth), min(low + value.shape[0], (at + 1) * depth)
            if begin < end:
                ref[begin - at * depth : end - at * depth, :] = value[begin - low : end - low, :].astype(ref.dtype)


def grouped(refs, counts):
    refs = list(refs)
    return [Cut([refs.pop(0) for _ in range(count)]) for count in counts]


def rows_kernel(tables, counts, block, first, last, n_row, *refs):
    refs = list(refs)
    take = lambda count: [refs.pop(0) for _ in range(count)]
    x_ref, f_ref, ft_ref, bend_ref, shrink_ref = take(5)
    shares = take(n_row) if first else None
    carried_in = None if first else take(3)
    rows_out = grouped(take(sum(counts)), counts)
    carried_out = None if last else take(3 if first else 1)
    parts_out = take(n_row) if last else None
    me = lax.axis_index("row")

    if first:
        (piece,) = take(1)
        depth = shares[0].shape[0]
        for hop in range(n_row):
            start = pl.multiple_of(source(me, hop, n_row) * depth, depth)
            piece[pl.ds(start, depth), :] = shares[hop][...]
        whole = piece[...].astype(jnp.float32)
        wide = jnp.transpose(whole).astype(jnp.bfloat16)
        scaled = (whole * shrink_ref[...]).astype(jnp.bfloat16)
        total = None
    else:
        total, wide, scaled = (ref[...] for ref in carried_in)

    bend = bend_ref[...]
    step = tile_of(block, 256)
    tiles = []
    for table, out in zip(tables, rows_out):
        origin = pick("gene", table) * block if len(table) > 1 else 0
        for at in range(0, block, step):
            start = origin + at
            if len(table) > 1:
                start = pl.multiple_of(start, math.gcd(block, step))
            tiles.append((out, at, pl.ds(start, step)))

    def predict(here):
        return jnp.dot(f_ref[here, :], wide, preferred_element_type=jnp.float32)

    def gradients(tile, infl, total):
        out, at, here = tile
        cols = jnp.dot(ft_ref[:, here], infl, preferred_element_type=jnp.float32)
        out.store(at, jnp.dot(infl, scaled, preferred_element_type=jnp.float32))
        return cols if total is None else total + cols

    pred = predict(tiles[0][2])
    infl = None
    for at, tile in enumerate(tiles):
        later = predict(tiles[at + 1][2]) if at + 1 < len(tiles) else None
        now = influence(x_ref[tile[2], :], pred, bend)
        if at:
            total = gradients(tiles[at - 1], infl, total)
        infl, pred = now, later
    total = gradients(tiles[-1], infl, total)

    if first and not last:
        carried_out[1][...] = wide
        carried_out[2][...] = scaled
    if not last:
        carried_out[0][...] = total
        return
    (turned,) = take(1)
    turned[...] = jnp.transpose(total) * shrink_ref[...]
    depth = parts_out[0].shape[0]
    for hop in range(n_row):
        start = pl.multiple_of(partner(me, hop, n_row) * depth, depth)
        parts_out[hop][...] = turned[pl.ds(start, depth), :].astype(parts_out[hop].dtype)


def block_rows(tables, kinds, counts, block, first, last, n_row, fixed, carried):
    genes, rank = fixed[4].shape
    out = [jax.ShapeDtypeStruct((block // count, rank), kind) for kind, count in zip(kinds, counts) for _ in range(count)]
    n_rows = len(out)
    if last:
        out += [jax.ShapeDtypeStruct((genes // n_row, rank), jnp.bfloat16 if hop else jnp.float32) for hop in range(n_row)]
    else:
        out += [VMEM((rank, genes), jnp.float32)]
    if first and not last:
        out += [VMEM((rank, genes), jnp.bfloat16), VMEM((genes, rank), jnp.bfloat16)]
    scratch = [VMEM((genes, rank), jnp.bfloat16)] if first else []
    if last:
        scratch.append(VMEM((genes, rank), jnp.float32))
    ins = pinned(*fixed) + (list(carried) if first else pinned(*carried))
    work = len(tables) * block * genes
    out = pl.pallas_call(
        functools.partial(rows_kernel, tables, counts, block, first, last, n_row),
        out_shape=tuple(out),
        in_specs=[IN_VMEM] * len(ins),
        out_specs=(IN_VMEM,) * len(out),
        scratch_shapes=scratch,
        compiler_params=params(),
        cost_estimate=cost(6 * work * rank, work * 2),
        name="block_rows",
    )(*ins)
    done, rest = [cut.refs for cut in grouped(out[:n_rows], counts)], list(out[n_rows:])
    return done, rest if first or last else rest + list(carried[1:])


def lane_parts(genes, depth, n_row):
    if n_row != 4:
        return None
    pairs = [(2 * depth * (place // 2), 2 * depth * (place // 2 + 1)) for place in range(n_row)]
    low = [-(-begin // 128) * 128 for begin, _ in pairs]
    width = min(end // 128 * 128 - begin for begin, (_, end) in zip(low, pairs))
    if width <= 0 or any(begin not in (0, genes - width) for begin in low):
        return None
    return low, width, [width if begin == 0 else 0 for begin in low]


def lanes(table, width):
    return pl.ds(pl.multiple_of(pick("row", table), 128), width)


def influence(x, pred, bend):
    resid = x.astype(jnp.float32) - pred
    inside = jnp.maximum(1.0 - resid * resid * bend, 0.0)
    return (resid * (inside * inside)).astype(jnp.bfloat16)


def part_of_block(table, block, here, x_ref, f_ref, ft_ref, bend_ref, wide, scaled):
    step = tile_of(block, 256)
    origin = pick("gene", table) * block
    tiles = [pl.ds(pl.multiple_of(origin + at, math.gcd(block, step)), step) for at in range(0, block, step)]
    bend = bend_ref[:, here]
    preds = [jnp.dot(f_ref[tile, :], wide, preferred_element_type=jnp.float32) for tile in tiles]
    infls = [influence(x_ref[tile, here], pred, bend) for tile, pred in zip(tiles, preds)]
    rows, total = [], None
    for tile, infl in zip(tiles, infls):
        cols = jnp.dot(ft_ref[:, tile], infl, preferred_element_type=jnp.float32)
        rows.append(jnp.dot(infl, scaled, preferred_element_type=jnp.float32))
        total = cols if total is None else total + cols
    return rows, total


def early_kernel(table, block, parts, x_ref, f_ref, ft_ref, bend_ref, shrink_ref, own, other, *refs):
    rows_out, total_out, wide_out, scaled_out, pair = refs
    low, width, _ = parts
    depth = own.shape[0]
    odd = lax.axis_index("row") % 2
    pair[pl.ds(pl.multiple_of(odd * depth, depth), depth), :] = own[...]
    pair[pl.ds(pl.multiple_of((1 - odd) * depth, depth), depth), :] = other[...]
    inset = [begin - 2 * depth * (place // 2) for place, begin in enumerate(low)]
    whole = pair[pl.ds(pl.multiple_of(pick("row", inset), math.gcd(*inset, 128)), width), :].astype(jnp.float32)
    here = lanes(low, width)
    wide = jnp.transpose(whole).astype(jnp.bfloat16)
    scaled = (whole * shrink_ref[here, :]).astype(jnp.bfloat16)
    wide_out[...] = wide
    scaled_out[...] = scaled
    rows, total = part_of_block(table, block, here, x_ref, f_ref, ft_ref, bend_ref, wide, scaled)
    for at, value in enumerate(rows):
        rows_out[at * value.shape[0] : (at + 1) * value.shape[0], :] = value
    total_out[...] = total


def rest_kernel(table, count, block, parts, n_row, x_ref, f_ref, ft_ref, bend_ref, shrink_ref, *refs):
    shares, (rows_in, total_in, wide_in, scaled_in) = refs[:n_row], refs[n_row : n_row + 4]
    *rows_out, total_out, wide_out, scaled_out, piece = refs[n_row + 4 :]
    rows_out = Cut(rows_out)
    low, width, rest = parts
    me = lax.axis_index("row")
    depth = shares[0].shape[0]
    for hop in range(n_row):
        start = pl.multiple_of(source(me, hop, n_row) * depth, depth)
        piece[pl.ds(start, depth), :] = shares[hop][...]
    here = lanes(rest, n_row * depth - width)
    whole = piece[here, :].astype(jnp.float32)
    wide = jnp.transpose(whole).astype(jnp.bfloat16)
    scaled = (whole * shrink_ref[here, :]).astype(jnp.bfloat16)
    rows, total = part_of_block(table, block, here, x_ref, f_ref, ft_ref, bend_ref, wide, scaled)
    for at, value in enumerate(rows):
        span = slice(at * value.shape[0], (at + 1) * value.shape[0])
        rows_out.store(span.start, rows_in[span, :] + value)
    done = lanes(low, width)
    total_out[:, here] = total
    total_out[:, done] = total_in[...]
    wide_out[:, here] = wide
    wide_out[:, done] = wide_in[...]
    scaled_out[here, :] = scaled
    scaled_out[done, :] = scaled_in[...]


def first_block(table, count, block, parts, n_row, fixed, shares):
    genes, rank = fixed[4].shape
    depth = genes // n_row
    width = parts[1]
    ins = pinned(*fixed)
    early = pl.pallas_call(
        functools.partial(early_kernel, table, block, parts),
        out_shape=(
            VMEM((block, rank), jnp.float32),
            VMEM((rank, width), jnp.float32),
            VMEM((rank, width), jnp.bfloat16),
            VMEM((width, rank), jnp.bfloat16),
        ),
        in_specs=[IN_VMEM] * 7,
        out_specs=(IN_VMEM,) * 4,
        scratch_shapes=[VMEM((2 * depth, rank), jnp.bfloat16)],
        compiler_params=params(),
        cost_estimate=cost(12 * block * width * rank, block * width * 4),
        name="early_part",
    )(*ins, *shares[:2])
    out = pl.pallas_call(
        functools.partial(rest_kernel, table, count, block, parts, n_row),
        out_shape=(
            *[jax.ShapeDtypeStruct((block // count, rank), jnp.bfloat16)] * count,
            VMEM((rank, genes), jnp.float32),
            VMEM((rank, genes), jnp.bfloat16),
            VMEM((genes, rank), jnp.bfloat16),
        ),
        in_specs=[IN_VMEM] * (9 + n_row),
        out_specs=(IN_VMEM,) * (count + 3),
        scratch_shapes=[VMEM((genes, rank), jnp.bfloat16)],
        compiler_params=params(),
        cost_estimate=cost(12 * block * (genes - width) * rank, block * (genes - width) * 4),
        name="rest_part",
    )(*ins, *shares, *pinned(*early))
    return [list(out[:count])], list(out[count:])


def swap_row(value, hop, size):
    return lax.ppermute(value, "row", [(me, partner(me, hop, size)) for me in range(size)])


def ring_of(size):
    return [*range(0, size, 2), *reversed(range(1, size, 2))]


def steps_of(size):
    ahead = [(1, distance) for distance in range(size // 2, 0, -1)]
    back = [(-1, distance) for distance in range((size - 1) // 2, 0, -1)]
    return [step for pair in itertools.zip_longest(ahead, back) for step in pair if step]


def around(size, hops):
    ring = ring_of(size)
    return tuple(ring[(ring.index(place) + hops) % size] for place in range(size))


def plus(wide, narrow):
    return wide.astype(jnp.float32) + narrow.astype(jnp.float32)


def finish_kernel(counts, n_parts, *refs):
    n_ends = sum(counts)
    n_ins = n_ends + n_parts + 3
    ins, outs = refs[:n_ins], refs[n_ins : n_ins + 3 + bool(n_ends)]
    *held, sems = refs[n_ins + len(outs) :]
    ends, parts = [cut.refs for cut in grouped(ins[:n_ends], counts)], ins[n_ends : n_ends + n_parts]
    factor, first, second = ins[n_ends + n_parts :]
    copies = []

    def send(at, span, value):
        held[at][span, :] = value
        copies.append(pltpu.make_async_copy(held[at].at[span, :], outs[at].at[span, :], sems.at[len(copies)]))
        copies[-1].start()

    if ends:
        ((own,), *others) = ends
        step = tile_of(min(end[0].shape[0] for end in ends), 256)
        for low in range(0, own.shape[0], step):
            span = pl.ds(low, step)
            rows = own[span, :]
            for end in others:
                at, inner = divmod(low, end[0].shape[0])
                rows = plus(rows, end[at][pl.ds(inner, step), :])
            send(3, span, rows)
    grad = parts[0][...]
    for part in parts[1:]:
        grad = plus(grad, part[...])
    span = pl.ds(0, grad.shape[0])
    new_first = beta_one * first[...] + (1.0 - beta_one) * grad
    new_second = beta_two * second[...] + (1.0 - beta_two) * grad * grad
    send(1, span, new_first)
    send(2, span, new_second)
    first_hat = new_first / (1.0 - beta_one**10)
    second_hat = new_second / (1.0 - beta_two**10)
    send(0, span, factor[...] - learn_rate * first_hat / (jnp.sqrt(second_hat) + adam_eps))
    for copy in copies:
        copy.wait()


def finish(ends, parts, factor, first, second):
    ins = [*itertools.chain(*ends), *parts, factor, first, second]
    shapes = [factor, factor, factor] + ([ends[0][0]] if ends else [])
    n_copies = 3 + (ends[0][0].shape[0] // tile_of(min(end[0].shape[0] for end in ends), 256) if ends else 0)
    return pl.pallas_call(
        functools.partial(finish_kernel, [len(end) for end in ends], len(parts)),
        out_shape=tuple(jax.ShapeDtypeStruct(like.shape, jnp.float32) for like in shapes),
        in_specs=[IN_VMEM] * len(ins),
        out_specs=(IN_ANY,) * len(shapes),
        scratch_shapes=[VMEM(like.shape, jnp.float32) for like in shapes] + [pltpu.SemaphoreType.DMA((n_copies,))],
        compiler_params=params(),
        cost_estimate=cost(20 * factor.size, sum(4 * a.size for a in ins)),
        name="finish",
    )(*ins)


def local(x_slab, cell_factor, row_index, gene_scale, gene_factor, first_moment, second_moment):
    rows_dev, genes_dev = x_slab.shape
    n_gene = lax.axis_size("gene")
    n_row = lax.axis_size("row")
    block = rows_dev // n_gene
    scale_k = 4.0 / math.sqrt(genes_dev * n_gene)
    factor_bf = gene_factor.astype(jnp.bfloat16)
    shares = [factor_bf] + [swap_row(factor_bf, hop, n_row) for hop in range(1, n_row)]
    fixed = prepare(x_slab, row_index, cell_factor, gene_scale, scale_k)
    adam = (gene_factor, first_moment, second_moment)

    if n_gene == 1 or n_gene > RING_MOST or block % 128:
        ((rows,),), parts = block_rows([(0,)], [jnp.float32], [1], rows_dev, True, True, n_row, fixed, shares)
        grad_cells = lax.psum_scatter(rows, "gene", scatter_dimension=0, tiled=True)
        others = [swap_row(parts[hop], hop, n_row) for hop in range(1, n_row)]
        return (grad_cells, *finish([], [parts[0], *others], *adam))

    steps = steps_of(n_gene)
    tables = [around(n_gene, way * distance) for way, distance in steps] + [tuple(range(n_gene))]
    kinds = [jnp.bfloat16] * len(steps) + [jnp.float32]
    counts = [2 if way == 1 and n_gene > 2 and block % 256 == 0 else 1 for way, _ in steps] + [1]
    cuts = [0, 1, 2, len(tables)] if len(steps) > 2 else [0, 1, len(tables)]
    parted = lane_parts(genes_dev, genes_dev // n_row, n_row)
    carried, blocks = shares, []
    for low, high in zip(cuts, cuts[1:]):
        last = high == len(tables)
        if low == 0 and parted:
            done, carried = first_block(tables[0], counts[0], block, parted, n_row, fixed, shares)
            blocks += done
            continue
        done, carried = block_rows(tables[low:high], kinds[low:high], counts[low:high], block, low == 0, last, n_row, fixed, carried)
        blocks += done
    parts = carried

    came = {}
    for (way, _), halves in zip(steps, blocks):
        targets = list(enumerate(around(n_gene, way)))
        if way in came:
            halves = [plus(own, value).astype(jnp.bfloat16) for own, value in zip(halves, came[way])]
        came[way] = [lax.ppermute(half, "gene", targets) for half in halves]
    others = [swap_row(parts[hop], hop, n_row) for hop in range(1, n_row)]
    *adam_out, grad_cells = finish([blocks[-1], *came.values()], [parts[0], *others], *adam)
    return (grad_cells, *adam_out)


def solution(mesh):
    in_specs = (
        P(("grp", "row"), "gene"),
        P(("grp", "row"), None),
        P(("grp", "row")),
        P(("grp", "gene")),
        P(("grp", "gene", "row"), None),
        P(("grp", "gene", "row"), None),
        P(("grp", "gene", "row"), None),
    )
    out_specs = (
        P(("grp", "row", "gene"), None),
        P(("grp", "gene", "row"), None),
        P(("grp", "gene", "row"), None),
        P(("grp", "gene", "row"), None),
    )
    return jax.shard_map(local, mesh=mesh, in_specs=in_specs, out_specs=out_specs, check_vma=False)
```

```python
import functools
import itertools
import math

import jax
import jax.numpy as jnp
from jax import lax
from jax.experimental import pallas as pl
from jax.experimental.pallas import tpu as pltpu
from jax.sharding import PartitionSpec as P

tukey_c = 4.685
beta_one = 0.9
beta_two = 0.999
learn_rate = 0.02
adam_eps = 1e-08

RING_MOST = 8
LINES = ("gene", "row")
VMEM = pltpu.VMEM
IN_VMEM = pl.BlockSpec(memory_space=VMEM)
IN_ANY = pl.BlockSpec(memory_space=pl.ANY)


def tile_of(rows, most):
    best = [t for t in range(128, most + 1, 128) if rows % t == 0]
    return best[-1] if best else rows


def params():
    return pltpu.CompilerParams(vmem_limit_bytes=24 * 1024 * 1024)


def cost(flops, moved):
    return pl.CostEstimate(flops=int(flops), bytes_accessed=int(moved), transcendentals=0)


def pinned(*arrays):
    return [pltpu.with_memory_space_constraint(a, VMEM) for a in arrays]


def prepare_kernel(scale_k, x_in, index_in, cell_in, scale_in, x_out, f_out, ft_out, bend_out, shrink_out, index, cell, scale, sems):
    loads = [
        pltpu.make_async_copy(src, dst, sems.at[at])
        for at, (src, dst) in enumerate(((scale_in, scale), (cell_in, cell), (index_in, index), (x_in, x_out)))
    ]
    for load in loads:
        load.start()
    cells, rank = cell.shape
    rows = index.shape[0]
    genes = scale.shape[0]
    loads[0].wait()
    inverse = 1.0 / scale[...].reshape(1, genes)
    bend_out[...] = (inverse * inverse) * (1.0 / (tukey_c * tukey_c))
    shrink_out[...] = jnp.transpose(jnp.broadcast_to(-scale_k * (inverse * inverse), (rank, genes)))
    loads[1].wait()
    table = jnp.transpose(cell[...].astype(jnp.float32)).astype(jnp.bfloat16)
    base = lax.axis_index("row") * cells
    loads[2].wait()
    step = tile_of(rows, 512)
    for at in range(0, rows, step):
        local = index[at : at + step].reshape(1, step) - base
        hot = lax.broadcasted_iota(jnp.int32, (cells, step), 0) == local
        hot = jnp.where(hot, 1.0, 0.0).astype(jnp.bfloat16)
        picked = jnp.dot(table, hot, preferred_element_type=jnp.float32)
        ft_out[:, at : at + step] = picked.astype(jnp.bfloat16)
        f_out[at : at + step, :] = jnp.transpose(picked).astype(jnp.bfloat16)
    loads[3].wait()


def prepare(x_slab, row_index, cell_factor, gene_scale, scale_k):
    rows, genes = x_slab.shape
    cells, rank = cell_factor.shape
    ins = (x_slab, row_index, cell_factor, gene_scale)
    return pl.pallas_call(
        functools.partial(prepare_kernel, scale_k),
        out_shape=(
            VMEM((rows, genes), jnp.bfloat16),
            VMEM((rows, rank), jnp.bfloat16),
            VMEM((rank, rows), jnp.bfloat16),
            VMEM((1, genes), jnp.float32),
            VMEM((genes, rank), jnp.float32),
        ),
        in_specs=[IN_ANY] * 4,
        out_specs=(IN_VMEM,) * 5,
        scratch_shapes=[
            VMEM((rows,), jnp.int32),
            VMEM((cells, rank), jnp.bfloat16),
            VMEM((genes,), jnp.float32),
            pltpu.SemaphoreType.DMA((4,)),
        ],
        compiler_params=params(),
        cost_estimate=cost(8 * rows * cells * rank, 8 * rows * genes * 2),
        name="prepare",
    )(*(pltpu.with_memory_space_constraint(a, pltpu.HBM) for a in ins))


def pick(axis, table):
    me = lax.axis_index(axis)
    value = jnp.int32(table[0])
    for place, entry in enumerate(table[1:], 1):
        value = jnp.where(me == place, jnp.int32(entry), value)
    return value


def partner(me, hop, size):
    return me ^ hop if size & (size - 1) == 0 else (me + hop) % size


def source(me, hop, size):
    return me ^ hop if size & (size - 1) == 0 else (me + size - hop) % size


def rows_kernel(tables, block, first, last, n_row, *refs):
    refs = list(refs)
    take = lambda count: [refs.pop(0) for _ in range(count)]
    x_ref, f_ref, ft_ref, bend_ref, shrink_ref = take(5)
    shares = take(n_row) if first else None
    carried_in = None if first else take(3)
    rows_out = take(len(tables))
    carried_out = None if last else take(3 if first else 1)
    parts_out = take(n_row) if last else None
    me = lax.axis_index("row")

    if first:
        (piece,) = take(1)
        depth = shares[0].shape[0]
        for hop in range(n_row):
            start = pl.multiple_of(source(me, hop, n_row) * depth, depth)
            piece[pl.ds(start, depth), :] = shares[hop][...]
        whole = piece[...].astype(jnp.float32)
        wide = jnp.transpose(whole).astype(jnp.bfloat16)
        scaled = (whole * shrink_ref[...]).astype(jnp.bfloat16)
        total = None
    else:
        total, wide, scaled = (ref[...] for ref in carried_in)

    bend = bend_ref[...]
    step = tile_of(block, 256)
    tiles = []
    for table, out in zip(tables, rows_out):
        origin = pick(LINES, table) * block if len(table) > 1 else 0
        for at in range(0, block, step):
            start = origin + at
            if len(table) > 1:
                start = pl.multiple_of(start, math.gcd(block, step))
            tiles.append((out, at, pl.ds(start, step)))

    def predict(here):
        return jnp.dot(f_ref[here, :], wide, preferred_element_type=jnp.float32)

    def gradients(tile, infl, total):
        out, at, here = tile
        cols = jnp.dot(ft_ref[:, here], infl, preferred_element_type=jnp.float32)
        out[at : at + step, :] = jnp.dot(infl, scaled, preferred_element_type=jnp.float32).astype(out.dtype)
        return cols if total is None else total + cols

    pred = predict(tiles[0][2])
    infl = None
    for at, tile in enumerate(tiles):
        later = predict(tiles[at + 1][2]) if at + 1 < len(tiles) else None
        now = influence(x_ref[tile[2], :], pred, bend)
        if at:
            total = gradients(tiles[at - 1], infl, total)
        infl, pred = now, later
    total = gradients(tiles[-1], infl, total)

    if first and not last:
        carried_out[1][...] = wide
        carried_out[2][...] = scaled
    if not last:
        carried_out[0][...] = total
        return
    (turned,) = take(1)
    turned[...] = jnp.transpose(total) * shrink_ref[...]
    depth = parts_out[0].shape[0]
    for hop in range(n_row):
        start = pl.multiple_of(partner(me, hop, n_row) * depth, depth)
        parts_out[hop][...] = turned[pl.ds(start, depth), :].astype(parts_out[hop].dtype)


def block_rows(tables, kinds, block, first, last, n_row, fixed, carried):
    genes, rank = fixed[4].shape
    out = [jax.ShapeDtypeStruct((block, rank), kind) for kind in kinds]
    if last:
        out += [jax.ShapeDtypeStruct((genes // n_row, rank), jnp.bfloat16 if hop else jnp.float32) for hop in range(n_row)]
    else:
        out += [VMEM((rank, genes), jnp.float32)]
    if first and not last:
        out += [VMEM((rank, genes), jnp.bfloat16), VMEM((genes, rank), jnp.bfloat16)]
    scratch = [VMEM((genes, rank), jnp.bfloat16)] if first else []
    if last:
        scratch.append(VMEM((genes, rank), jnp.float32))
    ins = pinned(*fixed) + (list(carried) if first else pinned(*carried))
    work = len(tables) * block * genes
    out = pl.pallas_call(
        functools.partial(rows_kernel, tables, block, first, last, n_row),
        out_shape=tuple(out),
        in_specs=[IN_VMEM] * len(ins),
        out_specs=(IN_VMEM,) * len(out),
        scratch_shapes=scratch,
        compiler_params=params(),
        cost_estimate=cost(6 * work * rank, work * 2),
        name="block_rows",
    )(*ins)
    done, rest = list(out[: len(tables)]), list(out[len(tables) :])
    return done, rest if first or last else rest + list(carried[1:])


def lane_parts(genes, depth, n_row):
    if n_row != 4:
        return None
    pairs = [(2 * depth * (place // 2), 2 * depth * (place // 2 + 1)) for place in range(n_row)]
    low = [-(-begin // 128) * 128 for begin, _ in pairs]
    width = min(end // 128 * 128 - begin for begin, (_, end) in zip(low, pairs))
    if width <= 0 or any(begin not in (0, genes - width) for begin in low):
        return None
    return low, width, [width if begin == 0 else 0 for begin in low]


def lanes(table, width):
    return pl.ds(pl.multiple_of(pick("row", table), 128), width)


def influence(x, pred, bend):
    resid = x.astype(jnp.float32) - pred
    inside = jnp.maximum(1.0 - resid * resid * bend, 0.0)
    return (resid * (inside * inside)).astype(jnp.bfloat16)


def part_of_block(table, block, here, x_ref, f_ref, ft_ref, bend_ref, wide, scaled):
    step = tile_of(block, 256)
    origin = pick(LINES, table) * block
    tiles = [pl.ds(pl.multiple_of(origin + at, math.gcd(block, step)), step) for at in range(0, block, step)]
    bend = bend_ref[:, here]
    preds = [jnp.dot(f_ref[tile, :], wide, preferred_element_type=jnp.float32) for tile in tiles]
    infls = [influence(x_ref[tile, here], pred, bend) for tile, pred in zip(tiles, preds)]
    rows, total = [], None
    for tile, infl in zip(tiles, infls):
        cols = jnp.dot(ft_ref[:, tile], infl, preferred_element_type=jnp.float32)
        rows.append(jnp.dot(infl, scaled, preferred_element_type=jnp.float32))
        total = cols if total is None else total + cols
    return rows, total


def early_kernel(table, block, parts, x_ref, f_ref, ft_ref, bend_ref, shrink_ref, own, other, *refs):
    rows_out, total_out, wide_out, scaled_out, pair = refs
    low, width, _ = parts
    depth = own.shape[0]
    odd = lax.axis_index("row") % 2
    pair[pl.ds(pl.multiple_of(odd * depth, depth), depth), :] = own[...]
    pair[pl.ds(pl.multiple_of((1 - odd) * depth, depth), depth), :] = other[...]
    inset = [begin - 2 * depth * (place // 2) for place, begin in enumerate(low)]
    whole = pair[pl.ds(pl.multiple_of(pick("row", inset), math.gcd(*inset, 128)), width), :].astype(jnp.float32)
    here = lanes(low, width)
    wide = jnp.transpose(whole).astype(jnp.bfloat16)
    scaled = (whole * shrink_ref[here, :]).astype(jnp.bfloat16)
    wide_out[...] = wide
    scaled_out[...] = scaled
    rows, total = part_of_block(table, block, here, x_ref, f_ref, ft_ref, bend_ref, wide, scaled)
    for at, value in enumerate(rows):
        rows_out[at * value.shape[0] : (at + 1) * value.shape[0], :] = value
    total_out[...] = total


def rest_kernel(table, block, parts, n_row, x_ref, f_ref, ft_ref, bend_ref, shrink_ref, *refs):
    shares, (rows_in, total_in, wide_in, scaled_in) = refs[:n_row], refs[n_row : n_row + 4]
    rows_out, total_out, wide_out, scaled_out, piece = refs[n_row + 4 :]
    low, width, rest = parts
    me = lax.axis_index("row")
    depth = shares[0].shape[0]
    for hop in range(n_row):
        start = pl.multiple_of(source(me, hop, n_row) * depth, depth)
        piece[pl.ds(start, depth), :] = shares[hop][...]
    here = lanes(rest, n_row * depth - width)
    whole = piece[here, :].astype(jnp.float32)
    wide = jnp.transpose(whole).astype(jnp.bfloat16)
    scaled = (whole * shrink_ref[here, :]).astype(jnp.bfloat16)
    rows, total = part_of_block(table, block, here, x_ref, f_ref, ft_ref, bend_ref, wide, scaled)
    for at, value in enumerate(rows):
        span = slice(at * value.shape[0], (at + 1) * value.shape[0])
        rows_out[span, :] = (rows_in[span, :] + value).astype(rows_out.dtype)
    done = lanes(low, width)
    total_out[:, here] = total
    total_out[:, done] = total_in[...]
    wide_out[:, here] = wide
    wide_out[:, done] = wide_in[...]
    scaled_out[here, :] = scaled
    scaled_out[done, :] = scaled_in[...]


def first_block(table, block, parts, n_row, fixed, shares):
    genes, rank = fixed[4].shape
    depth = genes // n_row
    width = parts[1]
    ins = pinned(*fixed)
    early = pl.pallas_call(
        functools.partial(early_kernel, table, block, parts),
        out_shape=(
            VMEM((block, rank), jnp.float32),
            VMEM((rank, width), jnp.float32),
            VMEM((rank, width), jnp.bfloat16),
            VMEM((width, rank), jnp.bfloat16),
        ),
        in_specs=[IN_VMEM] * 7,
        out_specs=(IN_VMEM,) * 4,
        scratch_shapes=[VMEM((2 * depth, rank), jnp.bfloat16)],
        compiler_params=params(),
        cost_estimate=cost(12 * block * width * rank, block * width * 4),
        name="early_part",
    )(*ins, *shares[:2])
    done, *carried = pl.pallas_call(
        functools.partial(rest_kernel, table, block, parts, n_row),
        out_shape=(
            jax.ShapeDtypeStruct((block, rank), jnp.bfloat16),
            VMEM((rank, genes), jnp.float32),
            VMEM((rank, genes), jnp.bfloat16),
            VMEM((genes, rank), jnp.bfloat16),
        ),
        in_specs=[IN_VMEM] * (9 + n_row),
        out_specs=(IN_VMEM,) * 4,
        scratch_shapes=[VMEM((genes, rank), jnp.bfloat16)],
        compiler_params=params(),
        cost_estimate=cost(12 * block * (genes - width) * rank, block * (genes - width) * 4),
        name="rest_part",
    )(*ins, *shares, *pinned(*early))
    return [done], carried


def swap_row(value, hop, size):
    return lax.ppermute(value, "row", [(me, partner(me, hop, size)) for me in range(size)])


def ring_of(size):
    return [*range(0, size, 2), *reversed(range(1, size, 2))]


def steps_of(size):
    ahead = [(1, distance) for distance in range(size // 2, 0, -1)]
    back = [(-1, distance) for distance in range((size - 1) // 2, 0, -1)]
    return [step for pair in itertools.zip_longest(ahead, back) for step in pair if step]


def around(size, rows, hops):
    ring = ring_of(size)
    ways = [-hops if row % 2 else hops for row in range(rows)]
    return tuple(ring[(ring.index(place) + way) % size] for place in range(size) for way in ways)


def plus(wide, narrow):
    return wide.astype(jnp.float32) + narrow.astype(jnp.float32)


def finish_kernel(n_ends, n_parts, *refs):
    n_ins = n_ends + n_parts + 3
    ins, outs = refs[:n_ins], refs[n_ins : n_ins + 3 + bool(n_ends)]
    *held, sems = refs[n_ins + len(outs) :]
    ends, parts = ins[:n_ends], ins[n_ends : n_ends + n_parts]
    factor, first, second = ins[n_ends + n_parts :]
    copies = []

    def send(at, span, value):
        held[at][span, :] = value
        copies.append(pltpu.make_async_copy(held[at].at[span, :], outs[at].at[span, :], sems.at[len(copies)]))
        copies[-1].start()

    if ends:
        step = tile_of(ends[0].shape[0], 256)
        for low in range(0, ends[0].shape[0], step):
            span = pl.ds(low, step)
            rows = ends[0][span, :]
            for end in ends[1:]:
                rows = plus(rows, end[span, :])
            send(3, span, rows)
    grad = parts[0][...]
    for part in parts[1:]:
        grad = plus(grad, part[...])
    span = pl.ds(0, grad.shape[0])
    new_first = beta_one * first[...] + (1.0 - beta_one) * grad
    new_second = beta_two * second[...] + (1.0 - beta_two) * grad * grad
    send(1, span, new_first)
    send(2, span, new_second)
    first_hat = new_first / (1.0 - beta_one**10)
    second_hat = new_second / (1.0 - beta_two**10)
    send(0, span, factor[...] - learn_rate * first_hat / (jnp.sqrt(second_hat) + adam_eps))
    for copy in copies:
        copy.wait()


def finish(ends, parts, factor, first, second):
    ins = [*ends, *parts, factor, first, second]
    shapes = [factor, factor, factor] + list(ends[:1])
    n_copies = 3 + (ends[0].shape[0] // tile_of(ends[0].shape[0], 256) if ends else 0)
    return pl.pallas_call(
        functools.partial(finish_kernel, len(ends), len(parts)),
        out_shape=tuple(jax.ShapeDtypeStruct(like.shape, jnp.float32) for like in shapes),
        in_specs=[IN_VMEM] * len(ins),
        out_specs=(IN_ANY,) * len(shapes),
        scratch_shapes=[VMEM(like.shape, jnp.float32) for like in shapes] + [pltpu.SemaphoreType.DMA((n_copies,))],
        compiler_params=params(),
        cost_estimate=cost(20 * factor.size, sum(4 * a.size for a in ins)),
        name="finish",
    )(*ins)


def local(x_slab, cell_factor, row_index, gene_scale, gene_factor, first_moment, second_moment):
    rows_dev, genes_dev = x_slab.shape
    n_gene = lax.axis_size("gene")
    n_row = lax.axis_size("row")
    block = rows_dev // n_gene
    scale_k = 4.0 / math.sqrt(genes_dev * n_gene)
    factor_bf = gene_factor.astype(jnp.bfloat16)
    shares = [factor_bf] + [swap_row(factor_bf, hop, n_row) for hop in range(1, n_row)]
    fixed = prepare(x_slab, row_index, cell_factor, gene_scale, scale_k)
    adam = (gene_factor, first_moment, second_moment)

    if n_gene == 1 or n_gene > RING_MOST or block % 128:
        (rows,), parts = block_rows([(0,)], [jnp.float32], rows_dev, True, True, n_row, fixed, shares)
        grad_cells = lax.psum_scatter(rows, "gene", scatter_dimension=0, tiled=True)
        others = [swap_row(parts[hop], hop, n_row) for hop in range(1, n_row)]
        return (grad_cells, *finish([], [parts[0], *others], *adam))

    steps = steps_of(n_gene)
    tables = [around(n_gene, n_row, way * distance) for way, distance in steps] + [around(n_gene, n_row, 0)]
    kinds = [jnp.bfloat16] * len(steps) + [jnp.float32]
    cuts = [0, 1, 2, len(tables)] if len(steps) > 2 else [0, 1, len(tables)]
    parted = lane_parts(genes_dev, genes_dev // n_row, n_row)
    carried, blocks = shares, []
    for low, high in zip(cuts, cuts[1:]):
        last = high == len(tables)
        if low == 0 and parted:
            done, carried = first_block(tables[0], block, parted, n_row, fixed, shares)
            blocks += done
            continue
        done, carried = block_rows(tables[low:high], kinds[low:high], block, low == 0, last, n_row, fixed, carried)
        blocks += done
    parts = carried

    came = {}
    for (way, _), own in zip(steps, blocks):
        if way in came:
            own = plus(own, came[way]).astype(jnp.bfloat16)
        came[way] = lax.ppermute(own, LINES, [(at, to * n_row + at % n_row) for at, to in enumerate(around(n_gene, n_row, way))])
    others = [swap_row(parts[hop], hop, n_row) for hop in range(1, n_row)]
    *adam_out, grad_cells = finish([blocks[-1], *came.values()], [parts[0], *others], *adam)
    return (grad_cells, *adam_out)


def solution(mesh):
    in_specs = (
        P(("grp", "row"), "gene"),
        P(("grp", "row"), None),
        P(("grp", "row")),
        P(("grp", "gene")),
        P(("grp", "gene", "row"), None),
        P(("grp", "gene", "row"), None),
        P(("grp", "gene", "row"), None),
    )
    out_specs = (
        P(("grp", "row", "gene"), None),
        P(("grp", "gene", "row"), None),
        P(("grp", "gene", "row"), None),
        P(("grp", "gene", "row"), None),
    )
    return jax.shard_map(local, mesh=mesh, in_specs=in_specs, out_specs=out_specs, check_vma=False)
```

```python
import functools
import itertools
import math

import jax
import jax.numpy as jnp
from jax import lax
from jax.experimental import pallas as pl
from jax.experimental.pallas import tpu as pltpu
from jax.sharding import PartitionSpec as P

tukey_c = 4.685
beta_one = 0.9
beta_two = 0.999
learn_rate = 0.02
adam_eps = 1e-08

RING_MOST = 8
VMEM = pltpu.VMEM
IN_VMEM = pl.BlockSpec(memory_space=VMEM)
IN_ANY = pl.BlockSpec(memory_space=pl.ANY)


def tile_of(rows, most):
    best = [t for t in range(128, most + 1, 128) if rows % t == 0]
    return best[-1] if best else rows


def params():
    return pltpu.CompilerParams(vmem_limit_bytes=24 * 1024 * 1024)


def cost(flops, moved):
    return pl.CostEstimate(flops=int(flops), bytes_accessed=int(moved), transcendentals=0)


def pinned(*arrays):
    return [pltpu.with_memory_space_constraint(a, VMEM) for a in arrays]


def prepare_kernel(scale_k, x_in, index_in, cell_in, scale_in, x_out, f_out, ft_out, bend_out, shrink_out, index, cell, scale, sems):
    loads = [
        pltpu.make_async_copy(src, dst, sems.at[at])
        for at, (src, dst) in enumerate(((scale_in, scale), (cell_in, cell), (index_in, index), (x_in, x_out)))
    ]
    for load in loads:
        load.start()
    cells, rank = cell.shape
    rows = index.shape[0]
    genes = scale.shape[0]
    loads[0].wait()
    inverse = 1.0 / scale[...].reshape(1, genes)
    bend_out[...] = (inverse * inverse) * (1.0 / (tukey_c * tukey_c))
    shrink_out[...] = jnp.transpose(jnp.broadcast_to(-scale_k * (inverse * inverse), (rank, genes)))
    loads[1].wait()
    table = jnp.transpose(cell[...].astype(jnp.float32)).astype(jnp.bfloat16)
    base = lax.axis_index("row") * cells
    loads[2].wait()
    step = tile_of(rows, 512)
    for at in range(0, rows, step):
        local = index[at : at + step].reshape(1, step) - base
        hot = lax.broadcasted_iota(jnp.int32, (cells, step), 0) == local
        hot = jnp.where(hot, 1.0, 0.0).astype(jnp.bfloat16)
        picked = jnp.dot(table, hot, preferred_element_type=jnp.float32)
        ft_out[:, at : at + step] = picked.astype(jnp.bfloat16)
        f_out[at : at + step, :] = jnp.transpose(picked).astype(jnp.bfloat16)
    loads[3].wait()


def prepare(x_slab, row_index, cell_factor, gene_scale, scale_k):
    rows, genes = x_slab.shape
    cells, rank = cell_factor.shape
    ins = (x_slab, row_index, cell_factor, gene_scale)
    return pl.pallas_call(
        functools.partial(prepare_kernel, scale_k),
        out_shape=(
            VMEM((rows, genes), jnp.bfloat16),
            VMEM((rows, rank), jnp.bfloat16),
            VMEM((rank, rows), jnp.bfloat16),
            VMEM((1, genes), jnp.float32),
            VMEM((genes, rank), jnp.float32),
        ),
        in_specs=[IN_ANY] * 4,
        out_specs=(IN_VMEM,) * 5,
        scratch_shapes=[
            VMEM((rows,), jnp.int32),
            VMEM((cells, rank), jnp.bfloat16),
            VMEM((genes,), jnp.float32),
            pltpu.SemaphoreType.DMA((4,)),
        ],
        compiler_params=params(),
        cost_estimate=cost(8 * rows * cells * rank, 8 * rows * genes * 2),
        name="prepare",
    )(*(pltpu.with_memory_space_constraint(a, pltpu.HBM) for a in ins))


def pick(axis, table):
    me = lax.axis_index(axis)
    value = jnp.int32(table[0])
    for place, entry in enumerate(table[1:], 1):
        value = jnp.where(me == place, jnp.int32(entry), value)
    return value


def partner(me, hop, size):
    return me ^ hop if size & (size - 1) == 0 else (me + hop) % size


def source(me, hop, size):
    return me ^ hop if size & (size - 1) == 0 else (me + size - hop) % size


def rows_kernel(tables, block, first, last, n_row, *refs):
    refs = list(refs)
    take = lambda count: [refs.pop(0) for _ in range(count)]
    x_ref, f_ref, ft_ref, bend_ref, shrink_ref = take(5)
    shares = take(n_row) if first else None
    carried_in = None if first else take(3)
    rows_out = take(len(tables))
    carried_out = None if last else take(3 if first else 1)
    parts_out = take(n_row) if last else None
    me = lax.axis_index("row")

    if first:
        (piece,) = take(1)
        depth = shares[0].shape[0]
        for hop in range(n_row):
            start = pl.multiple_of(source(me, hop, n_row) * depth, depth)
            piece[pl.ds(start, depth), :] = shares[hop][...]
        whole = piece[...].astype(jnp.float32)
        wide = jnp.transpose(whole).astype(jnp.bfloat16)
        scaled = (whole * shrink_ref[...]).astype(jnp.bfloat16)
        total = None
    else:
        total, wide, scaled = (ref[...] for ref in carried_in)

    bend = bend_ref[...]
    step = tile_of(block, 256)
    tiles = []
    for table, out in zip(tables, rows_out):
        origin = pick("gene", table) * block if len(table) > 1 else 0
        for at in range(0, block, step):
            start = origin + at
            if len(table) > 1:
                start = pl.multiple_of(start, math.gcd(block, step))
            tiles.append((out, at, pl.ds(start, step)))

    def predict(here):
        return jnp.dot(f_ref[here, :], wide, preferred_element_type=jnp.float32)

    def gradients(tile, infl, total):
        out, at, here = tile
        cols = jnp.dot(ft_ref[:, here], infl, preferred_element_type=jnp.float32)
        out[at : at + step, :] = jnp.dot(infl, scaled, preferred_element_type=jnp.float32).astype(out.dtype)
        return cols if total is None else total + cols

    pred = predict(tiles[0][2])
    infl = None
    for at, tile in enumerate(tiles):
        later = predict(tiles[at + 1][2]) if at + 1 < len(tiles) else None
        now = influence(x_ref[tile[2], :], pred, bend)
        if at:
            total = gradients(tiles[at - 1], infl, total)
        infl, pred = now, later
    total = gradients(tiles[-1], infl, total)

    if first and not last:
        carried_out[1][...] = wide
        carried_out[2][...] = scaled
    if not last:
        carried_out[0][...] = total
        return
    (turned,) = take(1)
    turned[...] = jnp.transpose(total) * shrink_ref[...]
    depth = parts_out[0].shape[0]
    for hop in range(n_row):
        start = pl.multiple_of(partner(me, hop, n_row) * depth, depth)
        parts_out[hop][...] = turned[pl.ds(start, depth), :].astype(parts_out[hop].dtype)


def block_rows(tables, kinds, block, first, last, n_row, fixed, carried):
    genes, rank = fixed[4].shape
    out = [jax.ShapeDtypeStruct((block, rank), kind) for kind in kinds]
    if last:
        out += [jax.ShapeDtypeStruct((genes // n_row, rank), jnp.bfloat16 if hop else jnp.float32) for hop in range(n_row)]
    else:
        out += [VMEM((rank, genes), jnp.float32)]
    if first and not last:
        out += [VMEM((rank, genes), jnp.bfloat16), VMEM((genes, rank), jnp.bfloat16)]
    scratch = [VMEM((genes, rank), jnp.bfloat16)] if first else []
    if last:
        scratch.append(VMEM((genes, rank), jnp.float32))
    ins = pinned(*fixed) + (list(carried) if first else pinned(*carried))
    work = len(tables) * block * genes
    out = pl.pallas_call(
        functools.partial(rows_kernel, tables, block, first, last, n_row),
        out_shape=tuple(out),
        in_specs=[IN_VMEM] * len(ins),
        out_specs=(IN_VMEM,) * len(out),
        scratch_shapes=scratch,
        compiler_params=params(),
        cost_estimate=cost(6 * work * rank, work * 2),
        name="block_rows",
    )(*ins)
    done, rest = list(out[: len(tables)]), list(out[len(tables) :])
    return done, rest if first or last else rest + list(carried[1:])


def first_row(table, block):
    return pl.multiple_of(pick("gene", table) * block, block) if len(table) > 1 else 0


def gather(cells, local):
    hot = lax.broadcasted_iota(jnp.int32, (cells.shape[1], local.shape[1]), 0) == local
    hot = jnp.where(hot, 1.0, 0.0).astype(jnp.bfloat16)
    return jnp.dot(cells, hot, preferred_element_type=jnp.float32)


def prepare_first_kernel(scale_k, table, block, x_in, index_in, cell_in, scale_in, *refs):
    x_out, f_out, ft_out, bend_out, shrink_out, index, flat, cell, scale, sems = refs
    here = pl.ds(first_row(table, block), block)
    pairs = ((scale_in, scale), (cell_in, cell), (index_in, index), (x_in.at[here, :], x_out))
    loads = [pltpu.make_async_copy(src, dst, sems.at[at]) for at, (src, dst) in enumerate(pairs)]
    for load in loads:
        load.start()
    cells, rank = cell.shape
    rows = index.shape[0]
    genes = scale.shape[0]
    loads[0].wait()
    inverse = 1.0 / scale[...].reshape(1, genes)
    bend_out[...] = (inverse * inverse) * (1.0 / (tukey_c * tukey_c))
    shrink_out[...] = jnp.transpose(jnp.broadcast_to(-scale_k * (inverse * inverse), (rank, genes)))
    loads[1].wait()
    turned = jnp.transpose(cell[...].astype(jnp.float32)).astype(jnp.bfloat16)
    loads[2].wait()
    step = tile_of(rows, 512)
    for at in range(0, rows, step):
        flat[:, at : at + step] = index[at : at + step].reshape(1, step) - lax.axis_index("row") * cells
    step = tile_of(block, 256)
    for at in range(0, block, step):
        start = first_row(table, block) + at
        if len(table) > 1:
            start = pl.multiple_of(start, math.gcd(block, step))
        picked = gather(turned, flat[:, pl.ds(start, step)])
        ft_out[:, at : at + step] = picked.astype(jnp.bfloat16)
        f_out[at : at + step, :] = jnp.transpose(picked).astype(jnp.bfloat16)
    loads[3].wait()


def prepare_first(table, block, x_slab, row_index, cell_factor, gene_scale, scale_k):
    rows, genes = x_slab.shape
    cells, rank = cell_factor.shape
    ins = (x_slab, row_index, cell_factor, gene_scale)
    return pl.pallas_call(
        functools.partial(prepare_first_kernel, scale_k, table, block),
        out_shape=(
            VMEM((block, genes), jnp.bfloat16),
            VMEM((block, rank), jnp.bfloat16),
            VMEM((rank, block), jnp.bfloat16),
            VMEM((1, genes), jnp.float32),
            VMEM((genes, rank), jnp.float32),
        ),
        in_specs=[IN_ANY] * 4,
        out_specs=(IN_VMEM,) * 5,
        scratch_shapes=[
            VMEM((rows,), jnp.int32),
            VMEM((1, rows), jnp.int32),
            VMEM((cells, rank), jnp.bfloat16),
            VMEM((genes,), jnp.float32),
            pltpu.SemaphoreType.DMA((4,)),
        ],
        compiler_params=params(),
        cost_estimate=cost(32 * block * cells * rank, 64 * block * genes),
        name="prepare_first",
    )(*(pltpu.with_memory_space_constraint(a, pltpu.HBM) for a in ins))


def lane_parts(genes, depth, n_row):
    if n_row != 4:
        return None
    pairs = [(2 * depth * (place // 2), 2 * depth * (place // 2 + 1)) for place in range(n_row)]
    low = [-(-begin // 128) * 128 for begin, _ in pairs]
    width = min(end // 128 * 128 - begin for begin, (_, end) in zip(low, pairs))
    if width <= 0 or any(begin not in (0, genes - width) for begin in low):
        return None
    return low, width, [width if begin == 0 else 0 for begin in low]


def lanes(table, width):
    return pl.ds(pl.multiple_of(pick("row", table), 128), width)


def influence(x, pred, bend):
    resid = x.astype(jnp.float32) - pred
    inside = jnp.maximum(1.0 - resid * resid * bend, 0.0)
    return (resid * (inside * inside)).astype(jnp.bfloat16)


def add_to(total, cols):
    return cols if total is None else total + cols


def over_lanes(here, x_ref, f_ref, ft_ref, bend_ref, wide, scaled):
    block = x_ref.shape[0]
    step = tile_of(block, 256)
    tiles = [pl.ds(at, step) for at in range(0, block, step)]
    bend = bend_ref[:, here]
    preds = [jnp.dot(f_ref[tile, :], wide, preferred_element_type=jnp.float32) for tile in tiles]
    infls = [influence(x_ref[tile, here], pred, bend) for tile, pred in zip(tiles, preds)]
    rows, total = [], None
    for tile, infl in zip(tiles, infls):
        rows.append((tile, jnp.dot(infl, scaled, preferred_element_type=jnp.float32)))
        total = add_to(total, jnp.dot(ft_ref[:, tile], infl, preferred_element_type=jnp.float32))
    return rows, total


def early_kernel(parts, x_ref, f_ref, ft_ref, bend_ref, shrink_ref, own, other, *refs):
    rows_out, total_out, wide_out, scaled_out, pair = refs
    low, width, _ = parts
    depth = own.shape[0]
    odd = lax.axis_index("row") % 2
    pair[pl.ds(pl.multiple_of(odd * depth, depth), depth), :] = own[...]
    pair[pl.ds(pl.multiple_of((1 - odd) * depth, depth), depth), :] = other[...]
    inset = [begin - 2 * depth * (place // 2) for place, begin in enumerate(low)]
    whole = pair[pl.ds(pl.multiple_of(pick("row", inset), math.gcd(*inset, 128)), width), :].astype(jnp.float32)
    here = lanes(low, width)
    wide = jnp.transpose(whole).astype(jnp.bfloat16)
    scaled = (whole * shrink_ref[here, :]).astype(jnp.bfloat16)
    wide_out[...] = wide
    scaled_out[...] = scaled
    rows, total = over_lanes(here, x_ref, f_ref, ft_ref, bend_ref, wide, scaled)
    for tile, value in rows:
        rows_out[tile, :] = value
    total_out[...] = total


def rest_kernel(parts, n_row, x_ref, f_ref, ft_ref, bend_ref, shrink_ref, *refs):
    shares, refs = refs[:n_row], refs[n_row:]
    if parts:
        (rows_in, total_in, wide_in, scaled_in), refs = refs[:4], refs[4:]
    rows_out, total_out, wide_out, scaled_out, piece = refs
    me = lax.axis_index("row")
    depth = shares[0].shape[0]
    for hop in range(n_row):
        start = pl.multiple_of(source(me, hop, n_row) * depth, depth)
        piece[pl.ds(start, depth), :] = shares[hop][...]
    here = lanes(parts[2], n_row * depth - parts[1]) if parts else pl.ds(0, n_row * depth)
    whole = piece[here, :].astype(jnp.float32)
    wide = jnp.transpose(whole).astype(jnp.bfloat16)
    scaled = (whole * shrink_ref[here, :]).astype(jnp.bfloat16)
    rows, total = over_lanes(here, x_ref, f_ref, ft_ref, bend_ref, wide, scaled)
    for tile, value in rows:
        rows_out[tile, :] = (rows_in[tile, :] + value if parts else value).astype(rows_out.dtype)
    total_out[:, here] = total
    wide_out[:, here] = wide
    scaled_out[here, :] = scaled
    if parts:
        done = lanes(parts[0], parts[1])
        total_out[:, done] = total_in[...]
        wide_out[:, done] = wide_in[...]
        scaled_out[done, :] = scaled_in[...]


def first_block(kind, parts, n_row, fixed, shares):
    block, genes = fixed[0].shape
    rank = fixed[1].shape[1]
    width = parts[1] if parts else 0
    ins = pinned(*fixed)
    early = []
    if parts:
        early = pl.pallas_call(
            functools.partial(early_kernel, parts),
            out_shape=(
                VMEM((block, rank), jnp.float32),
                VMEM((rank, width), jnp.float32),
                VMEM((rank, width), jnp.bfloat16),
                VMEM((width, rank), jnp.bfloat16),
            ),
            in_specs=[IN_VMEM] * 7,
            out_specs=(IN_VMEM,) * 4,
            scratch_shapes=[VMEM((2 * (genes // n_row), rank), jnp.bfloat16)],
            compiler_params=params(),
            cost_estimate=cost(12 * block * width * rank, block * width * 4),
            name="early_part",
        )(*ins, *shares[:2])
    done, *carried = pl.pallas_call(
        functools.partial(rest_kernel, parts, n_row),
        out_shape=(
            jax.ShapeDtypeStruct((block, rank), kind),
            VMEM((rank, genes), jnp.float32),
            VMEM((rank, genes), jnp.bfloat16),
            VMEM((genes, rank), jnp.bfloat16),
        ),
        in_specs=[IN_VMEM] * (5 + n_row + len(early)),
        out_specs=(IN_VMEM,) * 4,
        scratch_shapes=[VMEM((genes, rank), jnp.bfloat16)],
        compiler_params=params(),
        cost_estimate=cost(12 * block * (genes - width) * rank, block * (genes - width) * 4),
        name="rest_part",
    )(*ins, *shares, *pinned(*early))
    return done, carried


def swap_row(value, hop, size):
    return lax.ppermute(value, "row", [(me, partner(me, hop, size)) for me in range(size)])


def ring_of(size):
    return [*range(0, size, 2), *reversed(range(1, size, 2))]


def steps_of(size):
    ahead = [(1, distance) for distance in range(size // 2, 0, -1)]
    back = [(-1, distance) for distance in range((size - 1) // 2, 0, -1)]
    return [step for pair in itertools.zip_longest(ahead, back) for step in pair if step]


def around(size, hops):
    ring = ring_of(size)
    return tuple(ring[(ring.index(place) + hops) % size] for place in range(size))


def plus(wide, narrow):
    return wide.astype(jnp.float32) + narrow.astype(jnp.float32)


def finish_kernel(n_ends, n_parts, *refs):
    n_ins = n_ends + n_parts + 3
    ins, outs = refs[:n_ins], refs[n_ins : n_ins + 3 + bool(n_ends)]
    *held, sems = refs[n_ins + len(outs) :]
    ends, parts = ins[:n_ends], ins[n_ends : n_ends + n_parts]
    factor, first, second = ins[n_ends + n_parts :]
    copies = []

    def send(at, span, value):
        held[at][span, :] = value
        copies.append(pltpu.make_async_copy(held[at].at[span, :], outs[at].at[span, :], sems.at[len(copies)]))
        copies[-1].start()

    if ends:
        step = tile_of(ends[0].shape[0], 256)
        for low in range(0, ends[0].shape[0], step):
            span = pl.ds(low, step)
            rows = ends[0][span, :]
            for end in ends[1:]:
                rows = plus(rows, end[span, :])
            send(3, span, rows)
    grad = parts[0][...]
    for part in parts[1:]:
        grad = plus(grad, part[...])
    span = pl.ds(0, grad.shape[0])
    new_first = beta_one * first[...] + (1.0 - beta_one) * grad
    new_second = beta_two * second[...] + (1.0 - beta_two) * grad * grad
    send(1, span, new_first)
    send(2, span, new_second)
    first_hat = new_first / (1.0 - beta_one**10)
    second_hat = new_second / (1.0 - beta_two**10)
    send(0, span, factor[...] - learn_rate * first_hat / (jnp.sqrt(second_hat) + adam_eps))
    for copy in copies:
        copy.wait()


def finish(ends, parts, factor, first, second):
    ins = [*ends, *parts, factor, first, second]
    shapes = [factor, factor, factor] + list(ends[:1])
    n_copies = 3 + (ends[0].shape[0] // tile_of(ends[0].shape[0], 256) if ends else 0)
    return pl.pallas_call(
        functools.partial(finish_kernel, len(ends), len(parts)),
        out_shape=tuple(jax.ShapeDtypeStruct(like.shape, jnp.float32) for like in shapes),
        in_specs=[IN_VMEM] * len(ins),
        out_specs=(IN_ANY,) * len(shapes),
        scratch_shapes=[VMEM(like.shape, jnp.float32) for like in shapes] + [pltpu.SemaphoreType.DMA((n_copies,))],
        compiler_params=params(),
        cost_estimate=cost(20 * factor.size, sum(4 * a.size for a in ins)),
        name="finish",
    )(*ins)


def local(x_slab, cell_factor, row_index, gene_scale, gene_factor, first_moment, second_moment):
    rows_dev, genes_dev = x_slab.shape
    n_gene = lax.axis_size("gene")
    n_row = lax.axis_size("row")
    block = rows_dev // n_gene
    scale_k = 4.0 / math.sqrt(genes_dev * n_gene)
    factor_bf = gene_factor.astype(jnp.bfloat16)
    shares = [factor_bf] + [swap_row(factor_bf, hop, n_row) for hop in range(1, n_row)]
    adam = (gene_factor, first_moment, second_moment)
    values = (x_slab, row_index, cell_factor)

    if n_gene == 1 or n_gene > RING_MOST or block % 128:
        fixed = prepare(*values, gene_scale, scale_k)
        (rows,), parts = block_rows([(0,)], [jnp.float32], rows_dev, True, True, n_row, fixed, shares)
        grad_cells = lax.psum_scatter(rows, "gene", scatter_dimension=0, tiled=True)
        others = [swap_row(parts[hop], hop, n_row) for hop in range(1, n_row)]
        return (grad_cells, *finish([], [parts[0], *others], *adam))

    steps = steps_of(n_gene)
    tables = [around(n_gene, way * distance) for way, distance in steps] + [tuple(range(n_gene))]
    kinds = [jnp.bfloat16] * len(steps) + [jnp.float32]
    parted = lane_parts(genes_dev, genes_dev // n_row, n_row)
    near = prepare_first(tables[0], block, *values, gene_scale, scale_k)
    done, carried = first_block(kinds[0], parted, n_row, near, shares)
    blocks = [done]
    late_scale, _ = lax.optimization_barrier((gene_scale, carried[0]))
    fixed = prepare(*values, late_scale, scale_k)
    cuts = [1, 2, len(tables)] if len(steps) > 2 else [1, len(tables)]
    for low, high in zip(cuts, cuts[1:]):
        last = high == len(tables)
        done, carried = block_rows(tables[low:high], kinds[low:high], block, False, last, n_row, fixed, carried)
        blocks += done
    parts = carried

    came = {}
    for (way, _), own in zip(steps, blocks):
        if way in came:
            own = plus(own, came[way]).astype(jnp.bfloat16)
        came[way] = lax.ppermute(own, "gene", list(enumerate(around(n_gene, way))))
    others = [swap_row(parts[hop], hop, n_row) for hop in range(1, n_row)]
    *adam_out, grad_cells = finish([blocks[-1], *came.values()], [parts[0], *others], *adam)
    return (grad_cells, *adam_out)


def solution(mesh):
    in_specs = (
        P(("grp", "row"), "gene"),
        P(("grp", "row"), None),
        P(("grp", "row")),
        P(("grp", "gene")),
        P(("grp", "gene", "row"), None),
        P(("grp", "gene", "row"), None),
        P(("grp", "gene", "row"), None),
    )
    out_specs = (
        P(("grp", "row", "gene"), None),
        P(("grp", "gene", "row"), None),
        P(("grp", "gene", "row"), None),
        P(("grp", "gene", "row"), None),
    )
    return jax.shard_map(local, mesh=mesh, in_specs=in_specs, out_specs=out_specs, check_vma=False)
```

```python
import functools
import itertools
import math

import jax
import jax.numpy as jnp
from jax import lax
from jax.experimental import pallas as pl
from jax.experimental.pallas import tpu as pltpu
from jax.sharding import PartitionSpec as P

tukey_c = 4.685
beta_one = 0.9
beta_two = 0.999
learn_rate = 0.02
adam_eps = 1e-08

RING_MOST = 8
VMEM = pltpu.VMEM
IN_VMEM = pl.BlockSpec(memory_space=VMEM)
IN_ANY = pl.BlockSpec(memory_space=pl.ANY)


def tile_of(rows, most):
    best = [t for t in range(128, most + 1, 128) if rows % t == 0]
    return best[-1] if best else rows


def params():
    return pltpu.CompilerParams(vmem_limit_bytes=24 * 1024 * 1024)


def cost(flops, moved):
    return pl.CostEstimate(flops=int(flops), bytes_accessed=int(moved), transcendentals=0)


def pinned(*arrays):
    return [pltpu.with_memory_space_constraint(a, VMEM) for a in arrays]


def prepare_kernel(scale_k, x_in, index_in, cell_in, scale_in, x_out, f_out, ft_out, bend_out, shrink_out, index, cell, scale, sems):
    loads = [
        pltpu.make_async_copy(src, dst, sems.at[at])
        for at, (src, dst) in enumerate(((scale_in, scale), (cell_in, cell), (index_in, index), (x_in, x_out)))
    ]
    for load in loads:
        load.start()
    cells, rank = cell.shape
    rows = index.shape[0]
    genes = scale.shape[0]
    loads[0].wait()
    inverse = 1.0 / scale[...].reshape(1, genes)
    bend_out[...] = (inverse * inverse) * (1.0 / (tukey_c * tukey_c))
    shrink_out[...] = jnp.transpose(jnp.broadcast_to(-scale_k * (inverse * inverse), (rank, genes)))
    loads[1].wait()
    table = jnp.transpose(cell[...].astype(jnp.float32)).astype(jnp.bfloat16)
    base = lax.axis_index("row") * cells
    loads[2].wait()
    step = tile_of(rows, 512)
    for at in range(0, rows, step):
        local = index[at : at + step].reshape(1, step) - base
        hot = lax.broadcasted_iota(jnp.int32, (cells, step), 0) == local
        hot = jnp.where(hot, 1.0, 0.0).astype(jnp.bfloat16)
        picked = jnp.dot(table, hot, preferred_element_type=jnp.float32)
        ft_out[:, at : at + step] = picked.astype(jnp.bfloat16)
        f_out[at : at + step, :] = jnp.transpose(picked).astype(jnp.bfloat16)
    loads[3].wait()


def prepare(x_slab, row_index, cell_factor, gene_scale, scale_k):
    rows, genes = x_slab.shape
    cells, rank = cell_factor.shape
    ins = (x_slab, row_index, cell_factor, gene_scale)
    return pl.pallas_call(
        functools.partial(prepare_kernel, scale_k),
        out_shape=(
            VMEM((rows, genes), jnp.bfloat16),
            VMEM((rows, rank), jnp.bfloat16),
            VMEM((rank, rows), jnp.bfloat16),
            VMEM((1, genes), jnp.float32),
            VMEM((genes, rank), jnp.float32),
        ),
        in_specs=[IN_ANY] * 4,
        out_specs=(IN_VMEM,) * 5,
        scratch_shapes=[
            VMEM((rows,), jnp.int32),
            VMEM((cells, rank), jnp.bfloat16),
            VMEM((genes,), jnp.float32),
            pltpu.SemaphoreType.DMA((4,)),
        ],
        compiler_params=params(),
        cost_estimate=cost(2 * rows * cells * rank, 2 * rows * genes * 2),
        name="prepare",
    )(*(pltpu.with_memory_space_constraint(a, pltpu.HBM) for a in ins))


def pick(axis, table):
    me = lax.axis_index(axis)
    value = jnp.int32(table[0])
    for place, entry in enumerate(table[1:], 1):
        value = jnp.where(me == place, jnp.int32(entry), value)
    return value


def partner(me, hop, size):
    return me ^ hop if size & (size - 1) == 0 else (me + hop) % size


def source(me, hop, size):
    return me ^ hop if size & (size - 1) == 0 else (me + size - hop) % size


def rows_kernel(tables, block, first, last, n_row, *refs):
    refs = list(refs)
    take = lambda count: [refs.pop(0) for _ in range(count)]
    x_ref, f_ref, ft_ref, bend_ref, shrink_ref = take(5)
    shares = take(n_row) if first else None
    carried_in = None if first else take(3)
    rows_out = take(len(tables))
    carried_out = None if last else take(3 if first else 1)
    parts_out = take(n_row) if last else None
    me = lax.axis_index("row")

    if first:
        (piece,) = take(1)
        depth = shares[0].shape[0]
        for hop in range(n_row):
            start = pl.multiple_of(source(me, hop, n_row) * depth, depth)
            piece[pl.ds(start, depth), :] = shares[hop][...]
        whole = piece[...].astype(jnp.float32)
        wide = jnp.transpose(whole).astype(jnp.bfloat16)
        scaled = (whole * shrink_ref[...]).astype(jnp.bfloat16)
        total = None
    else:
        total, wide, scaled = (ref[...] for ref in carried_in)

    bend = bend_ref[...]
    step = tile_of(block, 256)
    tiles = []
    for table, out in zip(tables, rows_out):
        origin = pick("gene", table) * block if len(table) > 1 else 0
        for at in range(0, block, step):
            start = origin + at
            if len(table) > 1:
                start = pl.multiple_of(start, math.gcd(block, step))
            tiles.append((out, at, pl.ds(start, step)))

    def predict(here):
        return jnp.dot(f_ref[here, :], wide, preferred_element_type=jnp.float32)

    def gradients(tile, infl, total):
        out, at, here = tile
        cols = jnp.dot(ft_ref[:, here], infl, preferred_element_type=jnp.float32)
        out[at : at + step, :] = jnp.dot(infl, scaled, preferred_element_type=jnp.float32).astype(out.dtype)
        return cols if total is None else total + cols

    pred = predict(tiles[0][2])
    infl = None
    for at, tile in enumerate(tiles):
        later = predict(tiles[at + 1][2]) if at + 1 < len(tiles) else None
        now = influence(x_ref[tile[2], :], pred, bend)
        if at:
            total = gradients(tiles[at - 1], infl, total)
        infl, pred = now, later
    total = gradients(tiles[-1], infl, total)

    if first and not last:
        carried_out[1][...] = wide
        carried_out[2][...] = scaled
    if not last:
        carried_out[0][...] = total
        return
    (turned,) = take(1)
    turned[...] = jnp.transpose(total) * shrink_ref[...]
    depth = parts_out[0].shape[0]
    for hop in range(n_row):
        start = pl.multiple_of(partner(me, hop, n_row) * depth, depth)
        parts_out[hop][...] = turned[pl.ds(start, depth), :].astype(parts_out[hop].dtype)


def block_rows(tables, kinds, block, first, last, n_row, fixed, carried):
    genes, rank = fixed[4].shape
    out = [jax.ShapeDtypeStruct((block, rank), kind) for kind in kinds]
    if last:
        out += [jax.ShapeDtypeStruct((genes // n_row, rank), jnp.bfloat16 if hop else jnp.float32) for hop in range(n_row)]
    else:
        out += [VMEM((rank, genes), jnp.float32)]
    if first and not last:
        out += [VMEM((rank, genes), jnp.bfloat16), VMEM((genes, rank), jnp.bfloat16)]
    scratch = [VMEM((genes, rank), jnp.bfloat16)] if first else []
    if last:
        scratch.append(VMEM((genes, rank), jnp.float32))
    ins = pinned(*fixed) + (list(carried) if first else pinned(*carried))
    work = len(tables) * block * genes
    out = pl.pallas_call(
        functools.partial(rows_kernel, tables, block, first, last, n_row),
        out_shape=tuple(out),
        in_specs=[IN_VMEM] * len(ins),
        out_specs=(IN_VMEM,) * len(out),
        scratch_shapes=scratch,
        compiler_params=params(),
        cost_estimate=cost(6 * work * rank, work * 2),
        name="block_rows",
    )(*ins)
    done, rest = list(out[: len(tables)]), list(out[len(tables) :])
    return done, rest if first or last else rest + list(carried[1:])


def lane_parts(genes, depth, n_row):
    if n_row != 4:
        return None
    pairs = [(2 * depth * (place // 2), 2 * depth * (place // 2 + 1)) for place in range(n_row)]
    low = [-(-begin // 128) * 128 for begin, _ in pairs]
    width = min(end // 128 * 128 - begin for begin, (_, end) in zip(low, pairs))
    if width <= 0 or any(begin not in (0, genes - width) for begin in low):
        return None
    return low, width, [width if begin == 0 else 0 for begin in low]


def lanes(table, width):
    return pl.ds(pl.multiple_of(pick("row", table), 128), width)


def influence(x, pred, bend):
    resid = x.astype(jnp.float32) - pred
    inside = jnp.maximum(1.0 - resid * resid * bend, 0.0)
    return (resid * (inside * inside)).astype(jnp.bfloat16)


def part_of_block(table, block, here, x_ref, f_ref, ft_ref, bend_ref, wide, scaled):
    step = tile_of(block, 256)
    origin = pick("gene", table) * block
    tiles = [pl.ds(pl.multiple_of(origin + at, math.gcd(block, step)), step) for at in range(0, block, step)]
    bend = bend_ref[:, here]
    preds = [jnp.dot(f_ref[tile, :], wide, preferred_element_type=jnp.float32) for tile in tiles]
    infls = [influence(x_ref[tile, here], pred, bend) for tile, pred in zip(tiles, preds)]
    rows, total = [], None
    for tile, infl in zip(tiles, infls):
        cols = jnp.dot(ft_ref[:, tile], infl, preferred_element_type=jnp.float32)
        rows.append(jnp.dot(infl, scaled, preferred_element_type=jnp.float32))
        total = cols if total is None else total + cols
    return rows, total


def early_kernel(table, block, parts, x_ref, f_ref, ft_ref, bend_ref, shrink_ref, own, other, *refs):
    rows_out, total_out, wide_out, scaled_out, pair = refs
    low, width, _ = parts
    depth = own.shape[0]
    odd = lax.axis_index("row") % 2
    pair[pl.ds(pl.multiple_of(odd * depth, depth), depth), :] = own[...]
    pair[pl.ds(pl.multiple_of((1 - odd) * depth, depth), depth), :] = other[...]
    inset = [begin - 2 * depth * (place // 2) for place, begin in enumerate(low)]
    whole = pair[pl.ds(pl.multiple_of(pick("row", inset), math.gcd(*inset, 128)), width), :].astype(jnp.float32)
    here = lanes(low, width)
    wide = jnp.transpose(whole).astype(jnp.bfloat16)
    scaled = (whole * shrink_ref[here, :]).astype(jnp.bfloat16)
    wide_out[...] = wide
    scaled_out[...] = scaled
    rows, total = part_of_block(table, block, here, x_ref, f_ref, ft_ref, bend_ref, wide, scaled)
    for at, value in enumerate(rows):
        rows_out[at * value.shape[0] : (at + 1) * value.shape[0], :] = value
    total_out[...] = total


def rest_kernel(table, block, parts, n_row, x_ref, f_ref, ft_ref, bend_ref, shrink_ref, *refs):
    shares, (rows_in, total_in, wide_in, scaled_in) = refs[:n_row], refs[n_row : n_row + 4]
    rows_out, total_out, wide_out, scaled_out, piece = refs[n_row + 4 :]
    low, width, rest = parts
    me = lax.axis_index("row")
    depth = shares[0].shape[0]
    for hop in range(n_row):
        start = pl.multiple_of(source(me, hop, n_row) * depth, depth)
        piece[pl.ds(start, depth), :] = shares[hop][...]
    here = lanes(rest, n_row * depth - width)
    whole = piece[here, :].astype(jnp.float32)
    wide = jnp.transpose(whole).astype(jnp.bfloat16)
    scaled = (whole * shrink_ref[here, :]).astype(jnp.bfloat16)
    rows, total = part_of_block(table, block, here, x_ref, f_ref, ft_ref, bend_ref, wide, scaled)
    for at, value in enumerate(rows):
        span = slice(at * value.shape[0], (at + 1) * value.shape[0])
        rows_out[span, :] = (rows_in[span, :] + value).astype(rows_out.dtype)
    done = lanes(low, width)
    total_out[:, here] = total
    total_out[:, done] = total_in[...]
    wide_out[:, here] = wide
    wide_out[:, done] = wide_in[...]
    scaled_out[here, :] = scaled
    scaled_out[done, :] = scaled_in[...]


def first_block(table, block, parts, n_row, fixed, shares):
    genes, rank = fixed[4].shape
    depth = genes // n_row
    width = parts[1]
    ins = pinned(*fixed)
    early = pl.pallas_call(
        functools.partial(early_kernel, table, block, parts),
        out_shape=(
            VMEM((block, rank), jnp.float32),
            VMEM((rank, width), jnp.float32),
            VMEM((rank, width), jnp.bfloat16),
            VMEM((width, rank), jnp.bfloat16),
        ),
        in_specs=[IN_VMEM] * 7,
        out_specs=(IN_VMEM,) * 4,
        scratch_shapes=[VMEM((2 * depth, rank), jnp.bfloat16)],
        compiler_params=params(),
        cost_estimate=cost(12 * block * width * rank, block * width * 4),
        name="early_part",
    )(*ins, *shares[:2])
    done, *carried = pl.pallas_call(
        functools.partial(rest_kernel, table, block, parts, n_row),
        out_shape=(
            jax.ShapeDtypeStruct((block, rank), jnp.bfloat16),
            VMEM((rank, genes), jnp.float32),
            VMEM((rank, genes), jnp.bfloat16),
            VMEM((genes, rank), jnp.bfloat16),
        ),
        in_specs=[IN_VMEM] * (9 + n_row),
        out_specs=(IN_VMEM,) * 4,
        scratch_shapes=[VMEM((genes, rank), jnp.bfloat16)],
        compiler_params=params(),
        cost_estimate=cost(12 * block * (genes - width) * rank, block * (genes - width) * 4),
        name="rest_part",
    )(*ins, *shares, *pinned(*early))
    return [done], carried


def far_first(size):
    return sorted(range(1, size), key=lambda hop: (-hop.bit_length(), hop))


def swap_row(value, hop, size):
    return lax.ppermute(value, "row", [(me, partner(me, hop, size)) for me in range(size)])


def ring_of(size):
    return [*range(0, size, 2), *reversed(range(1, size, 2))]


def steps_of(size):
    ahead = [(1, distance) for distance in range(size // 2, 0, -1)]
    back = [(-1, distance) for distance in range((size - 1) // 2, 0, -1)]
    return [step for pair in itertools.zip_longest(ahead, back) for step in pair if step]


def around(size, hops):
    ring = ring_of(size)
    return tuple(ring[(ring.index(place) + hops) % size] for place in range(size))


def plus(wide, narrow):
    return wide.astype(jnp.float32) + narrow.astype(jnp.float32)


def finish_kernel(n_ends, n_parts, *refs):
    n_ins = n_ends + n_parts + 3
    ins, outs = refs[:n_ins], refs[n_ins : n_ins + 3 + bool(n_ends)]
    *held, sems = refs[n_ins + len(outs) :]
    ends, parts = ins[:n_ends], ins[n_ends : n_ends + n_parts]
    factor, first, second = ins[n_ends + n_parts :]
    copies = []

    def send(at, span, value):
        held[at][span, :] = value
        copies.append(pltpu.make_async_copy(held[at].at[span, :], outs[at].at[span, :], sems.at[len(copies)]))
        copies[-1].start()

    if ends:
        step = tile_of(ends[0].shape[0], 256)
        for low in range(0, ends[0].shape[0], step):
            span = pl.ds(low, step)
            rows = ends[0][span, :]
            for end in ends[1:]:
                rows = plus(rows, end[span, :])
            send(3, span, rows)
    grad = parts[0][...]
    for part in parts[1:]:
        grad = plus(grad, part[...])
    span = pl.ds(0, grad.shape[0])
    new_first = beta_one * first[...] + (1.0 - beta_one) * grad
    new_second = beta_two * second[...] + (1.0 - beta_two) * grad * grad
    send(1, span, new_first)
    send(2, span, new_second)
    first_hat = new_first / (1.0 - beta_one**10)
    second_hat = new_second / (1.0 - beta_two**10)
    send(0, span, factor[...] - learn_rate * first_hat / (jnp.sqrt(second_hat) + adam_eps))
    for copy in copies:
        copy.wait()


def finish(ends, parts, factor, first, second):
    ins = [*ends, *parts, factor, first, second]
    shapes = [factor, factor, factor] + list(ends[:1])
    n_copies = 3 + (ends[0].shape[0] // tile_of(ends[0].shape[0], 256) if ends else 0)
    return pl.pallas_call(
        functools.partial(finish_kernel, len(ends), len(parts)),
        out_shape=tuple(jax.ShapeDtypeStruct(like.shape, jnp.float32) for like in shapes),
        in_specs=[IN_VMEM] * len(ins),
        out_specs=(IN_ANY,) * len(shapes),
        scratch_shapes=[VMEM(like.shape, jnp.float32) for like in shapes] + [pltpu.SemaphoreType.DMA((n_copies,))],
        compiler_params=params(),
        cost_estimate=cost(20 * factor.size, sum(4 * a.size for a in ins)),
        name="finish",
    )(*ins)


def local(x_slab, cell_factor, row_index, gene_scale, gene_factor, first_moment, second_moment):
    rows_dev, genes_dev = x_slab.shape
    n_gene = lax.axis_size("gene")
    n_row = lax.axis_size("row")
    block = rows_dev // n_gene
    scale_k = 4.0 / math.sqrt(genes_dev * n_gene)
    factor_bf = gene_factor.astype(jnp.bfloat16)
    shares = [factor_bf] + [swap_row(factor_bf, hop, n_row) for hop in range(1, n_row)]
    fixed = prepare(x_slab, row_index, cell_factor, gene_scale, scale_k)
    adam = (gene_factor, first_moment, second_moment)

    if n_gene == 1 or n_gene > RING_MOST or block % 128:
        (rows,), parts = block_rows([(0,)], [jnp.float32], rows_dev, True, True, n_row, fixed, shares)
        grad_cells = lax.psum_scatter(rows, "gene", scatter_dimension=0, tiled=True)
        others = [swap_row(parts[hop], hop, n_row) for hop in far_first(n_row)]
        return (grad_cells, *finish([], [parts[0], *others], *adam))

    steps = steps_of(n_gene)
    tables = [around(n_gene, way * distance) for way, distance in steps] + [tuple(range(n_gene))]
    kinds = [jnp.bfloat16] * len(steps) + [jnp.float32]
    cuts = [0, 1, 2, len(tables)] if len(steps) > 2 else [0, 1, len(tables)]
    parted = lane_parts(genes_dev, genes_dev // n_row, n_row)
    carried, blocks = shares, []
    for low, high in zip(cuts, cuts[1:]):
        last = high == len(tables)
        if low == 0 and parted:
            done, carried = first_block(tables[0], block, parted, n_row, fixed, shares)
            blocks += done
            continue
        done, carried = block_rows(tables[low:high], kinds[low:high], block, low == 0, last, n_row, fixed, carried)
        blocks += done
    parts = carried

    came = {}
    for (way, _), own in zip(steps, blocks):
        if way in came:
            own = plus(own, came[way]).astype(jnp.bfloat16)
        came[way] = lax.ppermute(own, "gene", list(enumerate(around(n_gene, way))))
    others = [swap_row(parts[hop], hop, n_row) for hop in far_first(n_row)]
    *adam_out, grad_cells = finish([blocks[-1], *came.values()], [parts[0], *others], *adam)
    return (grad_cells, *adam_out)


def solution(mesh):
    in_specs = (
        P(("grp", "row"), "gene"),
        P(("grp", "row"), None),
        P(("grp", "row")),
        P(("grp", "gene")),
        P(("grp", "gene", "row"), None),
        P(("grp", "gene", "row"), None),
        P(("grp", "gene", "row"), None),
    )
    out_specs = (
        P(("grp", "row", "gene"), None),
        P(("grp", "gene", "row"), None),
        P(("grp", "gene", "row"), None),
        P(("grp", "gene", "row"), None),
    )
    return jax.shard_map(local, mesh=mesh, in_specs=in_specs, out_specs=out_specs, check_vma=False)
```

```python
import functools
import itertools
import math

import jax
import jax.numpy as jnp
from jax import lax
from jax.experimental import pallas as pl
from jax.experimental.pallas import tpu as pltpu
from jax.sharding import PartitionSpec as P

tukey_c = 4.685
beta_one = 0.9
beta_two = 0.999
learn_rate = 0.02
adam_eps = 1e-08

RING_MOST = 8
LINES = ("gene", "row")
VMEM = pltpu.VMEM
IN_VMEM = pl.BlockSpec(memory_space=VMEM)
IN_ANY = pl.BlockSpec(memory_space=pl.ANY)


def tile_of(rows, most):
    best = [t for t in range(128, most + 1, 128) if rows % t == 0]
    return best[-1] if best else rows


def params():
    return pltpu.CompilerParams(vmem_limit_bytes=24 * 1024 * 1024)


def cost(flops, moved):
    return pl.CostEstimate(flops=int(flops), bytes_accessed=int(moved), transcendentals=0)


def pinned(*arrays):
    return [pltpu.with_memory_space_constraint(a, VMEM) for a in arrays]


def prepare_kernel(scale_k, x_in, index_in, cell_in, scale_in, x_out, f_out, ft_out, bend_out, shrink_out, index, cell, scale, sems):
    loads = [
        pltpu.make_async_copy(src, dst, sems.at[at])
        for at, (src, dst) in enumerate(((scale_in, scale), (cell_in, cell), (index_in, index), (x_in, x_out)))
    ]
    for load in loads:
        load.start()
    cells, rank = cell.shape
    rows = index.shape[0]
    genes = scale.shape[0]
    loads[0].wait()
    inverse = 1.0 / scale[...].reshape(1, genes)
    bend_out[...] = (inverse * inverse) * (1.0 / (tukey_c * tukey_c))
    shrink_out[...] = jnp.transpose(jnp.broadcast_to(-scale_k * (inverse * inverse), (rank, genes)))
    loads[1].wait()
    table = jnp.transpose(cell[...].astype(jnp.float32)).astype(jnp.bfloat16)
    base = lax.axis_index("row") * cells
    loads[2].wait()
    step = tile_of(rows, 512)
    for at in range(0, rows, step):
        local = index[at : at + step].reshape(1, step) - base
        hot = lax.broadcasted_iota(jnp.int32, (cells, step), 0) == local
        hot = jnp.where(hot, 1.0, 0.0).astype(jnp.bfloat16)
        picked = jnp.dot(table, hot, preferred_element_type=jnp.float32)
        ft_out[:, at : at + step] = picked.astype(jnp.bfloat16)
        f_out[at : at + step, :] = jnp.transpose(picked).astype(jnp.bfloat16)
    loads[3].wait()


def prepare(x_slab, row_index, cell_factor, gene_scale, scale_k):
    rows, genes = x_slab.shape
    cells, rank = cell_factor.shape
    ins = (x_slab, row_index, cell_factor, gene_scale)
    return pl.pallas_call(
        functools.partial(prepare_kernel, scale_k),
        out_shape=(
            VMEM((rows, genes), jnp.bfloat16),
            VMEM((rows, rank), jnp.bfloat16),
            VMEM((rank, rows), jnp.bfloat16),
            VMEM((1, genes), jnp.float32),
            VMEM((genes, rank), jnp.float32),
        ),
        in_specs=[IN_ANY] * 4,
        out_specs=(IN_VMEM,) * 5,
        scratch_shapes=[
            VMEM((rows,), jnp.int32),
            VMEM((cells, rank), jnp.bfloat16),
            VMEM((genes,), jnp.float32),
            pltpu.SemaphoreType.DMA((4,)),
        ],
        compiler_params=params(),
        cost_estimate=cost(2 * rows * cells * rank, 2 * rows * genes * 2),
        name="prepare",
    )(*(pltpu.with_memory_space_constraint(a, pltpu.HBM) for a in ins))


def pick(axis, table):
    me = lax.axis_index(axis)
    value = jnp.int32(table[0])
    for place, entry in enumerate(table[1:], 1):
        value = jnp.where(me == place, jnp.int32(entry), value)
    return value


def partner(me, hop, size):
    return me ^ hop if size & (size - 1) == 0 else (me + hop) % size


def source(me, hop, size):
    return me ^ hop if size & (size - 1) == 0 else (me + size - hop) % size


def rows_kernel(tables, block, first, last, n_row, *refs):
    refs = list(refs)
    take = lambda count: [refs.pop(0) for _ in range(count)]
    x_ref, f_ref, ft_ref, bend_ref, shrink_ref = take(5)
    shares = take(n_row) if first else None
    carried_in = None if first else take(3)
    rows_out = take(len(tables))
    carried_out = None if last else take(3 if first else 1)
    parts_out = take(n_row) if last else None
    me = lax.axis_index("row")

    if first:
        (piece,) = take(1)
        depth = shares[0].shape[0]
        for hop in range(n_row):
            start = pl.multiple_of(source(me, hop, n_row) * depth, depth)
            piece[pl.ds(start, depth), :] = shares[hop][...]
        whole = piece[...].astype(jnp.float32)
        wide = jnp.transpose(whole).astype(jnp.bfloat16)
        scaled = (whole * shrink_ref[...]).astype(jnp.bfloat16)
        total = None
    else:
        total, wide, scaled = (ref[...] for ref in carried_in)

    bend = bend_ref[...]
    step = tile_of(block, 256)
    tiles = []
    for table, out in zip(tables, rows_out):
        origin = pick(LINES, table) * block if len(table) > 1 else 0
        for at in range(0, block, step):
            start = origin + at
            if len(table) > 1:
                start = pl.multiple_of(start, math.gcd(block, step))
            tiles.append((out, at, pl.ds(start, step)))

    def predict(here):
        return jnp.dot(f_ref[here, :], wide, preferred_element_type=jnp.float32)

    def gradients(tile, infl, total):
        out, at, here = tile
        cols = jnp.dot(ft_ref[:, here], infl, preferred_element_type=jnp.float32)
        out[at : at + step, :] = jnp.dot(infl, scaled, preferred_element_type=jnp.float32).astype(out.dtype)
        return cols if total is None else total + cols

    pred = predict(tiles[0][2])
    infl = None
    for at, tile in enumerate(tiles):
        later = predict(tiles[at + 1][2]) if at + 1 < len(tiles) else None
        now = influence(x_ref[tile[2], :], pred, bend)
        if at:
            total = gradients(tiles[at - 1], infl, total)
        infl, pred = now, later
    total = gradients(tiles[-1], infl, total)

    if first and not last:
        carried_out[1][...] = wide
        carried_out[2][...] = scaled
    if not last:
        carried_out[0][...] = total
        return
    (turned,) = take(1)
    turned[...] = jnp.transpose(total) * shrink_ref[...]
    depth = parts_out[0].shape[0]
    for hop in range(n_row):
        start = pl.multiple_of(partner(me, hop, n_row) * depth, depth)
        parts_out[hop][...] = turned[pl.ds(start, depth), :].astype(parts_out[hop].dtype)


def block_rows(tables, kinds, block, first, last, n_row, fixed, carried):
    genes, rank = fixed[4].shape
    out = [jax.ShapeDtypeStruct((block, rank), kind) for kind in kinds]
    if last:
        out += [jax.ShapeDtypeStruct((genes // n_row, rank), jnp.bfloat16 if hop else jnp.float32) for hop in range(n_row)]
    else:
        out += [VMEM((rank, genes), jnp.float32)]
    if first and not last:
        out += [VMEM((rank, genes), jnp.bfloat16), VMEM((genes, rank), jnp.bfloat16)]
    scratch = [VMEM((genes, rank), jnp.bfloat16)] if first else []
    if last:
        scratch.append(VMEM((genes, rank), jnp.float32))
    ins = pinned(*fixed) + (list(carried) if first else pinned(*carried))
    work = len(tables) * block * genes
    out = pl.pallas_call(
        functools.partial(rows_kernel, tables, block, first, last, n_row),
        out_shape=tuple(out),
        in_specs=[IN_VMEM] * len(ins),
        out_specs=(IN_VMEM,) * len(out),
        scratch_shapes=scratch,
        compiler_params=params(),
        cost_estimate=cost(6 * work * rank, work * 2),
        name="block_rows",
    )(*ins)
    done, rest = list(out[: len(tables)]), list(out[len(tables) :])
    return done, rest if first or last else rest + list(carried[1:])


def lane_parts(genes, depth, n_row):
    if n_row != 4:
        return None
    pairs = [(2 * depth * (place // 2), 2 * depth * (place // 2 + 1)) for place in range(n_row)]
    low = [-(-begin // 128) * 128 for begin, _ in pairs]
    width = min(end // 128 * 128 - begin for begin, (_, end) in zip(low, pairs))
    if width <= 0 or any(begin not in (0, genes - width) for begin in low):
        return None
    return low, width, [width if begin == 0 else 0 for begin in low]


def lanes(table, width):
    return pl.ds(pl.multiple_of(pick("row", table), 128), width)


def influence(x, pred, bend):
    resid = x.astype(jnp.float32) - pred
    inside = jnp.maximum(1.0 - resid * resid * bend, 0.0)
    return (resid * (inside * inside)).astype(jnp.bfloat16)


def part_of_block(table, block, here, x_ref, f_ref, ft_ref, bend_ref, wide, scaled):
    step = tile_of(block, 256)
    origin = pick(LINES, table) * block
    tiles = [pl.ds(pl.multiple_of(origin + at, math.gcd(block, step)), step) for at in range(0, block, step)]
    bend = bend_ref[:, here]
    preds = [jnp.dot(f_ref[tile, :], wide, preferred_element_type=jnp.float32) for tile in tiles]
    infls = [influence(x_ref[tile, here], pred, bend) for tile, pred in zip(tiles, preds)]
    rows, total = [], None
    for tile, infl in zip(tiles, infls):
        cols = jnp.dot(ft_ref[:, tile], infl, preferred_element_type=jnp.float32)
        rows.append(jnp.dot(infl, scaled, preferred_element_type=jnp.float32))
        total = cols if total is None else total + cols
    return rows, total


def early_kernel(table, block, parts, x_ref, f_ref, ft_ref, bend_ref, shrink_ref, own, other, *refs):
    rows_out, total_out, wide_out, scaled_out, pair = refs
    low, width, _ = parts
    depth = own.shape[0]
    odd = lax.axis_index("row") % 2
    pair[pl.ds(pl.multiple_of(odd * depth, depth), depth), :] = own[...]
    pair[pl.ds(pl.multiple_of((1 - odd) * depth, depth), depth), :] = other[...]
    inset = [begin - 2 * depth * (place // 2) for place, begin in enumerate(low)]
    whole = pair[pl.ds(pl.multiple_of(pick("row", inset), math.gcd(*inset, 128)), width), :].astype(jnp.float32)
    here = lanes(low, width)
    wide = jnp.transpose(whole).astype(jnp.bfloat16)
    scaled = (whole * shrink_ref[here, :]).astype(jnp.bfloat16)
    wide_out[...] = wide
    scaled_out[...] = scaled
    rows, total = part_of_block(table, block, here, x_ref, f_ref, ft_ref, bend_ref, wide, scaled)
    for at, value in enumerate(rows):
        rows_out[at * value.shape[0] : (at + 1) * value.shape[0], :] = value
    total_out[...] = total


def rest_kernel(table, block, parts, n_row, x_ref, f_ref, ft_ref, bend_ref, shrink_ref, *refs):
    shares, (rows_in, total_in, wide_in, scaled_in) = refs[:n_row], refs[n_row : n_row + 4]
    rows_out, total_out, wide_out, scaled_out, piece = refs[n_row + 4 :]
    low, width, rest = parts
    me = lax.axis_index("row")
    depth = shares[0].shape[0]
    for hop in range(n_row):
        start = pl.multiple_of(source(me, hop, n_row) * depth, depth)
        piece[pl.ds(start, depth), :] = shares[hop][...]
    here = lanes(rest, n_row * depth - width)
    whole = piece[here, :].astype(jnp.float32)
    wide = jnp.transpose(whole).astype(jnp.bfloat16)
    scaled = (whole * shrink_ref[here, :]).astype(jnp.bfloat16)
    rows, total = part_of_block(table, block, here, x_ref, f_ref, ft_ref, bend_ref, wide, scaled)
    for at, value in enumerate(rows):
        span = slice(at * value.shape[0], (at + 1) * value.shape[0])
        rows_out[span, :] = (rows_in[span, :] + value).astype(rows_out.dtype)
    done = lanes(low, width)
    total_out[:, here] = total
    total_out[:, done] = total_in[...]
    wide_out[:, here] = wide
    wide_out[:, done] = wide_in[...]
    scaled_out[here, :] = scaled
    scaled_out[done, :] = scaled_in[...]


def first_block(table, block, parts, n_row, fixed, shares):
    genes, rank = fixed[4].shape
    depth = genes // n_row
    width = parts[1]
    ins = pinned(*fixed)
    early = pl.pallas_call(
        functools.partial(early_kernel, table, block, parts),
        out_shape=(
            VMEM((block, rank), jnp.float32),
            VMEM((rank, width), jnp.float32),
            VMEM((rank, width), jnp.bfloat16),
            VMEM((width, rank), jnp.bfloat16),
        ),
        in_specs=[IN_VMEM] * 7,
        out_specs=(IN_VMEM,) * 4,
        scratch_shapes=[VMEM((2 * depth, rank), jnp.bfloat16)],
        compiler_params=params(),
        cost_estimate=cost(12 * block * width * rank, block * width * 4),
        name="early_part",
    )(*ins, *shares[:2])
    done, *carried = pl.pallas_call(
        functools.partial(rest_kernel, table, block, parts, n_row),
        out_shape=(
            jax.ShapeDtypeStruct((block, rank), jnp.bfloat16),
            VMEM((rank, genes), jnp.float32),
            VMEM((rank, genes), jnp.bfloat16),
            VMEM((genes, rank), jnp.bfloat16),
        ),
        in_specs=[IN_VMEM] * (9 + n_row),
        out_specs=(IN_VMEM,) * 4,
        scratch_shapes=[VMEM((genes, rank), jnp.bfloat16)],
        compiler_params=params(),
        cost_estimate=cost(12 * block * (genes - width) * rank, block * (genes - width) * 4),
        name="rest_part",
    )(*ins, *shares, *pinned(*early))
    return [done], carried


def swap_row(value, hop, size):
    return lax.ppermute(value, "row", [(me, partner(me, hop, size)) for me in range(size)])


def ring_of(size):
    return [*range(0, size, 2), *reversed(range(1, size, 2))]


def steps_of(size):
    ahead = [(1, distance) for distance in range(size // 2, 0, -1)]
    back = [(-1, distance) for distance in range((size - 1) // 2, 0, -1)]
    return [step for pair in itertools.zip_longest(ahead, back) for step in pair if step]


def around(size, rows, hops):
    rings = [list(range(size)) if row % 2 else ring_of(size) for row in range(rows)]
    return tuple(ring[(ring.index(place) + hops) % size] for place in range(size) for ring in rings)


def plus(wide, narrow):
    return wide.astype(jnp.float32) + narrow.astype(jnp.float32)


def finish_kernel(n_ends, n_parts, *refs):
    n_ins = n_ends + n_parts + 3
    ins, outs = refs[:n_ins], refs[n_ins : n_ins + 3 + bool(n_ends)]
    *held, sems = refs[n_ins + len(outs) :]
    ends, parts = ins[:n_ends], ins[n_ends : n_ends + n_parts]
    factor, first, second = ins[n_ends + n_parts :]
    copies = []

    def send(at, span, value):
        held[at][span, :] = value
        copies.append(pltpu.make_async_copy(held[at].at[span, :], outs[at].at[span, :], sems.at[len(copies)]))
        copies[-1].start()

    if ends:
        step = tile_of(ends[0].shape[0], 256)
        for low in range(0, ends[0].shape[0], step):
            span = pl.ds(low, step)
            rows = ends[0][span, :]
            for end in ends[1:]:
                rows = plus(rows, end[span, :])
            send(3, span, rows)
    grad = parts[0][...]
    for part in parts[1:]:
        grad = plus(grad, part[...])
    span = pl.ds(0, grad.shape[0])
    new_first = beta_one * first[...] + (1.0 - beta_one) * grad
    new_second = beta_two * second[...] + (1.0 - beta_two) * grad * grad
    send(1, span, new_first)
    send(2, span, new_second)
    first_hat = new_first / (1.0 - beta_one**10)
    second_hat = new_second / (1.0 - beta_two**10)
    send(0, span, factor[...] - learn_rate * first_hat / (jnp.sqrt(second_hat) + adam_eps))
    for copy in copies:
        copy.wait()


def finish(ends, parts, factor, first, second):
    ins = [*ends, *parts, factor, first, second]
    shapes = [factor, factor, factor] + list(ends[:1])
    n_copies = 3 + (ends[0].shape[0] // tile_of(ends[0].shape[0], 256) if ends else 0)
    return pl.pallas_call(
        functools.partial(finish_kernel, len(ends), len(parts)),
        out_shape=tuple(jax.ShapeDtypeStruct(like.shape, jnp.float32) for like in shapes),
        in_specs=[IN_VMEM] * len(ins),
        out_specs=(IN_ANY,) * len(shapes),
        scratch_shapes=[VMEM(like.shape, jnp.float32) for like in shapes] + [pltpu.SemaphoreType.DMA((n_copies,))],
        compiler_params=params(),
        cost_estimate=cost(20 * factor.size, sum(4 * a.size for a in ins)),
        name="finish",
    )(*ins)


def local(x_slab, cell_factor, row_index, gene_scale, gene_factor, first_moment, second_moment):
    rows_dev, genes_dev = x_slab.shape
    n_gene = lax.axis_size("gene")
    n_row = lax.axis_size("row")
    block = rows_dev // n_gene
    scale_k = 4.0 / math.sqrt(genes_dev * n_gene)
    factor_bf = gene_factor.astype(jnp.bfloat16)
    shares = [factor_bf] + [swap_row(factor_bf, hop, n_row) for hop in range(1, n_row)]
    fixed = prepare(x_slab, row_index, cell_factor, gene_scale, scale_k)
    adam = (gene_factor, first_moment, second_moment)

    if n_gene == 1 or n_gene > RING_MOST or block % 128:
        (rows,), parts = block_rows([(0,)], [jnp.float32], rows_dev, True, True, n_row, fixed, shares)
        grad_cells = lax.psum_scatter(rows, "gene", scatter_dimension=0, tiled=True)
        others = [swap_row(parts[hop], hop, n_row) for hop in range(1, n_row)]
        return (grad_cells, *finish([], [parts[0], *others], *adam))

    steps = steps_of(n_gene)
    tables = [around(n_gene, n_row, way * distance) for way, distance in steps] + [around(n_gene, n_row, 0)]
    kinds = [jnp.bfloat16] * len(steps) + [jnp.float32]
    cuts = [0, 1, 2, len(tables)] if len(steps) > 2 else [0, 1, len(tables)]
    parted = lane_parts(genes_dev, genes_dev // n_row, n_row)
    carried, blocks = shares, []
    for low, high in zip(cuts, cuts[1:]):
        last = high == len(tables)
        if low == 0 and parted:
            done, carried = first_block(tables[0], block, parted, n_row, fixed, shares)
            blocks += done
            continue
        done, carried = block_rows(tables[low:high], kinds[low:high], block, low == 0, last, n_row, fixed, carried)
        blocks += done
    parts = carried

    came = {}
    for (way, _), own in zip(steps, blocks):
        if way in came:
            own = plus(own, came[way]).astype(jnp.bfloat16)
        came[way] = lax.ppermute(own, LINES, [(at, to * n_row + at % n_row) for at, to in enumerate(around(n_gene, n_row, way))])
    others = [swap_row(parts[hop], hop, n_row) for hop in range(1, n_row)]
    *adam_out, grad_cells = finish([blocks[-1], *came.values()], [parts[0], *others], *adam)
    return (grad_cells, *adam_out)


def solution(mesh):
    in_specs = (
        P(("grp", "row"), "gene"),
        P(("grp", "row"), None),
        P(("grp", "row")),
        P(("grp", "gene")),
        P(("grp", "gene", "row"), None),
        P(("grp", "gene", "row"), None),
        P(("grp", "gene", "row"), None),
    )
    out_specs = (
        P(("grp", "row", "gene"), None),
        P(("grp", "gene", "row"), None),
        P(("grp", "gene", "row"), None),
        P(("grp", "gene", "row"), None),
    )
    return jax.shard_map(local, mesh=mesh, in_specs=in_specs, out_specs=out_specs, check_vma=False)
```

```python
import functools
import itertools
import math

import jax
import jax.numpy as jnp
from jax import lax
from jax.experimental import pallas as pl
from jax.experimental.pallas import tpu as pltpu
from jax.sharding import PartitionSpec as P

tukey_c = 4.685
beta_one = 0.9
beta_two = 0.999
learn_rate = 0.02
adam_eps = 1e-08

RING_MOST = 8
VMEM = pltpu.VMEM
IN_VMEM = pl.BlockSpec(memory_space=VMEM)
IN_ANY = pl.BlockSpec(memory_space=pl.ANY)


def tile_of(rows, most):
    best = [t for t in range(128, most + 1, 128) if rows % t == 0]
    return best[-1] if best else rows


def params():
    return pltpu.CompilerParams(vmem_limit_bytes=24 * 1024 * 1024)


def cost(flops, moved):
    return pl.CostEstimate(flops=int(flops), bytes_accessed=int(moved), transcendentals=0)


def pinned(*arrays):
    return [pltpu.with_memory_space_constraint(a, VMEM) for a in arrays]


def prepare_kernel(scale_k, x_in, index_in, cell_in, scale_in, x_out, f_out, ft_out, bend_out, shrink_out, index, cell, scale, sems):
    loads = [
        pltpu.make_async_copy(src, dst, sems.at[at])
        for at, (src, dst) in enumerate(((scale_in, scale), (cell_in, cell), (index_in, index), (x_in, x_out)))
    ]
    for load in loads:
        load.start()
    cells, rank = cell.shape
    rows = index.shape[0]
    genes = scale.shape[0]
    loads[0].wait()
    inverse = 1.0 / scale[...].reshape(1, genes)
    bend_out[...] = (inverse * inverse) * (1.0 / (tukey_c * tukey_c))
    shrink_out[...] = jnp.transpose(jnp.broadcast_to(-scale_k * (inverse * inverse), (rank, genes)))
    loads[1].wait()
    table = jnp.transpose(cell[...].astype(jnp.float32)).astype(jnp.bfloat16)
    base = lax.axis_index("row") * cells
    loads[2].wait()
    step = tile_of(rows, 512)
    for at in range(0, rows, step):
        local = index[at : at + step].reshape(1, step) - base
        hot = lax.broadcasted_iota(jnp.int32, (cells, step), 0) == local
        hot = jnp.where(hot, 1.0, 0.0).astype(jnp.bfloat16)
        picked = jnp.dot(table, hot, preferred_element_type=jnp.float32)
        ft_out[:, at : at + step] = picked.astype(jnp.bfloat16)
        f_out[at : at + step, :] = jnp.transpose(picked).astype(jnp.bfloat16)
    loads[3].wait()


def prepare(x_slab, row_index, cell_factor, gene_scale, scale_k):
    rows, genes = x_slab.shape
    cells, rank = cell_factor.shape
    ins = (x_slab, row_index, cell_factor, gene_scale)
    return pl.pallas_call(
        functools.partial(prepare_kernel, scale_k),
        out_shape=(
            VMEM((rows, genes), jnp.bfloat16),
            VMEM((rows, rank), jnp.bfloat16),
            VMEM((rank, rows), jnp.bfloat16),
            VMEM((1, genes), jnp.float32),
            VMEM((genes, rank), jnp.float32),
        ),
        in_specs=[IN_ANY] * 4,
        out_specs=(IN_VMEM,) * 5,
        scratch_shapes=[
            VMEM((rows,), jnp.int32),
            VMEM((cells, rank), jnp.bfloat16),
            VMEM((genes,), jnp.float32),
            pltpu.SemaphoreType.DMA((4,)),
        ],
        compiler_params=params(),
        cost_estimate=cost(2 * rows * cells * rank, 2 * rows * genes * 2),
        name="prepare",
    )(*(pltpu.with_memory_space_constraint(a, pltpu.HBM) for a in ins))


def pick(axis, table):
    me = lax.axis_index(axis)
    value = jnp.int32(table[0])
    for place, entry in enumerate(table[1:], 1):
        value = jnp.where(me == place, jnp.int32(entry), value)
    return value


def partner(me, hop, size):
    return me ^ hop if size & (size - 1) == 0 else (me + hop) % size


def source(me, hop, size):
    return me ^ hop if size & (size - 1) == 0 else (me + size - hop) % size


def rows_kernel(tables, block, first, last, n_row, *refs):
    refs = list(refs)
    take = lambda count: [refs.pop(0) for _ in range(count)]
    x_ref, f_ref, ft_ref, bend_ref, shrink_ref = take(5)
    shares = take(n_row) if first else None
    carried_in = None if first else take(3)
    rows_out = take(len(tables))
    carried_out = None if last else take(3 if first else 1)
    parts_out = take(n_row) if last else None
    me = lax.axis_index("row")

    if first:
        (piece,) = take(1)
        depth = shares[0].shape[0]
        for hop in range(n_row):
            start = pl.multiple_of(source(me, hop, n_row) * depth, depth)
            piece[pl.ds(start, depth), :] = shares[hop][...]
        whole = piece[...].astype(jnp.float32)
        wide = jnp.transpose(whole).astype(jnp.bfloat16)
        scaled = (whole * shrink_ref[...]).astype(jnp.bfloat16)
        total = None
    else:
        total, wide, scaled = (ref[...] for ref in carried_in)

    bend = bend_ref[...]
    step = tile_of(block, 512)
    tiles = []
    for table, out in zip(tables, rows_out):
        origin = pick("gene", table) * block if len(table) > 1 else 0
        for at in range(0, block, step):
            start = origin + at
            if len(table) > 1:
                start = pl.multiple_of(start, math.gcd(block, step))
            tiles.append((out, at, pl.ds(start, step)))

    def predict(here):
        return jnp.dot(f_ref[here, :], wide, preferred_element_type=jnp.float32)

    def gradients(tile, infl, total):
        out, at, here = tile
        cols = jnp.dot(ft_ref[:, here], infl, preferred_element_type=jnp.float32)
        out[at : at + step, :] = jnp.dot(infl, scaled, preferred_element_type=jnp.float32).astype(out.dtype)
        return cols if total is None else total + cols

    pred = predict(tiles[0][2])
    infl = None
    for at, tile in enumerate(tiles):
        later = predict(tiles[at + 1][2]) if at + 1 < len(tiles) else None
        now = influence(x_ref[tile[2], :], pred, bend)
        if at:
            total = gradients(tiles[at - 1], infl, total)
        infl, pred = now, later
    total = gradients(tiles[-1], infl, total)

    if first and not last:
        carried_out[1][...] = wide
        carried_out[2][...] = scaled
    if not last:
        carried_out[0][...] = total
        return
    (turned,) = take(1)
    turned[...] = jnp.transpose(total) * shrink_ref[...]
    depth = parts_out[0].shape[0]
    for hop in range(n_row):
        start = pl.multiple_of(partner(me, hop, n_row) * depth, depth)
        parts_out[hop][...] = turned[pl.ds(start, depth), :].astype(parts_out[hop].dtype)


def block_rows(tables, kinds, block, first, last, n_row, fixed, carried):
    genes, rank = fixed[4].shape
    out = [jax.ShapeDtypeStruct((block, rank), kind) for kind in kinds]
    if last:
        out += [jax.ShapeDtypeStruct((genes // n_row, rank), jnp.bfloat16 if hop else jnp.float32) for hop in range(n_row)]
    else:
        out += [VMEM((rank, genes), jnp.float32)]
    if first and not last:
        out += [VMEM((rank, genes), jnp.bfloat16), VMEM((genes, rank), jnp.bfloat16)]
    scratch = [VMEM((genes, rank), jnp.bfloat16)] if first else []
    if last:
        scratch.append(VMEM((genes, rank), jnp.float32))
    ins = pinned(*fixed) + (list(carried) if first else pinned(*carried))
    work = len(tables) * block * genes
    out = pl.pallas_call(
        functools.partial(rows_kernel, tables, block, first, last, n_row),
        out_shape=tuple(out),
        in_specs=[IN_VMEM] * len(ins),
        out_specs=(IN_VMEM,) * len(out),
        scratch_shapes=scratch,
        compiler_params=params(),
        cost_estimate=cost(6 * work * rank, work * 2),
        name="block_rows",
    )(*ins)
    done, rest = list(out[: len(tables)]), list(out[len(tables) :])
    return done, rest if first or last else rest + list(carried[1:])


def lane_parts(genes, depth, n_row):
    if n_row != 4:
        return None
    pairs = [(2 * depth * (place // 2), 2 * depth * (place // 2 + 1)) for place in range(n_row)]
    low = [-(-begin // 128) * 128 for begin, _ in pairs]
    width = min(end // 128 * 128 - begin for begin, (_, end) in zip(low, pairs))
    if width <= 0 or any(begin not in (0, genes - width) for begin in low):
        return None
    return low, width, [width if begin == 0 else 0 for begin in low]


def lanes(table, width):
    return pl.ds(pl.multiple_of(pick("row", table), 128), width)


def influence(x, pred, bend):
    resid = x.astype(jnp.float32) - pred
    inside = jnp.maximum(1.0 - resid * resid * bend, 0.0)
    return (resid * (inside * inside)).astype(jnp.bfloat16)


def part_of_block(table, block, here, x_ref, f_ref, ft_ref, bend_ref, wide, scaled):
    step = tile_of(block, 256)
    origin = pick("gene", table) * block
    tiles = [pl.ds(pl.multiple_of(origin + at, math.gcd(block, step)), step) for at in range(0, block, step)]
    bend = bend_ref[:, here]
    preds = [jnp.dot(f_ref[tile, :], wide, preferred_element_type=jnp.float32) for tile in tiles]
    infls = [influence(x_ref[tile, here], pred, bend) for tile, pred in zip(tiles, preds)]
    rows, total = [], None
    for tile, infl in zip(tiles, infls):
        cols = jnp.dot(ft_ref[:, tile], infl, preferred_element_type=jnp.float32)
        rows.append(jnp.dot(infl, scaled, preferred_element_type=jnp.float32))
        total = cols if total is None else total + cols
    return rows, total


def early_kernel(table, block, parts, x_ref, f_ref, ft_ref, bend_ref, shrink_ref, own, other, *refs):
    rows_out, total_out, wide_out, scaled_out, pair = refs
    low, width, _ = parts
    depth = own.shape[0]
    odd = lax.axis_index("row") % 2
    pair[pl.ds(pl.multiple_of(odd * depth, depth), depth), :] = own[...]
    pair[pl.ds(pl.multiple_of((1 - odd) * depth, depth), depth), :] = other[...]
    inset = [begin - 2 * depth * (place // 2) for place, begin in enumerate(low)]
    whole = pair[pl.ds(pl.multiple_of(pick("row", inset), math.gcd(*inset, 128)), width), :].astype(jnp.float32)
    here = lanes(low, width)
    wide = jnp.transpose(whole).astype(jnp.bfloat16)
    scaled = (whole * shrink_ref[here, :]).astype(jnp.bfloat16)
    wide_out[...] = wide
    scaled_out[...] = scaled
    rows, total = part_of_block(table, block, here, x_ref, f_ref, ft_ref, bend_ref, wide, scaled)
    for at, value in enumerate(rows):
        rows_out[at * value.shape[0] : (at + 1) * value.shape[0], :] = value
    total_out[...] = total


def rest_kernel(table, block, parts, n_row, x_ref, f_ref, ft_ref, bend_ref, shrink_ref, *refs):
    shares, (rows_in, total_in, wide_in, scaled_in) = refs[:n_row], refs[n_row : n_row + 4]
    rows_out, total_out, wide_out, scaled_out, piece = refs[n_row + 4 :]
    low, width, rest = parts
    me = lax.axis_index("row")
    depth = shares[0].shape[0]
    for hop in range(n_row):
        start = pl.multiple_of(source(me, hop, n_row) * depth, depth)
        piece[pl.ds(start, depth), :] = shares[hop][...]
    here = lanes(rest, n_row * depth - width)
    whole = piece[here, :].astype(jnp.float32)
    wide = jnp.transpose(whole).astype(jnp.bfloat16)
    scaled = (whole * shrink_ref[here, :]).astype(jnp.bfloat16)
    rows, total = part_of_block(table, block, here, x_ref, f_ref, ft_ref, bend_ref, wide, scaled)
    for at, value in enumerate(rows):
        span = slice(at * value.shape[0], (at + 1) * value.shape[0])
        rows_out[span, :] = (rows_in[span, :] + value).astype(rows_out.dtype)
    done = lanes(low, width)
    total_out[:, here] = total
    total_out[:, done] = total_in[...]
    wide_out[:, here] = wide
    wide_out[:, done] = wide_in[...]
    scaled_out[here, :] = scaled
    scaled_out[done, :] = scaled_in[...]


def first_block(table, block, parts, n_row, fixed, shares):
    genes, rank = fixed[4].shape
    depth = genes // n_row
    width = parts[1]
    ins = pinned(*fixed)
    early = pl.pallas_call(
        functools.partial(early_kernel, table, block, parts),
        out_shape=(
            VMEM((block, rank), jnp.float32),
            VMEM((rank, width), jnp.float32),
            VMEM((rank, width), jnp.bfloat16),
            VMEM((width, rank), jnp.bfloat16),
        ),
        in_specs=[IN_VMEM] * 7,
        out_specs=(IN_VMEM,) * 4,
        scratch_shapes=[VMEM((2 * depth, rank), jnp.bfloat16)],
        compiler_params=params(),
        cost_estimate=cost(12 * block * width * rank, block * width * 4),
        name="early_part",
    )(*ins, *shares[:2])
    done, *carried = pl.pallas_call(
        functools.partial(rest_kernel, table, block, parts, n_row),
        out_shape=(
            jax.ShapeDtypeStruct((block, rank), jnp.bfloat16),
            VMEM((rank, genes), jnp.float32),
            VMEM((rank, genes), jnp.bfloat16),
            VMEM((genes, rank), jnp.bfloat16),
        ),
        in_specs=[IN_VMEM] * (9 + n_row),
        out_specs=(IN_VMEM,) * 4,
        scratch_shapes=[VMEM((genes, rank), jnp.bfloat16)],
        compiler_params=params(),
        cost_estimate=cost(12 * block * (genes - width) * rank, block * (genes - width) * 4),
        name="rest_part",
    )(*ins, *shares, *pinned(*early))
    return [done], carried


def swap_row(value, hop, size):
    return lax.ppermute(value, "row", [(me, partner(me, hop, size)) for me in range(size)])


def ring_of(size):
    return [*range(0, size, 2), *reversed(range(1, size, 2))]


def steps_of(size):
    ahead = [(1, distance) for distance in range(size // 2, 0, -1)]
    back = [(-1, distance) for distance in range((size - 1) // 2, 0, -1)]
    return [step for pair in itertools.zip_longest(ahead, back) for step in pair if step]


def around(size, hops):
    ring = ring_of(size)
    return tuple(ring[(ring.index(place) + hops) % size] for place in range(size))


def plus(wide, narrow):
    return wide.astype(jnp.float32) + narrow.astype(jnp.float32)


def finish_kernel(n_ends, n_parts, *refs):
    n_ins = n_ends + n_parts + 3
    ins, outs = refs[:n_ins], refs[n_ins : n_ins + 3 + bool(n_ends)]
    *held, sems = refs[n_ins + len(outs) :]
    ends, parts = ins[:n_ends], ins[n_ends : n_ends + n_parts]
    factor, first, second = ins[n_ends + n_parts :]
    copies = []

    def send(at, span, value):
        held[at][span, :] = value
        copies.append(pltpu.make_async_copy(held[at].at[span, :], outs[at].at[span, :], sems.at[len(copies)]))
        copies[-1].start()

    if ends:
        step = tile_of(ends[0].shape[0], 512)
        for low in range(0, ends[0].shape[0], step):
            span = pl.ds(low, step)
            rows = ends[0][span, :]
            for end in ends[1:]:
                rows = plus(rows, end[span, :])
            send(3, span, rows)
    grad = parts[0][...]
    for part in parts[1:]:
        grad = plus(grad, part[...])
    span = pl.ds(0, grad.shape[0])
    new_first = beta_one * first[...] + (1.0 - beta_one) * grad
    new_second = beta_two * second[...] + (1.0 - beta_two) * grad * grad
    send(1, span, new_first)
    send(2, span, new_second)
    first_hat = new_first / (1.0 - beta_one**10)
    second_hat = new_second / (1.0 - beta_two**10)
    send(0, span, factor[...] - learn_rate * first_hat / (jnp.sqrt(second_hat) + adam_eps))
    for copy in copies:
        copy.wait()


def finish(ends, parts, factor, first, second):
    ins = [*ends, *parts, factor, first, second]
    shapes = [factor, factor, factor] + list(ends[:1])
    n_copies = 3 + (ends[0].shape[0] // tile_of(ends[0].shape[0], 512) if ends else 0)
    return pl.pallas_call(
        functools.partial(finish_kernel, len(ends), len(parts)),
        out_shape=tuple(jax.ShapeDtypeStruct(like.shape, jnp.float32) for like in shapes),
        in_specs=[IN_VMEM] * len(ins),
        out_specs=(IN_ANY,) * len(shapes),
        scratch_shapes=[VMEM(like.shape, jnp.float32) for like in shapes] + [pltpu.SemaphoreType.DMA((n_copies,))],
        compiler_params=params(),
        cost_estimate=cost(20 * factor.size, sum(4 * a.size for a in ins)),
        name="finish",
    )(*ins)


def local(x_slab, cell_factor, row_index, gene_scale, gene_factor, first_moment, second_moment):
    rows_dev, genes_dev = x_slab.shape
    n_gene = lax.axis_size("gene")
    n_row = lax.axis_size("row")
    block = rows_dev // n_gene
    scale_k = 4.0 / math.sqrt(genes_dev * n_gene)
    factor_bf = gene_factor.astype(jnp.bfloat16)
    shares = [factor_bf] + [swap_row(factor_bf, hop, n_row) for hop in range(1, n_row)]
    fixed = prepare(x_slab, row_index, cell_factor, gene_scale, scale_k)
    adam = (gene_factor, first_moment, second_moment)

    if n_gene == 1 or n_gene > RING_MOST or block % 128:
        (rows,), parts = block_rows([(0,)], [jnp.float32], rows_dev, True, True, n_row, fixed, shares)
        grad_cells = lax.psum_scatter(rows, "gene", scatter_dimension=0, tiled=True)
        others = [swap_row(parts[hop], hop, n_row) for hop in range(1, n_row)]
        return (grad_cells, *finish([], [parts[0], *others], *adam))

    steps = steps_of(n_gene)
    tables = [around(n_gene, way * distance) for way, distance in steps] + [tuple(range(n_gene))]
    kinds = [jnp.bfloat16] * len(steps) + [jnp.float32]
    cuts = [0, 1, 2, len(tables)] if len(steps) > 2 else [0, 1, len(tables)]
    parted = lane_parts(genes_dev, genes_dev // n_row, n_row)
    carried, blocks = shares, []
    for low, high in zip(cuts, cuts[1:]):
        last = high == len(tables)
        if low == 0 and parted:
            done, carried = first_block(tables[0], block, parted, n_row, fixed, shares)
            blocks += done
            continue
        done, carried = block_rows(tables[low:high], kinds[low:high], block, low == 0, last, n_row, fixed, carried)
        blocks += done
    parts = carried

    came = {}
    for (way, _), own in zip(steps, blocks):
        if way in came:
            own = plus(own, came[way]).astype(jnp.bfloat16)
        came[way] = lax.ppermute(own, "gene", list(enumerate(around(n_gene, way))))
    others = [swap_row(parts[hop], hop, n_row) for hop in range(1, n_row)]
    *adam_out, grad_cells = finish([blocks[-1], *came.values()], [parts[0], *others], *adam)
    return (grad_cells, *adam_out)


def solution(mesh):
    in_specs = (
        P(("grp", "row"), "gene"),
        P(("grp", "row"), None),
        P(("grp", "row")),
        P(("grp", "gene")),
        P(("grp", "gene", "row"), None),
        P(("grp", "gene", "row"), None),
        P(("grp", "gene", "row"), None),
    )
    out_specs = (
        P(("grp", "row", "gene"), None),
        P(("grp", "gene", "row"), None),
        P(("grp", "gene", "row"), None),
        P(("grp", "gene", "row"), None),
    )
    return jax.shard_map(local, mesh=mesh, in_specs=in_specs, out_specs=out_specs, check_vma=False)
```

```python
import functools
import itertools
import math

import jax
import jax.numpy as jnp
from jax import lax
from jax.experimental import pallas as pl
from jax.experimental.pallas import tpu as pltpu
from jax.sharding import PartitionSpec as P

tukey_c = 4.685
beta_one = 0.9
beta_two = 0.999
learn_rate = 0.02
adam_eps = 1e-08

RING_MOST = 8
VMEM = pltpu.VMEM
IN_VMEM = pl.BlockSpec(memory_space=VMEM)
IN_ANY = pl.BlockSpec(memory_space=pl.ANY)


def tile_of(rows, most):
    best = [t for t in range(128, most + 1, 128) if rows % t == 0]
    return best[-1] if best else rows


def params():
    return pltpu.CompilerParams(vmem_limit_bytes=24 * 1024 * 1024)


def cost(flops, moved):
    return pl.CostEstimate(flops=int(flops), bytes_accessed=int(moved), transcendentals=0)


def pinned(*arrays):
    return [pltpu.with_memory_space_constraint(a, VMEM) for a in arrays]


def prepare_kernel(scale_k, x_in, index_in, cell_in, scale_in, x_out, f_out, ft_out, bend_out, shrink_out, index, cell, scale, sems):
    loads = [
        pltpu.make_async_copy(src, dst, sems.at[at])
        for at, (src, dst) in enumerate(((scale_in, scale), (cell_in, cell), (index_in, index), (x_in, x_out)))
    ]
    for load in loads:
        load.start()
    cells, rank = cell.shape
    rows = index.shape[0]
    genes = scale.shape[0]
    loads[0].wait()
    inverse = 1.0 / scale[...].reshape(1, genes)
    bend_out[...] = (inverse * inverse) * (1.0 / (tukey_c * tukey_c))
    shrink_out[...] = jnp.transpose(jnp.broadcast_to(-scale_k * (inverse * inverse), (rank, genes)))
    loads[1].wait()
    table = jnp.transpose(cell[...].astype(jnp.float32)).astype(jnp.bfloat16)
    base = lax.axis_index("row") * cells
    loads[2].wait()
    step = tile_of(rows, 512)
    for at in range(0, rows, step):
        local = index[at : at + step].reshape(1, step) - base
        hot = lax.broadcasted_iota(jnp.int32, (cells, step), 0) == local
        hot = jnp.where(hot, 1.0, 0.0).astype(jnp.bfloat16)
        picked = jnp.dot(table, hot, preferred_element_type=jnp.float32)
        ft_out[:, at : at + step] = picked.astype(jnp.bfloat16)
        f_out[at : at + step, :] = jnp.transpose(picked).astype(jnp.bfloat16)
    loads[3].wait()


def prepare(x_slab, row_index, cell_factor, gene_scale, scale_k):
    rows, genes = x_slab.shape
    cells, rank = cell_factor.shape
    ins = (x_slab, row_index, cell_factor, gene_scale)
    return pl.pallas_call(
        functools.partial(prepare_kernel, scale_k),
        out_shape=(
            VMEM((rows, genes), jnp.bfloat16),
            VMEM((rows, rank), jnp.bfloat16),
            VMEM((rank, rows), jnp.bfloat16),
            VMEM((1, genes), jnp.float32),
            VMEM((genes, rank), jnp.float32),
        ),
        in_specs=[IN_ANY] * 4,
        out_specs=(IN_VMEM,) * 5,
        scratch_shapes=[
            VMEM((rows,), jnp.int32),
            VMEM((cells, rank), jnp.bfloat16),
            VMEM((genes,), jnp.float32),
            pltpu.SemaphoreType.DMA((4,)),
        ],
        compiler_params=params(),
        cost_estimate=cost(2 * rows * cells * rank, 2 * rows * genes * 2),
        name="prepare",
    )(*(pltpu.with_memory_space_constraint(a, pltpu.HBM) for a in ins))


def pick(axis, table):
    me = lax.axis_index(axis)
    value = jnp.int32(table[0])
    for place, entry in enumerate(table[1:], 1):
        value = jnp.where(me == place, jnp.int32(entry), value)
    return value


def partner(me, hop, size):
    return me ^ hop if size & (size - 1) == 0 else (me + hop) % size


def source(me, hop, size):
    return me ^ hop if size & (size - 1) == 0 else (me + size - hop) % size


def rows_kernel(tables, block, first, last, n_row, *refs):
    refs = list(refs)
    take = lambda count: [refs.pop(0) for _ in range(count)]
    x_ref, f_ref, ft_ref, bend_ref, shrink_ref = take(5)
    shares = take(n_row) if first else None
    carried_in = None if first else take(3)
    rows_out = take(len(tables))
    carried_out = None if last else take(3 if first else 1)
    parts_out = take(n_row) if last else None
    me = lax.axis_index("row")

    if first:
        (piece,) = take(1)
        depth = shares[0].shape[0]
        for hop in range(n_row):
            start = pl.multiple_of(source(me, hop, n_row) * depth, depth)
            piece[pl.ds(start, depth), :] = shares[hop][...]
        whole = piece[...].astype(jnp.float32)
        wide = jnp.transpose(whole).astype(jnp.bfloat16)
        scaled = (whole * shrink_ref[...]).astype(jnp.bfloat16)
        total = None
    else:
        total, wide, scaled = (ref[...] for ref in carried_in)

    bend = bend_ref[...]
    step = tile_of(block, 512)
    tiles = []
    for table, out in zip(tables, rows_out):
        origin = pick("gene", table) * block if len(table) > 1 else 0
        for at in range(0, block, step):
            start = origin + at
            if len(table) > 1:
                start = pl.multiple_of(start, math.gcd(block, step))
            tiles.append((out, at, pl.ds(start, step)))

    def predict(here):
        return jnp.dot(f_ref[here, :], wide, preferred_element_type=jnp.float32)

    def gradients(tile, infl, total):
        out, at, here = tile
        cols = jnp.dot(ft_ref[:, here], infl, preferred_element_type=jnp.float32)
        out[at : at + step, :] = jnp.dot(infl, scaled, preferred_element_type=jnp.float32).astype(out.dtype)
        return cols if total is None else total + cols

    pred = predict(tiles[0][2])
    infl = None
    for at, tile in enumerate(tiles):
        later = predict(tiles[at + 1][2]) if at + 1 < len(tiles) else None
        now = influence(x_ref[tile[2], :], pred, bend)
        if at:
            total = gradients(tiles[at - 1], infl, total)
        infl, pred = now, later
    total = gradients(tiles[-1], infl, total)

    if first and not last:
        carried_out[1][...] = wide
        carried_out[2][...] = scaled
    if not last:
        carried_out[0][...] = total
        return
    (turned,) = take(1)
    turned[...] = jnp.transpose(total) * shrink_ref[...]
    depth = parts_out[0].shape[0]
    for hop in range(n_row):
        start = pl.multiple_of(partner(me, hop, n_row) * depth, depth)
        parts_out[hop][...] = turned[pl.ds(start, depth), :].astype(parts_out[hop].dtype)


def block_rows(tables, kinds, block, first, last, n_row, fixed, carried):
    genes, rank = fixed[4].shape
    out = [jax.ShapeDtypeStruct((block, rank), kind) for kind in kinds]
    if last:
        out += [jax.ShapeDtypeStruct((genes // n_row, rank), jnp.bfloat16 if hop else jnp.float32) for hop in range(n_row)]
    else:
        out += [VMEM((rank, genes), jnp.float32)]
    if first and not last:
        out += [VMEM((rank, genes), jnp.bfloat16), VMEM((genes, rank), jnp.bfloat16)]
    scratch = [VMEM((genes, rank), jnp.bfloat16)] if first else []
    if last:
        scratch.append(VMEM((genes, rank), jnp.float32))
    ins = pinned(*fixed) + (list(carried) if first else pinned(*carried))
    work = len(tables) * block * genes
    out = pl.pallas_call(
        functools.partial(rows_kernel, tables, block, first, last, n_row),
        out_shape=tuple(out),
        in_specs=[IN_VMEM] * len(ins),
        out_specs=(IN_VMEM,) * len(out),
        scratch_shapes=scratch,
        compiler_params=params(),
        cost_estimate=cost(6 * work * rank, work * 2),
        name="block_rows",
    )(*ins)
    done, rest = list(out[: len(tables)]), list(out[len(tables) :])
    return done, rest if first or last else rest + list(carried[1:])


def lane_parts(genes, depth, n_row):
    if n_row != 4:
        return None
    pairs = [(2 * depth * (place // 2), 2 * depth * (place // 2 + 1)) for place in range(n_row)]
    low = [-(-begin // 128) * 128 for begin, _ in pairs]
    width = min(end // 128 * 128 - begin for begin, (_, end) in zip(low, pairs))
    if width <= 0 or any(begin not in (0, genes - width) for begin in low):
        return None
    return low, width, [width if begin == 0 else 0 for begin in low]


def lanes(table, width):
    return pl.ds(pl.multiple_of(pick("row", table), 128), width)


def influence(x, pred, bend):
    resid = x.astype(jnp.float32) - pred
    inside = jnp.maximum(1.0 - resid * resid * bend, 0.0)
    return (resid * (inside * inside)).astype(jnp.bfloat16)


def part_of_block(table, block, here, x_ref, f_ref, ft_ref, bend_ref, wide, scaled):
    step = tile_of(block, 256)
    origin = pick("gene", table) * block
    tiles = [pl.ds(pl.multiple_of(origin + at, math.gcd(block, step)), step) for at in range(0, block, step)]
    bend = bend_ref[:, here]
    predict = lambda tile: jnp.dot(f_ref[tile, :], wide, preferred_element_type=jnp.float32)
    rows, total = [], None
    pred, behind = predict(tiles[0]), None
    for at, tile in enumerate([*tiles, None]):
        now = None
        if tile is not None:
            later = predict(tiles[at + 1]) if at + 1 < len(tiles) else None
            now = tile, influence(x_ref[tile, here], pred, bend)
            pred = later
        if behind is not None:
            last, infl = behind
            cols = jnp.dot(ft_ref[:, last], infl, preferred_element_type=jnp.float32)
            rows.append(jnp.dot(infl, scaled, preferred_element_type=jnp.float32))
            total = cols if total is None else total + cols
        behind = now
    return rows, total


def early_kernel(table, block, parts, x_ref, f_ref, ft_ref, bend_ref, shrink_ref, own, other, *refs):
    rows_out, total_out, wide_out, scaled_out, pair = refs
    low, width, _ = parts
    depth = own.shape[0]
    odd = lax.axis_index("row") % 2
    pair[pl.ds(pl.multiple_of(odd * depth, depth), depth), :] = own[...]
    pair[pl.ds(pl.multiple_of((1 - odd) * depth, depth), depth), :] = other[...]
    inset = [begin - 2 * depth * (place // 2) for place, begin in enumerate(low)]
    whole = pair[pl.ds(pl.multiple_of(pick("row", inset), math.gcd(*inset, 128)), width), :].astype(jnp.float32)
    here = lanes(low, width)
    wide = jnp.transpose(whole).astype(jnp.bfloat16)
    scaled = (whole * shrink_ref[here, :]).astype(jnp.bfloat16)
    wide_out[...] = wide
    scaled_out[...] = scaled
    rows, total = part_of_block(table, block, here, x_ref, f_ref, ft_ref, bend_ref, wide, scaled)
    for at, value in enumerate(rows):
        rows_out[at * value.shape[0] : (at + 1) * value.shape[0], :] = value
    total_out[...] = total


def rest_kernel(table, block, parts, n_row, x_ref, f_ref, ft_ref, bend_ref, shrink_ref, *refs):
    shares, (rows_in, total_in, wide_in, scaled_in) = refs[:n_row], refs[n_row : n_row + 4]
    rows_out, total_out, wide_out, scaled_out, piece = refs[n_row + 4 :]
    low, width, rest = parts
    me = lax.axis_index("row")
    depth = shares[0].shape[0]
    for hop in range(n_row):
        start = pl.multiple_of(source(me, hop, n_row) * depth, depth)
        piece[pl.ds(start, depth), :] = shares[hop][...]
    here = lanes(rest, n_row * depth - width)
    whole = piece[here, :].astype(jnp.float32)
    wide = jnp.transpose(whole).astype(jnp.bfloat16)
    scaled = (whole * shrink_ref[here, :]).astype(jnp.bfloat16)
    rows, total = part_of_block(table, block, here, x_ref, f_ref, ft_ref, bend_ref, wide, scaled)
    for at, value in enumerate(rows):
        span = slice(at * value.shape[0], (at + 1) * value.shape[0])
        rows_out[span, :] = (rows_in[span, :] + value).astype(rows_out.dtype)
    done = lanes(low, width)
    total_out[:, here] = total
    total_out[:, done] = total_in[...]
    wide_out[:, here] = wide
    wide_out[:, done] = wide_in[...]
    scaled_out[here, :] = scaled
    scaled_out[done, :] = scaled_in[...]


def first_block(table, block, parts, n_row, fixed, shares):
    genes, rank = fixed[4].shape
    depth = genes // n_row
    width = parts[1]
    ins = pinned(*fixed)
    early = pl.pallas_call(
        functools.partial(early_kernel, table, block, parts),
        out_shape=(
            VMEM((block, rank), jnp.float32),
            VMEM((rank, width), jnp.float32),
            VMEM((rank, width), jnp.bfloat16),
            VMEM((width, rank), jnp.bfloat16),
        ),
        in_specs=[IN_VMEM] * 7,
        out_specs=(IN_VMEM,) * 4,
        scratch_shapes=[VMEM((2 * depth, rank), jnp.bfloat16)],
        compiler_params=params(),
        cost_estimate=cost(12 * block * width * rank, block * width * 4),
        name="early_part",
    )(*ins, *shares[:2])
    done, *carried = pl.pallas_call(
        functools.partial(rest_kernel, table, block, parts, n_row),
        out_shape=(
            jax.ShapeDtypeStruct((block, rank), jnp.bfloat16),
            VMEM((rank, genes), jnp.float32),
            VMEM((rank, genes), jnp.bfloat16),
            VMEM((genes, rank), jnp.bfloat16),
        ),
        in_specs=[IN_VMEM] * (9 + n_row),
        out_specs=(IN_VMEM,) * 4,
        scratch_shapes=[VMEM((genes, rank), jnp.bfloat16)],
        compiler_params=params(),
        cost_estimate=cost(12 * block * (genes - width) * rank, block * (genes - width) * 4),
        name="rest_part",
    )(*ins, *shares, *pinned(*early))
    return [done], carried


def swap_row(value, hop, size):
    return lax.ppermute(value, "row", [(me, partner(me, hop, size)) for me in range(size)])


def ring_of(size):
    return [*range(0, size, 2), *reversed(range(1, size, 2))]


def steps_of(size):
    ahead = [(1, distance) for distance in range(size // 2, 0, -1)]
    back = [(-1, distance) for distance in range((size - 1) // 2, 0, -1)]
    return [step for pair in itertools.zip_longest(ahead, back) for step in pair if step]


def around(size, hops):
    ring = ring_of(size)
    return tuple(ring[(ring.index(place) + hops) % size] for place in range(size))


def plus(wide, narrow):
    return wide.astype(jnp.float32) + narrow.astype(jnp.float32)


def finish_kernel(n_ends, n_parts, *refs):
    n_ins = n_ends + n_parts + 3
    ins, outs = refs[:n_ins], refs[n_ins : n_ins + 3 + bool(n_ends)]
    *held, sems = refs[n_ins + len(outs) :]
    ends, parts = ins[:n_ends], ins[n_ends : n_ends + n_parts]
    factor, first, second = ins[n_ends + n_parts :]
    copies = []

    def send(at, span, value):
        held[at][span, :] = value
        copies.append(pltpu.make_async_copy(held[at].at[span, :], outs[at].at[span, :], sems.at[len(copies)]))
        copies[-1].start()

    if ends:
        step = tile_of(ends[0].shape[0], 512)
        for low in range(0, ends[0].shape[0], step):
            span = pl.ds(low, step)
            rows = ends[0][span, :]
            for end in ends[1:]:
                rows = plus(rows, end[span, :])
            send(3, span, rows)
    grad = parts[0][...]
    for part in parts[1:]:
        grad = plus(grad, part[...])
    span = pl.ds(0, grad.shape[0])
    new_first = beta_one * first[...] + (1.0 - beta_one) * grad
    new_second = beta_two * second[...] + (1.0 - beta_two) * grad * grad
    send(1, span, new_first)
    send(2, span, new_second)
    first_hat = new_first / (1.0 - beta_one**10)
    second_hat = new_second / (1.0 - beta_two**10)
    send(0, span, factor[...] - learn_rate * first_hat / (jnp.sqrt(second_hat) + adam_eps))
    for copy in copies:
        copy.wait()


def finish(ends, parts, factor, first, second):
    ins = [*ends, *parts, factor, first, second]
    shapes = [factor, factor, factor] + list(ends[:1])
    n_copies = 3 + (ends[0].shape[0] // tile_of(ends[0].shape[0], 512) if ends else 0)
    return pl.pallas_call(
        functools.partial(finish_kernel, len(ends), len(parts)),
        out_shape=tuple(jax.ShapeDtypeStruct(like.shape, jnp.float32) for like in shapes),
        in_specs=[IN_VMEM] * len(ins),
        out_specs=(IN_ANY,) * len(shapes),
        scratch_shapes=[VMEM(like.shape, jnp.float32) for like in shapes] + [pltpu.SemaphoreType.DMA((n_copies,))],
        compiler_params=params(),
        cost_estimate=cost(20 * factor.size, sum(4 * a.size for a in ins)),
        name="finish",
    )(*ins)


def local(x_slab, cell_factor, row_index, gene_scale, gene_factor, first_moment, second_moment):
    rows_dev, genes_dev = x_slab.shape
    n_gene = lax.axis_size("gene")
    n_row = lax.axis_size("row")
    block = rows_dev // n_gene
    scale_k = 4.0 / math.sqrt(genes_dev * n_gene)
    factor_bf = gene_factor.astype(jnp.bfloat16)
    shares = [factor_bf] + [swap_row(factor_bf, hop, n_row) for hop in range(1, n_row)]
    fixed = prepare(x_slab, row_index, cell_factor, gene_scale, scale_k)
    adam = (gene_factor, first_moment, second_moment)

    if n_gene == 1 or n_gene > RING_MOST or block % 128:
        (rows,), parts = block_rows([(0,)], [jnp.float32], rows_dev, True, True, n_row, fixed, shares)
        grad_cells = lax.psum_scatter(rows, "gene", scatter_dimension=0, tiled=True)
        others = [swap_row(parts[hop], hop, n_row) for hop in range(1, n_row)]
        return (grad_cells, *finish([], [parts[0], *others], *adam))

    steps = steps_of(n_gene)
    tables = [around(n_gene, way * distance) for way, distance in steps] + [tuple(range(n_gene))]
    kinds = [jnp.bfloat16] * len(steps) + [jnp.float32]
    cuts = [0, 1, 2, len(tables)] if len(steps) > 2 else [0, 1, len(tables)]
    parted = lane_parts(genes_dev, genes_dev // n_row, n_row)
    carried, blocks = shares, []
    for low, high in zip(cuts, cuts[1:]):
        last = high == len(tables)
        if low == 0 and parted:
            done, carried = first_block(tables[0], block, parted, n_row, fixed, shares)
            blocks += done
            continue
        done, carried = block_rows(tables[low:high], kinds[low:high], block, low == 0, last, n_row, fixed, carried)
        blocks += done
    parts = carried

    came = {}
    for (way, _), own in zip(steps, blocks):
        if way in came:
            own = plus(own, came[way]).astype(jnp.bfloat16)
        came[way] = lax.ppermute(own, "gene", list(enumerate(around(n_gene, way))))
    others = [swap_row(parts[hop], hop, n_row) for hop in range(1, n_row)]
    *adam_out, grad_cells = finish([blocks[-1], *came.values()], [parts[0], *others], *adam)
    return (grad_cells, *adam_out)


def solution(mesh):
    in_specs = (
        P(("grp", "row"), "gene"),
        P(("grp", "row"), None),
        P(("grp", "row")),
        P(("grp", "gene")),
        P(("grp", "gene", "row"), None),
        P(("grp", "gene", "row"), None),
        P(("grp", "gene", "row"), None),
    )
    out_specs = (
        P(("grp", "row", "gene"), None),
        P(("grp", "gene", "row"), None),
        P(("grp", "gene", "row"), None),
        P(("grp", "gene", "row"), None),
    )
    return jax.shard_map(local, mesh=mesh, in_specs=in_specs, out_specs=out_specs, check_vma=False)
```

```python
import functools
import itertools
import math

import jax
import jax.numpy as jnp
from jax import lax
from jax.experimental import pallas as pl
from jax.experimental.pallas import tpu as pltpu
from jax.sharding import PartitionSpec as P

tukey_c = 4.685
beta_one = 0.9
beta_two = 0.999
learn_rate = 0.02
adam_eps = 1e-08

RING_MOST = 8
VMEM = pltpu.VMEM
IN_VMEM = pl.BlockSpec(memory_space=VMEM)
IN_ANY = pl.BlockSpec(memory_space=pl.ANY)


def tile_of(rows, most):
    best = [t for t in range(128, most + 1, 128) if rows % t == 0]
    return best[-1] if best else rows


def params():
    return pltpu.CompilerParams(vmem_limit_bytes=24 * 1024 * 1024)


def cost(flops, moved):
    return pl.CostEstimate(flops=int(flops), bytes_accessed=int(moved), transcendentals=0)


def pinned(*arrays):
    return [pltpu.with_memory_space_constraint(a, VMEM) for a in arrays]


def prepare_kernel(scale_k, x_in, index_in, cell_in, scale_in, x_out, f_out, ft_out, bend_out, shrink_out, index, cell, scale, sems):
    loads = [
        pltpu.make_async_copy(src, dst, sems.at[at])
        for at, (src, dst) in enumerate(((scale_in, scale), (cell_in, cell), (index_in, index), (x_in, x_out)))
    ]
    for load in loads:
        load.start()
    cells, rank = cell.shape
    rows = index.shape[0]
    genes = scale.shape[0]
    loads[0].wait()
    inverse = 1.0 / scale[...].reshape(1, genes)
    bend_out[...] = (inverse * inverse) * (1.0 / (tukey_c * tukey_c))
    shrink_out[...] = jnp.transpose(jnp.broadcast_to(-scale_k * (inverse * inverse), (rank, genes)))
    loads[1].wait()
    table = jnp.transpose(cell[...].astype(jnp.float32)).astype(jnp.bfloat16)
    base = lax.axis_index("row") * cells
    loads[2].wait()
    step = tile_of(rows, 256)
    for at in range(0, rows, step):
        local = index[at : at + step].reshape(1, step) - base
        hot = lax.broadcasted_iota(jnp.int32, (cells, step), 0) == local
        hot = jnp.where(hot, 1.0, 0.0).astype(jnp.bfloat16)
        picked = jnp.dot(table, hot, preferred_element_type=jnp.float32)
        ft_out[:, at : at + step] = picked.astype(jnp.bfloat16)
        f_out[at : at + step, :] = jnp.transpose(picked).astype(jnp.bfloat16)
    loads[3].wait()


def prepare(x_slab, row_index, cell_factor, gene_scale, scale_k):
    rows, genes = x_slab.shape
    cells, rank = cell_factor.shape
    ins = (x_slab, row_index, cell_factor, gene_scale)
    return pl.pallas_call(
        functools.partial(prepare_kernel, scale_k),
        out_shape=(
            VMEM((rows, genes), jnp.bfloat16),
            VMEM((rows, rank), jnp.bfloat16),
            VMEM((rank, rows), jnp.bfloat16),
            VMEM((1, genes), jnp.float32),
            VMEM((genes, rank), jnp.float32),
        ),
        in_specs=[IN_ANY] * 4,
        out_specs=(IN_VMEM,) * 5,
        scratch_shapes=[
            VMEM((rows,), jnp.int32),
            VMEM((cells, rank), jnp.bfloat16),
            VMEM((genes,), jnp.float32),
            pltpu.SemaphoreType.DMA((4,)),
        ],
        compiler_params=params(),
        cost_estimate=cost(2 * rows * cells * rank, 2 * rows * genes * 2),
        name="prepare",
    )(*(pltpu.with_memory_space_constraint(a, pltpu.HBM) for a in ins))


def pick(axis, table):
    me = lax.axis_index(axis)
    value = jnp.int32(table[0])
    for place, entry in enumerate(table[1:], 1):
        value = jnp.where(me == place, jnp.int32(entry), value)
    return value


def partner(me, hop, size):
    return me ^ hop if size & (size - 1) == 0 else (me + hop) % size


def source(me, hop, size):
    return me ^ hop if size & (size - 1) == 0 else (me + size - hop) % size


def rows_kernel(tables, block, first, last, n_row, *refs):
    refs = list(refs)
    take = lambda count: [refs.pop(0) for _ in range(count)]
    x_ref, f_ref, ft_ref, bend_ref, shrink_ref = take(5)
    shares = take(n_row) if first else None
    carried_in = None if first else take(3)
    rows_out = take(len(tables))
    carried_out = None if last else take(3 if first else 1)
    parts_out = take(n_row) if last else None
    me = lax.axis_index("row")

    if first:
        (piece,) = take(1)
        depth = shares[0].shape[0]
        for hop in range(n_row):
            start = pl.multiple_of(source(me, hop, n_row) * depth, depth)
            piece[pl.ds(start, depth), :] = shares[hop][...]
        whole = piece[...].astype(jnp.float32)
        wide = jnp.transpose(whole).astype(jnp.bfloat16)
        scaled = (whole * shrink_ref[...]).astype(jnp.bfloat16)
        total = None
    else:
        total, wide, scaled = (ref[...] for ref in carried_in)

    bend = bend_ref[...]
    step = tile_of(block, 512)
    tiles = []
    for table, out in zip(tables, rows_out):
        origin = pick("gene", table) * block if len(table) > 1 else 0
        for at in range(0, block, step):
            start = origin + at
            if len(table) > 1:
                start = pl.multiple_of(start, math.gcd(block, step))
            tiles.append((out, at, pl.ds(start, step)))

    def predict(here):
        return jnp.dot(f_ref[here, :], wide, preferred_element_type=jnp.float32)

    def gradients(tile, infl, total):
        out, at, here = tile
        cols = jnp.dot(ft_ref[:, here], infl, preferred_element_type=jnp.float32)
        out[at : at + step, :] = jnp.dot(infl, scaled, preferred_element_type=jnp.float32).astype(out.dtype)
        return cols if total is None else total + cols

    pred = predict(tiles[0][2])
    infl = None
    for at, tile in enumerate(tiles):
        later = predict(tiles[at + 1][2]) if at + 1 < len(tiles) else None
        now = influence(x_ref[tile[2], :], pred, bend)
        if at:
            total = gradients(tiles[at - 1], infl, total)
        infl, pred = now, later
    total = gradients(tiles[-1], infl, total)

    if first and not last:
        carried_out[1][...] = wide
        carried_out[2][...] = scaled
    if not last:
        carried_out[0][...] = total
        return
    (turned,) = take(1)
    turned[...] = jnp.transpose(total) * shrink_ref[...]
    depth = parts_out[0].shape[0]
    for hop in range(n_row):
        start = pl.multiple_of(partner(me, hop, n_row) * depth, depth)
        parts_out[hop][...] = turned[pl.ds(start, depth), :].astype(parts_out[hop].dtype)


def block_rows(tables, kinds, block, first, last, n_row, fixed, carried):
    genes, rank = fixed[4].shape
    out = [jax.ShapeDtypeStruct((block, rank), kind) for kind in kinds]
    if last:
        out += [jax.ShapeDtypeStruct((genes // n_row, rank), jnp.bfloat16 if hop else jnp.float32) for hop in range(n_row)]
    else:
        out += [VMEM((rank, genes), jnp.float32)]
    if first and not last:
        out += [VMEM((rank, genes), jnp.bfloat16), VMEM((genes, rank), jnp.bfloat16)]
    scratch = [VMEM((genes, rank), jnp.bfloat16)] if first else []
    if last:
        scratch.append(VMEM((genes, rank), jnp.float32))
    ins = pinned(*fixed) + (list(carried) if first else pinned(*carried))
    work = len(tables) * block * genes
    out = pl.pallas_call(
        functools.partial(rows_kernel, tables, block, first, last, n_row),
        out_shape=tuple(out),
        in_specs=[IN_VMEM] * len(ins),
        out_specs=(IN_VMEM,) * len(out),
        scratch_shapes=scratch,
        compiler_params=params(),
        cost_estimate=cost(6 * work * rank, work * 2),
        name="block_rows",
    )(*ins)
    done, rest = list(out[: len(tables)]), list(out[len(tables) :])
    return done, rest if first or last else rest + list(carried[1:])


def lane_parts(genes, depth, n_row):
    if n_row != 4:
        return None
    pairs = [(2 * depth * (place // 2), 2 * depth * (place // 2 + 1)) for place in range(n_row)]
    low = [-(-begin // 128) * 128 for begin, _ in pairs]
    width = min(end // 128 * 128 - begin for begin, (_, end) in zip(low, pairs))
    if width <= 0 or any(begin not in (0, genes - width) for begin in low):
        return None
    return low, width, [width if begin == 0 else 0 for begin in low]


def lanes(table, width):
    return pl.ds(pl.multiple_of(pick("row", table), 128), width)


def influence(x, pred, bend):
    resid = x.astype(jnp.float32) - pred
    inside = jnp.maximum(1.0 - resid * resid * bend, 0.0)
    return (resid * (inside * inside)).astype(jnp.bfloat16)


def part_of_block(table, block, here, x_ref, f_ref, ft_ref, bend_ref, wide, scaled):
    step = tile_of(block, 256)
    origin = pick("gene", table) * block
    tiles = [pl.ds(pl.multiple_of(origin + at, math.gcd(block, step)), step) for at in range(0, block, step)]
    bend = bend_ref[:, here]
    predict = lambda tile: jnp.dot(f_ref[tile, :], wide, preferred_element_type=jnp.float32)
    rows, total = [], None
    pred, behind = predict(tiles[0]), None
    for at, tile in enumerate([*tiles, None]):
        now = None
        if tile is not None:
            later = predict(tiles[at + 1]) if at + 1 < len(tiles) else None
            now = tile, influence(x_ref[tile, here], pred, bend)
            pred = later
        if behind is not None:
            last, infl = behind
            cols = jnp.dot(ft_ref[:, last], infl, preferred_element_type=jnp.float32)
            rows.append(jnp.dot(infl, scaled, preferred_element_type=jnp.float32))
            total = cols if total is None else total + cols
        behind = now
    return rows, total


def early_kernel(table, block, parts, x_ref, f_ref, ft_ref, bend_ref, shrink_ref, own, other, *refs):
    rows_out, total_out, wide_out, scaled_out, pair = refs
    low, width, _ = parts
    depth = own.shape[0]
    odd = lax.axis_index("row") % 2
    pair[pl.ds(pl.multiple_of(odd * depth, depth), depth), :] = own[...]
    pair[pl.ds(pl.multiple_of((1 - odd) * depth, depth), depth), :] = other[...]
    inset = [begin - 2 * depth * (place // 2) for place, begin in enumerate(low)]
    whole = pair[pl.ds(pl.multiple_of(pick("row", inset), math.gcd(*inset, 128)), width), :].astype(jnp.float32)
    here = lanes(low, width)
    wide = jnp.transpose(whole).astype(jnp.bfloat16)
    scaled = (whole * shrink_ref[here, :]).astype(jnp.bfloat16)
    wide_out[...] = wide
    scaled_out[...] = scaled
    rows, total = part_of_block(table, block, here, x_ref, f_ref, ft_ref, bend_ref, wide, scaled)
    for at, value in enumerate(rows):
        rows_out[at * value.shape[0] : (at + 1) * value.shape[0], :] = value
    total_out[...] = total


def rest_kernel(table, block, parts, n_row, x_ref, f_ref, ft_ref, bend_ref, shrink_ref, *refs):
    shares, (rows_in, total_in, wide_in, scaled_in) = refs[:n_row], refs[n_row : n_row + 4]
    rows_out, total_out, wide_out, scaled_out, piece = refs[n_row + 4 :]
    low, width, rest = parts
    me = lax.axis_index("row")
    depth = shares[0].shape[0]
    for hop in range(n_row):
        start = pl.multiple_of(source(me, hop, n_row) * depth, depth)
        piece[pl.ds(start, depth), :] = shares[hop][...]
    here = lanes(rest, n_row * depth - width)
    whole = piece[here, :].astype(jnp.float32)
    wide = jnp.transpose(whole).astype(jnp.bfloat16)
    scaled = (whole * shrink_ref[here, :]).astype(jnp.bfloat16)
    rows, total = part_of_block(table, block, here, x_ref, f_ref, ft_ref, bend_ref, wide, scaled)
    for at, value in enumerate(rows):
        span = slice(at * value.shape[0], (at + 1) * value.shape[0])
        rows_out[span, :] = (rows_in[span, :] + value).astype(rows_out.dtype)
    done = lanes(low, width)
    total_out[:, here] = total
    total_out[:, done] = total_in[...]
    wide_out[:, here] = wide
    wide_out[:, done] = wide_in[...]
    scaled_out[here, :] = scaled
    scaled_out[done, :] = scaled_in[...]


def first_block(table, block, parts, n_row, fixed, shares):
    genes, rank = fixed[4].shape
    depth = genes // n_row
    width = parts[1]
    ins = pinned(*fixed)
    early = pl.pallas_call(
        functools.partial(early_kernel, table, block, parts),
        out_shape=(
            VMEM((block, rank), jnp.float32),
            VMEM((rank, width), jnp.float32),
            VMEM((rank, width), jnp.bfloat16),
            VMEM((width, rank), jnp.bfloat16),
        ),
        in_specs=[IN_VMEM] * 7,
        out_specs=(IN_VMEM,) * 4,
        scratch_shapes=[VMEM((2 * depth, rank), jnp.bfloat16)],
        compiler_params=params(),
        cost_estimate=cost(12 * block * width * rank, block * width * 4),
        name="early_part",
    )(*ins, *shares[:2])
    done, *carried = pl.pallas_call(
        functools.partial(rest_kernel, table, block, parts, n_row),
        out_shape=(
            jax.ShapeDtypeStruct((block, rank), jnp.bfloat16),
            VMEM((rank, genes), jnp.float32),
            VMEM((rank, genes), jnp.bfloat16),
            VMEM((genes, rank), jnp.bfloat16),
        ),
        in_specs=[IN_VMEM] * (9 + n_row),
        out_specs=(IN_VMEM,) * 4,
        scratch_shapes=[VMEM((genes, rank), jnp.bfloat16)],
        compiler_params=params(),
        cost_estimate=cost(12 * block * (genes - width) * rank, block * (genes - width) * 4),
        name="rest_part",
    )(*ins, *shares, *pinned(*early))
    return [done], carried


def swap_row(value, hop, size):
    return lax.ppermute(value, "row", [(me, partner(me, hop, size)) for me in range(size)])


def ring_of(size):
    return [*range(0, size, 2), *reversed(range(1, size, 2))]


def steps_of(size):
    ahead = [(1, distance) for distance in range(size // 2, 0, -1)]
    back = [(-1, distance) for distance in range((size - 1) // 2, 0, -1)]
    return [step for pair in itertools.zip_longest(ahead, back) for step in pair if step]


def around(size, hops):
    ring = ring_of(size)
    return tuple(ring[(ring.index(place) + hops) % size] for place in range(size))


def plus(wide, narrow):
    return wide.astype(jnp.float32) + narrow.astype(jnp.float32)


def finish_kernel(n_ends, n_parts, *refs):
    n_ins = n_ends + n_parts + 3
    ins, outs = refs[:n_ins], refs[n_ins : n_ins + 3 + bool(n_ends)]
    *held, sems = refs[n_ins + len(outs) :]
    ends, parts = ins[:n_ends], ins[n_ends : n_ends + n_parts]
    factor, first, second = ins[n_ends + n_parts :]
    copies = []

    def send(at, span, value):
        held[at][span, :] = value
        copies.append(pltpu.make_async_copy(held[at].at[span, :], outs[at].at[span, :], sems.at[len(copies)]))
        copies[-1].start()

    if ends:
        step = tile_of(ends[0].shape[0], 512)
        for low in range(0, ends[0].shape[0], step):
            span = pl.ds(low, step)
            rows = ends[0][span, :]
            for end in ends[1:]:
                rows = plus(rows, end[span, :])
            send(3, span, rows)
    grad = parts[0][...]
    for part in parts[1:]:
        grad = plus(grad, part[...])
    span = pl.ds(0, grad.shape[0])
    new_first = beta_one * first[...] + (1.0 - beta_one) * grad
    new_second = beta_two * second[...] + (1.0 - beta_two) * grad * grad
    send(1, span, new_first)
    send(2, span, new_second)
    first_hat = new_first / (1.0 - beta_one**10)
    second_hat = new_second / (1.0 - beta_two**10)
    send(0, span, factor[...] - learn_rate * first_hat / (jnp.sqrt(second_hat) + adam_eps))
    for copy in copies:
        copy.wait()


def finish(ends, parts, factor, first, second):
    ins = [*ends, *parts, factor, first, second]
    shapes = [factor, factor, factor] + list(ends[:1])
    n_copies = 3 + (ends[0].shape[0] // tile_of(ends[0].shape[0], 512) if ends else 0)
    return pl.pallas_call(
        functools.partial(finish_kernel, len(ends), len(parts)),
        out_shape=tuple(jax.ShapeDtypeStruct(like.shape, jnp.float32) for like in shapes),
        in_specs=[IN_VMEM] * len(ins),
        out_specs=(IN_ANY,) * len(shapes),
        scratch_shapes=[VMEM(like.shape, jnp.float32) for like in shapes] + [pltpu.SemaphoreType.DMA((n_copies,))],
        compiler_params=params(),
        cost_estimate=cost(20 * factor.size, sum(4 * a.size for a in ins)),
        name="finish",
    )(*ins)


def local(x_slab, cell_factor, row_index, gene_scale, gene_factor, first_moment, second_moment):
    rows_dev, genes_dev = x_slab.shape
    n_gene = lax.axis_size("gene")
    n_row = lax.axis_size("row")
    block = rows_dev // n_gene
    scale_k = 4.0 / math.sqrt(genes_dev * n_gene)
    factor_bf = gene_factor.astype(jnp.bfloat16)
    shares = [factor_bf] + [swap_row(factor_bf, hop, n_row) for hop in range(1, n_row)]
    fixed = prepare(x_slab, row_index, cell_factor, gene_scale, scale_k)
    adam = (gene_factor, first_moment, second_moment)

    if n_gene == 1 or n_gene > RING_MOST or block % 128:
        (rows,), parts = block_rows([(0,)], [jnp.float32], rows_dev, True, True, n_row, fixed, shares)
        grad_cells = lax.psum_scatter(rows, "gene", scatter_dimension=0, tiled=True)
        others = [swap_row(parts[hop], hop, n_row) for hop in range(1, n_row)]
        return (grad_cells, *finish([], [parts[0], *others], *adam))

    steps = steps_of(n_gene)
    tables = [around(n_gene, way * distance) for way, distance in steps] + [tuple(range(n_gene))]
    kinds = [jnp.bfloat16] * len(steps) + [jnp.float32]
    cuts = [0, 1, 2, len(tables)] if len(steps) > 2 else [0, 1, len(tables)]
    parted = lane_parts(genes_dev, genes_dev // n_row, n_row)
    carried, blocks = shares, []
    for low, high in zip(cuts, cuts[1:]):
        last = high == len(tables)
        if low == 0 and parted:
            done, carried = first_block(tables[0], block, parted, n_row, fixed, shares)
            blocks += done
            continue
        done, carried = block_rows(tables[low:high], kinds[low:high], block, low == 0, last, n_row, fixed, carried)
        blocks += done
    parts = carried

    came = {}
    for (way, _), own in zip(steps, blocks):
        if way in came:
            own = plus(own, came[way]).astype(jnp.bfloat16)
        came[way] = lax.ppermute(own, "gene", list(enumerate(around(n_gene, way))))
    others = [swap_row(parts[hop], hop, n_row) for hop in range(1, n_row)]
    *adam_out, grad_cells = finish([blocks[-1], *came.values()], [parts[0], *others], *adam)
    return (grad_cells, *adam_out)


def solution(mesh):
    in_specs = (
        P(("grp", "row"), "gene"),
        P(("grp", "row"), None),
        P(("grp", "row")),
        P(("grp", "gene")),
        P(("grp", "gene", "row"), None),
        P(("grp", "gene", "row"), None),
        P(("grp", "gene", "row"), None),
    )
    out_specs = (
        P(("grp", "row", "gene"), None),
        P(("grp", "gene", "row"), None),
        P(("grp", "gene", "row"), None),
        P(("grp", "gene", "row"), None),
    )
    return jax.shard_map(local, mesh=mesh, in_specs=in_specs, out_specs=out_specs, check_vma=False)
```

```python
import functools
import itertools
import math

import jax
import jax.numpy as jnp
from jax import lax
from jax.experimental import pallas as pl
from jax.experimental.pallas import tpu as pltpu
from jax.sharding import PartitionSpec as P

tukey_c = 4.685
beta_one = 0.9
beta_two = 0.999
learn_rate = 0.02
adam_eps = 1e-08

RING_MOST = 8
VMEM = pltpu.VMEM
IN_VMEM = pl.BlockSpec(memory_space=VMEM)
IN_ANY = pl.BlockSpec(memory_space=pl.ANY)


def tile_of(rows, most):
    best = [t for t in range(128, most + 1, 128) if rows % t == 0]
    return best[-1] if best else rows


def params():
    return pltpu.CompilerParams(vmem_limit_bytes=24 * 1024 * 1024)


def cost(flops, moved):
    return pl.CostEstimate(flops=int(flops), bytes_accessed=int(moved), transcendentals=0)


def pinned(*arrays):
    return [pltpu.with_memory_space_constraint(a, VMEM) for a in arrays]


def prepare_kernel(scale_k, x_in, index_in, cell_in, scale_in, x_out, f_out, ft_out, bend_out, shrink_out, index, cell, scale, sems):
    loads = [
        pltpu.make_async_copy(src, dst, sems.at[at])
        for at, (src, dst) in enumerate(((scale_in, scale), (cell_in, cell), (index_in, index), (x_in, x_out)))
    ]
    for load in loads:
        load.start()
    cells, rank = cell.shape
    rows = index.shape[0]
    genes = scale.shape[0]
    loads[0].wait()
    inverse = 1.0 / scale[...].reshape(1, genes)
    bend_out[...] = (inverse * inverse) * (1.0 / (tukey_c * tukey_c))
    shrink_out[...] = jnp.transpose(jnp.broadcast_to(-scale_k * (inverse * inverse), (rank, genes)))
    loads[1].wait()
    table = jnp.transpose(cell[...].astype(jnp.float32)).astype(jnp.bfloat16)
    base = lax.axis_index("row") * cells
    loads[2].wait()
    step = tile_of(rows, 256)
    for at in range(0, rows, step):
        local = index[at : at + step].reshape(1, step) - base
        hot = lax.broadcasted_iota(jnp.int32, (cells, step), 0) == local
        hot = jnp.where(hot, 1.0, 0.0).astype(jnp.bfloat16)
        picked = jnp.dot(table, hot, preferred_element_type=jnp.float32)
        ft_out[:, at : at + step] = picked.astype(jnp.bfloat16)
        f_out[at : at + step, :] = jnp.transpose(picked).astype(jnp.bfloat16)
    loads[3].wait()


def prepare(x_slab, row_index, cell_factor, gene_scale, scale_k):
    rows, genes = x_slab.shape
    cells, rank = cell_factor.shape
    ins = (x_slab, row_index, cell_factor, gene_scale)
    return pl.pallas_call(
        functools.partial(prepare_kernel, scale_k),
        out_shape=(
            VMEM((rows, genes), jnp.bfloat16),
            VMEM((rows, rank), jnp.bfloat16),
            VMEM((rank, rows), jnp.bfloat16),
            VMEM((1, genes), jnp.float32),
            VMEM((genes, rank), jnp.float32),
        ),
        in_specs=[IN_ANY] * 4,
        out_specs=(IN_VMEM,) * 5,
        scratch_shapes=[
            VMEM((rows,), jnp.int32),
            VMEM((cells, rank), jnp.bfloat16),
            VMEM((genes,), jnp.float32),
            pltpu.SemaphoreType.DMA((4,)),
        ],
        compiler_params=params(),
        cost_estimate=cost(2 * rows * cells * rank, 2 * rows * genes * 2),
        name="prepare",
    )(*(pltpu.with_memory_space_constraint(a, pltpu.HBM) for a in ins))


def pick(axis, table):
    me = lax.axis_index(axis)
    value = jnp.int32(table[0])
    for place, entry in enumerate(table[1:], 1):
        value = jnp.where(me == place, jnp.int32(entry), value)
    return value


def partner(me, hop, size):
    return me ^ hop if size & (size - 1) == 0 else (me + hop) % size


def source(me, hop, size):
    return me ^ hop if size & (size - 1) == 0 else (me + size - hop) % size


def rows_kernel(tables, block, first, last, n_row, *refs):
    refs = list(refs)
    take = lambda count: [refs.pop(0) for _ in range(count)]
    x_ref, f_ref, ft_ref, bend_ref, shrink_ref = take(5)
    shares = take(n_row) if first else None
    carried_in = None if first else take(3)
    rows_out = take(len(tables))
    carried_out = None if last else take(3 if first else 1)
    parts_out = take(n_row) if last else None
    me = lax.axis_index("row")

    if first:
        (piece,) = take(1)
        depth = shares[0].shape[0]
        for hop in range(n_row):
            start = pl.multiple_of(source(me, hop, n_row) * depth, depth)
            piece[pl.ds(start, depth), :] = shares[hop][...]
        whole = piece[...].astype(jnp.float32)
        wide = jnp.transpose(whole).astype(jnp.bfloat16)
        scaled = (whole * shrink_ref[...]).astype(jnp.bfloat16)
        total = None
    else:
        total, wide, scaled = (ref[...] for ref in carried_in)

    bend = bend_ref[...]
    step = tile_of(block, 512)
    tiles = []
    for table, out in zip(tables, rows_out):
        origin = pick("gene", table) * block if len(table) > 1 else 0
        for at in range(0, block, step):
            start = origin + at
            if len(table) > 1:
                start = pl.multiple_of(start, math.gcd(block, step))
            tiles.append((out, at, pl.ds(start, step)))

    def predict(here):
        return jnp.dot(f_ref[here, :], wide, preferred_element_type=jnp.float32)

    def gradients(tile, infl, total):
        out, at, here = tile
        cols = jnp.dot(ft_ref[:, here], infl, preferred_element_type=jnp.float32)
        out[at : at + step, :] = jnp.dot(infl, scaled, preferred_element_type=jnp.float32).astype(out.dtype)
        return cols if total is None else total + cols

    pred = predict(tiles[0][2])
    infl = None
    for at, tile in enumerate(tiles):
        later = predict(tiles[at + 1][2]) if at + 1 < len(tiles) else None
        now = influence(x_ref[tile[2], :], pred, bend)
        if at:
            total = gradients(tiles[at - 1], infl, total)
        infl, pred = now, later
    total = gradients(tiles[-1], infl, total)

    if first and not last:
        carried_out[1][...] = wide
        carried_out[2][...] = scaled
    if not last:
        carried_out[0][...] = total
        return
    (turned,) = take(1)
    turned[...] = jnp.transpose(total) * shrink_ref[...]
    depth = parts_out[0].shape[0]
    for hop in range(n_row):
        start = pl.multiple_of(partner(me, hop, n_row) * depth, depth)
        parts_out[hop][...] = turned[pl.ds(start, depth), :].astype(parts_out[hop].dtype)


def block_rows(tables, kinds, block, first, last, n_row, fixed, carried):
    genes, rank = fixed[4].shape
    out = [jax.ShapeDtypeStruct((block, rank), kind) for kind in kinds]
    if last:
        out += [jax.ShapeDtypeStruct((genes // n_row, rank), jnp.bfloat16 if hop else jnp.float32) for hop in range(n_row)]
    else:
        out += [VMEM((rank, genes), jnp.float32)]
    if first and not last:
        out += [VMEM((rank, genes), jnp.bfloat16), VMEM((genes, rank), jnp.bfloat16)]
    scratch = [VMEM((genes, rank), jnp.bfloat16)] if first else []
    if last:
        scratch.append(VMEM((genes, rank), jnp.float32))
    ins = pinned(*fixed) + (list(carried) if first else pinned(*carried))
    work = len(tables) * block * genes
    out = pl.pallas_call(
        functools.partial(rows_kernel, tables, block, first, last, n_row),
        out_shape=tuple(out),
        in_specs=[IN_VMEM] * len(ins),
        out_specs=(IN_VMEM,) * len(out),
        scratch_shapes=scratch,
        compiler_params=params(),
        cost_estimate=cost(6 * work * rank, work * 2),
        name="block_rows",
    )(*ins)
    done, rest = list(out[: len(tables)]), list(out[len(tables) :])
    return done, rest if first or last else rest + list(carried[1:])


def lane_parts(genes, depth, n_row):
    if n_row != 4:
        return None
    pairs = [(2 * depth * (place // 2), 2 * depth * (place // 2 + 1)) for place in range(n_row)]
    low = [-(-begin // 128) * 128 for begin, _ in pairs]
    width = min(end // 128 * 128 - begin for begin, (_, end) in zip(low, pairs))
    if width <= 0 or any(begin not in (0, genes - width) for begin in low):
        return None
    return low, width, [width if begin == 0 else 0 for begin in low]


def lanes(table, width):
    return pl.ds(pl.multiple_of(pick("row", table), 128), width)


def influence(x, pred, bend):
    resid = x.astype(jnp.float32) - pred
    inside = jnp.maximum(1.0 - resid * resid * bend, 0.0)
    return (resid * (inside * inside)).astype(jnp.bfloat16)


def part_of_block(table, block, here, x_ref, f_ref, ft_ref, bend_ref, wide, scaled):
    step = tile_of(block, 256)
    origin = pick("gene", table) * block
    tiles = [pl.ds(pl.multiple_of(origin + at, math.gcd(block, step)), step) for at in range(0, block, step)]
    bend = bend_ref[:, here]
    predict = lambda tile: jnp.dot(f_ref[tile, :], wide, preferred_element_type=jnp.float32)
    rows, total = [], None
    pred, behind = predict(tiles[0]), None
    for at, tile in enumerate([*tiles, None]):
        now = None
        if tile is not None:
            later = predict(tiles[at + 1]) if at + 1 < len(tiles) else None
            now = tile, influence(x_ref[tile, here], pred, bend)
            pred = later
        if behind is not None:
            last, infl = behind
            cols = jnp.dot(ft_ref[:, last], infl, preferred_element_type=jnp.float32)
            rows.append(jnp.dot(infl, scaled, preferred_element_type=jnp.float32))
            total = cols if total is None else total + cols
        behind = now
    return rows, total


def early_kernel(table, block, parts, x_ref, f_ref, ft_ref, bend_ref, shrink_ref, own, other, *refs):
    rows_out, total_out, wide_out, scaled_out, pair = refs
    low, width, _ = parts
    depth = own.shape[0]
    odd = lax.axis_index("row") % 2
    pair[pl.ds(pl.multiple_of(odd * depth, depth), depth), :] = own[...]
    pair[pl.ds(pl.multiple_of((1 - odd) * depth, depth), depth), :] = other[...]
    inset = [begin - 2 * depth * (place // 2) for place, begin in enumerate(low)]
    whole = pair[pl.ds(pl.multiple_of(pick("row", inset), math.gcd(*inset, 128)), width), :].astype(jnp.float32)
    here = lanes(low, width)
    wide = jnp.transpose(whole).astype(jnp.bfloat16)
    scaled = (whole * shrink_ref[here, :]).astype(jnp.bfloat16)
    wide_out[...] = wide
    scaled_out[...] = scaled
    rows, total = part_of_block(table, block, here, x_ref, f_ref, ft_ref, bend_ref, wide, scaled)
    for at, value in enumerate(rows):
        rows_out[at * value.shape[0] : (at + 1) * value.shape[0], :] = value
    total_out[...] = total


def rest_kernel(table, block, parts, n_row, x_ref, f_ref, ft_ref, bend_ref, shrink_ref, *refs):
    shares, (rows_in, total_in, wide_in, scaled_in) = refs[:n_row], refs[n_row : n_row + 4]
    rows_out, total_out, wide_out, scaled_out, piece = refs[n_row + 4 :]
    low, width, rest = parts
    me = lax.axis_index("row")
    depth = shares[0].shape[0]
    for hop in range(n_row):
        start = pl.multiple_of(source(me, hop, n_row) * depth, depth)
        piece[pl.ds(start, depth), :] = shares[hop][...]
    here = lanes(rest, n_row * depth - width)
    whole = piece[here, :].astype(jnp.float32)
    wide = jnp.transpose(whole).astype(jnp.bfloat16)
    scaled = (whole * shrink_ref[here, :]).astype(jnp.bfloat16)
    rows, total = part_of_block(table, block, here, x_ref, f_ref, ft_ref, bend_ref, wide, scaled)
    for at, value in enumerate(rows):
        span = slice(at * value.shape[0], (at + 1) * value.shape[0])
        rows_out[span, :] = (rows_in[span, :] + value).astype(rows_out.dtype)
    done = lanes(low, width)
    total_out[:, here] = total
    total_out[:, done] = total_in[...]
    wide_out[:, here] = wide
    wide_out[:, done] = wide_in[...]
    scaled_out[here, :] = scaled
    scaled_out[done, :] = scaled_in[...]


def first_block(table, block, parts, n_row, fixed, shares):
    genes, rank = fixed[4].shape
    depth = genes // n_row
    width = parts[1]
    ins = pinned(*fixed)
    early = pl.pallas_call(
        functools.partial(early_kernel, table, block, parts),
        out_shape=(
            VMEM((block, rank), jnp.float32),
            VMEM((rank, width), jnp.float32),
            VMEM((rank, width), jnp.bfloat16),
            VMEM((width, rank), jnp.bfloat16),
        ),
        in_specs=[IN_VMEM] * 7,
        out_specs=(IN_VMEM,) * 4,
        scratch_shapes=[VMEM((2 * depth, rank), jnp.bfloat16)],
        compiler_params=params(),
        cost_estimate=cost(12 * block * width * rank, block * width * 4),
        name="early_part",
    )(*ins, *shares[:2])
    done, *carried = pl.pallas_call(
        functools.partial(rest_kernel, table, block, parts, n_row),
        out_shape=(
            jax.ShapeDtypeStruct((block, rank), jnp.bfloat16),
            VMEM((rank, genes), jnp.float32),
            VMEM((rank, genes), jnp.bfloat16),
            VMEM((genes, rank), jnp.bfloat16),
        ),
        in_specs=[IN_VMEM] * (9 + n_row),
        out_specs=(IN_VMEM,) * 4,
        scratch_shapes=[VMEM((genes, rank), jnp.bfloat16)],
        compiler_params=params(),
        cost_estimate=cost(12 * block * (genes - width) * rank, block * (genes - width) * 4),
        name="rest_part",
    )(*ins, *shares, *pinned(*early))
    return [done], carried


def swap_row(value, hop, size):
    return lax.ppermute(value, "row", [(me, partner(me, hop, size)) for me in range(size)])


def ring_of(size):
    return [*range(0, size, 2), *reversed(range(1, size, 2))]


def steps_of(size):
    ahead = [(1, distance) for distance in range(size // 2, 0, -1)]
    back = [(-1, distance) for distance in range((size - 1) // 2, 0, -1)]
    return [step for pair in itertools.zip_longest(ahead, back) for step in pair if step]


def around(size, hops):
    ring = ring_of(size)
    return tuple(ring[(ring.index(place) + hops) % size] for place in range(size))


def plus(wide, narrow):
    return wide.astype(jnp.float32) + narrow.astype(jnp.float32)


def finish_kernel(n_ends, n_parts, *refs):
    n_ins = n_ends + n_parts + 3
    ins, outs = refs[:n_ins], refs[n_ins : n_ins + 3 + bool(n_ends)]
    *held, sems = refs[n_ins + len(outs) :]
    ends, parts = ins[:n_ends], ins[n_ends : n_ends + n_parts]
    factor, first, second = ins[n_ends + n_parts :]
    copies = []

    def send(at, span, value):
        held[at][span, :] = value
        copies.append(pltpu.make_async_copy(held[at].at[span, :], outs[at].at[span, :], sems.at[len(copies)]))
        copies[-1].start()

    if ends:
        step = tile_of(ends[0].shape[0], 512)
        for low in range(0, ends[0].shape[0], step):
            span = pl.ds(low, step)
            rows = ends[0][span, :]
            for end in ends[1:]:
                rows = plus(rows, end[span, :])
            send(3, span, rows)
    grad = parts[0][...]
    for part in parts[1:]:
        grad = plus(grad, part[...])
    span = pl.ds(0, grad.shape[0])
    new_first = beta_one * first[...] + (1.0 - beta_one) * grad
    new_second = beta_two * second[...] + (1.0 - beta_two) * grad * grad
    send(1, span, new_first)
    send(2, span, new_second)
    first_hat = new_first / (1.0 - beta_one**10)
    second_hat = new_second / (1.0 - beta_two**10)
    send(0, span, factor[...] - learn_rate * first_hat / (jnp.sqrt(second_hat) + adam_eps))
    for copy in copies:
        copy.wait()


def finish(ends, parts, factor, first, second):
    ins = [*ends, *parts, factor, first, second]
    shapes = [factor, factor, factor] + list(ends[:1])
    n_copies = 3 + (ends[0].shape[0] // tile_of(ends[0].shape[0], 512) if ends else 0)
    return pl.pallas_call(
        functools.partial(finish_kernel, len(ends), len(parts)),
        out_shape=tuple(jax.ShapeDtypeStruct(like.shape, jnp.float32) for like in shapes),
        in_specs=[IN_VMEM] * len(ins),
        out_specs=(IN_ANY,) * len(shapes),
        scratch_shapes=[VMEM(like.shape, jnp.float32) for like in shapes] + [pltpu.SemaphoreType.DMA((n_copies,))],
        compiler_params=params(),
        cost_estimate=cost(20 * factor.size, sum(4 * a.size for a in ins)),
        name="finish",
    )(*ins)


def local(x_slab, cell_factor, row_index, gene_scale, gene_factor, first_moment, second_moment):
    rows_dev, genes_dev = x_slab.shape
    n_gene = lax.axis_size("gene")
    n_row = lax.axis_size("row")
    block = rows_dev // n_gene
    scale_k = 4.0 / math.sqrt(genes_dev * n_gene)
    factor_bf = gene_factor.astype(jnp.bfloat16)
    shares = [factor_bf] + [swap_row(factor_bf, hop, n_row) for hop in range(1, n_row)]
    fixed = prepare(x_slab, row_index, cell_factor, gene_scale, scale_k)
    adam = (gene_factor, first_moment, second_moment)

    if n_gene == 1 or n_gene > RING_MOST or block % 128:
        (rows,), parts = block_rows([(0,)], [jnp.float32], rows_dev, True, True, n_row, fixed, shares)
        grad_cells = lax.psum_scatter(rows, "gene", scatter_dimension=0, tiled=True)
        others = [swap_row(parts[hop], hop, n_row) for hop in reversed(range(1, n_row))]
        return (grad_cells, *finish([], [parts[0], *others], *adam))

    steps = steps_of(n_gene)
    tables = [around(n_gene, way * distance) for way, distance in steps] + [tuple(range(n_gene))]
    kinds = [jnp.bfloat16] * len(steps) + [jnp.float32]
    cuts = [0, 1, 2, len(tables)] if len(steps) > 2 else [0, 1, len(tables)]
    parted = lane_parts(genes_dev, genes_dev // n_row, n_row)
    carried, blocks = shares, []
    for low, high in zip(cuts, cuts[1:]):
        last = high == len(tables)
        if low == 0 and parted:
            done, carried = first_block(tables[0], block, parted, n_row, fixed, shares)
            blocks += done
            continue
        done, carried = block_rows(tables[low:high], kinds[low:high], block, low == 0, last, n_row, fixed, carried)
        blocks += done
    parts = carried

    came = {}
    for (way, _), own in zip(steps, blocks):
        if way in came:
            own = plus(own, came[way]).astype(jnp.bfloat16)
        came[way] = lax.ppermute(own, "gene", list(enumerate(around(n_gene, way))))
    others = [swap_row(parts[hop], hop, n_row) for hop in reversed(range(1, n_row))]
    *adam_out, grad_cells = finish([blocks[-1], *came.values()], [parts[0], *others], *adam)
    return (grad_cells, *adam_out)


def solution(mesh):
    in_specs = (
        P(("grp", "row"), "gene"),
        P(("grp", "row"), None),
        P(("grp", "row")),
        P(("grp", "gene")),
        P(("grp", "gene", "row"), None),
        P(("grp", "gene", "row"), None),
        P(("grp", "gene", "row"), None),
    )
    out_specs = (
        P(("grp", "row", "gene"), None),
        P(("grp", "gene", "row"), None),
        P(("grp", "gene", "row"), None),
        P(("grp", "gene", "row"), None),
    )
    return jax.shard_map(local, mesh=mesh, in_specs=in_specs, out_specs=out_specs, check_vma=False)
```
